32 devices in a mesh: fibre: 8 (over y, x, core), tm: 4 (over z).
Axes of the slice: x: 2, y: 2, z: 4, core: 2. Of those that a mesh axis runs over, the one named last changes fastest.
Arguments:
- samples: bfloat16 [1024, 32, 1024], P('fibre', 'tm'), may hold values from -24 to 24
- band_gain: float32 [512], replicated, may hold values from 0.1 to 1
- dead_flags: int32 [1024], P('fibre'), may hold values 0 or 1
- section_ids: int32 [1024], P('fibre'), may hold values from 0 to 1, never falling along the last dimension, each value on 1 to 768 neighbouring positions
Outputs:
- stack: float32 [1024, 128, 128], P('fibre', 'tm')
The draws below stay inside these ranges and needn't reach their ends.
Inputs may be any that keep to these rules, and one draw needn't show every extreme that they name: `section_ids`: section numbers never fall along the channels; each section holds 1 to 768 channels.
All inputs are finite; a program needn't handle non-finite values. No bound on the sum of `dead_flags` on one device may be relied on, other than what follows from the above.
Results may differ from the reference program's by a relative error of at most 0.008.
Values may be sent and summed in bfloat16 or wider, within the bound.
No kernel may reach another device: no remote copies, remote signals or barrier semaphores. Data moves between devices by JAX's collectives and lax.ppermute only.
A program may use at most 64 MiB of HBM per device.

```python
import math
import jax
import jax.numpy as jnp
import numpy as np
from jax import lax

C_DEV = 128
SW_DEV = 8
NS = 1024
OFFS = 128
LAGS = 128
OBLK = 8
NSEC = 2
F = 512
CHANNELS = 1024
SUBWIN = 32
N_TM = 4


def draw_samples(key, part):
    base = jax.random.fold_in(key, 11)
    key_amp = jax.random.fold_in(base, 1)
    key_sig = jax.random.fold_in(base, 2)
    key_noise = jax.random.fold_in(base, 3)
    place = jnp.arange(CHANNELS, dtype=jnp.float32).reshape(CHANNELS, 1, 1) / CHANNELS
    rough = jax.random.uniform(key_amp, (CHANNELS, 1, 1), jnp.float32, -0.35, 0.35)
    coupling = jnp.exp(math.log(0.25) + math.log(16.0) * place + rough)
    noise = jax.random.truncated_normal(key_noise, -4.0, 4.0, (CHANNELS, SUBWIN, NS), jnp.float32)
    signal = jax.random.truncated_normal(key_sig, -3.0, 3.0, (1, SUBWIN, NS), jnp.float32)
    return (noise + coupling * signal).astype(jnp.bfloat16)


def plant(array, stream_key, least, largest):
    extent = array.shape
    spot = [jax.random.randint(jax.random.fold_in(stream_key, axis), (), 0, extent[axis]) for axis in range(len(extent))]
    array = array.at[tuple(spot)].set(least)
    longest = extent.index(max(extent))
    spot[longest] = (spot[longest] + 1) % extent[longest]
    return array.at[tuple(spot)].set(largest)


def profile(amount, total, bound, lean):
    portions = [(1 << 20) // math.isqrt(standing ** lean) + 1 for standing in range(2, amount + 1)]
    surplus, holding = total - bound - (amount - 1), [1] * (amount - 1)
    while surplus > 0:
        candidates = [i for i in range(amount - 1) if holding[i] < bound]
        whole, remaining = sum([portions[i] for i in candidates]), surplus
        for i in candidates:
            addition = min(bound - holding[i], max(1, remaining * portions[i] // whole), surplus)
            holding[i] = holding[i] + addition
            surplus = surplus - addition
    return np.array([bound] + holding)


def ragged(stream_key, number_of, total, bound, slope):
    if number_of == 2:
        one = jax.random.randint(stream_key, (), max(1, total - bound), min(bound, total - 1) + 1)
        return jnp.stack([one, total - one])
    lengths = jnp.asarray(profile(number_of, total, bound, slope), jnp.int32)
    twos = (number_of - 1) // 2
    source_of, receiver = lengths[1:1 + 2 * twos:2], lengths[2:2 + 2 * twos:2]
    room = jnp.minimum(source_of - 1, bound - receiver)
    passed = jax.random.randint(jax.random.fold_in(stream_key, 1), (twos,), 0, 1 << 20) % (room + 1)
    lengths = lengths.at[1:1 + 2 * twos:2].set(source_of - passed).at[2:2 + 2 * twos:2].set(receiver + passed)
    return lengths[jax.random.permutation(jax.random.fold_in(stream_key, 2), number_of)]


def setup_inputs(seed: int = 0) -> dict:
    streams_of = jax.random.split(jax.random.key(seed), 5)
    return {
        "samples": draw_samples(jax.random.fold_in(streams_of[4], 71), 0),
        "band_gain": jnp.clip(jnp.exp(jax.random.uniform(streams_of[1], (F,), jnp.float32, math.log(0.1), math.log(1.0))), 0.1, 1.0),
        "dead_flags": plant((jax.random.randint(streams_of[2], (CHANNELS,), 0, 8) < 1).astype(jnp.int32), jax.random.fold_in(streams_of[2], 1), 0, 1),
        "section_ids": jnp.searchsorted(jnp.cumsum(ragged(streams_of[3], NSEC, CHANNELS, CHANNELS - CHANNELS // (2 * NSEC), 1)), jnp.arange(CHANNELS), side="right").astype(jnp.int32),
    }


def tables(ns, nf, nlag):
    tick = jnp.arange(ns, dtype=jnp.int32)
    freq = jnp.arange(nf, dtype=jnp.int32)
    phase = (tick[:, None] * freq[None, :] % ns).astype(jnp.float32) * (2.0 * math.pi / ns)
    window = 0.5 - 0.5 * jnp.cos(tick.astype(jnp.float32) * (2.0 * math.pi / ns))
    forward = jnp.concatenate([window[:, None] * jnp.cos(phase), -window[:, None] * jnp.sin(phase)], axis=1).astype(jnp.bfloat16)
    shifts = jnp.arange(nlag, dtype=jnp.int32) - nlag // 2
    turn = (freq[:, None] * shifts[None, :] % ns).astype(jnp.float32) * (2.0 * math.pi / ns)
    inverse = jnp.concatenate([jnp.cos(turn), -jnp.sin(turn)], axis=0).astype(jnp.bfloat16)
    return (forward, inverse)

def reference(samples, band_gain, dead_flags, section_ids):
    nf = NS // 2
    nblocks = CHANNELS // C_DEV
    live = (1 - dead_flags).astype(jnp.float32)
    member = (section_ids[:, None] == jnp.arange(NSEC, dtype=jnp.int32)[None, :]).astype(jnp.float32)
    weighted = (member * live[:, None]).astype(jnp.bfloat16)
    flat = samples.reshape(CHANNELS, SUBWIN * NS)
    sec_sum = lax.dot_general(weighted, flat, (((0,), (0,)), ((), ())), preferred_element_type=jnp.float32)
    sec_count = lax.optimization_barrier(jnp.sum(member * live[:, None], axis=0))
    common = sec_sum / jnp.maximum(sec_count, 1.0)[:, None]
    forward, inverse = tables(NS, nf, LAGS)
    gain_pair = jnp.concatenate([band_gain, band_gain])

    def whiten_block(index):
        start = (index * C_DEV).astype(jnp.int32)
        block = lax.dynamic_slice_in_dim(flat, start, C_DEV, 0)
        block_member = lax.dynamic_slice_in_dim(member, start, C_DEV, 0)
        block_live = lax.dynamic_slice_in_dim(live, start, C_DEV, 0)
        local_common = jnp.dot(block_member, common, precision=lax.Precision.HIGHEST)
        cleaned = ((block.astype(jnp.float32) - local_common) * block_live[:, None]).astype(jnp.bfloat16)
        spec = jnp.dot(cleaned.reshape(C_DEV * SUBWIN, NS), forward, preferred_element_type=jnp.float32)
        power = lax.optimization_barrier(jnp.mean(spec * spec, axis=-1, keepdims=True))
        white = (spec * gain_pair * lax.rsqrt(power + 1e-06)).astype(jnp.bfloat16)
        return white.reshape(C_DEV, SUBWIN, 2 * nf)
    white = lax.map(whiten_block, jnp.arange(nblocks, dtype=jnp.int32)).reshape(CHANNELS, SUBWIN, 2 * nf)
    extended = jnp.concatenate([white, white[:OFFS]], axis=0)
    scale = 1.0 / math.sqrt(nf * SUBWIN)

    def correlate_block(index):
        start = (index * C_DEV).astype(jnp.int32)
        own = lax.dynamic_slice_in_dim(extended, start, C_DEV, 0).astype(jnp.float32).reshape(C_DEV, N_TM, SW_DEV, 2 * nf)
        near = lax.dynamic_slice_in_dim(extended, start, C_DEV + OFFS, 0)

        def one_group(step, buffer):
            first = (step * OBLK).astype(jnp.int32)
            rows = []
            for inner in range(OBLK):
                partner = lax.dynamic_slice_in_dim(near, first + inner + 1, C_DEV, 0).astype(jnp.float32).reshape(C_DEV, N_TM, SW_DEV, 2 * nf)
                pr, pi = (own[..., :nf], own[..., nf:])
                qr, qi = (partner[..., :nf], partner[..., nf:])
                real = lax.optimization_barrier(jnp.sum(pr * qr + pi * qi, axis=2))
                imag = lax.optimization_barrier(jnp.sum(pi * qr - pr * qi, axis=2))
                rows.append(jnp.concatenate([real, imag], axis=-1))
            cross = jnp.stack(rows, axis=1).astype(jnp.bfloat16)
            lagged = jnp.dot(cross.reshape(C_DEV * OBLK * N_TM, 2 * nf), inverse, preferred_element_type=jnp.float32) * scale
            lagged = lagged.astype(jnp.bfloat16)
            lagged = lax.optimization_barrier(lagged).astype(jnp.float32)
            summed = lax.optimization_barrier(jnp.sum(lagged.reshape(C_DEV, OBLK, N_TM, LAGS), axis=2))
            return lax.dynamic_update_slice_in_dim(buffer, summed, first, 1)
        return lax.fori_loop(0, OFFS // OBLK, one_group, jnp.zeros((C_DEV, OFFS, LAGS), jnp.float32))
    out = lax.map(correlate_block, jnp.arange(nblocks, dtype=jnp.int32))
    return out.reshape(CHANNELS, OFFS, LAGS)
```

```python
import functools
import math

import jax
import jax.numpy as jnp
import ml_dtypes
import numpy as np
from jax import lax
from jax.experimental import pallas as pl
from jax.experimental.pallas import tpu as pltpu
from jax.sharding import PartitionSpec as P

OFFS = 128
LAGS = 128
NSEC = 2
LANE = 128
CHUNKS = 2
VMEM = 56 * 1024 * 1024
NT = (((1,), (1,)), ((), ()))
F32 = jnp.float32
BF16 = jnp.bfloat16


def tables(ns, nf):
    tick = np.arange(ns)
    freq = np.arange(nf)
    phase = (tick[:, None] * freq[None, :] % ns) * (2.0 * math.pi / ns)
    window = 0.5 - 0.5 * np.cos(tick * (2.0 * math.pi / ns))
    forward = np.concatenate(
        [window[:, None] * np.cos(phase), -window[:, None] * np.sin(phase)], axis=1
    )
    back = np.concatenate([np.cos(phase), -np.sin(phase)], axis=1)
    back[:, 0] *= math.sqrt(0.5)
    size = 2 * LAGS
    bins = np.arange(size // 2)
    turn = math.pi / size * ((2 * bins[:, None] + 1) * np.arange(size)[None, :] % (2 * size))
    segment = np.stack([np.cos(turn), -np.sin(turn)], axis=1).reshape(size, size)
    lag = np.stack([np.cos(turn), -np.sin(turn)], axis=1).reshape(size, size)[:, :LAGS]
    cast = lambda a: a.astype(np.float32).astype(ml_dtypes.bfloat16)
    return cast(forward.T), cast(back), cast(segment), cast(lag)


def section_sums(dead_ref, sec_ref, x_ref, out_ref):
    chans, wins, ns = x_ref.shape

    def body(c, carry):
        value = x_ref[c].astype(F32)
        live = 1 - dead_ref[c]
        sums, counts = carry
        weights = [jnp.where(sec_ref[c] == s, live, 0).astype(F32) for s in range(NSEC)]
        return (
            tuple(sums[s] + weights[s] * value for s in range(NSEC)),
            tuple(counts[s] + weights[s] for s in range(NSEC)),
        )

    zero = jnp.zeros((wins, ns), F32)
    sums, counts = lax.fori_loop(
        0, chans, body, ((zero,) * NSEC, (jnp.float32(0),) * NSEC), unroll=4
    )
    for s in range(NSEC):
        out_ref[s, :, :ns] = sums[s]
        out_ref[s, :, ns:] = jnp.zeros((wins, LANE), F32) + counts[s]


def segments_kernel(
    both, dead_ref, sec_ref, x_ref, tot_ref, gain_ref, fwd_ref, back_ref, seg_ref, *rest
):
    if both:
        a_ref, b_ref, common, clean, rows, spec, white, series, a_s, b_s = rest
    else:
        b_ref, common, clean, rows, spec, white, series, b_s = rest
    chans, wins, ns = x_ref.shape
    nfr = spec.shape[0]
    pitch = wins + 1
    size = seg_ref.shape[0]
    half = size // 2
    blocks = ns // half
    jw = blocks * wins
    jpitch = jw + 1
    for s in range(NSEC):
        common[s] = tot_ref[s, :, :ns] / jnp.maximum(tot_ref[s, :, ns : ns + 1], 1.0)

    def clean_channel(c, _):
        live = (1 - dead_ref[c]).astype(F32)
        value = (x_ref[c].astype(F32) - common[sec_ref[c]]) * live
        for t in range(ns // LANE):
            clean[t, pl.ds(c * pitch, wins), :] = value[:, t * LANE : (t + 1) * LANE]
        return 0

    lax.fori_loop(0, chans, clean_channel, 0, unroll=4)

    def pair(step, _):
        for i in range(2):
            w = step * 2 + i
            for t in range(ns // LANE):
                rows[i * chans : (i + 1) * chans, t * LANE : (t + 1) * LANE] = clean[
                    t, pl.ds(w, chans, stride=pitch), :
                ].astype(BF16)
        power = jnp.zeros((1, 2 * chans), F32)
        tile = 256
        for f in range(nfr // tile):
            s = lax.dot_general(
                fwd_ref[f * tile : (f + 1) * tile, :], rows[...], NT, preferred_element_type=F32
            )
            spec[f * tile : (f + 1) * tile, :] = s
            power = power + jnp.sum(s * s, axis=0, keepdims=True)
        level = lax.rsqrt(power / nfr + 1e-06)
        for i in range(2):
            white[:, i * chans : (i + 1) * chans] = (
                spec[:, i * chans : (i + 1) * chans]
                * gain_ref[...]
                * level[:, i * chans : (i + 1) * chans]
            ).astype(BF16)
        for t in range(ns // tile):
            p = jnp.dot(
                back_ref[t * tile : (t + 1) * tile, :], white[...], preferred_element_type=F32
            ).astype(BF16)
            series[half // 2 + t * tile : half // 2 + (t + 1) * tile, :] = p
        series[: half // 2, :] = series[ns : ns + half // 2, :]
        series[ns + half // 2 :, :] = series[half // 2 : half, :]
        for j in range(blocks):
            if both:
                a = jnp.dot(
                    seg_ref[...], series[j * half : j * half + size, :], preferred_element_type=F32
                )
            b = jnp.dot(
                seg_ref[:, :half],
                series[j * half + half // 2 : j * half + half // 2 + half, :],
                preferred_element_type=F32,
            )
            for i in range(2):
                at = j * wins + step * 2 + i
                if both:
                    a_s[pl.ds(at, size, stride=jpitch), :] = a[:, i * chans : (i + 1) * chans]
                b_s[pl.ds(at, size, stride=jpitch), :] = b[:, i * chans : (i + 1) * chans]
        return 0

    lax.fori_loop(0, wins // 2, pair, 0)

    def one_bin(k, _):
        def both_parts(ref):
            return jnp.concatenate(
                [
                    ref[pl.ds(2 * k * jpitch, jw), :],
                    ref[pl.ds((2 * k + 1) * jpitch, jw), :],
                ],
                axis=0,
            )

        if both:
            a_ref[k] = both_parts(a_s).T.astype(BF16)
        b_ref[k] = both_parts(b_s).astype(BF16)
        return 0

    lax.fori_loop(0, half, one_bin, 0, unroll=2)


def segments(both, flags, x, total, gain, fwd, back, seg):
    chans, wins, ns = x.shape
    nfr = fwd.shape[0]
    size = seg.shape[0]
    half = size // 2
    depth = ns // half * wins * 2
    smem = pl.BlockSpec(memory_space=pltpu.SMEM)
    vmem = pl.BlockSpec(memory_space=pltpu.VMEM)
    out = [jax.ShapeDtypeStruct((half, depth, chans), BF16)]
    stage = [pltpu.VMEM((size * (depth // 2 + 1), chans), F32)]
    if both:
        out = [jax.ShapeDtypeStruct((half, chans, depth), BF16)] + out
        stage = stage * 2
    return pl.pallas_call(
        functools.partial(segments_kernel, both),
        out_shape=out,
        in_specs=[smem, smem] + [vmem] * 6,
        out_specs=[vmem] * len(out),
        scratch_shapes=[
            pltpu.VMEM((NSEC, wins, ns), F32),
            pltpu.VMEM((ns // LANE, chans * (wins + 1), LANE), F32),
            pltpu.VMEM((2 * chans, ns), BF16),
            pltpu.VMEM((nfr, 2 * chans), F32),
            pltpu.VMEM((nfr, 2 * chans), BF16),
            pltpu.VMEM((ns + half, 2 * chans), BF16),
        ]
        + stage,
        compiler_params=pltpu.CompilerParams(vmem_limit_bytes=VMEM),
        cost_estimate=pl.CostEstimate(
            flops=2 * wins * chans * ns * (2 * nfr + 3 * size),
            bytes_accessed=16 * 1024 * 1024,
            transcendentals=0,
        ),
    )(flags[0], flags[1], x, total, gain, fwd, back, seg)


def stack_kernel(first, scale, a_ref, b_ref, h_ref, lag_ref, out_ref, cross, one):
    bins, count, depth = a_ref.shape
    chans = b_ref.shape[2]
    nfr = 2 * bins
    pitch = nfr + 1
    row = lax.broadcasted_iota(jnp.int32, one.shape[1:], 0)
    column = lax.broadcasted_iota(jnp.int32, one.shape[1:], 1)
    for t in range(2):
        one[t] = jnp.where(row == column + t * chans, 1.0, 0.0)

    def one_bin(k, _):
        left = a_ref[k]
        for t, ref in enumerate((b_ref, h_ref)):
            right = ref[k]
            turned = jnp.concatenate([-right[depth // 2 :], right[: depth // 2]], axis=0)
            cross[t, pl.ds(2 * k, count, stride=pitch), :] = jnp.dot(
                left, right, preferred_element_type=F32
            )
            cross[t, pl.ds(2 * k + 1, count, stride=pitch), :] = jnp.dot(
                left, turned, preferred_element_type=F32
            )
        return 0

    lax.fori_loop(0, bins, one_bin, 0, unroll=2)
    shares, _, share, nlag = out_ref.shape

    def one_channel(c, _):
        value = jnp.concatenate(
            [cross[t, pl.ds(c * pitch, nfr), :] for t in range(2)], axis=1
        ).astype(BF16)
        pick = jnp.concatenate(
            [one[t, pl.ds(first + c + 1, OFFS), :] for t in range(2)], axis=1
        ).astype(BF16)
        band = lax.dot_general(pick, value, NT, preferred_element_type=F32).astype(BF16)
        lagged = jnp.dot(band, lag_ref[...], preferred_element_type=F32) * scale
        lagged = lagged.astype(BF16)
        for s in range(shares):
            out_ref[s, c] = lagged[s * share : (s + 1) * share, :]
        return 0

    lax.fori_loop(0, count, one_channel, 0, unroll=2)


def stacks(index, count, shares, scale, a, b, h, lag):
    bins, chans, depth = a.shape
    nlag = lag.shape[1]
    whole = lambda arr: pl.BlockSpec(arr.shape, lambda i: (0,) * arr.ndim)
    return pl.pallas_call(
        functools.partial(stack_kernel, index * count, scale),
        grid=(1,),
        out_shape=jax.ShapeDtypeStruct((shares, count, OFFS // shares, nlag), BF16),
        in_specs=[
            pl.BlockSpec((bins, count, depth), lambda i: (0, index, 0)),
            whole(b),
            whole(h),
            whole(lag),
        ],
        out_specs=pl.BlockSpec(
            (shares, count, OFFS // shares, nlag), lambda i: (0, 0, 0, 0)
        ),
        scratch_shapes=[
            pltpu.VMEM((2, count * (2 * bins + 1), chans), F32),
            pltpu.VMEM((2, chans + OFFS, chans), F32),
        ],
        compiler_params=pltpu.CompilerParams(vmem_limit_bytes=VMEM),
        cost_estimate=pl.CostEstimate(
            flops=2 * count * bins * 2 * (2 * depth * chans + 2 * OFFS * chans + OFFS * nlag),
            bytes_accessed=12 * 1024 * 1024,
            transcendentals=0,
        ),
    )(a, b, h, lag)


def add_over(value, axis):
    count = lax.axis_size(axis)
    if count & (count - 1):
        return lax.psum(value, axis)
    bit = 1
    while bit < count:
        value = value + lax.ppermute(value, axis, [(i, i ^ bit) for i in range(count)])
        bit *= 2
    return value


def scatter_sum(parts, axis):
    count = lax.axis_size(axis)
    me = lax.axis_index(axis)

    def take(s):
        return lax.dynamic_index_in_dim(parts, s, 0, keepdims=False).astype(F32)

    total = take(me)
    for way in (1, -1):
        arrived = None
        place = me if way == 1 else count - 1 - me
        for step in range(count - 1):
            s = (count - 1 - step + place) % count
            s = s if way == 1 else count - 1 - s
            value = take(s)
            if arrived is not None:
                value = value + arrived.astype(F32)
            line = range(count) if way == 1 else range(count - 1, -1, -1)
            pairs = [(z, z + way) for z in list(line)[: step + 1]]
            arrived = lax.ppermute(value.astype(BF16), axis, pairs)
        total = total + arrived.astype(F32)
    return total


def shards(samples, band_gain, dead_flags, section_ids):
    chans, wins, ns = samples.shape
    nf = ns // 2
    blocks = lax.axis_size("fibre")
    groups = lax.axis_size("tm")
    fwd, back, seg, lag = [jnp.asarray(t) for t in tables(ns, nf)]
    flags = jnp.stack([dead_flags, section_ids])
    ahead = [((i + 1) % blocks, i) for i in range(blocks)]
    smem = pl.BlockSpec(memory_space=pltpu.SMEM)
    vmem = pl.BlockSpec(memory_space=pltpu.VMEM)
    sums = pl.pallas_call(
        section_sums,
        out_shape=jax.ShapeDtypeStruct((NSEC, wins, ns + LANE), F32),
        in_specs=[smem, smem, vmem],
        out_specs=vmem,
        compiler_params=pltpu.CompilerParams(vmem_limit_bytes=VMEM),
    )(dead_flags, section_ids, samples)
    total = add_over(sums, "fibre")
    next_flags = lax.ppermute(flags, "fibre", ahead)
    next_samples = lax.ppermute(samples, "fibre", ahead)
    gain = jnp.broadcast_to(jnp.concatenate([band_gain, band_gain])[:, None], (2 * nf, chans))
    a, b = segments(True, (dead_flags, section_ids), samples, total, gain, fwd, back, seg)
    (h,) = segments(False, next_flags, next_samples, total, gain, fwd, back, seg)
    scale = 2.0 / ns / LAGS / math.sqrt(nf * wins * groups)
    count = chans // CHUNKS
    out = []
    for index in range(CHUNKS):
        parts = stacks(index, count, groups, scale, a, b, h, lag)
        out.append(scatter_sum(parts, "tm"))
    return jnp.concatenate(out, axis=0)


def solution(mesh):
    in_specs = (P("fibre", "tm", None), P(), P("fibre"), P("fibre"))
    out_specs = P("fibre", "tm", None)
    return jax.shard_map(shards, mesh=mesh, in_specs=in_specs, out_specs=out_specs, check_vma=False)
```

```python
import functools
import math

import jax
import jax.numpy as jnp
import ml_dtypes
import numpy as np
from jax import lax
from jax.experimental import pallas as pl
from jax.experimental.pallas import tpu as pltpu
from jax.sharding import PartitionSpec as P

OFFS = 128
LAGS = 128
NSEC = 2
LANE = 128
CHUNKS = 2
VMEM = 56 * 1024 * 1024
NT = (((1,), (1,)), ((), ()))
F32 = jnp.float32
BF16 = jnp.bfloat16


def tables(ns, nf):
    tick = np.arange(ns)
    freq = np.arange(nf)
    phase = (tick[:, None] * freq[None, :] % ns) * (2.0 * math.pi / ns)
    window = 0.5 - 0.5 * np.cos(tick * (2.0 * math.pi / ns))
    forward = np.concatenate(
        [window[:, None] * np.cos(phase), -window[:, None] * np.sin(phase)], axis=1
    )
    back = np.concatenate([np.cos(phase), -np.sin(phase)], axis=1)
    back[:, 0] *= math.sqrt(0.5)
    size = 2 * LAGS
    bins = np.arange(size // 2)
    turn = math.pi / size * ((2 * bins[:, None] + 1) * np.arange(size)[None, :] % (2 * size))
    segment = np.stack([np.cos(turn), -np.sin(turn)], axis=1).reshape(size, size)
    lag = np.stack([np.cos(turn), -np.sin(turn)], axis=1).reshape(size, size)[:, :LAGS].T
    cast = lambda a: a.astype(np.float32).astype(ml_dtypes.bfloat16)
    return cast(forward.T), cast(back), cast(segment), cast(lag)


def section_sums(dead_ref, sec_ref, x_ref, out_ref):
    chans, wins, ns = x_ref.shape

    def body(c, carry):
        value = x_ref[c].astype(F32)
        live = 1 - dead_ref[c]
        sums, counts = carry
        weights = [jnp.where(sec_ref[c] == s, live, 0).astype(F32) for s in range(NSEC)]
        return (
            tuple(sums[s] + weights[s] * value for s in range(NSEC)),
            tuple(counts[s] + weights[s] for s in range(NSEC)),
        )

    zero = jnp.zeros((wins, ns), F32)
    sums, counts = lax.fori_loop(
        0, chans, body, ((zero,) * NSEC, (jnp.float32(0),) * NSEC), unroll=4
    )
    for s in range(NSEC):
        out_ref[s, :, :ns] = sums[s]
        out_ref[s, :, ns:] = jnp.zeros((wins, LANE), F32) + counts[s]


def segments_kernel(
    both, dead_ref, sec_ref, x_ref, tot_ref, gain_ref, fwd_ref, back_ref, seg_ref, *rest
):
    if both:
        a_ref, b_ref, common, clean, rows, spec, white, series, a_s, b_s = rest
    else:
        b_ref, common, clean, rows, spec, white, series, b_s = rest
    chans, wins, ns = x_ref.shape
    nfr = spec.shape[0]
    pitch = wins + 1
    size = seg_ref.shape[0]
    half = size // 2
    blocks = ns // half
    jw = blocks * wins
    jpitch = jw + 1
    for s in range(NSEC):
        common[s] = tot_ref[s, :, :ns] / jnp.maximum(tot_ref[s, :, ns : ns + 1], 1.0)

    def clean_channel(c, _):
        live = (1 - dead_ref[c]).astype(F32)
        value = (x_ref[c].astype(F32) - common[sec_ref[c]]) * live
        for t in range(ns // LANE):
            clean[t, pl.ds(c * pitch, wins), :] = value[:, t * LANE : (t + 1) * LANE]
        return 0

    lax.fori_loop(0, chans, clean_channel, 0, unroll=8)

    def pair(step, _):
        for i in range(2):
            w = step * 2 + i
            for t in range(ns // LANE):
                rows[i * chans : (i + 1) * chans, t * LANE : (t + 1) * LANE] = clean[
                    t, pl.ds(w, chans, stride=pitch), :
                ].astype(BF16)
        power = jnp.zeros((1, 2 * chans), F32)
        tile = ns
        for f in range(nfr // tile):
            s = lax.dot_general(
                fwd_ref[f * tile : (f + 1) * tile, :], rows[...], NT, preferred_element_type=F32
            )
            spec[f * tile : (f + 1) * tile, :] = s
            power = power + jnp.sum(s * s, axis=0, keepdims=True)
        level = lax.rsqrt(power / nfr + 1e-06)
        for i in range(2):
            white[:, i * chans : (i + 1) * chans] = (
                spec[:, i * chans : (i + 1) * chans]
                * gain_ref[...]
                * level[:, i * chans : (i + 1) * chans]
            ).astype(BF16)
        for t in range(ns // tile):
            p = jnp.dot(
                back_ref[t * tile : (t + 1) * tile, :], white[...], preferred_element_type=F32
            ).astype(BF16)
            series[half // 2 + t * tile : half // 2 + (t + 1) * tile, :] = p
        series[: half // 2, :] = series[ns : ns + half // 2, :]
        series[ns + half // 2 :, :] = series[half // 2 : half, :]
        for j in range(blocks):
            if both:
                a = jnp.dot(
                    seg_ref[...], series[j * half : j * half + size, :], preferred_element_type=F32
                )
            b = jnp.dot(
                seg_ref[:, :half],
                series[j * half + half // 2 : j * half + half // 2 + half, :],
                preferred_element_type=F32,
            )
            for i in range(2):
                at = j * wins + step * 2 + i
                if both:
                    a_s[pl.ds(at, size, stride=jpitch), :] = a[:, i * chans : (i + 1) * chans]
                b_s[pl.ds(at, size, stride=jpitch), :] = b[:, i * chans : (i + 1) * chans]
        return 0

    lax.fori_loop(0, wins // 2, pair, 0)

    def one_bin(k, _):
        def both_parts(ref):
            return jnp.concatenate(
                [
                    ref[pl.ds(2 * k * jpitch, jw), :].astype(BF16),
                    ref[pl.ds((2 * k + 1) * jpitch, jw), :].astype(BF16),
                ],
                axis=0,
            )

        if both:
            a_ref[k] = both_parts(a_s).T
        b_ref[k] = both_parts(b_s)
        return 0

    lax.fori_loop(0, half, one_bin, 0, unroll=8)


def segments(both, flags, x, total, gain, fwd, back, seg):
    chans, wins, ns = x.shape
    nfr = fwd.shape[0]
    size = seg.shape[0]
    half = size // 2
    depth = ns // half * wins * 2
    smem = pl.BlockSpec(memory_space=pltpu.SMEM)
    vmem = pl.BlockSpec(memory_space=pltpu.VMEM)
    out = [jax.ShapeDtypeStruct((half, depth, chans), BF16)]
    stage = [pltpu.VMEM((size * (depth // 2 + 1), chans), F32)]
    if both:
        out = [jax.ShapeDtypeStruct((half, chans, depth), BF16)] + out
        stage = stage * 2
    return pl.pallas_call(
        functools.partial(segments_kernel, both),
        out_shape=out,
        in_specs=[smem, smem] + [vmem] * 6,
        out_specs=[vmem] * len(out),
        scratch_shapes=[
            pltpu.VMEM((NSEC, wins, ns), F32),
            pltpu.VMEM((ns // LANE, chans * (wins + 1), LANE), F32),
            pltpu.VMEM((2 * chans, ns), BF16),
            pltpu.VMEM((nfr, 2 * chans), F32),
            pltpu.VMEM((nfr, 2 * chans), BF16),
            pltpu.VMEM((ns + half, 2 * chans), BF16),
        ]
        + stage,
        compiler_params=pltpu.CompilerParams(vmem_limit_bytes=VMEM),
        cost_estimate=pl.CostEstimate(
            flops=2 * wins * chans * ns * (2 * nfr + 3 * size),
            bytes_accessed=16 * 1024 * 1024,
            transcendentals=0,
        ),
    )(flags[0], flags[1], x, total, gain, fwd, back, seg)


def stack_kernel(first, scale, a_ref, b_ref, h_ref, lag_ref, out_ref, cross, one):
    bins, count, depth = a_ref.shape
    chans = b_ref.shape[2]
    nfr = 2 * bins
    pitch = nfr + 1
    row = lax.broadcasted_iota(jnp.int32, one.shape[1:], 0)
    column = lax.broadcasted_iota(jnp.int32, one.shape[1:], 1)
    for t in range(2):
        one[t] = jnp.where(row == column + t * chans, 1.0, 0.0)

    def one_bin(k, _):
        left = a_ref[k]
        right = jnp.concatenate([b_ref[k], h_ref[k]], axis=1)
        turned = jnp.concatenate([-right[depth // 2 :], right[: depth // 2]], axis=0)
        for part, operand in enumerate((right, turned)):
            value = jnp.dot(left, operand, preferred_element_type=F32)
            for t in range(2):
                cross[t, pl.ds(2 * k + part, count, stride=pitch), :] = value[
                    :, t * chans : (t + 1) * chans
                ]
        return 0

    lax.fori_loop(0, bins, one_bin, 0, unroll=8)
    shares, _, share, nlag = out_ref.shape

    def one_channel(c, _):
        value = jnp.concatenate(
            [cross[t, pl.ds(c * pitch, nfr), :] for t in range(2)], axis=1
        ).astype(BF16)
        pick = jnp.concatenate(
            [one[t, pl.ds(first + c + 1, OFFS), :] for t in range(2)], axis=1
        ).astype(BF16)
        lagged = jnp.dot(lag_ref[...], value, preferred_element_type=F32) * scale
        lagged = lagged.astype(BF16)
        band = lax.dot_general(pick, lagged, NT, preferred_element_type=F32).astype(BF16)
        for s in range(shares):
            out_ref[s, c] = band[s * share : (s + 1) * share, :]
        return 0

    lax.fori_loop(0, count, one_channel, 0, unroll=4)


def stacks(index, count, shares, scale, a, b, h, lag):
    bins, chans, depth = a.shape
    nlag = lag.shape[0]
    whole = lambda arr: pl.BlockSpec(arr.shape, lambda i: (0,) * arr.ndim)
    return pl.pallas_call(
        functools.partial(stack_kernel, index * count, scale),
        grid=(1,),
        out_shape=jax.ShapeDtypeStruct((shares, count, OFFS // shares, nlag), BF16),
        in_specs=[
            pl.BlockSpec((bins, count, depth), lambda i: (0, index, 0)),
            whole(b),
            whole(h),
            whole(lag),
        ],
        out_specs=pl.BlockSpec(
            (shares, count, OFFS // shares, nlag), lambda i: (0, 0, 0, 0)
        ),
        scratch_shapes=[
            pltpu.VMEM((2, count * (2 * bins + 1), chans), F32),
            pltpu.VMEM((2, chans + OFFS, chans), F32),
        ],
        compiler_params=pltpu.CompilerParams(vmem_limit_bytes=VMEM),
        cost_estimate=pl.CostEstimate(
            flops=2 * count * bins * 2 * (2 * depth * chans + 2 * OFFS * chans + OFFS * nlag),
            bytes_accessed=12 * 1024 * 1024,
            transcendentals=0,
        ),
    )(a, b, h, lag)


def add_over(value, axis):
    count = lax.axis_size(axis)
    if count & (count - 1):
        return lax.psum(value, axis)
    bit = 1
    while bit < count:
        value = value + lax.ppermute(value, axis, [(i, i ^ bit) for i in range(count)])
        bit *= 2
    return value


def shards(samples, band_gain, dead_flags, section_ids):
    chans, wins, ns = samples.shape
    nf = ns // 2
    blocks = lax.axis_size("fibre")
    groups = lax.axis_size("tm")
    fwd, back, seg, lag = [jnp.asarray(t) for t in tables(ns, nf)]
    flags = jnp.stack([dead_flags, section_ids])
    ahead = [((i + 1) % blocks, i) for i in range(blocks)]
    smem = pl.BlockSpec(memory_space=pltpu.SMEM)
    vmem = pl.BlockSpec(memory_space=pltpu.VMEM)
    sums = pl.pallas_call(
        section_sums,
        out_shape=jax.ShapeDtypeStruct((NSEC, wins, ns + LANE), F32),
        in_specs=[smem, smem, vmem],
        out_specs=vmem,
        compiler_params=pltpu.CompilerParams(vmem_limit_bytes=VMEM),
    )(dead_flags, section_ids, samples)
    total = add_over(sums, "fibre")
    next_flags = lax.ppermute(flags, "fibre", ahead)
    total, to_send = lax.optimization_barrier((total, samples))
    next_samples = lax.ppermute(to_send, "fibre", ahead)
    gain = jnp.broadcast_to(jnp.concatenate([band_gain, band_gain])[:, None], (2 * nf, chans))
    a, b = segments(True, (dead_flags, section_ids), samples, total, gain, fwd, back, seg)
    (h,) = segments(False, next_flags, next_samples, total, gain, fwd, back, seg)
    scale = 2.0 / ns / LAGS / math.sqrt(nf * wins * groups)
    count = chans // CHUNKS
    out = []
    for index in range(CHUNKS):
        parts = stacks(index, count, groups, scale, a, b, h, lag)
        out.append(lax.psum_scatter(parts, "tm", scatter_dimension=0).astype(F32))
    return jnp.concatenate(out, axis=0)


def solution(mesh):
    in_specs = (P("fibre", "tm", None), P(), P("fibre"), P("fibre"))
    out_specs = P("fibre", "tm", None)
    return jax.shard_map(shards, mesh=mesh, in_specs=in_specs, out_specs=out_specs, check_vma=False)
```

```python
import functools
import math

import jax
import jax.numpy as jnp
import ml_dtypes
import numpy as np
from jax import lax
from jax.experimental import pallas as pl
from jax.experimental.pallas import tpu as pltpu
from jax.sharding import PartitionSpec as P

OFFS = 128
LAGS = 128
NSEC = 2
LANE = 128
VMEM = 56 * 1024 * 1024
NT = (((1,), (1,)), ((), ()))
F32 = jnp.float32
BF16 = jnp.bfloat16


def tables(ns, nf):
    tick = np.arange(ns)
    freq = np.arange(nf)
    phase = (tick[:, None] * freq[None, :] % ns) * (2.0 * math.pi / ns)
    window = 0.5 - 0.5 * np.cos(tick * (2.0 * math.pi / ns))
    forward = np.concatenate(
        [window[:, None] * np.cos(phase), -window[:, None] * np.sin(phase)], axis=1
    )
    back = np.concatenate([np.cos(phase), -np.sin(phase)], axis=1)
    back[:, 0] *= math.sqrt(0.5)
    size = 2 * LAGS
    bins = np.arange(size // 2)
    turn = math.pi / size * ((2 * bins[:, None] + 1) * np.arange(size)[None, :] % (2 * size))
    segment = np.stack([np.cos(turn), -np.sin(turn)], axis=1).reshape(size, size)
    lag = np.stack([np.cos(turn), -np.sin(turn)], axis=1).reshape(size, size)[:, :LAGS].T
    cast = lambda a: a.astype(np.float32).astype(ml_dtypes.bfloat16)
    return cast(forward.T), cast(back), cast(segment), cast(lag)


def section_sums(dead_ref, sec_ref, x_ref, out_ref):
    chans, wins, ns = x_ref.shape

    def body(c, carry):
        value = x_ref[c].astype(F32)
        live = 1 - dead_ref[c]
        sums, counts = carry
        weights = [jnp.where(sec_ref[c] == s, live, 0).astype(F32) for s in range(NSEC)]
        return (
            tuple(sums[s] + weights[s] * value for s in range(NSEC)),
            tuple(counts[s] + weights[s] for s in range(NSEC)),
        )

    zero = jnp.zeros((wins, ns), F32)
    sums, counts = lax.fori_loop(
        0, chans, body, ((zero,) * NSEC, (jnp.float32(0),) * NSEC), unroll=8
    )
    for s in range(NSEC):
        out_ref[s, :, :ns] = sums[s]
        out_ref[s, :, ns:] = jnp.zeros((wins, LANE), F32) + counts[s]


def segments_kernel(
    sets, info_ref, dead_ref, sec_ref, tot_ref, gain_ref, fwd_ref, back_ref, seg_ref, *rest
):
    pieces = rest[: len(sets)]
    a_ref, b_ref, common, clean, rows, spec, white, series, a_s, b_s = rest[len(sets) :]
    _, wins, ns = pieces[0].shape
    chans = b_ref.shape[2]
    nfr = spec.shape[0]
    pitch = wins + 1
    size = seg_ref.shape[0]
    half = size // 2
    blocks = ns // half
    jw = blocks * wins
    jpitch = jw + 1
    want = info_ref[0] != 0
    for g in range(tot_ref.shape[0]):
        for s in range(NSEC):
            count = jnp.maximum(tot_ref[g, s, :, ns : ns + 1], 1.0)
            common[g * NSEC + s] = tot_ref[g, s, :, :ns] / count

    for number, (group, x_ref) in enumerate(zip(sets, pieces)):
        base = info_ref[1 + number]

        def clean_channel(c, _):
            at = base + c
            live = (1 - dead_ref[at]).astype(F32)
            value = (x_ref[c].astype(F32) - common[group * NSEC + sec_ref[at]]) * live
            for t in range(ns // LANE):
                clean[t, pl.ds(at * pitch, wins), :] = value[:, t * LANE : (t + 1) * LANE]
            return 0

        lax.fori_loop(0, x_ref.shape[0], clean_channel, 0, unroll=8)

    def pair(step, _):
        for i in range(2):
            w = step * 2 + i
            for t in range(ns // LANE):
                rows[i * chans : (i + 1) * chans, t * LANE : (t + 1) * LANE] = clean[
                    t, pl.ds(w, chans, stride=pitch), :
                ].astype(BF16)
        s = lax.dot_general(fwd_ref[...], rows[...], NT, preferred_element_type=F32)
        spec[...] = s
        power = jnp.sum(s * s, axis=0, keepdims=True)
        level = lax.rsqrt(power / nfr + 1e-06)
        for i in range(2):
            white[:, i * chans : (i + 1) * chans] = (
                spec[:, i * chans : (i + 1) * chans]
                * gain_ref[...]
                * level[:, i * chans : (i + 1) * chans]
            ).astype(BF16)
        series[half // 2 : ns + half // 2, :] = jnp.dot(
            back_ref[...], white[...], preferred_element_type=F32
        ).astype(BF16)
        series[: half // 2, :] = series[ns : ns + half // 2, :]
        series[ns + half // 2 :, :] = series[half // 2 : half, :]
        for j in range(blocks):
            b = jnp.dot(
                seg_ref[:, :half],
                series[j * half + half // 2 : j * half + half // 2 + half, :],
                preferred_element_type=F32,
            )
            for i in range(2):
                at = j * wins + step * 2 + i
                b_s[pl.ds(at, size, stride=jpitch), :] = b[:, i * chans : (i + 1) * chans]

        @pl.when(want)
        def _():
            for j in range(blocks):
                a = jnp.dot(
                    seg_ref[...], series[j * half : j * half + size, :], preferred_element_type=F32
                )
                for i in range(2):
                    at = j * wins + step * 2 + i
                    a_s[pl.ds(at, size, stride=jpitch), :] = a[:, i * chans : (i + 1) * chans]

        return 0

    lax.fori_loop(0, wins // 2, pair, 0)

    def both_parts(ref, k):
        return jnp.concatenate(
            [ref[pl.ds((2 * k + part) * jpitch, jw), :].astype(BF16) for part in range(2)], axis=0
        )

    def second(k, _):
        b_ref[k] = both_parts(b_s, k)
        return 0

    lax.fori_loop(0, half, second, 0, unroll=8)

    @pl.when(want)
    def _():
        def first(k, _):
            a_ref[k] = both_parts(a_s, k).T
            return 0

        lax.fori_loop(0, half, first, 0, unroll=8)


def segments(sets, info, flags, pieces, total, gain, fwd, back, seg):
    chans = sum(x.shape[0] for x in pieces)
    _, wins, ns = pieces[0].shape
    nfr = fwd.shape[0]
    size = seg.shape[0]
    half = size // 2
    depth = ns // half * wins * 2
    smem = pl.BlockSpec(memory_space=pltpu.SMEM)
    vmem = pl.BlockSpec(memory_space=pltpu.VMEM)
    return pl.pallas_call(
        functools.partial(segments_kernel, sets),
        out_shape=[
            jax.ShapeDtypeStruct((half, chans, depth), BF16),
            jax.ShapeDtypeStruct((half, depth, chans), BF16),
        ],
        in_specs=[smem] * 3 + [vmem] * (5 + len(pieces)),
        out_specs=[vmem] * 2,
        scratch_shapes=[
            pltpu.VMEM((total.shape[0] * NSEC, wins, ns), F32),
            pltpu.VMEM((ns // LANE, chans * (wins + 1), LANE), F32),
            pltpu.VMEM((2 * chans, ns), BF16),
            pltpu.VMEM((nfr, 2 * chans), F32),
            pltpu.VMEM((nfr, 2 * chans), BF16),
            pltpu.VMEM((ns + half, 2 * chans), BF16),
            pltpu.VMEM((size * (depth // 2 + 1), chans), F32),
            pltpu.VMEM((size * (depth // 2 + 1), chans), F32),
        ],
        compiler_params=pltpu.CompilerParams(vmem_limit_bytes=VMEM),
        cost_estimate=pl.CostEstimate(
            flops=2 * wins * chans * ns * (2 * nfr + 3 * size),
            bytes_accessed=16 * 1024 * 1024,
            transcendentals=0,
        ),
    )(info, flags[0], flags[1], total, gain, fwd, back, seg, *pieces)


def stack_kernel(
    scale, odd_ref, a0_ref, a1_ref, ah_ref, b0_ref, b1_ref, bh_ref, lag_ref, out_ref, cross, one
):
    bins, count, depth = a0_ref.shape
    chans = b0_ref.shape[2]
    nfr = 2 * bins
    pitch = nfr + 1
    odd = odd_ref[0] != 0
    span = chans + count
    row = lax.broadcasted_iota(jnp.int32, one.shape[1:], 0)
    column = lax.broadcasted_iota(jnp.int32, one.shape[1:], 1)
    turned = jnp.where(row < count, row + chans, row - count)
    place = row + (turned - row) * odd_ref[0]
    for t in range(2):
        one[t] = jnp.where(place == column + t * chans, 1.0, 0.0)

    def bins_with(left_of):
        def one_bin(k, _):
            left = left_of(k)
            part = depth // 2
            swapped = jnp.concatenate(
                [left[:, part:depth], -left[:, :part], left[:, depth + part :], -left[:, depth : depth + part]],
                axis=1,
            )
            halo = bh_ref[k]
            other = jnp.concatenate([halo[:, count:], halo[:, :count]], axis=1)
            right = jnp.concatenate(
                [
                    jnp.concatenate([b0_ref[k], halo], axis=1),
                    jnp.concatenate([b1_ref[k], other], axis=1),
                ],
                axis=0,
            )
            value = jnp.dot(
                jnp.concatenate([left, swapped], axis=0), right, preferred_element_type=F32
            )
            for p in range(2):
                for t in range(2):
                    cross[t, pl.ds(2 * k + p, count, stride=pitch), :] = value[
                        p * count : (p + 1) * count, t * chans : (t + 1) * chans
                    ]
            return 0

        lax.fori_loop(0, bins, one_bin, 0, unroll=8)

    @pl.when(odd)
    def _():
        bins_with(lambda k: jnp.concatenate([ah_ref[k, :count], ah_ref[k, count:]], axis=1))

    @pl.when(jnp.logical_not(odd))
    def _():
        bins_with(lambda k: jnp.concatenate([a0_ref[k], a1_ref[k]], axis=1))

    shares, _, share, nlag = out_ref.shape

    def one_channel(c, _):
        value = jnp.concatenate(
            [cross[t, pl.ds(c * pitch, nfr), :] for t in range(2)], axis=1
        ).astype(BF16)
        pick = jnp.concatenate(
            [one[t, pl.ds(c + 1, OFFS), :] for t in range(2)], axis=1
        ).astype(BF16)
        lagged = jnp.dot(lag_ref[...], value, preferred_element_type=F32) * scale
        lagged = lagged.astype(BF16)
        band = lax.dot_general(pick, lagged, NT, preferred_element_type=F32).astype(BF16)
        for s in range(shares):
            out_ref[s, c] = band[s * share : (s + 1) * share, :]
        return 0

    lax.fori_loop(0, count, one_channel, 0, unroll=4)


def stacks(shares, scale, odd, a0, a1, ah, b0, b1, bh, lag):
    bins, chans, depth = a0.shape
    count = chans // 2
    nlag = lag.shape[0]
    whole = lambda arr: pl.BlockSpec(arr.shape, lambda i: (0,) * arr.ndim)
    lower = pl.BlockSpec((bins, count, depth), lambda i: (0, 0, 0))
    return pl.pallas_call(
        functools.partial(stack_kernel, scale),
        grid=(1,),
        out_shape=jax.ShapeDtypeStruct((shares, count, OFFS // shares, nlag), BF16),
        in_specs=[
            pl.BlockSpec(memory_space=pltpu.SMEM),
            lower,
            lower,
            whole(ah),
            whole(b0),
            whole(b1),
            whole(bh),
            whole(lag),
        ],
        out_specs=pl.BlockSpec((shares, count, OFFS // shares, nlag), lambda i: (0, 0, 0, 0)),
        scratch_shapes=[
            pltpu.VMEM((2, count * (2 * bins + 1), chans), F32),
            pltpu.VMEM((2, chans + count, chans), F32),
        ],
        compiler_params=pltpu.CompilerParams(vmem_limit_bytes=VMEM),
        cost_estimate=pl.CostEstimate(
            flops=2 * count * bins * 4 * (2 * depth * chans + 2 * OFFS * chans),
            bytes_accessed=20 * 1024 * 1024,
            transcendentals=0,
        ),
    )(odd, a0, a1, ah, b0, b1, bh, lag)


def add_over(value, axis):
    count = lax.axis_size(axis)
    if count & (count - 1):
        return lax.psum(value, axis)
    bit = 1
    while bit < count:
        value = value + lax.ppermute(value, axis, [(i, i ^ bit) for i in range(count)])
        bit *= 2
    return value


def shards(samples, band_gain, dead_flags, section_ids):
    chans, wins, ns = samples.shape
    nf = ns // 2
    count = chans // 2
    blocks = lax.axis_size("fibre")
    groups = lax.axis_size("tm")
    odd = lax.axis_index("tm") % 2
    fwd, back, seg, lag = [jnp.asarray(t) for t in tables(ns, nf)]
    gain = jnp.broadcast_to(jnp.concatenate([band_gain, band_gain])[:, None], (2 * nf, chans))
    swap = [(z, z ^ 1) for z in range(groups)]
    both = ("fibre", "tm")
    halo_pairs = [
        (b * groups + z, (b + (1 if z % 2 else -1)) % blocks * groups + z)
        for b in range(blocks)
        for z in range(groups)
    ]
    smem = pl.BlockSpec(memory_space=pltpu.SMEM)
    vmem = pl.BlockSpec(memory_space=pltpu.VMEM)

    def lower_or_upper(array, upper):
        return lax.dynamic_slice_in_dim(array, upper * count, count, array.ndim - 1 if array.ndim == 2 else 0)

    flags = jnp.stack([dead_flags, section_ids])
    halo_flags = lax.ppermute(lower_or_upper(flags, odd), both, halo_pairs)
    sums = pl.pallas_call(
        section_sums,
        out_shape=jax.ShapeDtypeStruct((NSEC, wins, ns + LANE), F32),
        in_specs=[smem, smem, vmem],
        out_specs=vmem,
        compiler_params=pltpu.CompilerParams(vmem_limit_bytes=VMEM),
    )(dead_flags, section_ids, samples)
    sums, first_half = lax.optimization_barrier((sums, lower_or_upper(samples, 1 - odd)))
    their_sums = lax.ppermute(sums, "tm", swap)
    their_first = lax.ppermute(first_half, "tm", swap)
    their_sums, halo_flags, second_half = lax.optimization_barrier(
        (their_sums, halo_flags, lower_or_upper(samples, odd))
    )
    their_second = lax.ppermute(second_half, "tm", swap)
    total = add_over(jnp.stack([sums, their_sums]), "fibre")
    total, own_half = lax.optimization_barrier((total, lower_or_upper(samples, odd)))
    halo = lax.ppermute(own_half, both, halo_pairs)
    their_halo = lax.ppermute(their_first, both, halo_pairs)

    even = 1 - odd
    zero = jnp.zeros((), jnp.int32)
    own_flags = (dead_flags, section_ids)
    twice = (jnp.tile(halo_flags[0], 2), jnp.tile(halo_flags[1], 2))
    parts = (total, gain, fwd, back, seg)
    a0, b0 = segments((0,), jnp.stack([even, zero]), own_flags, (samples,), *parts)
    ah, bh = segments(
        (0, 1), jnp.stack([odd, zero, zero + count]), twice, (halo, their_halo), *parts
    )
    a1, b1 = segments(
        (1, 1),
        jnp.stack([even, odd * count, even * count]),
        own_flags,
        (their_first, their_second),
        *parts,
    )
    scale = 2.0 / ns / LAGS / math.sqrt(nf * wins * groups)
    found = stacks(groups, scale, odd[None], a0, a1, ah, b0, b1, bh, lag)
    arrived = []
    for d in range(groups):
        pairs = [
            (b * groups + z, (b - z % 2) % blocks * groups + (z ^ d))
            for b in range(blocks)
            for z in range(groups)
        ]
        share = lax.dynamic_index_in_dim(found, lax.axis_index("tm") ^ d, 0, keepdims=False)
        arrived.append(lax.ppermute(share, both, pairs).astype(F32))
    same = sum(arrived[2::2], arrived[0])
    other = sum(arrived[3::2], arrived[1])
    return jnp.concatenate(
        [jnp.where(odd == 0, same, other), jnp.where(odd == 0, other, same)], axis=0
    )


def solution(mesh):
    in_specs = (P("fibre", "tm", None), P(), P("fibre"), P("fibre"))
    out_specs = P("fibre", "tm", None)
    return jax.shard_map(shards, mesh=mesh, in_specs=in_specs, out_specs=out_specs, check_vma=False)
```

```python
import functools
import math

import jax
import jax.numpy as jnp
import ml_dtypes
import numpy as np
from jax import lax
from jax.experimental import pallas as pl
from jax.experimental.pallas import tpu as pltpu
from jax.sharding import PartitionSpec as P

OFFS = 128
LAGS = 128
NSEC = 2
LANE = 128
CHUNKS = 2
TILE = 256
STEPS = 4
VMEM = 56 * 1024 * 1024
NT = (((1,), (1,)), ((), ()))
F32 = jnp.float32
BF16 = jnp.bfloat16


def tables(ns, nf):
    tick = np.arange(ns)
    freq = np.arange(nf)
    phase = (tick[:, None] * freq[None, :] % ns) * (2.0 * math.pi / ns)
    window = 0.5 - 0.5 * np.cos(tick * (2.0 * math.pi / ns))
    forward = np.concatenate(
        [window[:, None] * np.cos(phase), -window[:, None] * np.sin(phase)], axis=1
    )
    back = np.concatenate([np.cos(phase), -np.sin(phase)], axis=1)
    back[:, 0] *= math.sqrt(0.5)
    size = 2 * LAGS
    bins = np.arange(size // 2)
    turn = math.pi / size * ((2 * bins[:, None] + 1) * np.arange(size)[None, :] % (2 * size))
    segment = np.stack([np.cos(turn), -np.sin(turn)], axis=1).reshape(size, size)
    lag = np.stack([np.cos(turn), -np.sin(turn)], axis=1).reshape(size, size)[:, :LAGS].T
    cast = lambda a: a.astype(np.float32).astype(ml_dtypes.bfloat16)
    return cast(forward.T), cast(back), cast(segment), cast(lag)


def section_sums(dead_ref, sec_ref, x_ref, out_ref):
    chans, wins, ns = x_ref.shape
    first = pl.program_id(0) * chans

    @pl.when(pl.program_id(0) == 0)
    def _():
        out_ref[...] = jnp.zeros_like(out_ref)

    def body(c, carry):
        value = x_ref[c].astype(F32)
        live = 1 - dead_ref[first + c]
        sums, counts = carry
        weights = [jnp.where(sec_ref[first + c] == s, live, 0).astype(F32) for s in range(NSEC)]
        return (
            tuple(sums[s] + weights[s] * value for s in range(NSEC)),
            tuple(counts[s] + weights[s] for s in range(NSEC)),
        )

    zero = jnp.zeros((wins, ns), F32)
    sums, counts = lax.fori_loop(
        0, chans, body, ((zero,) * NSEC, (jnp.float32(0),) * NSEC), unroll=8
    )
    for s in range(NSEC):
        out_ref[s, :, :ns] += sums[s]
        out_ref[s, :, ns:] += jnp.zeros((wins, LANE), F32) + counts[s]


def segments_kernel(kind, odd_ref, flag_ref, *rest):
    sets = {"own": (0,), "halo": (0, 1), "other": (0, 0)}[kind]
    groups = max(sets) + 1
    count = len(sets)
    tot_hbm, rest = rest[:groups], rest[groups:]
    x_hbm, rest = rest[:count], rest[count:]
    gain_hbm, fwd_hbm, back_hbm, seg_hbm, a_hbm, b_hbm = rest[:6]
    tot, rest = rest[6 : 6 + groups], rest[6 + groups :]
    x, rest = rest[:count], rest[count:]
    gain, fwd, back, seg, common, clean, rows, spec, white, series, a_s, b_s, a_out, b_out = rest[:14]
    in_sem, out_sem = rest[14:]
    sources = list(tot_hbm) + list(x_hbm) + [fwd_hbm, gain_hbm, back_hbm, seg_hbm]
    targets = list(tot) + list(x) + [fwd, gain, back, seg]
    copies = [
        pltpu.make_async_copy(source, target, in_sem.at[n])
        for n, (source, target) in enumerate(zip(sources, targets))
    ]
    for copy in copies:
        copy.start()

    _, wins, ns = x[0].shape
    chans = b_out.shape[2]
    nfr = spec.shape[0]
    pitch = wins + 1
    size = seg.shape[0]
    half = size // 2
    blocks = ns // half
    jw = blocks * wins
    jpitch = jw + 1
    odd = odd_ref[0]
    want = (odd == 1) if kind == "halo" else (odd == 0)
    held = flag_ref.shape[1]
    for g in range(groups):
        copies[g].wait()
        for s in range(NSEC):
            common[g * NSEC + s] = tot[g][s, :, :ns] / jnp.maximum(tot[g][s, :, ns : ns + 1], 1.0)

    for number, group in enumerate(sets):
        copies[groups + number].wait()
        piece = x[number]
        length = piece.shape[0]
        base = number * length
        if kind == "other":
            base = odd * length if number == 0 else length - odd * length

        def clean_channel(c, _):
            at = base + c
            flag = lax.rem(at, held)
            live = (1 - flag_ref[0, flag]).astype(F32)
            value = (piece[c].astype(F32) - common[group * NSEC + flag_ref[1, flag]]) * live
            for t in range(ns // LANE):
                clean[t, pl.ds(at * pitch, wins), :] = value[:, t * LANE : (t + 1) * LANE]
            return 0

        lax.fori_loop(0, length, clean_channel, 0, unroll=8)
    for copy in copies[groups + count :]:
        copy.wait()

    def pair(step, _):
        for i in range(2):
            w = step * 2 + i
            for t in range(ns // LANE):
                rows[i * chans : (i + 1) * chans, t * LANE : (t + 1) * LANE] = clean[
                    t, pl.ds(w, chans, stride=pitch), :
                ].astype(BF16)
        power = jnp.zeros((1, 2 * chans), F32)
        for f in range(0, nfr, TILE):
            s = lax.dot_general(
                fwd[f : f + TILE, :], rows[...], NT, preferred_element_type=F32
            )
            spec[f : f + TILE, :] = s
            power = power + jnp.sum(s * s, axis=0, keepdims=True)
        level = lax.rsqrt(power / nfr + 1e-06)
        for i in range(2):
            white[:, i * chans : (i + 1) * chans] = (
                spec[:, i * chans : (i + 1) * chans]
                * gain[...]
                * level[:, i * chans : (i + 1) * chans]
            ).astype(BF16)
        for t in range(0, ns, TILE):
            series[half // 2 + t : half // 2 + t + TILE, :] = jnp.dot(
                back[t : t + TILE, :], white[...], preferred_element_type=F32
            ).astype(BF16)
        series[: half // 2, :] = series[ns : ns + half // 2, :]
        series[ns + half // 2 :, :] = series[half // 2 : half, :]
        for j in range(blocks):
            b = jnp.dot(
                seg[:, :half],
                series[j * half + half // 2 : j * half + half // 2 + half, :],
                preferred_element_type=F32,
            )
            for i in range(2):
                at = j * wins + step * 2 + i
                b_s[pl.ds(at, size, stride=jpitch), :] = b[:, i * chans : (i + 1) * chans]

        @pl.when(want)
        def _():
            for j in range(blocks):
                a = jnp.dot(
                    seg[...], series[j * half : j * half + size, :], preferred_element_type=F32
                )
                for i in range(2):
                    at = j * wins + step * 2 + i
                    a_s[pl.ds(at, size, stride=jpitch), :] = a[:, i * chans : (i + 1) * chans]

        return 0

    lax.fori_loop(0, wins // 2, pair, 0)

    def both_parts(ref, k):
        return jnp.concatenate(
            [ref[pl.ds((2 * k + part) * jpitch, jw), :].astype(BF16) for part in range(2)], axis=0
        )

    def second(k, _):
        b_out[k] = both_parts(b_s, k)
        return 0

    def first(k, _):
        a_out[k] = both_parts(a_s, k).T[: a_out.shape[1]]
        return 0

    step = half // STEPS

    def sends(n, stage, target):
        part = pl.ds(n % STEPS * step, step)
        return pltpu.make_async_copy(stage.at[part], target.at[part], out_sem.at[n])

    @pl.when(want)
    def _():
        for n in range(STEPS):
            lax.fori_loop(n * step, (n + 1) * step, first, 0, unroll=8)
            sends(n, a_out, a_hbm).start()

    for n in range(STEPS):
        lax.fori_loop(n * step, (n + 1) * step, second, 0, unroll=8)
        sends(STEPS + n, b_out, b_hbm).start()

    @pl.when(want)
    def _():
        for n in range(STEPS):
            sends(n, a_out, a_hbm).wait()

    for n in range(STEPS):
        sends(STEPS + n, b_out, b_hbm).wait()


def segments(kind, odd, flags, totals, pieces, gain, fwd, back, seg):
    chans = sum(x.shape[0] for x in pieces)
    _, wins, ns = pieces[0].shape
    nfr = fwd.shape[0]
    size = seg.shape[0]
    half = size // 2
    depth = ns // half * wins * 2
    kept = chans if kind == "halo" else chans // 2
    smem = pl.BlockSpec(memory_space=pltpu.SMEM)
    anywhere = pl.BlockSpec(memory_space=pl.ANY)
    tables_in = [gain, fwd, back, seg]
    operands = list(totals) + list(pieces) + tables_in
    a_shape = jax.ShapeDtypeStruct((half, kept, depth), BF16)
    b_shape = jax.ShapeDtypeStruct((half, depth, chans), BF16)
    return pl.pallas_call(
        functools.partial(segments_kernel, kind),
        out_shape=[a_shape, b_shape],
        in_specs=[smem] * 2 + [anywhere] * len(operands),
        out_specs=[anywhere] * 2,
        scratch_shapes=[pltpu.VMEM(value.shape, value.dtype) for value in operands]
        + [
            pltpu.VMEM((len(totals) * NSEC, wins, ns), F32),
            pltpu.VMEM((ns // LANE, chans * (wins + 1), LANE), F32),
            pltpu.VMEM((2 * chans, ns), BF16),
            pltpu.VMEM((nfr, 2 * chans), F32),
            pltpu.VMEM((nfr, 2 * chans), BF16),
            pltpu.VMEM((ns + half, 2 * chans), BF16),
            pltpu.VMEM((size * (depth // 2 + 1), chans), F32),
            pltpu.VMEM((size * (depth // 2 + 1), chans), F32),
            pltpu.VMEM(a_shape.shape, BF16),
            pltpu.VMEM(b_shape.shape, BF16),
            pltpu.SemaphoreType.DMA((len(operands),)),
            pltpu.SemaphoreType.DMA((2 * STEPS,)),
        ],
        compiler_params=pltpu.CompilerParams(vmem_limit_bytes=VMEM),
        cost_estimate=pl.CostEstimate(
            flops=2 * wins * chans * ns * (2 * nfr + 3 * size),
            bytes_accessed=16 * 1024 * 1024,
            transcendentals=0,
        ),
    )(odd, flags, *operands)


def stack_kernel(
    first, scale, me_ref, a0_ref, a1_ref, ah_ref, b0_ref, b1_ref, bh_ref, lag_ref, *rest
):
    outs, (cross, one) = rest[:-2], rest[-2:]
    bins, count, depth = a0_ref.shape
    chans = b0_ref.shape[2]
    width = chans // 2
    nfr = lag_ref.shape[1]
    pitch = nfr + 1
    me = me_ref[0]
    odd = lax.rem(me, 2)
    step = pl.program_id(0)

    def bins_with(left_of):
        def one_bin(k, _):
            left = left_of(k)
            part = depth // 2
            swapped = jnp.concatenate(
                [
                    left[:, part:depth],
                    -left[:, :part],
                    left[:, depth + part :],
                    -left[:, depth : depth + part],
                ],
                axis=1,
            )
            halo = bh_ref[k]
            other = jnp.concatenate([halo[:, width:], halo[:, :width]], axis=1)
            right = jnp.concatenate(
                [
                    jnp.concatenate([b0_ref[k], halo], axis=1),
                    jnp.concatenate([b1_ref[k], other], axis=1),
                ],
                axis=0,
            )
            value = jnp.dot(
                jnp.concatenate([left, swapped], axis=0), right, preferred_element_type=F32
            )
            at = 2 * (step * bins + k)
            for p in range(2):
                for t in range(2):
                    cross[t, pl.ds(at + p, count, stride=pitch), :] = value[
                        p * count : (p + 1) * count, t * chans : (t + 1) * chans
                    ]
            return 0

        lax.fori_loop(0, bins, one_bin, 0, unroll=8)

    @pl.when(odd == 1)
    def _():
        bins_with(lambda k: jnp.concatenate([ah_ref[k, 0], ah_ref[k, 1]], axis=1))

    @pl.when(odd == 0)
    def _():
        bins_with(lambda k: jnp.concatenate([a0_ref[k], a1_ref[k]], axis=1))

    @pl.when(step == pl.num_programs(0) - 1)
    def _():
        row = lax.broadcasted_iota(jnp.int32, one.shape[1:], 0)
        column = lax.broadcasted_iota(jnp.int32, one.shape[1:], 1)
        turned = jnp.where(row < width, row + chans, row - width)
        place = row + (turned - row) * odd
        for t in range(2):
            one[t] = jnp.where(place == column + t * chans, 1.0, 0.0)
        share = OFFS // len(outs)

        def one_channel(c, _):
            value = jnp.concatenate(
                [cross[t, pl.ds(c * pitch, nfr), :] for t in range(2)], axis=1
            ).astype(BF16)
            starts = [first + c + 1 + share * (me ^ d) for d in range(len(outs))]
            pick = jnp.concatenate(
                [
                    jnp.concatenate([one[t, pl.ds(start, share), :] for start in starts], axis=0)
                    for t in range(2)
                ],
                axis=1,
            ).astype(BF16)
            lagged = jnp.dot(lag_ref[...], value, preferred_element_type=F32) * scale
            band = lax.dot_general(pick, lagged.astype(BF16), NT, preferred_element_type=F32)
            for d, out in enumerate(outs):
                out[c] = band[d * share : (d + 1) * share, :].astype(BF16)
            return 0

        lax.fori_loop(0, count, one_channel, 0, unroll=4)


def stacks(index, shares, scale, me, a0, a1, ah, b0, b1, bh, lag):
    bins, width, depth = a0.shape
    chans = b0.shape[2]
    count = width // CHUNKS
    nlag, nfr = lag.shape
    ah = ah.reshape(bins, 2, width, depth)
    block = bins // 8
    left = pl.BlockSpec((block, count, depth), lambda i: (i, index, 0))
    right = pl.BlockSpec((block, depth, chans), lambda i: (i, 0, 0))
    return pl.pallas_call(
        functools.partial(stack_kernel, index * count, scale),
        grid=(bins // block,),
        out_shape=[jax.ShapeDtypeStruct((count, OFFS // shares, nlag), BF16)] * shares,
        in_specs=[
            pl.BlockSpec(memory_space=pltpu.SMEM),
            left,
            left,
            pl.BlockSpec((block, 2, count, depth), lambda i: (i, 0, index, 0)),
            right,
            right,
            right,
            pl.BlockSpec(lag.shape, lambda i: (0, 0)),
        ],
        out_specs=[pl.BlockSpec((count, OFFS // shares, nlag), lambda i: (0, 0, 0))] * shares,
        scratch_shapes=[
            pltpu.VMEM((2, count * (nfr + 1), chans), F32),
            pltpu.VMEM((2, chans + width, chans), F32),
        ],
        compiler_params=pltpu.CompilerParams(vmem_limit_bytes=VMEM),
        cost_estimate=pl.CostEstimate(
            flops=2 * count * bins * 4 * (2 * depth * chans + 2 * OFFS * chans),
            bytes_accessed=20 * 1024 * 1024,
            transcendentals=0,
        ),
    )(me, a0, a1, ah, b0, b1, bh, lag)


def add_over(value, axis):
    count = lax.axis_size(axis)
    if count & (count - 1):
        return lax.psum(value, axis)
    bit = 1
    while bit < count:
        value = value + lax.ppermute(value, axis, [(i, i ^ bit) for i in range(count)])
        bit *= 2
    return value


def shards(samples, band_gain, dead_flags, section_ids):
    chans, wins, ns = samples.shape
    nf = ns // 2
    width = chans // 2
    blocks = lax.axis_size("fibre")
    groups = lax.axis_size("tm")
    me = lax.axis_index("tm")
    odd = me % 2
    fwd, back, seg, lag = [jnp.asarray(t) for t in tables(ns, nf)]
    gain = jnp.broadcast_to(jnp.concatenate([band_gain, band_gain])[:, None], (2 * nf, chans))
    swap = [(z, z ^ 1) for z in range(groups)]
    both = ("fibre", "tm")
    halo_pairs = [
        (b * groups + z, (b + (1 if z % 2 else -1)) % blocks * groups + z)
        for b in range(blocks)
        for z in range(groups)
    ]

    first_half = lax.dynamic_slice_in_dim(samples, (1 - odd) * width, width, 0)
    their_first = lax.ppermute(first_half, "tm", swap)
    flags = jnp.stack([dead_flags, section_ids])
    halo_flags = lax.ppermute(
        lax.dynamic_slice_in_dim(flags, odd * width, width, 1), both, halo_pairs
    )
    smem = pl.BlockSpec(memory_space=pltpu.SMEM)
    steps = 4
    sums = pl.pallas_call(
        section_sums,
        grid=(steps,),
        out_shape=jax.ShapeDtypeStruct((NSEC, wins, ns + LANE), F32),
        in_specs=[smem, smem, pl.BlockSpec((chans // steps, wins, ns), lambda i: (i, 0, 0))],
        out_specs=pl.BlockSpec((NSEC, wins, ns + LANE), lambda i: (0, 0, 0)),
        compiler_params=pltpu.CompilerParams(vmem_limit_bytes=VMEM),
    )(dead_flags, section_ids, samples)
    total = add_over(sums, "fibre")
    total, halo_flags, kept = lax.optimization_barrier((total, halo_flags, samples))
    their_total = lax.ppermute(total, "tm", swap)
    own_half = lax.dynamic_slice_in_dim(kept, odd * width, width, 0)
    their_second = lax.ppermute(own_half, "tm", swap)
    halo = lax.ppermute(own_half, both, halo_pairs)

    side = odd[None]
    parts = (gain, fwd, back, seg)
    a0, b0 = segments("own", side, flags, (total,), (samples,), *parts)
    b0, forward = lax.optimization_barrier((b0, their_first))
    their_halo = lax.ppermute(forward, both, halo_pairs)
    ah, bh = segments("halo", side, halo_flags, (total, their_total), (halo, their_halo), *parts)
    a1, b1 = segments("other", side, flags, (their_total,), (their_first, their_second), *parts)
    scale = 2.0 / ns / LAGS / math.sqrt(nf * wins * groups)
    same, other = [], []
    for index in range(CHUNKS):
        found = stacks(index, groups, scale, me[None], a0, a1, ah, b0, b1, bh, lag)
        arrived = []
        for d in range(groups):
            pairs = [
                (b * groups + z, (b - z % 2) % blocks * groups + (z ^ d))
                for b in range(blocks)
                for z in range(groups)
            ]
            arrived.append(lax.ppermute(found[d], both, pairs).astype(F32))
        same.append(sum(arrived[2::2], arrived[0]))
        other.append(sum(arrived[3::2], arrived[1]))
    lower = [jnp.where(odd == 0, s, o) for s, o in zip(same, other)]
    upper = [jnp.where(odd == 0, o, s) for s, o in zip(same, other)]
    return jnp.concatenate(lower + upper, axis=0)


def solution(mesh):
    in_specs = (P("fibre", "tm", None), P(), P("fibre"), P("fibre"))
    out_specs = P("fibre", "tm", None)
    return jax.shard_map(shards, mesh=mesh, in_specs=in_specs, out_specs=out_specs, check_vma=False)
```

```python
import functools
import math

import jax
import jax.numpy as jnp
import ml_dtypes
import numpy as np
from jax import lax
from jax.experimental import pallas as pl
from jax.experimental.pallas import tpu as pltpu
from jax.sharding import PartitionSpec as P

OFFS = 128
LAGS = 128
NSEC = 2
LANE = 128
CHUNKS = 2
TILE = 256
STEPS = 4
VMEM = 60 * 1024 * 1024
NT = (((1,), (1,)), ((), ()))
F32 = jnp.float32
BF16 = jnp.bfloat16


def tables(ns, nf):
    tick = np.arange(ns)
    freq = np.arange(nf)
    window = 0.5 - 0.5 * np.cos(tick * (2.0 * math.pi / ns))
    waves = np.cos((freq[:, None] * tick[None, :] % ns) * (2.0 * math.pi / ns))
    waves[0] *= math.sqrt(0.5)
    size = 2 * LAGS
    bins = np.arange(size // 2)
    turn = math.pi / size * ((2 * bins[:, None] + 1) * np.arange(size)[None, :] % (2 * size))
    segment = np.stack([np.cos(turn), -np.sin(turn)], axis=1).reshape(size, size)
    lag = np.stack([np.cos(turn), -np.sin(turn)], axis=1).reshape(size, size)[:, :LAGS].T
    cast = lambda a: a.astype(np.float32).astype(ml_dtypes.bfloat16)
    return window.astype(np.float32), waves.astype(np.float32), cast(segment), cast(lag)


def section_sums(dead_ref, sec_ref, x_ref, out_ref):
    chans, wins, ns = x_ref.shape
    first = pl.program_id(0) * chans

    @pl.when(pl.program_id(0) == 0)
    def _():
        out_ref[...] = jnp.zeros_like(out_ref)

    def body(c, carry):
        value = x_ref[c].astype(F32)
        live = 1 - dead_ref[first + c]
        sums, counts = carry
        weights = [jnp.where(sec_ref[first + c] == s, live, 0).astype(F32) for s in range(NSEC)]
        return (
            tuple(sums[s] + weights[s] * value for s in range(NSEC)),
            tuple(counts[s] + weights[s] for s in range(NSEC)),
        )

    zero = jnp.zeros((wins, ns), F32)
    sums, counts = lax.fori_loop(
        0, chans, body, ((zero,) * NSEC, (jnp.float32(0),) * NSEC), unroll=8
    )
    for s in range(NSEC):
        out_ref[s, :, :ns] += sums[s]
        out_ref[s, :, ns:] += jnp.zeros((wins, LANE), F32) + counts[s]


def circulant_kernel(filter_ref, out_ref):
    ns = filter_ref.shape[1]
    rows = 16
    for t in range(0, ns, rows):
        block = jnp.broadcast_to(filter_ref[...], (rows, ns))
        out_ref[t : t + rows, :] = pltpu.roll(block, t, 1, stride=1, stride_axis=0).astype(BF16)


def segments_kernel(kind, odd_ref, flag_ref, *rest):
    sets = {"own": (0,), "halo": (0, 1), "other": (0, 0)}[kind]
    groups = max(sets) + 1
    count = len(sets)
    tot_hbm, rest = rest[:groups], rest[groups:]
    x_hbm, rest = rest[:count], rest[count:]
    hann_hbm, conv_hbm, seg_hbm, a_hbm, b_hbm = rest[:5]
    tot, rest = rest[5 : 5 + groups], rest[5 + groups :]
    x, rest = rest[:count], rest[count:]
    hann, conv, seg, common, clean, rows, series, a_s, b_s, a_out, b_out = rest[:11]
    in_sem, out_sem = rest[11:]
    sources = list(tot_hbm) + [hann_hbm] + list(x_hbm) + [conv_hbm, seg_hbm]
    targets = list(tot) + [hann] + list(x) + [conv, seg]
    copies = [
        pltpu.make_async_copy(source, target, in_sem.at[n])
        for n, (source, target) in enumerate(zip(sources, targets))
    ]
    for copy in copies:
        copy.start()

    _, wins, ns = x[0].shape
    chans = b_out.shape[2]
    pitch = wins + 1
    size = seg.shape[0]
    half = size // 2
    blocks = ns // half
    jw = blocks * wins
    jpitch = jw + 1
    odd = odd_ref[0]
    want = (odd == 1) if kind == "halo" else (odd == 0)
    held = flag_ref.shape[1]
    for g in range(groups):
        copies[g].wait()
        for s in range(NSEC):
            common[g * NSEC + s] = tot[g][s, :, :ns] / jnp.maximum(tot[g][s, :, ns : ns + 1], 1.0)

    copies[groups].wait()
    sign = 1.0 - 2.0 * (lax.broadcasted_iota(jnp.int32, (wins, LANE), 1) % 2).astype(F32)

    for number, group in enumerate(sets):
        copies[groups + 1 + number].wait()
        piece = x[number]
        length = piece.shape[0]
        base = number * length
        if kind == "other":
            base = odd * length if number == 0 else length - odd * length

        def clean_channel(c, _):
            at = base + c
            flag = lax.rem(at, held)
            live = (1 - flag_ref[0, flag]).astype(F32)
            value = (piece[c].astype(F32) - common[group * NSEC + flag_ref[1, flag]]) * hann[...]
            tiles = [value[:, t * LANE : (t + 1) * LANE] for t in range(ns // LANE)]
            mass = sum(tiles[1:], tiles[0])
            square = sum([tile * tile for tile in tiles[1:]], tiles[0] * tiles[0])
            lowest = jnp.sum(mass, axis=1, keepdims=True)
            highest = jnp.sum(mass * sign, axis=1, keepdims=True)
            square = jnp.sum(square, axis=1, keepdims=True)
            power = 0.5 * square + (lowest * lowest - highest * highest) * (0.5 / ns)
            value = value * (lax.rsqrt(power + 1e-06) * live)
            for t in range(ns // LANE):
                clean[t, pl.ds(at * pitch, wins), :] = value[:, t * LANE : (t + 1) * LANE]
            return 0

        lax.fori_loop(0, length, clean_channel, 0, unroll=8)
    for copy in copies[groups + 1 + count :]:
        copy.wait()

    def pair(step, _):
        for i in range(2):
            w = step * 2 + i
            for t in range(ns // LANE):
                rows[i * chans : (i + 1) * chans, t * LANE : (t + 1) * LANE] = clean[
                    t, pl.ds(w, chans, stride=pitch), :
                ].astype(BF16)
        for t in range(0, ns, TILE):
            series[half // 2 + t : half // 2 + t + TILE, :] = lax.dot_general(
                conv[t : t + TILE, :], rows[...], NT, preferred_element_type=F32
            ).astype(BF16)
        series[: half // 2, :] = series[ns : ns + half // 2, :]
        series[ns + half // 2 :, :] = series[half // 2 : half, :]
        for j in range(blocks):
            b = jnp.dot(
                seg[:, :half],
                series[j * half + half // 2 : j * half + half // 2 + half, :],
                preferred_element_type=F32,
            )
            for i in range(2):
                at = j * wins + step * 2 + i
                b_s[pl.ds(at, size, stride=jpitch), :] = b[:, i * chans : (i + 1) * chans]

        @pl.when(want)
        def _():
            for j in range(blocks):
                a = jnp.dot(
                    seg[...], series[j * half : j * half + size, :], preferred_element_type=F32
                )
                for i in range(2):
                    at = j * wins + step * 2 + i
                    a_s[pl.ds(at, size, stride=jpitch), :] = a[:, i * chans : (i + 1) * chans]

        return 0

    lax.fori_loop(0, wins // 2, pair, 0)

    def both_parts(ref, k):
        return jnp.concatenate(
            [ref[pl.ds((2 * k + part) * jpitch, jw), :].astype(BF16) for part in range(2)], axis=0
        )

    def second(k, _):
        b_out[k] = both_parts(b_s, k)
        return 0

    def first(k, _):
        a_out[k] = both_parts(a_s, k).T[: a_out.shape[1]]
        return 0

    step = half // STEPS

    def sends(n, stage, target):
        part = pl.ds(n % STEPS * step, step)
        return pltpu.make_async_copy(stage.at[part], target.at[part], out_sem.at[n])

    @pl.when(want)
    def _():
        for n in range(STEPS):
            lax.fori_loop(n * step, (n + 1) * step, first, 0, unroll=8)
            sends(n, a_out, a_hbm).start()

    for n in range(STEPS):
        lax.fori_loop(n * step, (n + 1) * step, second, 0, unroll=8)
        sends(STEPS + n, b_out, b_hbm).start()

    @pl.when(want)
    def _():
        for n in range(STEPS):
            sends(n, a_out, a_hbm).wait()

    for n in range(STEPS):
        sends(STEPS + n, b_out, b_hbm).wait()


def segments(kind, odd, flags, totals, pieces, hann, conv, seg):
    chans = sum(x.shape[0] for x in pieces)
    _, wins, ns = pieces[0].shape
    size = seg.shape[0]
    half = size // 2
    depth = ns // half * wins * 2
    kept = chans if kind == "halo" else chans // 2
    smem = pl.BlockSpec(memory_space=pltpu.SMEM)
    anywhere = pl.BlockSpec(memory_space=pl.ANY)
    tables_in = [hann, conv, seg]
    operands = list(totals) + list(pieces) + tables_in
    a_shape = jax.ShapeDtypeStruct((half, kept, depth), BF16)
    b_shape = jax.ShapeDtypeStruct((half, depth, chans), BF16)
    return pl.pallas_call(
        functools.partial(segments_kernel, kind),
        out_shape=[a_shape, b_shape],
        in_specs=[smem] * 2 + [anywhere] * len(operands),
        out_specs=[anywhere] * 2,
        scratch_shapes=[pltpu.VMEM(value.shape, value.dtype) for value in operands]
        + [
            pltpu.VMEM((len(totals) * NSEC, wins, ns), F32),
            pltpu.VMEM((ns // LANE, chans * (wins + 1), LANE), F32),
            pltpu.VMEM((2 * chans, ns), BF16),
            pltpu.VMEM((ns + half, 2 * chans), BF16),
            pltpu.VMEM((size * (depth // 2 + 1), chans), F32),
            pltpu.VMEM((size * (depth // 2 + 1), chans), F32),
            pltpu.VMEM(a_shape.shape, BF16),
            pltpu.VMEM(b_shape.shape, BF16),
            pltpu.SemaphoreType.DMA((len(operands),)),
            pltpu.SemaphoreType.DMA((2 * STEPS,)),
        ],
        compiler_params=pltpu.CompilerParams(vmem_limit_bytes=VMEM),
        cost_estimate=pl.CostEstimate(
            flops=2 * wins * chans * ns * (ns + 3 * size),
            bytes_accessed=16 * 1024 * 1024,
            transcendentals=0,
        ),
    )(odd, flags, *operands)


def stack_kernel(
    first, scale, me_ref, a0_ref, a1_ref, ah_ref, b0_ref, b1_ref, bh_ref, lag_ref, *rest
):
    outs, (cross, one) = rest[:-2], rest[-2:]
    bins, count, depth = a0_ref.shape
    chans = b0_ref.shape[2]
    width = chans // 2
    nfr = lag_ref.shape[1]
    pitch = nfr + 1
    me = me_ref[0]
    odd = lax.rem(me, 2)
    step = pl.program_id(0)

    def bins_with(left_of):
        def one_bin(k, _):
            left = left_of(k)
            part = depth // 2
            swapped = jnp.concatenate(
                [
                    left[:, part:depth],
                    -left[:, :part],
                    left[:, depth + part :],
                    -left[:, depth : depth + part],
                ],
                axis=1,
            )
            halo = bh_ref[k]
            other = jnp.concatenate([halo[:, width:], halo[:, :width]], axis=1)
            right = jnp.concatenate(
                [
                    jnp.concatenate([b0_ref[k], halo], axis=1),
                    jnp.concatenate([b1_ref[k], other], axis=1),
                ],
                axis=0,
            )
            value = jnp.dot(
                jnp.concatenate([left, swapped], axis=0), right, preferred_element_type=F32
            )
            at = 2 * (step * bins + k)
            for p in range(2):
                for t in range(2):
                    cross[t, pl.ds(at + p, count, stride=pitch), :] = value[
                        p * count : (p + 1) * count, t * chans : (t + 1) * chans
                    ]
            return 0

        lax.fori_loop(0, bins, one_bin, 0, unroll=8)

    @pl.when(odd == 1)
    def _():
        bins_with(lambda k: jnp.concatenate([ah_ref[k, 0], ah_ref[k, 1]], axis=1))

    @pl.when(odd == 0)
    def _():
        bins_with(lambda k: jnp.concatenate([a0_ref[k], a1_ref[k]], axis=1))

    @pl.when(step == pl.num_programs(0) - 1)
    def _():
        row = lax.broadcasted_iota(jnp.int32, one.shape[1:], 0)
        column = lax.broadcasted_iota(jnp.int32, one.shape[1:], 1)
        turned = jnp.where(row < width, row + chans, row - width)
        place = row + (turned - row) * odd
        for t in range(2):
            one[t] = jnp.where(place == column + t * chans, 1.0, 0.0)
        share = OFFS // len(outs)

        def one_channel(c, _):
            value = jnp.concatenate(
                [cross[t, pl.ds(c * pitch, nfr), :] for t in range(2)], axis=1
            ).astype(BF16)
            starts = [first + c + 1 + share * (me ^ d) for d in range(len(outs))]
            pick = jnp.concatenate(
                [
                    jnp.concatenate([one[t, pl.ds(start, share), :] for start in starts], axis=0)
                    for t in range(2)
                ],
                axis=1,
            ).astype(BF16)
            lagged = jnp.dot(lag_ref[...], value, preferred_element_type=F32) * scale
            band = lax.dot_general(pick, lagged.astype(BF16), NT, preferred_element_type=F32)
            for d, out in enumerate(outs):
                out[c] = band[d * share : (d + 1) * share, :].astype(BF16)
            return 0

        lax.fori_loop(0, count, one_channel, 0, unroll=4)


def stacks(index, shares, scale, me, a0, a1, ah, b0, b1, bh, lag):
    bins, width, depth = a0.shape
    chans = b0.shape[2]
    count = width // CHUNKS
    nlag, nfr = lag.shape
    ah = ah.reshape(bins, 2, width, depth)
    block = bins // 8
    left = pl.BlockSpec((block, count, depth), lambda i: (i, index, 0))
    right = pl.BlockSpec((block, depth, chans), lambda i: (i, 0, 0))
    return pl.pallas_call(
        functools.partial(stack_kernel, index * count, scale),
        grid=(bins // block,),
        out_shape=[jax.ShapeDtypeStruct((count, OFFS // shares, nlag), BF16)] * shares,
        in_specs=[
            pl.BlockSpec(memory_space=pltpu.SMEM),
            left,
            left,
            pl.BlockSpec((block, 2, count, depth), lambda i: (i, 0, index, 0)),
            right,
            right,
            right,
            pl.BlockSpec(lag.shape, lambda i: (0, 0)),
        ],
        out_specs=[pl.BlockSpec((count, OFFS // shares, nlag), lambda i: (0, 0, 0))] * shares,
        scratch_shapes=[
            pltpu.VMEM((2, count * (nfr + 1), chans), F32),
            pltpu.VMEM((2, chans + width, chans), F32),
        ],
        compiler_params=pltpu.CompilerParams(vmem_limit_bytes=VMEM),
        cost_estimate=pl.CostEstimate(
            flops=2 * count * bins * 4 * (2 * depth * chans + 2 * OFFS * chans),
            bytes_accessed=20 * 1024 * 1024,
            transcendentals=0,
        ),
    )(me, a0, a1, ah, b0, b1, bh, lag)


def add_over(value, axis):
    count = lax.axis_size(axis)
    if count & (count - 1):
        return lax.psum(value, axis)
    bit = 1
    while bit < count:
        steps = [bit] if bit == 1 or 2 * bit == count else [bit, 2 * bit, 3 * bit]
        value = sum(
            [lax.ppermute(value, axis, [(i, i ^ s) for i in range(count)]) for s in steps], value
        )
        bit *= 1 + len(steps)
    return value


def shards(samples, band_gain, dead_flags, section_ids):
    chans, wins, ns = samples.shape
    nf = ns // 2
    width = chans // 2
    blocks = lax.axis_size("fibre")
    groups = lax.axis_size("tm")
    me = lax.axis_index("tm")
    odd = me % 2
    window, waves, seg, lag = [jnp.asarray(t) for t in tables(ns, nf)]
    hann = jnp.broadcast_to(window[None, :], (wins, ns))
    response = jnp.sum(band_gain[:, None] * waves, axis=0, keepdims=True)
    conv = pl.pallas_call(
        circulant_kernel,
        out_shape=jax.ShapeDtypeStruct((ns, ns), BF16),
        compiler_params=pltpu.CompilerParams(vmem_limit_bytes=VMEM),
    )(response)
    swap = [(z, z ^ 1) for z in range(groups)]
    both = ("fibre", "tm")
    halo_pairs = [
        (b * groups + z, (b + (1 if z % 2 else -1)) % blocks * groups + z)
        for b in range(blocks)
        for z in range(groups)
    ]

    first_half = lax.dynamic_slice_in_dim(samples, (1 - odd) * width, width, 0)
    own_half = lax.dynamic_slice_in_dim(samples, odd * width, width, 0)
    their_first = lax.ppermute(first_half, "tm", swap)
    halo = lax.ppermute(own_half, both, halo_pairs)
    flags = jnp.stack([dead_flags, section_ids])
    halo_flags = lax.ppermute(
        lax.dynamic_slice_in_dim(flags, odd * width, width, 1), both, halo_pairs
    )
    smem = pl.BlockSpec(memory_space=pltpu.SMEM)
    steps = 4
    sums = pl.pallas_call(
        section_sums,
        grid=(steps,),
        out_shape=jax.ShapeDtypeStruct((NSEC, wins, ns + LANE), F32),
        in_specs=[smem, smem, pl.BlockSpec((chans // steps, wins, ns), lambda i: (i, 0, 0))],
        out_specs=pl.BlockSpec((NSEC, wins, ns + LANE), lambda i: (0, 0, 0)),
        compiler_params=pltpu.CompilerParams(vmem_limit_bytes=VMEM),
    )(dead_flags, section_ids, samples)
    total = add_over(sums, "fibre")
    total, halo, halo_flags = lax.optimization_barrier((total, halo, halo_flags))
    their_total = lax.ppermute(total, "tm", swap)
    ready = (total, their_total, their_first, own_half, flags, hann, conv, seg, lag)
    ready = lax.optimization_barrier(ready)
    total, their_total, their_first, own_half, flags, hann, conv, seg, lag = ready
    their_halo = lax.ppermute(their_first, both, halo_pairs)
    their_second = lax.ppermute(own_half, "tm", swap)

    side = odd[None]
    parts = (hann, conv, seg)
    a0, b0 = segments("own", side, flags, (total,), (samples,), *parts)
    ah, bh = segments("halo", side, halo_flags, (total, their_total), (halo, their_halo), *parts)
    bh, their_second = lax.optimization_barrier((bh, their_second))
    a1, b1 = segments("other", side, flags, (their_total,), (their_first, their_second), *parts)
    scale = 2.0 / ns / LAGS / math.sqrt(nf * wins * groups)
    same, other = [], []
    for index in range(CHUNKS):
        found = stacks(index, groups, scale, me[None], a0, a1, ah, b0, b1, bh, lag)
        arrived = []
        for d in range(groups):
            pairs = [
                (b * groups + z, (b - z % 2) % blocks * groups + (z ^ d))
                for b in range(blocks)
                for z in range(groups)
            ]
            arrived.append(lax.ppermute(found[d], both, pairs).astype(F32))
        same.append(sum(arrived[2::2], arrived[0]))
        other.append(sum(arrived[3::2], arrived[1]))
    lower = [jnp.where(odd == 0, s, o) for s, o in zip(same, other)]
    upper = [jnp.where(odd == 0, o, s) for s, o in zip(same, other)]
    return jnp.concatenate(lower + upper, axis=0)


def solution(mesh):
    in_specs = (P("fibre", "tm", None), P(), P("fibre"), P("fibre"))
    out_specs = P("fibre", "tm", None)
    return jax.shard_map(shards, mesh=mesh, in_specs=in_specs, out_specs=out_specs, check_vma=False)
```

```python
import functools
import math

import jax
import jax.numpy as jnp
import ml_dtypes
import numpy as np
from jax import lax
from jax.experimental import pallas as pl
from jax.experimental.pallas import tpu as pltpu
from jax.sharding import PartitionSpec as P

OFFS = 128
LAGS = 128
NSEC = 2
LANE = 128
CHUNKS = 2
TILE = 256
STEPS = 4
TOGETHER = 4
VMEM = 60 * 1024 * 1024
NT = (((1,), (1,)), ((), ()))
F32 = jnp.float32
BF16 = jnp.bfloat16


def tables(ns, nf):
    tick = np.arange(ns)
    freq = np.arange(nf)
    window = 0.5 - 0.5 * np.cos(tick * (2.0 * math.pi / ns))
    waves = np.cos((freq[:, None] * tick[None, :] % ns) * (2.0 * math.pi / ns))
    waves[0] *= math.sqrt(0.5)
    size = 2 * LAGS
    bins = np.arange(size // 2)
    turn = math.pi / size * ((2 * bins[:, None] + 1) * np.arange(size)[None, :] % (2 * size))
    segment = np.stack([np.cos(turn), -np.sin(turn)], axis=1).reshape(size, size)
    lag = np.stack([np.cos(turn), -np.sin(turn)], axis=1).reshape(size, size)[:, :LAGS].T
    cast = lambda a: a.astype(np.float32).astype(ml_dtypes.bfloat16)
    return window.astype(np.float32), waves.astype(np.float32), cast(segment), cast(lag)


def section_sums(dead_ref, sec_ref, x_ref, out_ref):
    chans, wins, ns = x_ref.shape
    first = pl.program_id(0) * chans

    @pl.when(pl.program_id(0) == 0)
    def _():
        out_ref[...] = jnp.zeros_like(out_ref)

    def body(c, carry):
        value = x_ref[c].astype(F32)
        live = 1 - dead_ref[first + c]
        sums, counts = carry
        weights = [jnp.where(sec_ref[first + c] == s, live, 0).astype(F32) for s in range(NSEC)]
        return (
            tuple(sums[s] + weights[s] * value for s in range(NSEC)),
            tuple(counts[s] + weights[s] for s in range(NSEC)),
        )

    zero = jnp.zeros((wins, ns), F32)
    sums, counts = lax.fori_loop(
        0, chans, body, ((zero,) * NSEC, (jnp.float32(0),) * NSEC), unroll=8
    )
    for s in range(NSEC):
        out_ref[s, :, :ns] += sums[s]
        out_ref[s, :, ns:] += jnp.zeros((wins, LANE), F32) + counts[s]


def circulant_kernel(filter_ref, out_ref):
    ns = filter_ref.shape[1]
    rows = 16
    for t in range(0, ns, rows):
        block = jnp.broadcast_to(filter_ref[...], (rows, ns))
        out_ref[t : t + rows, :] = pltpu.roll(block, t, 1, stride=1, stride_axis=0).astype(BF16)


def segments_kernel(kind, odd_ref, flag_ref, *rest):
    sets = {"own": (0,), "halo": (0, 1), "other": (0, 0)}[kind]
    groups = max(sets) + 1
    count = len(sets)
    tot_hbm, rest = rest[:groups], rest[groups:]
    x_hbm, rest = rest[:count], rest[count:]
    hann_hbm, conv_hbm, seg_hbm, a_hbm, b_hbm = rest[:5]
    tot, rest = rest[5 : 5 + groups], rest[5 + groups :]
    x, rest = rest[:count], rest[count:]
    hann, conv, seg, common, clean, rows, series, a_s, b_s, a_out, b_out = rest[:11]
    in_sem, out_sem = rest[11:]
    sources = list(tot_hbm) + [hann_hbm] + list(x_hbm) + [conv_hbm, seg_hbm]
    targets = list(tot) + [hann] + list(x) + [conv, seg]
    copies = [
        pltpu.make_async_copy(source, target, in_sem.at[n])
        for n, (source, target) in enumerate(zip(sources, targets))
    ]
    for copy in copies:
        copy.start()

    _, wins, ns = x[0].shape
    chans = b_out.shape[2]
    pitch = wins + 1
    size = seg.shape[0]
    half = size // 2
    blocks = ns // half
    jw = blocks * wins
    jpitch = jw + 1
    odd = odd_ref[0]
    want = (odd == 1) if kind == "halo" else (odd == 0)
    held = flag_ref.shape[1]
    for g in range(groups):
        copies[g].wait()
        for s in range(NSEC):
            common[g * NSEC + s] = tot[g][s, :, :ns] / jnp.maximum(tot[g][s, :, ns : ns + 1], 1.0)

    copies[groups].wait()
    sign = 1.0 - 2.0 * (lax.broadcasted_iota(jnp.int32, (wins, LANE), 1) % 2).astype(F32)

    for number, group in enumerate(sets):
        copies[groups + 1 + number].wait()
        piece = x[number]
        length = piece.shape[0]
        base = number * length
        if kind == "other":
            base = odd * length if number == 0 else length - odd * length

        def clean_channel(c, _):
            at = base + c
            flag = lax.rem(at, held)
            live = (1 - flag_ref[0, flag]).astype(F32)
            value = (piece[c].astype(F32) - common[group * NSEC + flag_ref[1, flag]]) * hann[...]
            tiles = [value[:, t * LANE : (t + 1) * LANE] for t in range(ns // LANE)]
            mass = sum(tiles[1:], tiles[0])
            square = sum([tile * tile for tile in tiles[1:]], tiles[0] * tiles[0])
            lowest = jnp.sum(mass, axis=1, keepdims=True)
            highest = jnp.sum(mass * sign, axis=1, keepdims=True)
            square = jnp.sum(square, axis=1, keepdims=True)
            power = 0.5 * square + (lowest * lowest - highest * highest) * (0.5 / ns)
            value = value * (lax.rsqrt(power + 1e-06) * live)
            for t in range(ns // LANE):
                clean[t, pl.ds(at * pitch, wins), :] = value[:, t * LANE : (t + 1) * LANE]
            return 0

        lax.fori_loop(0, length, clean_channel, 0, unroll=8)
    for copy in copies[groups + 1 + count :]:
        copy.wait()

    def some_windows(step, _):
        for i in range(TOGETHER):
            w = step * TOGETHER + i
            for t in range(ns // LANE):
                rows[i * chans : (i + 1) * chans, t * LANE : (t + 1) * LANE] = clean[
                    t, pl.ds(w, chans, stride=pitch), :
                ].astype(BF16)
        for t in range(0, ns, TILE):
            series[half // 2 + t : half // 2 + t + TILE, :] = lax.dot_general(
                conv[t : t + TILE, :], rows[...], NT, preferred_element_type=F32
            ).astype(BF16)
        series[: half // 2, :] = series[ns : ns + half // 2, :]
        series[ns + half // 2 :, :] = series[half // 2 : half, :]

        def place(stage, j, value):
            for i in range(TOGETHER):
                at = j * wins + step * TOGETHER + i
                stage[pl.ds(at, size, stride=jpitch), :] = value[:, i * chans : (i + 1) * chans]

        for j in range(blocks):
            start = j * half + half // 2
            b = jnp.dot(
                seg[:, :half], series[start : start + half, :], preferred_element_type=F32
            )
            place(b_s, j, b)

        @pl.when(want)
        def _():
            for j in range(blocks):
                a = jnp.dot(
                    seg[...], series[j * half : j * half + size, :], preferred_element_type=F32
                )
                place(a_s, j, a)

        return 0

    lax.fori_loop(0, wins // TOGETHER, some_windows, 0)

    def both_parts(ref, k):
        return jnp.concatenate(
            [ref[pl.ds((2 * k + part) * jpitch, jw), :].astype(BF16) for part in range(2)], axis=0
        )

    def second(k, _):
        b_out[k] = both_parts(b_s, k)
        return 0

    def first(k, _):
        a_out[k] = both_parts(a_s, k).T[: a_out.shape[1]]
        return 0

    step = half // STEPS

    def sends(n, stage, target):
        part = pl.ds(n % STEPS * step, step)
        return pltpu.make_async_copy(stage.at[part], target.at[part], out_sem.at[n])

    @pl.when(want)
    def _():
        for n in range(STEPS):
            lax.fori_loop(n * step, (n + 1) * step, first, 0, unroll=8)
            sends(n, a_out, a_hbm).start()

    for n in range(STEPS):
        lax.fori_loop(n * step, (n + 1) * step, second, 0, unroll=8)
        sends(STEPS + n, b_out, b_hbm).start()

    @pl.when(want)
    def _():
        for n in range(STEPS):
            sends(n, a_out, a_hbm).wait()

    for n in range(STEPS):
        sends(STEPS + n, b_out, b_hbm).wait()


def segments(kind, odd, flags, totals, pieces, hann, conv, seg):
    chans = sum(x.shape[0] for x in pieces)
    _, wins, ns = pieces[0].shape
    size = seg.shape[0]
    half = size // 2
    depth = ns // half * wins * 2
    kept = chans if kind == "halo" else chans // 2
    smem = pl.BlockSpec(memory_space=pltpu.SMEM)
    anywhere = pl.BlockSpec(memory_space=pl.ANY)
    tables_in = [hann, conv, seg]
    operands = list(totals) + list(pieces) + tables_in
    a_shape = jax.ShapeDtypeStruct((half, kept, depth), BF16)
    b_shape = jax.ShapeDtypeStruct((half, depth, chans), BF16)
    return pl.pallas_call(
        functools.partial(segments_kernel, kind),
        out_shape=[a_shape, b_shape],
        in_specs=[smem] * 2 + [anywhere] * len(operands),
        out_specs=[anywhere] * 2,
        scratch_shapes=[pltpu.VMEM(value.shape, value.dtype) for value in operands]
        + [
            pltpu.VMEM((len(totals) * NSEC, wins, ns), F32),
            pltpu.VMEM((ns // LANE, chans * (wins + 1), LANE), F32),
            pltpu.VMEM((TOGETHER * chans, ns), BF16),
            pltpu.VMEM((ns + half, TOGETHER * chans), BF16),
            pltpu.VMEM((size * (depth // 2 + 1), chans), F32),
            pltpu.VMEM((size * (depth // 2 + 1), chans), F32),
            pltpu.VMEM(a_shape.shape, BF16),
            pltpu.VMEM(b_shape.shape, BF16),
            pltpu.SemaphoreType.DMA((len(operands),)),
            pltpu.SemaphoreType.DMA((2 * STEPS,)),
        ],
        compiler_params=pltpu.CompilerParams(vmem_limit_bytes=VMEM),
        cost_estimate=pl.CostEstimate(
            flops=2 * wins * chans * ns * (ns + 3 * size),
            bytes_accessed=16 * 1024 * 1024,
            transcendentals=0,
        ),
    )(odd, flags, *operands)


def stack_kernel(
    first, scale, me_ref, a0_ref, a1_ref, ah_ref, b0_ref, b1_ref, bh_ref, lag_ref, *rest
):
    outs, (cross, one) = rest[:-2], rest[-2:]
    bins, count, depth = a0_ref.shape
    chans = b0_ref.shape[2]
    width = chans // 2
    nfr = lag_ref.shape[1]
    pitch = nfr + 1
    me = me_ref[0]
    odd = lax.rem(me, 2)
    step = pl.program_id(0)

    def bins_with(left_of):
        def one_bin(k, _):
            part = depth // 2
            halo = bh_ref[k]
            other = jnp.concatenate([halo[:, width:], halo[:, :width]], axis=1)
            right = [
                jnp.concatenate([b0_ref[k], halo], axis=1),
                jnp.concatenate([b1_ref[k], other], axis=1),
            ]
            turned = [piece for r in right for piece in (-r[part:], r[:part])]
            value = jnp.dot(
                left_of(k),
                jnp.concatenate(
                    [jnp.concatenate(right, axis=0), jnp.concatenate(turned, axis=0)], axis=1
                ),
                preferred_element_type=F32,
            )
            at = 2 * (step * bins + k)
            for p in range(2):
                for t in range(2):
                    column = (2 * p + t) * chans
                    cross[t, pl.ds(at + p, count, stride=pitch), :] = value[
                        :, column : column + chans
                    ]
            return 0

        lax.fori_loop(0, bins, one_bin, 0, unroll=8)

    @pl.when(odd == 1)
    def _():
        bins_with(lambda k: jnp.concatenate([ah_ref[k, 0], ah_ref[k, 1]], axis=1))

    @pl.when(odd == 0)
    def _():
        bins_with(lambda k: jnp.concatenate([a0_ref[k], a1_ref[k]], axis=1))

    @pl.when(step == pl.num_programs(0) - 1)
    def _():
        row = lax.broadcasted_iota(jnp.int32, one.shape[1:], 0)
        column = lax.broadcasted_iota(jnp.int32, one.shape[1:], 1)
        turned = jnp.where(row < width, row + chans, row - width)
        place = row + (turned - row) * odd
        for t in range(2):
            one[t] = jnp.where(place == column + t * chans, 1.0, 0.0)
        share = OFFS // len(outs)

        def two_channels(n, _):
            def taken(c):
                return [cross[t, pl.ds(c * pitch, nfr), :] for t in range(2)]

            def pick(c):
                starts = [first + c + 1 + share * (me ^ d) for d in range(len(outs))]
                return jnp.concatenate(
                    [
                        jnp.concatenate([one[t, pl.ds(at, share), :] for at in starts], axis=0)
                        for t in range(2)
                    ],
                    axis=1,
                ).astype(BF16)

            value = jnp.concatenate(taken(2 * n) + taken(2 * n + 1), axis=1).astype(BF16)
            lagged = jnp.dot(lag_ref[...], value, preferred_element_type=F32) * scale
            lagged = lagged.astype(BF16)
            for i in range(2):
                band = lax.dot_general(
                    pick(2 * n + i),
                    lagged[:, 2 * i * chans : 2 * (i + 1) * chans],
                    NT,
                    preferred_element_type=F32,
                )
                for d, out in enumerate(outs):
                    out[2 * n + i] = band[d * share : (d + 1) * share, :].astype(BF16)
            return 0

        lax.fori_loop(0, count // 2, two_channels, 0, unroll=4)


def stacks(index, shares, scale, me, a0, a1, ah, b0, b1, bh, lag):
    bins, width, depth = a0.shape
    chans = b0.shape[2]
    count = width // CHUNKS
    nlag, nfr = lag.shape
    ah = ah.reshape(bins, 2, width, depth)
    block = bins // 8
    left = pl.BlockSpec((block, count, depth), lambda i: (i, index, 0))
    right = pl.BlockSpec((block, depth, chans), lambda i: (i, 0, 0))
    return pl.pallas_call(
        functools.partial(stack_kernel, index * count, scale),
        grid=(bins // block,),
        out_shape=[jax.ShapeDtypeStruct((count, OFFS // shares, nlag), BF16)] * shares,
        in_specs=[
            pl.BlockSpec(memory_space=pltpu.SMEM),
            left,
            left,
            pl.BlockSpec((block, 2, count, depth), lambda i: (i, 0, index, 0)),
            right,
            right,
            right,
            pl.BlockSpec(lag.shape, lambda i: (0, 0)),
        ],
        out_specs=[pl.BlockSpec((count, OFFS // shares, nlag), lambda i: (0, 0, 0))] * shares,
        scratch_shapes=[
            pltpu.VMEM((2, count * (nfr + 1), chans), F32),
            pltpu.VMEM((2, chans + width, chans), F32),
        ],
        compiler_params=pltpu.CompilerParams(vmem_limit_bytes=VMEM),
        cost_estimate=pl.CostEstimate(
            flops=2 * count * bins * 4 * (2 * depth * chans + 2 * OFFS * chans),
            bytes_accessed=20 * 1024 * 1024,
            transcendentals=0,
        ),
    )(me, a0, a1, ah, b0, b1, bh, lag)


def add_over(value, axis):
    count = lax.axis_size(axis)
    if count & (count - 1):
        return lax.psum(value, axis)
    bit = 1
    while bit < count:
        steps = [bit] if bit == 1 or 2 * bit == count else [bit, 2 * bit, 3 * bit]
        value = sum(
            [lax.ppermute(value, axis, [(i, i ^ s) for i in range(count)]) for s in steps], value
        )
        bit *= 1 + len(steps)
    return value


def shards(samples, band_gain, dead_flags, section_ids):
    chans, wins, ns = samples.shape
    nf = ns // 2
    width = chans // 2
    blocks = lax.axis_size("fibre")
    groups = lax.axis_size("tm")
    me = lax.axis_index("tm")
    odd = me % 2
    window, waves, seg, lag = [jnp.asarray(t) for t in tables(ns, nf)]
    hann = jnp.broadcast_to(window[None, :], (wins, ns))
    response = jnp.sum(band_gain[:, None] * waves, axis=0, keepdims=True)
    conv = pl.pallas_call(
        circulant_kernel,
        out_shape=jax.ShapeDtypeStruct((ns, ns), BF16),
        compiler_params=pltpu.CompilerParams(vmem_limit_bytes=VMEM),
    )(response)
    swap = [(z, z ^ 1) for z in range(groups)]
    both = ("fibre", "tm")
    halo_pairs = [
        (b * groups + z, (b + (1 if z % 2 else -1)) % blocks * groups + z)
        for b in range(blocks)
        for z in range(groups)
    ]

    first_half = lax.dynamic_slice_in_dim(samples, (1 - odd) * width, width, 0)
    their_first = lax.ppermute(first_half, "tm", swap)
    flags = jnp.stack([dead_flags, section_ids])
    halo_flags = lax.ppermute(
        lax.dynamic_slice_in_dim(flags, odd * width, width, 1), both, halo_pairs
    )
    smem = pl.BlockSpec(memory_space=pltpu.SMEM)
    steps = 4
    sums = pl.pallas_call(
        section_sums,
        grid=(steps,),
        out_shape=jax.ShapeDtypeStruct((NSEC, wins, ns + LANE), F32),
        in_specs=[smem, smem, pl.BlockSpec((chans // steps, wins, ns), lambda i: (i, 0, 0))],
        out_specs=pl.BlockSpec((NSEC, wins, ns + LANE), lambda i: (0, 0, 0)),
        compiler_params=pltpu.CompilerParams(vmem_limit_bytes=VMEM),
    )(dead_flags, section_ids, samples)
    total = add_over(sums, "fibre")
    total, halo_flags, kept = lax.optimization_barrier((total, halo_flags, samples))
    their_total = lax.ppermute(total, "tm", swap)
    own_half = lax.dynamic_slice_in_dim(kept, odd * width, width, 0)
    halo = lax.ppermute(own_half, both, halo_pairs)
    ready = (total, their_total, their_first, own_half, flags, hann, conv, seg, lag)
    ready = lax.optimization_barrier(ready)
    total, their_total, their_first, own_half, flags, hann, conv, seg, lag = ready
    their_halo = lax.ppermute(their_first, both, halo_pairs)
    their_second = lax.ppermute(own_half, "tm", swap)

    side = odd[None]
    parts = (hann, conv, seg)
    a0, b0 = segments("own", side, flags, (total,), (samples,), *parts)
    ah, bh = segments("halo", side, halo_flags, (total, their_total), (halo, their_halo), *parts)
    bh, their_second = lax.optimization_barrier((bh, their_second))
    a1, b1 = segments("other", side, flags, (their_total,), (their_first, their_second), *parts)
    scale = 2.0 / ns / LAGS / math.sqrt(nf * wins * groups)
    same, other = [], []
    for index in range(CHUNKS):
        found = stacks(index, groups, scale, me[None], a0, a1, ah, b0, b1, bh, lag)
        arrived = []
        for d in range(groups):
            pairs = [
                (b * groups + z, (b - z % 2) % blocks * groups + (z ^ d))
                for b in range(blocks)
                for z in range(groups)
            ]
            arrived.append(lax.ppermute(found[d], both, pairs).astype(F32))
        same.append(sum(arrived[2::2], arrived[0]))
        other.append(sum(arrived[3::2], arrived[1]))
    lower = [jnp.where(odd == 0, s, o) for s, o in zip(same, other)]
    upper = [jnp.where(odd == 0, o, s) for s, o in zip(same, other)]
    return jnp.concatenate(lower + upper, axis=0)


def solution(mesh):
    in_specs = (P("fibre", "tm", None), P(), P("fibre"), P("fibre"))
    out_specs = P("fibre", "tm", None)
    return jax.shard_map(shards, mesh=mesh, in_specs=in_specs, out_specs=out_specs, check_vma=False)
```

```python
import functools
import math

import jax
import jax.numpy as jnp
import ml_dtypes
import numpy as np
from jax import lax
from jax.experimental import pallas as pl
from jax.experimental.pallas import tpu as pltpu
from jax.sharding import PartitionSpec as P

OFFS = 128
LAGS = 128
NSEC = 2
LANE = 128
PIECES = 4
TILE = 256
STEPS = 4
TOGETHER = 4
VMEM = 60 * 1024 * 1024
NT = (((1,), (1,)), ((), ()))
F32 = jnp.float32
BF16 = jnp.bfloat16


def tables(ns, nf):
    tick = np.arange(ns)
    freq = np.arange(nf)
    window = 0.5 - 0.5 * np.cos(tick * (2.0 * math.pi / ns))
    waves = np.cos((freq[:, None] * tick[None, :] % ns) * (2.0 * math.pi / ns))
    waves[0] *= math.sqrt(0.5)
    size = 2 * LAGS
    bins = np.arange(size // 2)
    turn = math.pi / size * ((2 * bins[:, None] + 1) * np.arange(size)[None, :] % (2 * size))
    segment = np.stack([np.cos(turn), -np.sin(turn)], axis=1).reshape(size, size)
    lag = np.stack([np.cos(turn), -np.sin(turn)], axis=1).reshape(size, size)[:, :LAGS].T
    cast = lambda a: a.astype(np.float32).astype(ml_dtypes.bfloat16)
    return window.astype(np.float32), waves.astype(np.float32), cast(segment), cast(lag)


def section_sums(dead_ref, sec_ref, x_ref, out_ref):
    chans, wins, ns = x_ref.shape
    first = pl.program_id(0) * chans

    @pl.when(pl.program_id(0) == 0)
    def _():
        out_ref[...] = jnp.zeros_like(out_ref)

    def body(c, carry):
        value = x_ref[c].astype(F32)
        live = 1 - dead_ref[first + c]
        sums, counts = carry
        weights = [jnp.where(sec_ref[first + c] == s, live, 0).astype(F32) for s in range(NSEC)]
        return (
            tuple(sums[s] + weights[s] * value for s in range(NSEC)),
            tuple(counts[s] + weights[s] for s in range(NSEC)),
        )

    zero = jnp.zeros((wins, ns), F32)
    sums, counts = lax.fori_loop(
        0, chans, body, ((zero,) * NSEC, (jnp.float32(0),) * NSEC), unroll=8
    )
    for s in range(NSEC):
        out_ref[s, :, :ns] += sums[s]
        out_ref[s, :, ns:] += jnp.zeros((wins, LANE), F32) + counts[s]


def circulant_kernel(filter_ref, out_ref):
    ns = filter_ref.shape[1]
    rows = 16
    for t in range(0, ns, rows):
        block = jnp.broadcast_to(filter_ref[...], (rows, ns))
        out_ref[t : t + rows, :] = pltpu.roll(block, t, 1, stride=1, stride_axis=0).astype(BF16)


def segment_factors(kind, odd, flag_ref, tot, x, hann, conv, seg, work, copied, emit):
    common, clean, rows, series, stage = work
    sets = {"own": (0,), "halo": (0, 1), "other": (0, 0)}[kind]
    _, wins, ns = x[0].shape
    chans = sum(piece.shape[0] for piece in x)
    pitch = wins + 1
    size = seg.shape[0]
    half = size // 2
    blocks = ns // half
    jw = blocks * wins
    jpitch = jw + 1
    held = flag_ref.shape[1]
    for copy in copied["first"]:
        copy.wait()
    for g in range(len(tot)):
        for s in range(NSEC):
            common[g * NSEC + s] = tot[g][s, :, :ns] / jnp.maximum(tot[g][s, :, ns : ns + 1], 1.0)
    sign = 1.0 - 2.0 * (lax.broadcasted_iota(jnp.int32, (wins, LANE), 1) % 2).astype(F32)

    for number, group in enumerate(sets):
        piece = x[number]
        length = piece.shape[0]
        base = number * length
        if kind == "other":
            base = odd * length if number == 0 else length - odd * length

        def clean_channel(c, _):
            at = base + c
            flag = lax.rem(at, held)
            live = (1 - flag_ref[0, flag]).astype(F32)
            value = (piece[c].astype(F32) - common[group * NSEC + flag_ref[1, flag]]) * hann[...]
            tiles = [value[:, t * LANE : (t + 1) * LANE] for t in range(ns // LANE)]
            mass = sum(tiles[1:], tiles[0])
            square = sum([tile * tile for tile in tiles[1:]], tiles[0] * tiles[0])
            lowest = jnp.sum(mass, axis=1, keepdims=True)
            highest = jnp.sum(mass * sign, axis=1, keepdims=True)
            square = jnp.sum(square, axis=1, keepdims=True)
            power = 0.5 * square + (lowest * lowest - highest * highest) * (0.5 / ns)
            value = value * (lax.rsqrt(power + 1e-06) * live)
            for t in range(ns // LANE):
                clean[t, pl.ds(at * pitch, wins), :] = value[:, t * LANE : (t + 1) * LANE]
            return 0

        parts = copied["x"][number]
        part = length // len(parts)
        for n, copy in enumerate(parts):
            copy.wait()
            lax.fori_loop(n * part, (n + 1) * part, clean_channel, 0, unroll=8)
    for copy in copied["tables"]:
        copy.wait()
    want = (odd == 1) if kind == "halo" else (odd == 0)

    def some_windows(step, _):
        for i in range(TOGETHER):
            w = step * TOGETHER + i
            for t in range(ns // LANE):
                rows[i * chans : (i + 1) * chans, t * LANE : (t + 1) * LANE] = clean[
                    t, pl.ds(w, chans, stride=pitch), :
                ].astype(BF16)
        for t in range(0, ns, TILE):
            series[half // 2 + t : half // 2 + t + TILE, :] = lax.dot_general(
                conv[t : t + TILE, :], rows[...], NT, preferred_element_type=F32
            ).astype(BF16)
        series[: half // 2, :] = series[ns : ns + half // 2, :]
        series[ns + half // 2 :, :] = series[half // 2 : half, :]

        def place(which, j, value):
            for i in range(TOGETHER):
                at = j * wins + step * TOGETHER + i
                stage[which, pl.ds(at, size, stride=jpitch), :] = value[
                    :, i * chans : (i + 1) * chans
                ]

        for j in range(blocks):
            start = j * half + half // 2
            b = jnp.dot(
                seg[:, :half], series[start : start + half, :], preferred_element_type=F32
            )
            place(1, j, b)

        @pl.when(want)
        def _():
            for j in range(blocks):
                a = jnp.dot(
                    seg[...], series[j * half : j * half + size, :], preferred_element_type=F32
                )
                place(0, j, a)

        return 0

    lax.fori_loop(0, wins // TOGETHER, some_windows, 0)

    def factor(which, k):
        return jnp.concatenate(
            [
                stage[which, pl.ds((2 * k + part) * jpitch, jw), :].astype(BF16)
                for part in range(2)
            ],
            axis=0,
        )

    emit(want, factor)


def work_shapes(groups, chans, wins, ns):
    half = LAGS
    rows = 2 * half * (ns // half * wins + 1)
    return [
        pltpu.VMEM((groups * NSEC, wins, ns), F32),
        pltpu.VMEM((ns // LANE, chans * (wins + 1), LANE), F32),
        pltpu.VMEM((TOGETHER * chans, ns), BF16),
        pltpu.VMEM((ns + half, TOGETHER * chans), BF16),
        pltpu.VMEM((2, rows, chans), F32),
    ]


def input_copies(first, x, tables_in, sem):
    copied = {"first": [], "x": [], "tables": []}
    used = 0

    def copy(source, target):
        nonlocal used
        made = pltpu.make_async_copy(source, target, sem.at[used])
        made.start()
        used += 1
        return made

    copied["first"] = [copy(*pair) for pair in first]
    for source, target in x:
        part = target.shape[0] // PIECES
        copied["x"].append(
            [
                copy(source.at[pl.ds(n * part, part)], target.at[pl.ds(n * part, part)])
                for n in range(PIECES)
            ]
        )
    copied["tables"] = [copy(*pair) for pair in tables_in]
    return copied


def segments_kernel(kind, groups, count, odd_ref, flag_ref, *rest):
    tot_hbm, rest = rest[:groups], rest[groups:]
    x_hbm, rest = rest[:count], rest[count:]
    hann_hbm, conv_hbm, seg_hbm, a_hbm, b_hbm = rest[:5]
    tot, rest = rest[5 : 5 + groups], rest[5 + groups :]
    x, rest = rest[:count], rest[count:]
    hann, conv, seg = rest[:3]
    work, (a_out, b_out, in_sem, out_sem) = rest[3:-4], rest[-4:]
    copied = input_copies(
        list(zip(tot_hbm, tot)) + [(hann_hbm, hann)],
        list(zip(x_hbm, x)),
        [(conv_hbm, conv), (seg_hbm, seg)],
        in_sem,
    )
    bins = b_out.shape[0]
    step = bins // STEPS

    def emit(want, factor):
        def first(k, _):
            a_out[k] = factor(0, k).T[: a_out.shape[1]]
            return 0

        def second(k, _):
            b_out[k] = factor(1, k)
            return 0

        def send(n, source, target):
            part = pl.ds(n % STEPS * step, step)
            return pltpu.make_async_copy(source.at[part], target.at[part], out_sem.at[n])

        @pl.when(want)
        def _():
            for n in range(STEPS):
                lax.fori_loop(n * step, (n + 1) * step, first, 0, unroll=8)
                send(n, a_out, a_hbm).start()

        for n in range(STEPS):
            lax.fori_loop(n * step, (n + 1) * step, second, 0, unroll=8)
            send(STEPS + n, b_out, b_hbm).start()

        @pl.when(want)
        def _():
            for n in range(STEPS):
                send(n, a_out, a_hbm).wait()

        for n in range(STEPS):
            send(STEPS + n, b_out, b_hbm).wait()

    segment_factors(
        kind, odd_ref[0], flag_ref, tot, x, hann, conv, seg, work, copied, emit
    )


def segments(kind, odd, flags, totals, pieces, hann, conv, seg):
    chans = sum(x.shape[0] for x in pieces)
    _, wins, ns = pieces[0].shape
    size = seg.shape[0]
    half = size // 2
    depth = ns // half * wins * 2
    kept = chans if kind == "halo" else chans // 2
    smem = pl.BlockSpec(memory_space=pltpu.SMEM)
    anywhere = pl.BlockSpec(memory_space=pl.ANY)
    operands = list(totals) + list(pieces) + [hann, conv, seg]
    a_shape = jax.ShapeDtypeStruct((half, kept, depth), BF16)
    b_shape = jax.ShapeDtypeStruct((half, depth, chans), BF16)
    return pl.pallas_call(
        functools.partial(segments_kernel, kind, len(totals), len(pieces)),
        out_shape=[a_shape, b_shape],
        in_specs=[smem] * 2 + [anywhere] * len(operands),
        out_specs=[anywhere] * 2,
        scratch_shapes=[pltpu.VMEM(value.shape, value.dtype) for value in operands]
        + work_shapes(len(totals), chans, wins, ns)
        + [
            pltpu.VMEM(a_shape.shape, BF16),
            pltpu.VMEM(b_shape.shape, BF16),
            pltpu.SemaphoreType.DMA((len(operands) + len(pieces) * PIECES,)),
            pltpu.SemaphoreType.DMA((2 * STEPS,)),
        ],
        compiler_params=pltpu.CompilerParams(vmem_limit_bytes=VMEM),
        cost_estimate=pl.CostEstimate(
            flops=2 * wins * chans * ns * (ns + 3 * size),
            bytes_accessed=16 * 1024 * 1024,
            transcendentals=0,
        ),
    )(odd, flags, *operands)


def stack_kernel(scale, shares, me_ref, flag_ref, *rest):
    tot_hbm, x0_hbm, x1_hbm, hann_hbm, conv_hbm, seg_hbm, lag_hbm = rest[:7]
    left_hbm, rest = rest[7:11], rest[11:]
    outs, rest = rest[:shares], rest[shares:]
    tot, x0, x1, hann, conv, seg, lag = rest[:7]
    (a0, ah, b0, bh), rest = rest[7:11], rest[11:]
    work, (a1, b1, one, in_sem, late_sem) = rest[:-5], rest[-5:]
    me = me_ref[0]
    odd = lax.rem(me, 2)
    copied = input_copies(
        [(tot_hbm, tot), (hann_hbm, hann)],
        [(x0_hbm, x0), (x1_hbm, x1)],
        [(conv_hbm, conv), (seg_hbm, seg), (lag_hbm, lag)],
        in_sem,
    )
    late = [
        pltpu.make_async_copy(source, target, late_sem.at[n])
        for n, (source, target) in enumerate(zip(left_hbm, (a0, ah, b0, bh)))
    ]
    for copy in late:
        copy.start()
    bins, width, depth = a0.shape
    chans = b0.shape[2]
    nfr = lag.shape[1]
    pitch = nfr + 1
    cross = work[-1]

    def emit(want, factor):
        def first(k, _):
            a1[k] = factor(0, k).T[:width]
            return 0

        def second(k, _):
            b1[k] = factor(1, k)
            return 0

        @pl.when(want)
        def _():
            lax.fori_loop(0, bins, first, 0, unroll=8)

        lax.fori_loop(0, bins, second, 0, unroll=8)

    segment_factors(
        "other", odd, flag_ref, [tot], [x0, x1], hann, conv, seg, work, copied, emit
    )
    for copy in late:
        copy.wait()

    def bins_with(left_of):
        def one_bin(k, _):
            left = left_of(k)
            part = depth // 2
            swapped = jnp.concatenate(
                [
                    left[:, part:depth],
                    -left[:, :part],
                    left[:, depth + part :],
                    -left[:, depth : depth + part],
                ],
                axis=1,
            )
            halo = bh[k]
            other = jnp.concatenate([halo[:, width:], halo[:, :width]], axis=1)
            right = jnp.concatenate(
                [
                    jnp.concatenate([b0[k], halo], axis=1),
                    jnp.concatenate([b1[k], other], axis=1),
                ],
                axis=0,
            )
            value = jnp.dot(
                jnp.concatenate([left, swapped], axis=0), right, preferred_element_type=F32
            )
            for p in range(2):
                for t in range(2):
                    cross[t, pl.ds(2 * k + p, width, stride=pitch), :] = value[
                        p * width : (p + 1) * width, t * chans : (t + 1) * chans
                    ]
            return 0

        lax.fori_loop(0, bins, one_bin, 0, unroll=8)

    @pl.when(odd == 1)
    def _():
        bins_with(lambda k: jnp.concatenate([ah[k, :width], ah[k, width:]], axis=1))

    @pl.when(odd == 0)
    def _():
        bins_with(lambda k: jnp.concatenate([a0[k], a1[k]], axis=1))

    row = lax.broadcasted_iota(jnp.int32, one.shape[1:], 0)
    column = lax.broadcasted_iota(jnp.int32, one.shape[1:], 1)
    turned = jnp.where(row < width, row + chans, row - width)
    place = row + (turned - row) * odd
    for t in range(2):
        one[t] = jnp.where(place == column + t * chans, 1.0, 0.0)
    share = OFFS // shares

    def one_channel(c, _):
        value = jnp.concatenate(
            [cross[t, pl.ds(c * pitch, nfr), :] for t in range(2)], axis=1
        ).astype(BF16)
        starts = [c + 1 + share * (me ^ d) for d in range(shares)]
        pick = jnp.concatenate(
            [
                jnp.concatenate([one[t, pl.ds(start, share), :] for start in starts], axis=0)
                for t in range(2)
            ],
            axis=1,
        ).astype(BF16)
        lagged = jnp.dot(lag[...], value, preferred_element_type=F32) * scale
        band = lax.dot_general(pick, lagged.astype(BF16), NT, preferred_element_type=F32)
        for d, out in enumerate(outs):
            out[c] = band[d * share : (d + 1) * share, :].astype(BF16)
        return 0

    lax.fori_loop(0, width, one_channel, 0, unroll=4)


def stacks(shares, scale, me, flags, total, pieces, hann, conv, seg, lag, a0, ah, b0, bh):
    bins, width, depth = a0.shape
    chans = b0.shape[2]
    _, wins, ns = pieces[0].shape
    nlag, nfr = lag.shape
    smem = pl.BlockSpec(memory_space=pltpu.SMEM)
    vmem = pl.BlockSpec(memory_space=pltpu.VMEM)
    anywhere = pl.BlockSpec(memory_space=pl.ANY)
    operands = [total, *pieces, hann, conv, seg, lag, a0, ah, b0, bh]
    return pl.pallas_call(
        functools.partial(stack_kernel, scale, shares),
        out_shape=[jax.ShapeDtypeStruct((width, OFFS // shares, nlag), BF16)] * shares,
        in_specs=[smem] * 2 + [anywhere] * len(operands),
        out_specs=[vmem] * shares,
        scratch_shapes=[pltpu.VMEM(value.shape, value.dtype) for value in operands]
        + work_shapes(1, chans, wins, ns)
        + [
            pltpu.VMEM(a0.shape, BF16),
            pltpu.VMEM(b0.shape, BF16),
            pltpu.VMEM((2, chans + width, chans), F32),
            pltpu.SemaphoreType.DMA((8 + len(pieces) * PIECES,)),
            pltpu.SemaphoreType.DMA((4,)),
        ],
        compiler_params=pltpu.CompilerParams(vmem_limit_bytes=VMEM),
        cost_estimate=pl.CostEstimate(
            flops=2 * width * bins * 4 * (2 * depth * chans + 2 * OFFS * chans),
            bytes_accessed=20 * 1024 * 1024,
            transcendentals=0,
        ),
    )(me, flags, *operands)


def add_over(value, axis):
    count = lax.axis_size(axis)
    if count & (count - 1):
        return lax.psum(value, axis)
    bit = 1
    while bit < count:
        steps = [bit] if bit == 1 or 2 * bit == count else [bit, 2 * bit, 3 * bit]
        value = sum(
            [lax.ppermute(value, axis, [(i, i ^ s) for i in range(count)]) for s in steps], value
        )
        bit *= 1 + len(steps)
    return value


def shards(samples, band_gain, dead_flags, section_ids):
    chans, wins, ns = samples.shape
    nf = ns // 2
    width = chans // 2
    blocks = lax.axis_size("fibre")
    groups = lax.axis_size("tm")
    me = lax.axis_index("tm")
    odd = me % 2
    window, waves, seg, lag = [jnp.asarray(t) for t in tables(ns, nf)]
    hann = jnp.broadcast_to(window[None, :], (wins, ns))
    response = jnp.sum(band_gain[:, None] * waves, axis=0, keepdims=True)
    conv = pl.pallas_call(
        circulant_kernel,
        out_shape=jax.ShapeDtypeStruct((ns, ns), BF16),
        compiler_params=pltpu.CompilerParams(vmem_limit_bytes=VMEM),
    )(response)
    swap = [(z, z ^ 1) for z in range(groups)]
    both = ("fibre", "tm")
    halo_pairs = [
        (b * groups + z, (b + (1 if z % 2 else -1)) % blocks * groups + z)
        for b in range(blocks)
        for z in range(groups)
    ]

    first_half = lax.dynamic_slice_in_dim(samples, (1 - odd) * width, width, 0)
    their_first = lax.ppermute(first_half, "tm", swap)
    flags = jnp.stack([dead_flags, section_ids])
    halo_flags = lax.ppermute(
        lax.dynamic_slice_in_dim(flags, odd * width, width, 1), both, halo_pairs
    )
    smem = pl.BlockSpec(memory_space=pltpu.SMEM)
    steps = 4
    sums = pl.pallas_call(
        section_sums,
        grid=(steps,),
        out_shape=jax.ShapeDtypeStruct((NSEC, wins, ns + LANE), F32),
        in_specs=[smem, smem, pl.BlockSpec((chans // steps, wins, ns), lambda i: (i, 0, 0))],
        out_specs=pl.BlockSpec((NSEC, wins, ns + LANE), lambda i: (0, 0, 0)),
        compiler_params=pltpu.CompilerParams(vmem_limit_bytes=VMEM),
    )(dead_flags, section_ids, samples)
    total = add_over(sums, "fibre")
    total, halo_flags, kept = lax.optimization_barrier((total, halo_flags, samples))
    their_total = lax.ppermute(total, "tm", swap)
    own_half = lax.dynamic_slice_in_dim(kept, odd * width, width, 0)
    halo = lax.ppermute(own_half, both, halo_pairs)
    ready = (total, their_total, their_first, own_half, flags, hann, conv, seg, lag)
    ready = lax.optimization_barrier(ready)
    total, their_total, their_first, own_half, flags, hann, conv, seg, lag = ready
    their_halo = lax.ppermute(their_first, both, halo_pairs)
    their_second = lax.ppermute(own_half, "tm", swap)

    side = odd[None]
    parts = (hann, conv, seg)
    a0, b0 = segments("own", side, flags, (total,), (samples,), *parts)
    ah, bh = segments("halo", side, halo_flags, (total, their_total), (halo, their_halo), *parts)
    scale = 2.0 / ns / LAGS / math.sqrt(nf * wins * groups)
    found = stacks(
        groups,
        scale,
        me[None],
        flags,
        their_total,
        (their_first, their_second),
        *(hann, conv, seg, lag),
        *(a0, ah, b0, bh),
    )
    arrived = []
    for d in range(groups):
        pairs = [
            (b * groups + z, (b - z % 2) % blocks * groups + (z ^ d))
            for b in range(blocks)
            for z in range(groups)
        ]
        arrived.append(lax.ppermute(found[d], both, pairs).astype(F32))
    same = sum(arrived[2::2], arrived[0])
    other = sum(arrived[3::2], arrived[1])
    return jnp.concatenate(
        [jnp.where(odd == 0, same, other), jnp.where(odd == 0, other, same)], axis=0
    )


def solution(mesh):
    in_specs = (P("fibre", "tm", None), P(), P("fibre"), P("fibre"))
    out_specs = P("fibre", "tm", None)
    return jax.shard_map(shards, mesh=mesh, in_specs=in_specs, out_specs=out_specs, check_vma=False)
```

```python
import functools
import math

import jax
import jax.numpy as jnp
import ml_dtypes
import numpy as np
from jax import lax
from jax.experimental import pallas as pl
from jax.experimental.pallas import tpu as pltpu
from jax.sharding import PartitionSpec as P

OFFS = 128
LAGS = 128
NSEC = 2
LANE = 128
PART = 16
TILE = 256
STEPS = 4
TOGETHER = 4
VMEM = 63 * 1024 * 1024
NT = (((1,), (1,)), ((), ()))
F32 = jnp.float32
BF16 = jnp.bfloat16


def tables(ns, nf):
    tick = np.arange(ns)
    freq = np.arange(nf)
    window = 0.5 - 0.5 * np.cos(tick * (2.0 * math.pi / ns))
    waves = np.cos((freq[:, None] * tick[None, :] % ns) * (2.0 * math.pi / ns))
    waves[0] *= math.sqrt(0.5)
    size = 2 * LAGS
    bins = np.arange(size // 2)
    turn = math.pi / size * ((2 * bins[:, None] + 1) * np.arange(size)[None, :] % (2 * size))
    segment = np.stack([np.cos(turn), -np.sin(turn)], axis=1).reshape(size, size)
    lag = np.stack([np.cos(turn), -np.sin(turn)], axis=1).reshape(size, size)[:, :LAGS].T
    cast = lambda a: a.astype(np.float32).astype(ml_dtypes.bfloat16)
    return window.astype(np.float32), waves.astype(np.float32), cast(segment), cast(lag)


def section_sums(dead_ref, sec_ref, x_ref, out_ref):
    chans, wins, ns = x_ref.shape
    first = pl.program_id(0) * chans

    @pl.when(pl.program_id(0) == 0)
    def _():
        out_ref[...] = jnp.zeros_like(out_ref)

    def body(c, carry):
        value = x_ref[c].astype(F32)
        live = 1 - dead_ref[first + c]
        sums, counts = carry
        weights = [jnp.where(sec_ref[first + c] == s, live, 0).astype(F32) for s in range(NSEC)]
        return (
            tuple(sums[s] + weights[s] * value for s in range(NSEC)),
            tuple(counts[s] + weights[s] for s in range(NSEC)),
        )

    zero = jnp.zeros((wins, ns), F32)
    sums, counts = lax.fori_loop(
        0, chans, body, ((zero,) * NSEC, (jnp.float32(0),) * NSEC), unroll=8
    )
    for s in range(NSEC):
        out_ref[s, :, :ns] += sums[s]
        out_ref[s, :, ns:] += jnp.zeros((wins, LANE), F32) + counts[s]


def circulant(filter_ref, out_ref):
    ns = filter_ref.shape[1]

    for t in range(0, ns, 16):
        block = jnp.broadcast_to(filter_ref[...], (16, ns))
        out_ref[t : t + 16, :] = pltpu.roll(block, t, 1, stride=1, stride_axis=0).astype(BF16)


def segment_factors(places, want, odd, flag_ref, tot, x, hann, response, seg, work, copied, emit):
    common, clean, rows, series, conv, stage = work
    _, wins, ns = x[0].shape
    chans = sum(piece.shape[0] for piece in x)
    pitch = wins + 1
    size = seg.shape[0]
    half = size // 2
    blocks = ns // half
    jw = blocks * wins
    jpitch = jw + 1
    held = flag_ref.shape[1]
    for copy in copied["first"]:
        copy.wait()
    circulant(response, conv)
    for g in range(len(tot)):
        for s in range(NSEC):
            common[g * NSEC + s] = tot[g][s, :, :ns] / jnp.maximum(tot[g][s, :, ns : ns + 1], 1.0)
    sign = 1.0 - 2.0 * (lax.broadcasted_iota(jnp.int32, (wins, LANE), 1) % 2).astype(F32)

    for number, (group, even_base, odd_base) in enumerate(places):
        piece = x[number]
        length = piece.shape[0]
        base = even_base + odd * (odd_base - even_base)

        def clean_channel(c, _):
            at = base + c
            flag = lax.rem(at, held)
            live = (1 - flag_ref[0, flag]).astype(F32)
            value = (piece[c].astype(F32) - common[group * NSEC + flag_ref[1, flag]]) * hann[...]
            tiles = [value[:, t * LANE : (t + 1) * LANE] for t in range(ns // LANE)]
            mass = sum(tiles[1:], tiles[0])
            square = sum([tile * tile for tile in tiles[1:]], tiles[0] * tiles[0])
            lowest = jnp.sum(mass, axis=1, keepdims=True)
            highest = jnp.sum(mass * sign, axis=1, keepdims=True)
            square = jnp.sum(square, axis=1, keepdims=True)
            power = 0.5 * square + (lowest * lowest - highest * highest) * (0.5 / ns)
            value = value * (lax.rsqrt(power + 1e-06) * live)
            for t in range(ns // LANE):
                clean[t, pl.ds(at * pitch, wins), :] = value[:, t * LANE : (t + 1) * LANE]
            return 0

        parts = copied["x"][number]
        part = length // len(parts)
        for n, copy in enumerate(parts):
            copy.wait()
            lax.fori_loop(n * part, (n + 1) * part, clean_channel, 0, unroll=4)
    for copy in copied["tables"]:
        copy.wait()

    def some_windows(step, _):
        for i in range(TOGETHER):
            w = step * TOGETHER + i
            for t in range(ns // LANE):
                rows[i * chans : (i + 1) * chans, t * LANE : (t + 1) * LANE] = clean[
                    t, pl.ds(w, chans, stride=pitch), :
                ].astype(BF16)
        for t in range(0, ns, TILE):
            series[half // 2 + t : half // 2 + t + TILE, :] = lax.dot_general(
                conv[t : t + TILE, :], rows[...], NT, preferred_element_type=F32
            ).astype(BF16)
        series[: half // 2, :] = series[ns : ns + half // 2, :]
        series[ns + half // 2 :, :] = series[half // 2 : half, :]

        def place(which, j, value):
            for i in range(TOGETHER):
                at = j * wins + step * TOGETHER + i
                stage[which, pl.ds(at, size, stride=jpitch), :] = value[
                    :, i * chans : (i + 1) * chans
                ]

        for j in range(blocks):
            start = j * half + half // 2
            b = jnp.dot(
                seg[:, :half], series[start : start + half, :], preferred_element_type=F32
            )
            place(1, j, b)

        @pl.when(want)
        def _():
            for j in range(blocks):
                a = jnp.dot(
                    seg[...], series[j * half : j * half + size, :], preferred_element_type=F32
                )
                place(0, j, a)

        return 0

    lax.fori_loop(0, wins // TOGETHER, some_windows, 0)

    def factor(which, k):
        return jnp.concatenate(
            [
                stage[which, pl.ds((2 * k + part) * jpitch, jw), :].astype(BF16)
                for part in range(2)
            ],
            axis=0,
        )

    emit(want, factor)


def work_shapes(groups, chans, wins, ns):
    half = LAGS
    rows = 2 * half * (ns // half * wins + 1)
    return [
        pltpu.VMEM((groups * NSEC, wins, ns), F32),
        pltpu.VMEM((ns // LANE, chans * (wins + 1), LANE), F32),
        pltpu.VMEM((TOGETHER * chans, ns), BF16),
        pltpu.VMEM((ns + half, TOGETHER * chans), BF16),
        pltpu.VMEM((ns, ns), BF16),
        pltpu.VMEM((2, rows, chans), F32),
    ]


def input_copies(first, x, tables_in, sem):
    copied = {"first": [], "x": [], "tables": []}
    used = 0

    def copy(source, target):
        nonlocal used
        made = pltpu.make_async_copy(source, target, sem.at[used])
        made.start()
        used += 1
        return made

    copied["first"] = [copy(*pair) for pair in first]
    for source, target in x:
        parts = max(target.shape[0] // PART, 1)
        part = target.shape[0] // parts
        copied["x"].append(
            [
                copy(source.at[pl.ds(n * part, part)], target.at[pl.ds(n * part, part)])
                for n in range(parts)
            ]
        )
    copied["tables"] = [copy(*pair) for pair in tables_in]
    return copied


def segments_kernel(places, wanted, groups, odd_ref, flag_ref, *rest):
    count = len(places)
    tot_hbm, rest = rest[:groups], rest[groups:]
    x_hbm, rest = rest[:count], rest[count:]
    hann_hbm, response_hbm, seg_hbm, a_hbm, b_hbm = rest[:5]
    tot, rest = rest[5 : 5 + groups], rest[5 + groups :]
    x, rest = rest[:count], rest[count:]
    hann, response, seg = rest[:3]
    work, (a_out, b_out, in_sem, out_sem) = rest[3:-4], rest[-4:]
    copied = input_copies(
        list(zip(tot_hbm, tot)) + [(hann_hbm, hann), (response_hbm, response)],
        list(zip(x_hbm, x)),
        [(seg_hbm, seg)],
        in_sem,
    )
    bins = b_out.shape[0]
    step = bins // STEPS

    def emit(want, factor):
        def first(k, _):
            a_out[k] = factor(0, k).T[: a_out.shape[1]]
            return 0

        def second(k, _):
            b_out[k] = factor(1, k)
            return 0

        def send(n, source, target):
            part = pl.ds(n % STEPS * step, step)
            return pltpu.make_async_copy(source.at[part], target.at[part], out_sem.at[n])

        @pl.when(want)
        def _():
            for n in range(STEPS):
                lax.fori_loop(n * step, (n + 1) * step, first, 0, unroll=8)
                send(n, a_out, a_hbm).start()

        for n in range(STEPS):
            lax.fori_loop(n * step, (n + 1) * step, second, 0, unroll=8)
            send(STEPS + n, b_out, b_hbm).start()

        @pl.when(want)
        def _():
            for n in range(STEPS):
                send(n, a_out, a_hbm).wait()

        for n in range(STEPS):
            send(STEPS + n, b_out, b_hbm).wait()

    odd = odd_ref[0]
    segment_factors(
        places, odd == wanted, odd, flag_ref, tot, x, hann, response, seg, work, copied, emit
    )


def segments(places, wanted, odd, flags, totals, pieces, hann, response, seg):
    chans = sum(x.shape[0] for x in pieces)
    _, wins, ns = pieces[0].shape
    size = seg.shape[0]
    half = size // 2
    depth = ns // half * wins * 2
    kept = chans if wanted else chans // 2
    smem = pl.BlockSpec(memory_space=pltpu.SMEM)
    anywhere = pl.BlockSpec(memory_space=pl.ANY)
    operands = list(totals) + list(pieces) + [hann, response, seg]
    a_shape = jax.ShapeDtypeStruct((half, kept, depth), BF16)
    b_shape = jax.ShapeDtypeStruct((half, depth, chans), BF16)
    return pl.pallas_call(
        functools.partial(segments_kernel, places, wanted, len(totals)),
        out_shape=[a_shape, b_shape],
        in_specs=[smem] * 2 + [anywhere] * len(operands),
        out_specs=[anywhere] * 2,
        scratch_shapes=[pltpu.VMEM(value.shape, value.dtype) for value in operands]
        + work_shapes(len(totals), chans, wins, ns)
        + [
            pltpu.VMEM(a_shape.shape, BF16),
            pltpu.VMEM(b_shape.shape, BF16),
            pltpu.SemaphoreType.DMA((len(operands) + chans // PART,)),
            pltpu.SemaphoreType.DMA((2 * STEPS,)),
        ],
        compiler_params=pltpu.CompilerParams(vmem_limit_bytes=VMEM),
        cost_estimate=pl.CostEstimate(
            flops=2 * wins * chans * ns * (ns + 3 * size),
            bytes_accessed=16 * 1024 * 1024,
            transcendentals=0,
        ),
    )(odd, flags, *operands)


def stack_kernel(places, scale, shares, me_ref, flag_ref, *rest):
    count = len(places)
    x_hbm, rest = rest[:count], rest[count:]
    tot_hbm, hann_hbm, response_hbm, seg_hbm, lag_hbm = rest[:5]
    left_hbm, rest = rest[5:9], rest[9:]
    outs, rest = rest[:shares], rest[shares:]
    x, rest = rest[:count], rest[count:]
    tot, hann, response, seg, lag = rest[:5]
    (a0, ah, b0, bh), rest = rest[5:9], rest[9:]
    work, (a1, b1, one, in_sem, late_sem) = rest[:-5], rest[-5:]
    me = me_ref[0]
    odd = lax.rem(me, 2)
    copied = input_copies(
        [(tot_hbm, tot), (hann_hbm, hann), (response_hbm, response)],
        list(zip(x_hbm, x)),
        [(seg_hbm, seg), (lag_hbm, lag)],
        in_sem,
    )
    late = [
        pltpu.make_async_copy(source, target, late_sem.at[n])
        for n, (source, target) in enumerate(zip(left_hbm, (a0, ah, b0, bh)))
    ]
    for copy in late:
        copy.start()
    bins, width, depth = a0.shape
    chans = b0.shape[2]
    nfr = lag.shape[1]
    pitch = nfr + 1
    cross = work[-1]

    def emit(want, factor):
        def first(k, _):
            a1[k] = factor(0, k).T[:width]
            return 0

        def second(k, _):
            b1[k] = factor(1, k)
            return 0

        @pl.when(want)
        def _():
            lax.fori_loop(0, bins, first, 0, unroll=8)

        lax.fori_loop(0, bins, second, 0, unroll=8)

    segment_factors(
        places, odd == 0, odd, flag_ref, [tot], x, hann, response, seg, work, copied, emit
    )
    for copy in late:
        copy.wait()

    def bins_with(left_of):
        def one_bin(k, _):
            left = left_of(k)
            part = depth // 2
            swapped = jnp.concatenate(
                [
                    left[:, part:depth],
                    -left[:, :part],
                    left[:, depth + part :],
                    -left[:, depth : depth + part],
                ],
                axis=1,
            )
            halo = bh[k]
            other = jnp.concatenate([halo[:, width:], halo[:, :width]], axis=1)
            right = jnp.concatenate(
                [
                    jnp.concatenate([b0[k], halo], axis=1),
                    jnp.concatenate([b1[k], other], axis=1),
                ],
                axis=0,
            )
            value = jnp.dot(
                jnp.concatenate([left, swapped], axis=0), right, preferred_element_type=F32
            )
            for p in range(2):
                for t in range(2):
                    cross[t, pl.ds(2 * k + p, width, stride=pitch), :] = value[
                        p * width : (p + 1) * width, t * chans : (t + 1) * chans
                    ]
            return 0

        lax.fori_loop(0, bins, one_bin, 0, unroll=8)

    @pl.when(odd == 1)
    def _():
        bins_with(lambda k: jnp.concatenate([ah[k, :width], ah[k, width:]], axis=1))

    @pl.when(odd == 0)
    def _():
        bins_with(lambda k: jnp.concatenate([a0[k], a1[k]], axis=1))

    row = lax.broadcasted_iota(jnp.int32, one.shape[1:], 0)
    column = lax.broadcasted_iota(jnp.int32, one.shape[1:], 1)
    turned = jnp.where(row < width, row + chans, row - width)
    place = row + (turned - row) * odd
    for t in range(2):
        one[t] = jnp.where(place == column + t * chans, 1.0, 0.0)
    share = OFFS // shares

    def one_channel(c, _):
        value = jnp.concatenate(
            [cross[t, pl.ds(c * pitch, nfr), :] for t in range(2)], axis=1
        ).astype(BF16)
        starts = [c + 1 + share * (me ^ d) for d in range(shares)]
        pick = jnp.concatenate(
            [
                jnp.concatenate([one[t, pl.ds(start, share), :] for start in starts], axis=0)
                for t in range(2)
            ],
            axis=1,
        ).astype(BF16)
        lagged = jnp.dot(lag[...], value, preferred_element_type=F32) * scale
        band = lax.dot_general(pick, lagged.astype(BF16), NT, preferred_element_type=F32)
        for d, out in enumerate(outs):
            out[c] = band[d * share : (d + 1) * share, :].astype(BF16)
        return 0

    lax.fori_loop(0, width, one_channel, 0, unroll=4)


def stacks(places, shares, scale, me, flags, total, pieces, hann, response, seg, lag, a0, ah, b0, bh):
    bins, width, depth = a0.shape
    chans = b0.shape[2]
    _, wins, ns = pieces[0].shape
    nlag, nfr = lag.shape
    smem = pl.BlockSpec(memory_space=pltpu.SMEM)
    vmem = pl.BlockSpec(memory_space=pltpu.VMEM)
    anywhere = pl.BlockSpec(memory_space=pl.ANY)
    operands = [*pieces, total, hann, response, seg, lag, a0, ah, b0, bh]
    return pl.pallas_call(
        functools.partial(stack_kernel, places, scale, shares),
        out_shape=[jax.ShapeDtypeStruct((width, OFFS // shares, nlag), BF16)] * shares,
        in_specs=[smem] * 2 + [anywhere] * len(operands),
        out_specs=[vmem] * shares,
        scratch_shapes=[pltpu.VMEM(value.shape, value.dtype) for value in operands]
        + work_shapes(1, chans, wins, ns)
        + [
            pltpu.VMEM(a0.shape, BF16),
            pltpu.VMEM(b0.shape, BF16),
            pltpu.VMEM((2, chans + width, chans), F32),
            pltpu.SemaphoreType.DMA((8 + chans // PART,)),
            pltpu.SemaphoreType.DMA((4,)),
        ],
        compiler_params=pltpu.CompilerParams(vmem_limit_bytes=VMEM),
        cost_estimate=pl.CostEstimate(
            flops=2 * width * bins * 4 * (2 * depth * chans + 2 * OFFS * chans),
            bytes_accessed=20 * 1024 * 1024,
            transcendentals=0,
        ),
    )(me, flags, *operands)


def add_over(value, axis):
    count = lax.axis_size(axis)
    if count & (count - 1):
        return lax.psum(value, axis)
    bit = 1
    while bit < count:
        steps = [bit] if bit == 1 or 2 * bit == count else [bit, 2 * bit, 3 * bit]
        value = sum(
            [lax.ppermute(value, axis, [(i, i ^ s) for i in range(count)]) for s in steps], value
        )
        bit *= 1 + len(steps)
    return value


def shards(samples, band_gain, dead_flags, section_ids):
    chans, wins, ns = samples.shape
    nf = ns // 2
    width = chans // 2
    blocks = lax.axis_size("fibre")
    groups = lax.axis_size("tm")
    me = lax.axis_index("tm")
    odd = me % 2
    window, waves, seg, lag = [jnp.asarray(t) for t in tables(ns, nf)]
    hann = jnp.broadcast_to(window[None, :], (wins, ns))
    response = jnp.sum(band_gain[:, None] * waves, axis=0, keepdims=True)
    swap = [(z, z ^ 1) for z in range(groups)]
    both = ("fibre", "tm")
    halo_pairs = [
        (b * groups + z, (b + (1 if z % 2 else -1)) % blocks * groups + z)
        for b in range(blocks)
        for z in range(groups)
    ]

    head = width * 5 // 8

    def part_of(array, upper, start, length):
        return lax.dynamic_slice_in_dim(array, upper * width + start, length, 0)

    their_head = lax.ppermute(part_of(samples, 1 - odd, 0, head), "tm", swap)
    flags = jnp.stack([dead_flags, section_ids])
    halo_flags = lax.ppermute(
        lax.dynamic_slice_in_dim(flags, odd * width, width, 1), both, halo_pairs
    )
    smem = pl.BlockSpec(memory_space=pltpu.SMEM)
    steps = 4
    sums = pl.pallas_call(
        section_sums,
        grid=(steps,),
        out_shape=jax.ShapeDtypeStruct((NSEC, wins, ns + LANE), F32),
        in_specs=[smem, smem, pl.BlockSpec((chans // steps, wins, ns), lambda i: (i, 0, 0))],
        out_specs=pl.BlockSpec((NSEC, wins, ns + LANE), lambda i: (0, 0, 0)),
        compiler_params=pltpu.CompilerParams(vmem_limit_bytes=VMEM),
    )(dead_flags, section_ids, samples)
    total = add_over(sums, "fibre")
    total, halo_flags, kept, their_head, response = lax.optimization_barrier(
        (total, halo_flags, samples, their_head, response)
    )
    their_total = lax.ppermute(total, "tm", swap)
    own_half = part_of(kept, odd, 0, width)
    tail = part_of(kept, 1 - odd, head, width - head)
    halo = lax.ppermute(own_half, both, halo_pairs)
    ready = (total, their_total, their_head, own_half, tail, flags, hann, response, seg, lag)
    ready = lax.optimization_barrier(ready)
    total, their_total, their_head, own_half, tail, flags, hann, response, seg, lag = ready
    their_tail = lax.ppermute(tail, "tm", swap)
    their_second = lax.ppermute(own_half, "tm", swap)
    halo_head = lax.ppermute(their_head, both, halo_pairs)

    side = odd[None]
    parts = (hann, response, seg)
    a0, b0 = segments(((0, 0, 0),), 0, side, flags, (total,), (samples,), *parts)
    b0, forward = lax.optimization_barrier((b0, their_tail))
    halo_tail = lax.ppermute(forward, both, halo_pairs)
    ah, bh = segments(
        ((0, 0, 0), (1, width, width), (1, width + head, width + head)),
        1,
        side,
        halo_flags,
        (total, their_total),
        (halo, halo_head, halo_tail),
        *parts,
    )
    scale = 2.0 / ns / LAGS / math.sqrt(nf * wins * groups)
    found = stacks(
        ((0, 0, width), (0, head, width + head), (0, width, 0)),
        groups,
        scale,
        me[None],
        flags,
        their_total,
        (their_head, their_tail, their_second),
        *(hann, response, seg, lag),
        *(a0, ah, b0, bh),
    )
    arrived = []
    for d in range(groups):
        pairs = [
            (b * groups + z, (b - z % 2) % blocks * groups + (z ^ d))
            for b in range(blocks)
            for z in range(groups)
        ]
        arrived.append(lax.ppermute(found[d], both, pairs).astype(F32))
    same = sum(arrived[2::2], arrived[0])
    other = sum(arrived[3::2], arrived[1])
    return jnp.concatenate(
        [jnp.where(odd == 0, same, other), jnp.where(odd == 0, other, same)], axis=0
    )


def solution(mesh):
    in_specs = (P("fibre", "tm", None), P(), P("fibre"), P("fibre"))
    out_specs = P("fibre", "tm", None)
    return jax.shard_map(shards, mesh=mesh, in_specs=in_specs, out_specs=out_specs, check_vma=False)
```

```python
import functools
import math

import jax
import jax.numpy as jnp
import ml_dtypes
import numpy as np
from jax import lax
from jax.experimental import pallas as pl
from jax.experimental.pallas import tpu as pltpu
from jax.sharding import PartitionSpec as P

OFFS = 128
LAGS = 128
NSEC = 2
LANE = 128
PART = 16
TILE = 256
STEPS = 4
TOGETHER = 4
VMEM = 63 * 1024 * 1024
NT = (((1,), (1,)), ((), ()))
F32 = jnp.float32
BF16 = jnp.bfloat16


def tables(ns, nf):
    tick = np.arange(ns)
    freq = np.arange(nf)
    window = 0.5 - 0.5 * np.cos(tick * (2.0 * math.pi / ns))
    waves = np.cos((freq[:, None] * tick[None, :] % ns) * (2.0 * math.pi / ns))
    waves[0] *= math.sqrt(0.5)
    size = 2 * LAGS
    bins = np.arange(size // 2)
    turn = math.pi / size * ((2 * bins[:, None] + 1) * np.arange(size)[None, :] % (2 * size))
    segment = np.stack([np.cos(turn), -np.sin(turn)], axis=1).reshape(size, size)
    lag = np.stack([np.cos(turn), -np.sin(turn)], axis=1).reshape(size, size)[:, :LAGS].T
    cast = lambda a: a.astype(np.float32).astype(ml_dtypes.bfloat16)
    return window.astype(np.float32), waves.astype(np.float32), cast(segment), cast(lag)


def section_sums(dead_ref, sec_ref, x_ref, out_ref):
    chans, wins, ns = x_ref.shape
    first = pl.program_id(0) * chans

    @pl.when(pl.program_id(0) == 0)
    def _():
        out_ref[...] = jnp.zeros_like(out_ref)

    def body(c, carry):
        value = x_ref[c].astype(F32)
        live = 1 - dead_ref[first + c]
        sums, counts = carry
        weights = [jnp.where(sec_ref[first + c] == s, live, 0).astype(F32) for s in range(NSEC)]
        return (
            tuple(sums[s] + weights[s] * value for s in range(NSEC)),
            tuple(counts[s] + weights[s] for s in range(NSEC)),
        )

    zero = jnp.zeros((wins, ns), F32)
    sums, counts = lax.fori_loop(
        0, chans, body, ((zero,) * NSEC, (jnp.float32(0),) * NSEC), unroll=8
    )
    for s in range(NSEC):
        out_ref[s, :, :ns] += sums[s]
        out_ref[s, :, ns:] += jnp.zeros((wins, LANE), F32) + counts[s]


def circulant_kernel(filter_ref, out_ref):
    ns = filter_ref.shape[1]
    for t in range(0, ns, 16):
        block = jnp.broadcast_to(filter_ref[...], (16, ns))
        out_ref[t : t + 16, :] = pltpu.roll(block, t, 1, stride=1, stride_axis=0).astype(BF16)


def segment_factors(places, want, odd, flag_ref, tot, x, hann, conv, seg, work, copied, emit):
    common, clean, rows, series, stage = work
    _, wins, ns = x[0].shape
    chans = sum(piece.shape[0] for piece in x)
    pitch = wins + 1
    size = seg.shape[0]
    half = size // 2
    blocks = ns // half
    jw = blocks * wins
    jpitch = jw + 1
    held = flag_ref.shape[1]
    for copy in copied["first"]:
        copy.wait()
    for g in range(len(tot)):
        for s in range(NSEC):
            common[g * NSEC + s] = tot[g][s, :, :ns] / jnp.maximum(tot[g][s, :, ns : ns + 1], 1.0)
    sign = 1.0 - 2.0 * (lax.broadcasted_iota(jnp.int32, (wins, LANE), 1) % 2).astype(F32)

    for number, (group, even_base, odd_base) in enumerate(places):
        piece = x[number]
        length = piece.shape[0]
        base = even_base + odd * (odd_base - even_base)

        def clean_channel(c, _):
            at = base + c
            flag = lax.rem(at, held)
            live = (1 - flag_ref[0, flag]).astype(F32)
            value = (piece[c].astype(F32) - common[group * NSEC + flag_ref[1, flag]]) * hann[...]
            tiles = [value[:, t * LANE : (t + 1) * LANE] for t in range(ns // LANE)]
            mass = sum(tiles[1:], tiles[0])
            square = sum([tile * tile for tile in tiles[1:]], tiles[0] * tiles[0])
            lowest = jnp.sum(mass, axis=1, keepdims=True)
            highest = jnp.sum(mass * sign, axis=1, keepdims=True)
            square = jnp.sum(square, axis=1, keepdims=True)
            power = 0.5 * square + (lowest * lowest - highest * highest) * (0.5 / ns)
            value = value * (lax.rsqrt(power + 1e-06) * live)
            for t in range(ns // LANE):
                clean[t, pl.ds(at * pitch, wins), :] = value[:, t * LANE : (t + 1) * LANE]
            return 0

        parts = copied["x"][number]
        part = length // len(parts)
        for n, copy in enumerate(parts):
            copy.wait()
            lax.fori_loop(n * part, (n + 1) * part, clean_channel, 0, unroll=4)
    for copy in copied["tables"]:
        copy.wait()

    def some_windows(step, _):
        for i in range(TOGETHER):
            w = step * TOGETHER + i
            for t in range(ns // LANE):
                rows[i * chans : (i + 1) * chans, t * LANE : (t + 1) * LANE] = clean[
                    t, pl.ds(w, chans, stride=pitch), :
                ].astype(BF16)
        for t in range(0, ns, TILE):
            series[half // 2 + t : half // 2 + t + TILE, :] = lax.dot_general(
                conv[t : t + TILE, :], rows[...], NT, preferred_element_type=F32
            ).astype(BF16)
        series[: half // 2, :] = series[ns : ns + half // 2, :]
        series[ns + half // 2 :, :] = series[half // 2 : half, :]

        def place(which, j, value):
            for i in range(TOGETHER):
                at = j * wins + step * TOGETHER + i
                stage[which, pl.ds(at, size, stride=jpitch), :] = value[
                    :, i * chans : (i + 1) * chans
                ]

        for j in range(blocks):
            start = j * half + half // 2
            b = jnp.dot(
                seg[:, :half], series[start : start + half, :], preferred_element_type=F32
            )
            place(1, j, b)

        @pl.when(want)
        def _():
            for j in range(blocks):
                a = jnp.dot(
                    seg[...], series[j * half : j * half + size, :], preferred_element_type=F32
                )
                place(0, j, a)

        return 0

    lax.fori_loop(0, wins // TOGETHER, some_windows, 0)

    def factor(which, k):
        return jnp.concatenate(
            [
                stage[which, pl.ds((2 * k + part) * jpitch, jw), :].astype(BF16)
                for part in range(2)
            ],
            axis=0,
        )

    emit(want, factor)


def work_shapes(groups, chans, wins, ns):
    half = LAGS
    rows = 2 * half * (ns // half * wins + 1)
    return [
        pltpu.VMEM((groups * NSEC, wins, ns), F32),
        pltpu.VMEM((ns // LANE, chans * (wins + 1), LANE), F32),
        pltpu.VMEM((TOGETHER * chans, ns), BF16),
        pltpu.VMEM((ns + half, TOGETHER * chans), BF16),
        pltpu.VMEM((2, rows, chans), F32),
    ]


def input_copies(first, x, tables_in, sem):
    copied = {"first": [], "x": [], "tables": []}
    used = 0

    def copy(source, target):
        nonlocal used
        made = pltpu.make_async_copy(source, target, sem.at[used])
        made.start()
        used += 1
        return made

    copied["first"] = [copy(*pair) for pair in first]
    for source, target in x:
        parts = max(target.shape[0] // PART, 1)
        part = target.shape[0] // parts
        copied["x"].append(
            [
                copy(source.at[pl.ds(n * part, part)], target.at[pl.ds(n * part, part)])
                for n in range(parts)
            ]
        )
    copied["tables"] = [copy(*pair) for pair in tables_in]
    return copied


def segments_kernel(places, wanted, groups, odd_ref, flag_ref, *rest):
    count = len(places)
    tot_hbm, rest = rest[:groups], rest[groups:]
    x_hbm, rest = rest[:count], rest[count:]
    hann_hbm, conv_hbm, seg_hbm, a_hbm, b_hbm = rest[:5]
    tot, rest = rest[5 : 5 + groups], rest[5 + groups :]
    x, rest = rest[:count], rest[count:]
    hann, conv, seg = rest[:3]
    work, (a_out, b_out, in_sem, out_sem) = rest[3:-4], rest[-4:]
    copied = input_copies(
        list(zip(tot_hbm, tot)) + [(hann_hbm, hann)],
        list(zip(x_hbm, x)),
        [(conv_hbm, conv), (seg_hbm, seg)],
        in_sem,
    )
    bins = b_out.shape[0]
    step = bins // STEPS

    def emit(want, factor):
        def first(k, _):
            a_out[k] = factor(0, k).T[: a_out.shape[1]]
            return 0

        def second(k, _):
            b_out[k] = factor(1, k)
            return 0

        def send(n, source, target):
            part = pl.ds(n % STEPS * step, step)
            return pltpu.make_async_copy(source.at[part], target.at[part], out_sem.at[n])

        @pl.when(want)
        def _():
            for n in range(STEPS):
                lax.fori_loop(n * step, (n + 1) * step, first, 0, unroll=8)
                send(n, a_out, a_hbm).start()

        for n in range(STEPS):
            lax.fori_loop(n * step, (n + 1) * step, second, 0, unroll=8)
            send(STEPS + n, b_out, b_hbm).start()

        @pl.when(want)
        def _():
            for n in range(STEPS):
                send(n, a_out, a_hbm).wait()

        for n in range(STEPS):
            send(STEPS + n, b_out, b_hbm).wait()

    odd = odd_ref[0]
    segment_factors(
        places, odd == wanted, odd, flag_ref, tot, x, hann, conv, seg, work, copied, emit
    )


def segments(places, wanted, odd, flags, totals, pieces, hann, conv, seg):
    chans = sum(x.shape[0] for x in pieces)
    _, wins, ns = pieces[0].shape
    size = seg.shape[0]
    half = size // 2
    depth = ns // half * wins * 2
    kept = chans if wanted else chans // 2
    smem = pl.BlockSpec(memory_space=pltpu.SMEM)
    anywhere = pl.BlockSpec(memory_space=pl.ANY)
    operands = list(totals) + list(pieces) + [hann, conv, seg]
    a_shape = jax.ShapeDtypeStruct((half, kept, depth), BF16)
    b_shape = jax.ShapeDtypeStruct((half, depth, chans), BF16)
    return pl.pallas_call(
        functools.partial(segments_kernel, places, wanted, len(totals)),
        out_shape=[a_shape, b_shape],
        in_specs=[smem] * 2 + [anywhere] * len(operands),
        out_specs=[anywhere] * 2,
        scratch_shapes=[pltpu.VMEM(value.shape, value.dtype) for value in operands]
        + work_shapes(len(totals), chans, wins, ns)
        + [
            pltpu.VMEM(a_shape.shape, BF16),
            pltpu.VMEM(b_shape.shape, BF16),
            pltpu.SemaphoreType.DMA((len(operands) + chans // PART,)),
            pltpu.SemaphoreType.DMA((2 * STEPS,)),
        ],
        compiler_params=pltpu.CompilerParams(vmem_limit_bytes=VMEM),
        cost_estimate=pl.CostEstimate(
            flops=2 * wins * chans * ns * (ns + 3 * size),
            bytes_accessed=16 * 1024 * 1024,
            transcendentals=0,
        ),
    )(odd, flags, *operands)


def stack_kernel(places, scale, shares, me_ref, flag_ref, *rest):
    count = len(places)
    x_hbm, rest = rest[:count], rest[count:]
    tot_hbm, hann_hbm, conv_hbm, seg_hbm, lag_hbm = rest[:5]
    left_hbm, rest = rest[5:9], rest[9:]
    outs, rest = rest[:shares], rest[shares:]
    x, rest = rest[:count], rest[count:]
    tot, hann, conv, seg, lag = rest[:5]
    (a0, ah, b0, bh), rest = rest[5:9], rest[9:]
    work, (a1, b1, one, in_sem, late_sem) = rest[:-5], rest[-5:]
    me = me_ref[0]
    odd = lax.rem(me, 2)
    copied = input_copies(
        [(tot_hbm, tot), (hann_hbm, hann)],
        list(zip(x_hbm, x)),
        [(conv_hbm, conv), (seg_hbm, seg), (lag_hbm, lag)],
        in_sem,
    )
    late = [
        pltpu.make_async_copy(source, target, late_sem.at[n])
        for n, (source, target) in enumerate(zip(left_hbm, (a0, ah, b0, bh)))
    ]
    for copy in late:
        copy.start()
    bins, width, depth = a0.shape
    chans = b0.shape[2]
    nfr = lag.shape[1]
    pitch = nfr + 1
    cross = work[-1]

    def emit(want, factor):
        def first(k, _):
            a1[k] = factor(0, k).T[:width]
            return 0

        def second(k, _):
            b1[k] = factor(1, k)
            return 0

        @pl.when(want)
        def _():
            lax.fori_loop(0, bins, first, 0, unroll=8)

        lax.fori_loop(0, bins, second, 0, unroll=8)

    segment_factors(
        places, odd == 0, odd, flag_ref, [tot], x, hann, conv, seg, work, copied, emit
    )
    for copy in late:
        copy.wait()

    def bins_with(left_of):
        def one_bin(k, _):
            left = left_of(k)
            part = depth // 2
            swapped = jnp.concatenate(
                [
                    left[:, part:depth],
                    -left[:, :part],
                    left[:, depth + part :],
                    -left[:, depth : depth + part],
                ],
                axis=1,
            )
            halo = bh[k]
            other = jnp.concatenate([halo[:, width:], halo[:, :width]], axis=1)
            right = jnp.concatenate(
                [
                    jnp.concatenate([b0[k], halo], axis=1),
                    jnp.concatenate([b1[k], other], axis=1),
                ],
                axis=0,
            )
            value = jnp.dot(
                jnp.concatenate([left, swapped], axis=0), right, preferred_element_type=F32
            )
            for p in range(2):
                for t in range(2):
                    cross[t, pl.ds(2 * k + p, width, stride=pitch), :] = value[
                        p * width : (p + 1) * width, t * chans : (t + 1) * chans
                    ]
            return 0

        lax.fori_loop(0, bins, one_bin, 0, unroll=8)

    @pl.when(odd == 1)
    def _():
        bins_with(lambda k: jnp.concatenate([ah[k, :width], ah[k, width:]], axis=1))

    @pl.when(odd == 0)
    def _():
        bins_with(lambda k: jnp.concatenate([a0[k], a1[k]], axis=1))

    row = lax.broadcasted_iota(jnp.int32, one.shape[1:], 0)
    column = lax.broadcasted_iota(jnp.int32, one.shape[1:], 1)
    turned = jnp.where(row < width, row + chans, row - width)
    place = row + (turned - row) * odd
    for t in range(2):
        one[t] = jnp.where(place == column + t * chans, 1.0, 0.0)
    share = OFFS // shares

    def one_channel(c, _):
        value = jnp.concatenate(
            [cross[t, pl.ds(c * pitch, nfr), :] for t in range(2)], axis=1
        ).astype(BF16)
        starts = [c + 1 + share * (me ^ d) for d in range(shares)]
        pick = jnp.concatenate(
            [
                jnp.concatenate([one[t, pl.ds(start, share), :] for start in starts], axis=0)
                for t in range(2)
            ],
            axis=1,
        ).astype(BF16)
        lagged = jnp.dot(lag[...], value, preferred_element_type=F32) * scale
        band = lax.dot_general(pick, lagged.astype(BF16), NT, preferred_element_type=F32)
        for d, out in enumerate(outs):
            out[c] = band[d * share : (d + 1) * share, :].astype(BF16)
        return 0

    lax.fori_loop(0, width, one_channel, 0, unroll=4)


def stacks(places, shares, scale, me, flags, total, pieces, hann, conv, seg, lag, a0, ah, b0, bh):
    bins, width, depth = a0.shape
    chans = b0.shape[2]
    _, wins, ns = pieces[0].shape
    nlag, nfr = lag.shape
    smem = pl.BlockSpec(memory_space=pltpu.SMEM)
    vmem = pl.BlockSpec(memory_space=pltpu.VMEM)
    anywhere = pl.BlockSpec(memory_space=pl.ANY)
    operands = [*pieces, total, hann, conv, seg, lag, a0, ah, b0, bh]
    return pl.pallas_call(
        functools.partial(stack_kernel, places, scale, shares),
        out_shape=[jax.ShapeDtypeStruct((width, OFFS // shares, nlag), BF16)] * shares,
        in_specs=[smem] * 2 + [anywhere] * len(operands),
        out_specs=[vmem] * shares,
        scratch_shapes=[pltpu.VMEM(value.shape, value.dtype) for value in operands]
        + work_shapes(1, chans, wins, ns)
        + [
            pltpu.VMEM(a0.shape, BF16),
            pltpu.VMEM(b0.shape, BF16),
            pltpu.VMEM((2, chans + width, chans), F32),
            pltpu.SemaphoreType.DMA((8 + chans // PART,)),
            pltpu.SemaphoreType.DMA((4,)),
        ],
        compiler_params=pltpu.CompilerParams(vmem_limit_bytes=VMEM),
        cost_estimate=pl.CostEstimate(
            flops=2 * width * bins * 4 * (2 * depth * chans + 2 * OFFS * chans),
            bytes_accessed=20 * 1024 * 1024,
            transcendentals=0,
        ),
    )(me, flags, *operands)


def add_over(value, axis, beside):
    count = lax.axis_size(axis)
    if count & (count - 1):
        return lax.psum(value, axis), beside
    bit = 1
    while bit < count:
        steps = [bit] if bit == 1 or 2 * bit == count else [bit, 2 * bit, 3 * bit]
        arrived = [lax.ppermute(value, axis, [(i, i ^ s) for i in range(count)]) for s in steps]
        bit *= 1 + len(steps)
        if bit == count:
            arrived, beside = lax.optimization_barrier((arrived, beside))
        value = sum(arrived, value)
    return value, beside


def shards(samples, band_gain, dead_flags, section_ids):
    chans, wins, ns = samples.shape
    nf = ns // 2
    width = chans // 2
    blocks = lax.axis_size("fibre")
    groups = lax.axis_size("tm")
    me = lax.axis_index("tm")
    odd = me % 2
    window, waves, seg, lag = [jnp.asarray(t) for t in tables(ns, nf)]
    hann = jnp.broadcast_to(window[None, :], (wins, ns))
    response = jnp.sum(band_gain[:, None] * waves, axis=0, keepdims=True)
    conv = pl.pallas_call(
        circulant_kernel,
        out_shape=jax.ShapeDtypeStruct((ns, ns), BF16),
        compiler_params=pltpu.CompilerParams(vmem_limit_bytes=VMEM),
        cost_estimate=pl.CostEstimate(flops=1, bytes_accessed=1, transcendentals=0),
    )(response)
    swap = [(z, z ^ 1) for z in range(groups)]
    both = ("fibre", "tm")
    halo_pairs = [
        (b * groups + z, (b + (1 if z % 2 else -1)) % blocks * groups + z)
        for b in range(blocks)
        for z in range(groups)
    ]

    head = width * 5 // 8

    def part_of(array, upper, start, length):
        return lax.dynamic_slice_in_dim(array, upper * width + start, length, 0)

    their_head = lax.ppermute(part_of(samples, 1 - odd, 0, head), "tm", swap)
    flags = jnp.stack([dead_flags, section_ids])
    halo_flags = lax.ppermute(
        lax.dynamic_slice_in_dim(flags, odd * width, width, 1), both, halo_pairs
    )
    smem = pl.BlockSpec(memory_space=pltpu.SMEM)
    steps = 4
    sums = pl.pallas_call(
        section_sums,
        grid=(steps,),
        out_shape=jax.ShapeDtypeStruct((NSEC, wins, ns + LANE), F32),
        in_specs=[smem, smem, pl.BlockSpec((chans // steps, wins, ns), lambda i: (i, 0, 0))],
        out_specs=pl.BlockSpec((NSEC, wins, ns + LANE), lambda i: (0, 0, 0)),
        compiler_params=pltpu.CompilerParams(vmem_limit_bytes=VMEM),
        cost_estimate=pl.CostEstimate(flops=1, bytes_accessed=1, transcendentals=0),
    )(dead_flags, section_ids, samples)
    total, their_head = add_over(sums, "fibre", their_head)
    total, halo_flags, kept, conv = lax.optimization_barrier(
        (total, halo_flags, samples, conv)
    )
    their_total = lax.ppermute(total, "tm", swap)
    own_half = part_of(kept, odd, 0, width)
    tail = part_of(kept, 1 - odd, head, width - head)
    halo = lax.ppermute(own_half, both, halo_pairs)
    ready = (total, their_total, their_head, own_half, tail, flags, hann, conv, seg, lag)
    ready = lax.optimization_barrier(ready)
    total, their_total, their_head, own_half, tail, flags, hann, conv, seg, lag = ready
    their_tail = lax.ppermute(tail, "tm", swap)
    their_second = lax.ppermute(own_half, "tm", swap)
    halo_head = lax.ppermute(their_head, both, halo_pairs)

    side = odd[None]
    parts = (hann, conv, seg)
    a0, b0 = segments(((0, 0, 0),), 0, side, flags, (total,), (samples,), *parts)
    b0, forward = lax.optimization_barrier((b0, their_tail))
    halo_tail = lax.ppermute(forward, both, halo_pairs)
    ah, bh = segments(
        ((0, 0, 0), (1, width, width), (1, width + head, width + head)),
        1,
        side,
        halo_flags,
        (total, their_total),
        (halo, halo_head, halo_tail),
        *parts,
    )
    scale = 2.0 / ns / LAGS / math.sqrt(nf * wins * groups)
    found = stacks(
        ((0, 0, width), (0, head, width + head), (0, width, 0)),
        groups,
        scale,
        me[None],
        flags,
        their_total,
        (their_head, their_tail, their_second),
        *(hann, conv, seg, lag),
        *(a0, ah, b0, bh),
    )
    arrived = []
    for d in range(groups):
        pairs = [
            (b * groups + z, (b - z % 2) % blocks * groups + (z ^ d))
            for b in range(blocks)
            for z in range(groups)
        ]
        arrived.append(lax.ppermute(found[d], both, pairs).astype(F32))
    same = sum(arrived[2::2], arrived[0])
    other = sum(arrived[3::2], arrived[1])
    return jnp.concatenate(
        [jnp.where(odd == 0, same, other), jnp.where(odd == 0, other, same)], axis=0
    )


def solution(mesh):
    in_specs = (P("fibre", "tm", None), P(), P("fibre"), P("fibre"))
    out_specs = P("fibre", "tm", None)
    return jax.shard_map(shards, mesh=mesh, in_specs=in_specs, out_specs=out_specs, check_vma=False)
```

```python
import functools
import math

import jax
import jax.numpy as jnp
import ml_dtypes
import numpy as np
from jax import lax
from jax.experimental import pallas as pl
from jax.experimental.pallas import tpu as pltpu
from jax.sharding import PartitionSpec as P

OFFS = 128
LAGS = 128
NSEC = 2
LANE = 128
PART = 16
TILE = 256
STEPS = 4
TOGETHER = 4
VMEM = 63 * 1024 * 1024
NT = (((1,), (1,)), ((), ()))
F32 = jnp.float32
BF16 = jnp.bfloat16


def tables(ns, nf):
    tick = np.arange(ns)
    freq = np.arange(nf)
    window = 0.5 - 0.5 * np.cos(tick * (2.0 * math.pi / ns))
    waves = np.cos((freq[:, None] * tick[None, :] % ns) * (2.0 * math.pi / ns))
    waves[0] *= math.sqrt(0.5)
    size = 2 * LAGS
    bins = np.arange(size // 2)
    turn = math.pi / size * ((2 * bins[:, None] + 1) * np.arange(size)[None, :] % (2 * size))
    segment = np.stack([np.cos(turn), -np.sin(turn)], axis=1).reshape(size, size)
    lag = np.stack([np.cos(turn), -np.sin(turn)], axis=1).reshape(size, size)[:, :LAGS].T
    cast = lambda a: a.astype(np.float32).astype(ml_dtypes.bfloat16)
    return window.astype(np.float32), waves.astype(np.float32), cast(segment), cast(lag)


def section_sums(odd_ref, dead_ref, sec_ref, x_ref, whole_ref, out_ref, half_ref, tail_ref, sem):
    chans, wins, ns = x_ref.shape
    first = pl.program_id(0) * chans
    width, length = half_ref.shape[0], tail_ref.shape[0]
    odd = odd_ref[0]
    copies = [
        pltpu.make_async_copy(whole_ref.at[pl.ds(odd * width, width)], half_ref, sem.at[0]),
        pltpu.make_async_copy(
            whole_ref.at[pl.ds((2 - odd) * width - length, length)], tail_ref, sem.at[1]
        ),
    ]

    @pl.when(pl.program_id(0) == 0)
    def _():
        out_ref[...] = jnp.zeros_like(out_ref)
        for copy in copies:
            copy.start()

    def body(c, carry):
        value = x_ref[c].astype(F32)
        live = 1 - dead_ref[first + c]
        sums, counts = carry
        weights = [jnp.where(sec_ref[first + c] == s, live, 0).astype(F32) for s in range(NSEC)]
        return (
            tuple(sums[s] + weights[s] * value for s in range(NSEC)),
            tuple(counts[s] + weights[s] for s in range(NSEC)),
        )

    zero = jnp.zeros((wins, ns), F32)
    sums, counts = lax.fori_loop(
        0, chans, body, ((zero,) * NSEC, (jnp.float32(0),) * NSEC), unroll=8
    )
    for s in range(NSEC):
        out_ref[s, :, :ns] += sums[s]
        out_ref[s, :, ns:] += jnp.zeros((wins, LANE), F32) + counts[s]

    @pl.when(pl.program_id(0) == pl.num_programs(0) - 1)
    def _():
        for copy in copies:
            copy.wait()


def circulant_kernel(filter_ref, out_ref):
    ns = filter_ref.shape[1]
    for t in range(0, ns, 16):
        block = jnp.broadcast_to(filter_ref[...], (16, ns))
        out_ref[t : t + 16, :] = pltpu.roll(block, t, 1, stride=1, stride_axis=0).astype(BF16)


def segment_factors(places, want, repeat, odd, flag_ref, tot, x, hann, conv, seg, work, copied, emit):
    common, clean, mass, square, rows, series, series_a, stage = work
    _, wins, ns = x[0].shape
    chans = sum(piece.shape[0] for piece in x)
    pitch = wins + 1
    size = seg.shape[0]
    half = size // 2
    blocks = ns // half
    jw = blocks * wins
    jpitch = jw + 1
    held = flag_ref.shape[1]
    for copy in copied["first"]:
        copy.wait()
    for g in range(len(tot)):
        for s in range(NSEC):
            common[g * NSEC + s] = tot[g][s, :, :ns] / jnp.maximum(tot[g][s, :, ns : ns + 1], 1.0)
    sign = 1.0 - 2.0 * (lax.broadcasted_iota(jnp.int32, (chans, LANE), 1) % 2).astype(F32)
    lower = lax.broadcasted_iota(jnp.int32, (1, LANE), 1) < LANE // 2

    for number, (group, even_base, odd_base) in enumerate(places):
        piece = x[number]
        length = piece.shape[0]
        base = even_base + odd * (odd_base - even_base)

        def clean_channel(c, _):
            at = base + c
            flag = lax.rem(at, held)
            live = (1 - flag_ref[0, flag]).astype(F32)
            value = (piece[c].astype(F32) - common[group * NSEC + flag_ref[1, flag]]) * (
                hann[...] * live
            )
            tiles = [value[:, t * LANE : (t + 1) * LANE] for t in range(ns // LANE)]
            row = pl.ds(at * pitch, wins)
            mass[row, :] = sum(tiles[1:], tiles[0])
            square[row, :] = sum([tile * tile for tile in tiles[1:]], tiles[0] * tiles[0])
            for t, tile in enumerate(tiles):
                clean[t, row, :] = tile
            return 0

        parts = copied["x"][number]
        part = length // len(parts)
        for n, copy in enumerate(parts):
            copy.wait()
            lax.fori_loop(n * part, (n + 1) * part, clean_channel, 0, unroll=8)
    for copy in copied["tables"]:
        copy.wait()

    def some_windows(step, _):
        for i in range(TOGETHER):
            window = pl.ds(step * TOGETHER + i, chans, stride=pitch)
            total = mass[window, :]
            lowest = jnp.sum(total, axis=1, keepdims=True)
            highest = jnp.sum(total * sign, axis=1, keepdims=True)
            power = 0.5 * jnp.sum(square[window, :], axis=1, keepdims=True)
            power = power + (lowest * lowest - highest * highest) * (0.5 / ns)
            level = lax.rsqrt(power + 1e-06)
            for t in range(ns // LANE):
                rows[i * chans : (i + 1) * chans, t * LANE : (t + 1) * LANE] = (
                    clean[t, window, :] * level
                ).astype(BF16)
        for t in range(0, ns, TILE):
            series[half // 2 + t : half // 2 + t + TILE, :] = lax.dot_general(
                conv[t : t + TILE, :], rows[...], NT, preferred_element_type=F32
            ).astype(BF16)
        series[: half // 2, :] = series[ns : ns + half // 2, :]
        series[ns + half // 2 :, :] = series[half // 2 : half, :]

        def place(which, j, value):
            for i in range(TOGETHER):
                at = j * wins + step * TOGETHER + i
                stage[which, pl.ds(at, size, stride=jpitch), :] = value[
                    :, i * chans : (i + 1) * chans
                ]

        for j in range(blocks):
            start = j * half + half // 2
            b = jnp.dot(
                seg[:, :half], series[start : start + half, :], preferred_element_type=F32
            )
            place(1, j, b)

        @pl.when(want)
        def _():
            source = series
            if repeat:
                source = series_a
                for i in range(TOGETHER):
                    value = series[:, i * chans : (i + 1) * chans]
                    turned = jnp.concatenate(
                        [value[:, chans // 2 :], value[:, : chans // 2]], axis=1
                    )
                    series_a[:, i * chans : (i + 1) * chans] = jnp.where(lower, value, turned)
            for j in range(blocks):
                a = jnp.dot(
                    seg[...], source[j * half : j * half + size, :], preferred_element_type=F32
                )
                place(0, j, a)

        return 0

    lax.fori_loop(0, wins // TOGETHER, some_windows, 0)

    def factor(which, k, turn=False):
        real, imag = [
            stage[which, pl.ds((2 * k + part) * jpitch, jw), :] for part in range(2)
        ]
        if turn:
            real, imag = imag, -real
        return jnp.concatenate([real.astype(BF16), imag.astype(BF16)], axis=0)

    def first_factor(k, put):
        if repeat:
            put(0, slice(None), jnp.where(lower, factor(0, k), factor(0, k, True)).T)
        else:
            width = chans // 2
            for part in range(2):
                value = factor(0, k, part == 1).T
                for group in range(2):
                    put(
                        group,
                        slice(part * width, (part + 1) * width),
                        value[group * width : (group + 1) * width],
                    )

    emit(want, first_factor, lambda k: factor(1, k))


def work_shapes(groups, chans, wins, ns):
    half = LAGS
    rows = 2 * half * (ns // half * wins + 1)
    return [
        pltpu.VMEM((groups * NSEC, wins, ns), F32),
        pltpu.VMEM((ns // LANE, chans * (wins + 1), LANE), F32),
        pltpu.VMEM((chans * (wins + 1), LANE), F32),
        pltpu.VMEM((chans * (wins + 1), LANE), F32),
        pltpu.VMEM((TOGETHER * chans, ns), BF16),
        pltpu.VMEM((ns + half, TOGETHER * chans), BF16),
        pltpu.VMEM((ns + half, TOGETHER * chans), BF16),
        pltpu.VMEM((2, rows, chans), F32),
    ]


def input_copies(first, x, tables_in, sem):
    copied = {"first": [], "x": [], "tables": []}
    used = 0

    def copy(source, target):
        nonlocal used
        made = pltpu.make_async_copy(source, target, sem.at[used])
        made.start()
        used += 1
        return made

    copied["first"] = [copy(*pair) for pair in first]
    for source, target in x:
        parts = max(target.shape[0] // PART, 1)
        part = target.shape[0] // parts
        copied["x"].append(
            [
                copy(source.at[pl.ds(n * part, part)], target.at[pl.ds(n * part, part)])
                for n in range(parts)
            ]
        )
    copied["tables"] = [copy(*pair) for pair in tables_in]
    return copied


def segments_kernel(places, wanted, groups, odd_ref, flag_ref, *rest):
    count = len(places)
    tot_hbm, rest = rest[:groups], rest[groups:]
    x_hbm, rest = rest[:count], rest[count:]
    hann_hbm, conv_hbm, seg_hbm, a_hbm, b_hbm = rest[:5]
    tot, rest = rest[5 : 5 + groups], rest[5 + groups :]
    x, rest = rest[:count], rest[count:]
    hann, conv, seg = rest[:3]
    work, (a_out, b_out, in_sem, out_sem) = rest[3:-4], rest[-4:]
    copied = input_copies(
        list(zip(tot_hbm, tot)) + [(hann_hbm, hann)],
        list(zip(x_hbm, x)),
        [(conv_hbm, conv), (seg_hbm, seg)],
        in_sem,
    )
    bins = b_out.shape[0]
    step = bins // STEPS

    def emit(want, first_factor, second_factor):
        def first(k, _):
            def put(group, rows, value):
                a_out[k, group, rows] = value

            first_factor(k, put)
            return 0

        def second(k, _):
            b_out[k] = second_factor(k)
            return 0

        def send(n, source, target):
            part = pl.ds(n % STEPS * step, step)
            return pltpu.make_async_copy(source.at[part], target.at[part], out_sem.at[n])

        @pl.when(want)
        def _():
            for n in range(STEPS):
                lax.fori_loop(n * step, (n + 1) * step, first, 0, unroll=8)
                send(n, a_out, a_hbm).start()

        for n in range(STEPS):
            lax.fori_loop(n * step, (n + 1) * step, second, 0, unroll=8)
            send(STEPS + n, b_out, b_hbm).start()

        @pl.when(want)
        def _():
            for n in range(STEPS):
                send(n, a_out, a_hbm).wait()

        for n in range(STEPS):
            send(STEPS + n, b_out, b_hbm).wait()

    odd = odd_ref[0]
    segment_factors(
        *(places, odd == wanted, wanted == 0, odd, flag_ref),
        *(tot, x, hann, conv, seg, work, copied, emit),
    )


def segments(places, wanted, odd, flags, totals, pieces, hann, conv, seg):
    chans = sum(x.shape[0] for x in pieces)
    _, wins, ns = pieces[0].shape
    size = seg.shape[0]
    half = size // 2
    depth = ns // half * wins * 2
    smem = pl.BlockSpec(memory_space=pltpu.SMEM)
    anywhere = pl.BlockSpec(memory_space=pl.ANY)
    operands = list(totals) + list(pieces) + [hann, conv, seg]
    a_shape = jax.ShapeDtypeStruct((half, 2 if wanted else 1, chans, depth), BF16)
    b_shape = jax.ShapeDtypeStruct((half, depth, chans), BF16)
    return pl.pallas_call(
        functools.partial(segments_kernel, places, wanted, len(totals)),
        out_shape=[a_shape, b_shape],
        in_specs=[smem] * 2 + [anywhere] * len(operands),
        out_specs=[anywhere] * 2,
        scratch_shapes=[pltpu.VMEM(value.shape, value.dtype) for value in operands]
        + work_shapes(len(totals), chans, wins, ns)
        + [
            pltpu.VMEM(a_shape.shape, BF16),
            pltpu.VMEM(b_shape.shape, BF16),
            pltpu.SemaphoreType.DMA((len(operands) + chans // PART,)),
            pltpu.SemaphoreType.DMA((2 * STEPS,)),
        ],
        compiler_params=pltpu.CompilerParams(vmem_limit_bytes=VMEM),
        cost_estimate=pl.CostEstimate(
            flops=2 * wins * chans * ns * (ns + 3 * size),
            bytes_accessed=16 * 1024 * 1024,
            transcendentals=0,
        ),
    )(odd, flags, *operands)


def stack_kernel(places, scale, shares, me_ref, flag_ref, *rest):
    count = len(places)
    x_hbm, rest = rest[:count], rest[count:]
    tot_hbm, hann_hbm, conv_hbm, seg_hbm, lag_hbm = rest[:5]
    left_hbm, rest = rest[5:9], rest[9:]
    outs, rest = rest[:shares], rest[shares:]
    x, rest = rest[:count], rest[count:]
    tot, hann, conv, seg, lag = rest[:5]
    (a, b0, bh), rest = rest[5:8], rest[8:]
    work, (b1, one, in_sem, late_sem) = rest[:-4], rest[-4:]
    me = me_ref[0]
    odd = lax.rem(me, 2)
    copied = input_copies(
        [(tot_hbm, tot), (hann_hbm, hann)],
        list(zip(x_hbm, x)),
        [(conv_hbm, conv), (seg_hbm, seg), (lag_hbm, lag)],
        in_sem,
    )
    a0_hbm, ah_hbm, b0_hbm, bh_hbm = left_hbm
    own_a = pltpu.make_async_copy(a0_hbm.at[:, 0], a.at[:, 0], late_sem.at[0])
    halo_a = pltpu.make_async_copy(ah_hbm, a, late_sem.at[0])
    late = [
        pltpu.make_async_copy(b0_hbm, b0, late_sem.at[1]),
        pltpu.make_async_copy(bh_hbm, bh, late_sem.at[2]),
    ]
    for copy in late:
        copy.start()

    @pl.when(odd == 0)
    def _():
        own_a.start()

    @pl.when(odd == 1)
    def _():
        halo_a.start()

    bins, depth, chans = b0.shape
    width = chans // 2
    nfr = lag.shape[1]
    pitch = nfr + 1
    cross = work[-1]

    def emit(want, first_factor, second_factor):
        def first(k, _):
            def put(group, rows, value):
                a[k, 1, rows] = value

            first_factor(k, put)
            return 0

        def second(k, _):
            b1[k] = second_factor(k)
            return 0

        @pl.when(want)
        def _():
            lax.fori_loop(0, bins, first, 0, unroll=8)

        lax.fori_loop(0, bins, second, 0, unroll=8)

    segment_factors(
        *(places, odd == 0, True, odd, flag_ref),
        *([tot], x, hann, conv, seg, work, copied, emit),
    )
    for copy in late:
        copy.wait()

    @pl.when(odd == 0)
    def _():
        own_a.wait()

    @pl.when(odd == 1)
    def _():
        halo_a.wait()

    lane = lax.broadcasted_iota(jnp.int32, (1, chans), 1)
    keep = [jnp.where((lane < width) == (g == 0), 1.0, 0.0).astype(BF16) for g in range(2)]

    def one_bin(k, _):
        halo = bh[k]
        right = jnp.concatenate(
            [
                jnp.concatenate([b0[k], halo * keep[0]], axis=1),
                jnp.concatenate([b1[k], halo * keep[1]], axis=1),
            ],
            axis=0,
        )
        left = jnp.concatenate([a[k, 0], a[k, 1]], axis=1)
        value = jnp.dot(left, right, preferred_element_type=F32)
        for p in range(2):
            for t in range(2):
                cross[t, pl.ds(2 * k + p, width, stride=pitch), :] = value[
                    p * width : (p + 1) * width, t * chans : (t + 1) * chans
                ]
        return 0

    lax.fori_loop(0, bins, one_bin, 0, unroll=8)

    row = lax.broadcasted_iota(jnp.int32, one.shape[1:], 0)
    column = lax.broadcasted_iota(jnp.int32, one.shape[1:], 1)
    turned = jnp.where(row < width, row + chans, row - width)
    place = row + (turned - row) * odd
    for t in range(2):
        here = column + t * chans
        found = (place == here) | ((here >= chans + width) & (place == here - width))
        one[t] = jnp.where(found, 1.0, 0.0)
    share = OFFS // shares

    def one_channel(c, _):
        value = jnp.concatenate(
            [cross[t, pl.ds(c * pitch, nfr), :] for t in range(2)], axis=1
        ).astype(BF16)
        starts = [c + 1 + share * (me ^ d) for d in range(shares)]
        pick = jnp.concatenate(
            [
                jnp.concatenate([one[t, pl.ds(start, share), :] for start in starts], axis=0)
                for t in range(2)
            ],
            axis=1,
        ).astype(BF16)
        lagged = jnp.dot(lag[...], value, preferred_element_type=F32) * scale
        band = lax.dot_general(pick, lagged.astype(BF16), NT, preferred_element_type=F32)
        for d, out in enumerate(outs):
            out[c] = band[d * share : (d + 1) * share, :].astype(BF16)
        return 0

    lax.fori_loop(0, width, one_channel, 0, unroll=4)


def stacks(places, shares, scale, me, flags, total, pieces, hann, conv, seg, lag, a0, ah, b0, bh):
    bins, depth, chans = b0.shape
    width = chans // 2
    _, wins, ns = pieces[0].shape
    nlag, nfr = lag.shape
    smem = pl.BlockSpec(memory_space=pltpu.SMEM)
    vmem = pl.BlockSpec(memory_space=pltpu.VMEM)
    anywhere = pl.BlockSpec(memory_space=pl.ANY)
    operands = [*pieces, total, hann, conv, seg, lag, a0, ah, b0, bh]
    return pl.pallas_call(
        functools.partial(stack_kernel, places, scale, shares),
        out_shape=[jax.ShapeDtypeStruct((width, OFFS // shares, nlag), BF16)] * shares,
        in_specs=[smem] * 2 + [anywhere] * len(operands),
        out_specs=[vmem] * shares,
        scratch_shapes=[
            pltpu.VMEM(value.shape, value.dtype) for value in operands if value is not a0
        ]
        + work_shapes(1, chans, wins, ns)
        + [
            pltpu.VMEM(b0.shape, BF16),
            pltpu.VMEM((2, chans + width, chans), F32),
            pltpu.SemaphoreType.DMA((8 + chans // PART,)),
            pltpu.SemaphoreType.DMA((3,)),
        ],
        compiler_params=pltpu.CompilerParams(vmem_limit_bytes=VMEM),
        cost_estimate=pl.CostEstimate(
            flops=2 * width * bins * 4 * (2 * depth * chans + 2 * OFFS * chans),
            bytes_accessed=20 * 1024 * 1024,
            transcendentals=0,
        ),
    )(me, flags, *operands)


def add_over(value, axis, beside):
    count = lax.axis_size(axis)
    if count & (count - 1):
        return lax.psum(value, axis), beside
    bit = 1
    while bit < count:
        steps = [bit] if bit == 1 or 2 * bit == count else [bit, 2 * bit, 3 * bit]
        arrived = [lax.ppermute(value, axis, [(i, i ^ s) for i in range(count)]) for s in steps]
        bit *= 1 + len(steps)
        if bit == count:
            arrived, beside = lax.optimization_barrier((arrived, beside))
        value = sum(arrived, value)
    return value, beside


def shards(samples, band_gain, dead_flags, section_ids):
    chans, wins, ns = samples.shape
    nf = ns // 2
    width = chans // 2
    blocks = lax.axis_size("fibre")
    groups = lax.axis_size("tm")
    me = lax.axis_index("tm")
    odd = me % 2
    window, waves, seg, lag = tables(ns, nf)
    waves, seg, lag = jnp.asarray(waves), jnp.asarray(seg), jnp.asarray(lag)
    hann = jnp.asarray(np.broadcast_to(window[None, :], (wins, ns)))
    response = jnp.sum(band_gain[:, None] * waves, axis=0, keepdims=True)
    conv = pl.pallas_call(
        circulant_kernel,
        out_shape=jax.ShapeDtypeStruct((ns, ns), BF16),
        compiler_params=pltpu.CompilerParams(vmem_limit_bytes=VMEM),
        cost_estimate=pl.CostEstimate(flops=1, bytes_accessed=1, transcendentals=0),
    )(response)
    swap = [(z, z ^ 1) for z in range(groups)]
    both = ("fibre", "tm")
    halo_pairs = [
        (b * groups + z, (b + (1 if z % 2 else -1)) % blocks * groups + z)
        for b in range(blocks)
        for z in range(groups)
    ]

    head = width * 5 // 8

    their_head = lax.ppermute(
        lax.dynamic_slice_in_dim(samples, (1 - odd) * width, head, 0), "tm", swap
    )
    flags = jnp.stack([dead_flags, section_ids])
    halo_flags = lax.ppermute(
        lax.dynamic_slice_in_dim(flags, odd * width, width, 1), both, halo_pairs
    )
    smem = pl.BlockSpec(memory_space=pltpu.SMEM)
    steps = 4
    anywhere = pl.BlockSpec(memory_space=pl.ANY)
    sums, own_half, tail = pl.pallas_call(
        section_sums,
        grid=(steps,),
        out_shape=[
            jax.ShapeDtypeStruct((NSEC, wins, ns + LANE), F32),
            jax.ShapeDtypeStruct((width, wins, ns), BF16),
            jax.ShapeDtypeStruct((width - head, wins, ns), BF16),
        ],
        in_specs=[smem] * 3
        + [pl.BlockSpec((chans // steps, wins, ns), lambda i: (i, 0, 0)), anywhere],
        out_specs=[pl.BlockSpec((NSEC, wins, ns + LANE), lambda i: (0, 0, 0)), anywhere, anywhere],
        scratch_shapes=[pltpu.SemaphoreType.DMA((2,))],
        compiler_params=pltpu.CompilerParams(vmem_limit_bytes=VMEM),
        cost_estimate=pl.CostEstimate(flops=1, bytes_accessed=1, transcendentals=0),
    )(odd[None], dead_flags, section_ids, samples, samples)
    total, their_head = add_over(sums, "fibre", their_head)
    total, halo_flags, own_half, conv = lax.optimization_barrier(
        (total, halo_flags, own_half, conv)
    )
    their_total = lax.ppermute(total, "tm", swap)
    halo = lax.ppermute(own_half, both, halo_pairs)
    ready = (total, their_total, their_head, own_half, tail, flags, hann, conv, seg, lag)
    ready = lax.optimization_barrier(ready)
    total, their_total, their_head, own_half, tail, flags, hann, conv, seg, lag = ready
    their_tail = lax.ppermute(tail, "tm", swap)
    their_second = lax.ppermute(own_half, "tm", swap)
    halo_head = lax.ppermute(their_head, both, halo_pairs)

    side = odd[None]
    parts = (hann, conv, seg)
    a0, b0 = segments(((0, 0, 0),), 0, side, flags, (total,), (samples,), *parts)
    b0, forward = lax.optimization_barrier((b0, their_tail))
    halo_tail = lax.ppermute(forward, both, halo_pairs)
    ah, bh = segments(
        ((0, 0, 0), (1, width, width), (1, width + head, width + head)),
        1,
        side,
        halo_flags,
        (total, their_total),
        (halo, halo_head, halo_tail),
        *parts,
    )
    scale = 2.0 / ns / LAGS / math.sqrt(nf * wins * groups)
    found = stacks(
        ((0, 0, width), (0, head, width + head), (0, width, 0)),
        groups,
        scale,
        me[None],
        flags,
        their_total,
        (their_head, their_tail, their_second),
        *(hann, conv, seg, lag),
        *(a0, ah, b0, bh),
    )
    arrived = []
    for d in range(groups):
        pairs = [
            (b * groups + z, (b - z % 2) % blocks * groups + (z ^ d))
            for b in range(blocks)
            for z in range(groups)
        ]
        arrived.append(lax.ppermute(found[d], both, pairs).astype(F32))
    same = sum(arrived[2::2], arrived[0])
    other = sum(arrived[3::2], arrived[1])
    return jnp.concatenate(
        [jnp.where(odd == 0, same, other), jnp.where(odd == 0, other, same)], axis=0
    )


def solution(mesh):
    in_specs = (P("fibre", "tm", None), P(), P("fibre"), P("fibre"))
    out_specs = P("fibre", "tm", None)
    return jax.shard_map(shards, mesh=mesh, in_specs=in_specs, out_specs=out_specs, check_vma=False)
```

```python
import functools
import math

import jax
import jax.numpy as jnp
import ml_dtypes
import numpy as np
from jax import lax
from jax.experimental import pallas as pl
from jax.experimental.pallas import tpu as pltpu
from jax.sharding import PartitionSpec as P

OFFS = 128
LAGS = 128
NSEC = 2
LANE = 128
PART = 16
TILE = 256
STEPS = 4
TOGETHER = 4
VMEM = 63 * 1024 * 1024
NT = (((1,), (1,)), ((), ()))
F32 = jnp.float32
BF16 = jnp.bfloat16


def tables(ns, nf):
    tick = np.arange(ns)
    freq = np.arange(nf)
    window = 0.5 - 0.5 * np.cos(tick * (2.0 * math.pi / ns))
    waves = np.cos((freq[:, None] * tick[None, :] % ns) * (2.0 * math.pi / ns))
    waves[0] *= math.sqrt(0.5)
    size = 2 * LAGS
    bins = np.arange(size // 2)
    turn = math.pi / size * ((2 * bins[:, None] + 1) * np.arange(size)[None, :] % (2 * size))
    segment = np.stack([np.cos(turn), -np.sin(turn)], axis=1).reshape(size, size)
    lag = np.stack([np.cos(turn), -np.sin(turn)], axis=1).reshape(size, size)[:, :LAGS].T
    cast = lambda a: a.astype(np.float32).astype(ml_dtypes.bfloat16)
    return window.astype(np.float32), waves.astype(np.float32), cast(segment), cast(lag)


def section_sums(odd_ref, dead_ref, sec_ref, x_hbm, out_ref, half_hbm, tail_hbm, x, in_sem, sem):
    chans, wins, ns = x.shape
    width, length = half_hbm.shape[0], tail_hbm.shape[0]
    odd = odd_ref[0]
    part = chans // STEPS
    arriving = [
        pltpu.make_async_copy(
            x_hbm.at[pl.ds(n * part, part)], x.at[pl.ds(n * part, part)], in_sem.at[n]
        )
        for n in range(STEPS)
    ]
    for copy in arriving:
        copy.start()
    leaving = [
        pltpu.make_async_copy(x.at[pl.ds(odd * width, width)], half_hbm, sem.at[0]),
        pltpu.make_async_copy(
            x.at[pl.ds((2 - odd) * width - length, length)], tail_hbm, sem.at[1]
        ),
    ]

    def body(c, carry):
        value = x[c].astype(F32)
        live = 1 - dead_ref[c]
        sums, counts = carry
        weights = [jnp.where(sec_ref[c] == s, live, 0).astype(F32) for s in range(NSEC)]
        return (
            tuple(sums[s] + weights[s] * value for s in range(NSEC)),
            tuple(counts[s] + weights[s] for s in range(NSEC)),
        )

    zero = jnp.zeros((wins, ns), F32)
    carry = ((zero,) * NSEC, (jnp.float32(0),) * NSEC)
    for n, copy in enumerate(arriving):
        copy.wait()
        if n == STEPS - 1:
            for out in leaving:
                out.start()
        carry = lax.fori_loop(n * part, (n + 1) * part, body, carry, unroll=8)
    sums, counts = carry
    for s in range(NSEC):
        out_ref[s, :, :ns] = sums[s]
        out_ref[s, :, ns:] = jnp.zeros((wins, LANE), F32) + counts[s]
    for out in leaving:
        out.wait()


def circulant_kernel(filter_ref, out_ref):
    ns = filter_ref.shape[1]
    for t in range(0, ns, 16):
        block = jnp.broadcast_to(filter_ref[...], (16, ns))
        out_ref[t : t + 16, :] = pltpu.roll(block, t, 1, stride=1, stride_axis=0).astype(BF16)


def segment_factors(places, want, repeat, odd, flag_ref, tot, x, hann, conv, seg, work, copied, emit):
    common, clean, mass, square, rows, series, series_a, stage = work
    _, wins, ns = x[0].shape
    chans = sum(piece.shape[0] for piece in x)
    pitch = wins + 1
    size = seg.shape[0]
    half = size // 2
    blocks = ns // half
    jw = blocks * wins
    jpitch = jw + 1
    held = flag_ref.shape[1]
    for copy in copied["first"]:
        copy.wait()
    for g in range(len(tot)):
        for s in range(NSEC):
            common[g * NSEC + s] = tot[g][s, :, :ns] / jnp.maximum(tot[g][s, :, ns : ns + 1], 1.0)
    sign = 1.0 - 2.0 * (lax.broadcasted_iota(jnp.int32, (chans, LANE), 1) % 2).astype(F32)
    lower = lax.broadcasted_iota(jnp.int32, (1, LANE), 1) < LANE // 2

    for number, (group, even_base, odd_base) in enumerate(places):
        piece = x[number]
        length = piece.shape[0]
        base = even_base + odd * (odd_base - even_base)

        def clean_channel(c, _):
            at = base + c
            flag = lax.rem(at, held)
            live = (1 - flag_ref[0, flag]).astype(F32)
            value = (piece[c].astype(F32) - common[group * NSEC + flag_ref[1, flag]]) * (
                hann[...] * live
            )
            tiles = [value[:, t * LANE : (t + 1) * LANE] for t in range(ns // LANE)]
            row = pl.ds(at * pitch, wins)
            mass[row, :] = sum(tiles[1:], tiles[0])
            square[row, :] = sum([tile * tile for tile in tiles[1:]], tiles[0] * tiles[0])
            for t, tile in enumerate(tiles):
                clean[t, row, :] = tile
            return 0

        parts = copied["x"][number]
        part = length // len(parts)
        for n, copy in enumerate(parts):
            copy.wait()
            lax.fori_loop(n * part, (n + 1) * part, clean_channel, 0, unroll=8)
    for copy in copied["tables"]:
        copy.wait()

    def some_windows(step, _):
        for i in range(TOGETHER):
            window = pl.ds(step * TOGETHER + i, chans, stride=pitch)
            total = mass[window, :]
            lowest = jnp.sum(total, axis=1, keepdims=True)
            highest = jnp.sum(total * sign, axis=1, keepdims=True)
            power = 0.5 * jnp.sum(square[window, :], axis=1, keepdims=True)
            power = power + (lowest * lowest - highest * highest) * (0.5 / ns)
            level = lax.rsqrt(power + 1e-06)
            for t in range(ns // LANE):
                rows[i * chans : (i + 1) * chans, t * LANE : (t + 1) * LANE] = (
                    clean[t, window, :] * level
                ).astype(BF16)
        for t in range(0, ns, TILE):
            series[half // 2 + t : half // 2 + t + TILE, :] = lax.dot_general(
                conv[t : t + TILE, :], rows[...], NT, preferred_element_type=F32
            ).astype(BF16)
        series[: half // 2, :] = series[ns : ns + half // 2, :]
        series[ns + half // 2 :, :] = series[half // 2 : half, :]

        def place(which, j, value):
            for i in range(TOGETHER):
                at = j * wins + step * TOGETHER + i
                stage[which, pl.ds(at, size, stride=jpitch), :] = value[
                    :, i * chans : (i + 1) * chans
                ]

        for j in range(blocks):
            start = j * half + half // 2
            b = jnp.dot(
                seg[:, :half], series[start : start + half, :], preferred_element_type=F32
            )
            place(1, j, b)

        @pl.when(want)
        def _():
            source = series
            if repeat:
                source = series_a
                for i in range(TOGETHER):
                    value = series[:, i * chans : (i + 1) * chans]
                    turned = jnp.concatenate(
                        [value[:, chans // 2 :], value[:, : chans // 2]], axis=1
                    )
                    series_a[:, i * chans : (i + 1) * chans] = jnp.where(lower, value, turned)
            for j in range(blocks):
                a = jnp.dot(
                    seg[...], source[j * half : j * half + size, :], preferred_element_type=F32
                )
                place(0, j, a)

        return 0

    lax.fori_loop(0, wins // TOGETHER, some_windows, 0)

    def factor(which, k, turn=False):
        real, imag = [
            stage[which, pl.ds((2 * k + part) * jpitch, jw), :] for part in range(2)
        ]
        if turn:
            real, imag = imag, -real
        return jnp.concatenate([real.astype(BF16), imag.astype(BF16)], axis=0)

    def first_factor(k, put):
        if repeat:
            put(0, slice(None), jnp.where(lower, factor(0, k), factor(0, k, True)).T)
        else:
            width = chans // 2
            for part in range(2):
                value = factor(0, k, part == 1).T
                for group in range(2):
                    put(
                        group,
                        slice(part * width, (part + 1) * width),
                        value[group * width : (group + 1) * width],
                    )

    emit(want, first_factor, lambda k: factor(1, k))


def work_shapes(groups, chans, wins, ns):
    half = LAGS
    rows = 2 * half * (ns // half * wins + 1)
    return [
        pltpu.VMEM((groups * NSEC, wins, ns), F32),
        pltpu.VMEM((ns // LANE, chans * (wins + 1), LANE), F32),
        pltpu.VMEM((chans * (wins + 1), LANE), F32),
        pltpu.VMEM((chans * (wins + 1), LANE), F32),
        pltpu.VMEM((TOGETHER * chans, ns), BF16),
        pltpu.VMEM((ns + half, TOGETHER * chans), BF16),
        pltpu.VMEM((ns + half, TOGETHER * chans), BF16),
        pltpu.VMEM((2, rows, chans), F32),
    ]


def input_copies(first, x, tables_in, sem):
    copied = {"first": [], "x": [], "tables": []}
    used = 0

    def copy(source, target):
        nonlocal used
        made = pltpu.make_async_copy(source, target, sem.at[used])
        made.start()
        used += 1
        return made

    copied["first"] = [copy(*pair) for pair in first]
    for source, target in x:
        parts = max(target.shape[0] // PART, 1)
        part = target.shape[0] // parts
        copied["x"].append(
            [
                copy(source.at[pl.ds(n * part, part)], target.at[pl.ds(n * part, part)])
                for n in range(parts)
            ]
        )
    copied["tables"] = [copy(*pair) for pair in tables_in]
    return copied


def segments_kernel(places, wanted, groups, odd_ref, flag_ref, *rest):
    count = len(places)
    tot_hbm, rest = rest[:groups], rest[groups:]
    x_hbm, rest = rest[:count], rest[count:]
    hann_hbm, conv_hbm, seg_hbm, a_hbm, b_hbm = rest[:5]
    tot, rest = rest[5 : 5 + groups], rest[5 + groups :]
    x, rest = rest[:count], rest[count:]
    hann, conv, seg = rest[:3]
    work, (a_out, b_out, in_sem, out_sem) = rest[3:-4], rest[-4:]
    copied = input_copies(
        list(zip(tot_hbm, tot)) + [(hann_hbm, hann)],
        list(zip(x_hbm, x)),
        [(conv_hbm, conv), (seg_hbm, seg)],
        in_sem,
    )
    bins = b_out.shape[0]
    step = bins // STEPS

    def emit(want, first_factor, second_factor):
        def first(k, _):
            def put(group, rows, value):
                a_out[k, group, rows] = value

            first_factor(k, put)
            return 0

        def second(k, _):
            b_out[k] = second_factor(k)
            return 0

        def send(n, source, target):
            part = pl.ds(n % STEPS * step, step)
            return pltpu.make_async_copy(source.at[part], target.at[part], out_sem.at[n])

        @pl.when(want)
        def _():
            for n in range(STEPS):
                lax.fori_loop(n * step, (n + 1) * step, first, 0, unroll=8)
                send(n, a_out, a_hbm).start()

        for n in range(STEPS):
            lax.fori_loop(n * step, (n + 1) * step, second, 0, unroll=8)
            send(STEPS + n, b_out, b_hbm).start()

        @pl.when(want)
        def _():
            for n in range(STEPS):
                send(n, a_out, a_hbm).wait()

        for n in range(STEPS):
            send(STEPS + n, b_out, b_hbm).wait()

    odd = odd_ref[0]
    segment_factors(
        *(places, odd == wanted, wanted == 0, odd, flag_ref),
        *(tot, x, hann, conv, seg, work, copied, emit),
    )


def segments(places, wanted, odd, flags, totals, pieces, hann, conv, seg):
    chans = sum(x.shape[0] for x in pieces)
    _, wins, ns = pieces[0].shape
    size = seg.shape[0]
    half = size // 2
    depth = ns // half * wins * 2
    smem = pl.BlockSpec(memory_space=pltpu.SMEM)
    anywhere = pl.BlockSpec(memory_space=pl.ANY)
    operands = list(totals) + list(pieces) + [hann, conv, seg]
    a_shape = jax.ShapeDtypeStruct((half, 2 if wanted else 1, chans, depth), BF16)
    b_shape = jax.ShapeDtypeStruct((half, depth, chans), BF16)
    return pl.pallas_call(
        functools.partial(segments_kernel, places, wanted, len(totals)),
        out_shape=[a_shape, b_shape],
        in_specs=[smem] * 2 + [anywhere] * len(operands),
        out_specs=[anywhere] * 2,
        scratch_shapes=[pltpu.VMEM(value.shape, value.dtype) for value in operands]
        + work_shapes(len(totals), chans, wins, ns)
        + [
            pltpu.VMEM(a_shape.shape, BF16),
            pltpu.VMEM(b_shape.shape, BF16),
            pltpu.SemaphoreType.DMA((len(operands) + chans // PART,)),
            pltpu.SemaphoreType.DMA((2 * STEPS,)),
        ],
        compiler_params=pltpu.CompilerParams(vmem_limit_bytes=VMEM),
        cost_estimate=pl.CostEstimate(
            flops=2 * wins * chans * ns * (ns + 3 * size),
            bytes_accessed=16 * 1024 * 1024,
            transcendentals=0,
        ),
    )(odd, flags, *operands)


def stack_kernel(places, scale, shares, me_ref, flag_ref, *rest):
    count = len(places)
    x_hbm, rest = rest[:count], rest[count:]
    tot_hbm, hann_hbm, conv_hbm, seg_hbm, lag_hbm = rest[:5]
    left_hbm, rest = rest[5:9], rest[9:]
    outs, rest = rest[:shares], rest[shares:]
    x, rest = rest[:count], rest[count:]
    tot, hann, conv, seg, lag = rest[:5]
    (a, b0, bh), rest = rest[5:8], rest[8:]
    work, (b1, one, in_sem, late_sem) = rest[:-4], rest[-4:]
    me = me_ref[0]
    odd = lax.rem(me, 2)
    copied = input_copies(
        [(tot_hbm, tot), (hann_hbm, hann)],
        list(zip(x_hbm, x)),
        [(conv_hbm, conv), (seg_hbm, seg), (lag_hbm, lag)],
        in_sem,
    )
    a0_hbm, ah_hbm, b0_hbm, bh_hbm = left_hbm
    own_a = pltpu.make_async_copy(a0_hbm.at[:, 0], a.at[:, 0], late_sem.at[0])
    halo_a = pltpu.make_async_copy(ah_hbm, a, late_sem.at[0])
    late = [
        pltpu.make_async_copy(b0_hbm, b0, late_sem.at[1]),
        pltpu.make_async_copy(bh_hbm, bh, late_sem.at[2]),
    ]
    for copy in late:
        copy.start()

    @pl.when(odd == 0)
    def _():
        own_a.start()

    @pl.when(odd == 1)
    def _():
        halo_a.start()

    bins, depth, chans = b0.shape
    width = chans // 2
    nfr = lag.shape[1]
    pitch = nfr + 1
    cross = work[-1]

    def emit(want, first_factor, second_factor):
        def first(k, _):
            def put(group, rows, value):
                a[k, 1, rows] = value

            first_factor(k, put)
            return 0

        def second(k, _):
            b1[k] = second_factor(k)
            return 0

        @pl.when(want)
        def _():
            lax.fori_loop(0, bins, first, 0, unroll=8)

        lax.fori_loop(0, bins, second, 0, unroll=8)

    segment_factors(
        *(places, odd == 0, True, odd, flag_ref),
        *([tot], x, hann, conv, seg, work, copied, emit),
    )
    for copy in late:
        copy.wait()

    @pl.when(odd == 0)
    def _():
        own_a.wait()

    @pl.when(odd == 1)
    def _():
        halo_a.wait()

    lane = lax.broadcasted_iota(jnp.int32, (1, chans), 1)
    keep = [jnp.where((lane < width) == (g == 0), 1.0, 0.0).astype(BF16) for g in range(2)]

    def one_bin(k, _):
        halo = bh[k]
        right = jnp.concatenate(
            [
                jnp.concatenate([b0[k], halo * keep[0]], axis=1),
                jnp.concatenate([b1[k], halo * keep[1]], axis=1),
            ],
            axis=0,
        )
        left = jnp.concatenate([a[k, 0], a[k, 1]], axis=1)
        value = jnp.dot(left, right, preferred_element_type=F32)
        for p in range(2):
            for t in range(2):
                cross[t, pl.ds(2 * k + p, width, stride=pitch), :] = value[
                    p * width : (p + 1) * width, t * chans : (t + 1) * chans
                ]
        return 0

    lax.fori_loop(0, bins, one_bin, 0, unroll=8)

    row = lax.broadcasted_iota(jnp.int32, one.shape[1:], 0)
    column = lax.broadcasted_iota(jnp.int32, one.shape[1:], 1)
    turned = jnp.where(row < width, row + chans, row - width)
    place = row + (turned - row) * odd
    for t in range(2):
        here = column + t * chans
        found = (place == here) | ((here >= chans + width) & (place == here - width))
        one[t] = jnp.where(found, 1.0, 0.0)
    share = OFFS // shares

    def one_channel(c, _):
        value = jnp.concatenate(
            [cross[t, pl.ds(c * pitch, nfr), :] for t in range(2)], axis=1
        ).astype(BF16)
        starts = [c + 1 + share * (me ^ d) for d in range(shares)]
        pick = jnp.concatenate(
            [
                jnp.concatenate([one[t, pl.ds(start, share), :] for start in starts], axis=0)
                for t in range(2)
            ],
            axis=1,
        ).astype(BF16)
        lagged = jnp.dot(lag[...], value, preferred_element_type=F32) * scale
        band = lax.dot_general(pick, lagged.astype(BF16), NT, preferred_element_type=F32)
        for d, out in enumerate(outs):
            out[c] = band[d * share : (d + 1) * share, :].astype(BF16)
        return 0

    lax.fori_loop(0, width, one_channel, 0, unroll=4)


def stacks(places, shares, scale, me, flags, total, pieces, hann, conv, seg, lag, a0, ah, b0, bh):
    bins, depth, chans = b0.shape
    width = chans // 2
    _, wins, ns = pieces[0].shape
    nlag, nfr = lag.shape
    smem = pl.BlockSpec(memory_space=pltpu.SMEM)
    vmem = pl.BlockSpec(memory_space=pltpu.VMEM)
    anywhere = pl.BlockSpec(memory_space=pl.ANY)
    operands = [*pieces, total, hann, conv, seg, lag, a0, ah, b0, bh]
    return pl.pallas_call(
        functools.partial(stack_kernel, places, scale, shares),
        out_shape=[jax.ShapeDtypeStruct((width, OFFS // shares, nlag), BF16)] * shares,
        in_specs=[smem] * 2 + [anywhere] * len(operands),
        out_specs=[vmem] * shares,
        scratch_shapes=[
            pltpu.VMEM(value.shape, value.dtype) for value in operands if value is not a0
        ]
        + work_shapes(1, chans, wins, ns)
        + [
            pltpu.VMEM(b0.shape, BF16),
            pltpu.VMEM((2, chans + width, chans), F32),
            pltpu.SemaphoreType.DMA((8 + chans // PART,)),
            pltpu.SemaphoreType.DMA((3,)),
        ],
        compiler_params=pltpu.CompilerParams(vmem_limit_bytes=VMEM),
        cost_estimate=pl.CostEstimate(
            flops=2 * width * bins * 4 * (2 * depth * chans + 2 * OFFS * chans),
            bytes_accessed=20 * 1024 * 1024,
            transcendentals=0,
        ),
    )(me, flags, *operands)


def add_over(value, axis, beside):
    count = lax.axis_size(axis)
    if count & (count - 1):
        return lax.psum(value, axis), beside
    bit = 1
    while bit < count:
        steps = [bit] if bit == 1 or 2 * bit == count else [bit, 2 * bit, 3 * bit]
        arrived = [lax.ppermute(value, axis, [(i, i ^ s) for i in range(count)]) for s in steps]
        bit *= 1 + len(steps)
        if bit == count:
            arrived, beside = lax.optimization_barrier((arrived, beside))
        value = sum(arrived, value)
    return value, beside


def shards(samples, band_gain, dead_flags, section_ids):
    chans, wins, ns = samples.shape
    nf = ns // 2
    width = chans // 2
    blocks = lax.axis_size("fibre")
    groups = lax.axis_size("tm")
    me = lax.axis_index("tm")
    odd = me % 2
    window, waves, seg, lag = tables(ns, nf)
    waves, seg, lag = jnp.asarray(waves), jnp.asarray(seg), jnp.asarray(lag)
    hann = jnp.asarray(np.broadcast_to(window[None, :], (wins, ns)))
    response = jnp.sum(band_gain[:, None] * waves, axis=0, keepdims=True)
    conv = pl.pallas_call(
        circulant_kernel,
        out_shape=jax.ShapeDtypeStruct((ns, ns), BF16),
        compiler_params=pltpu.CompilerParams(vmem_limit_bytes=VMEM),
        cost_estimate=pl.CostEstimate(flops=1, bytes_accessed=1, transcendentals=0),
    )(response)
    swap = [(z, z ^ 1) for z in range(groups)]
    both = ("fibre", "tm")
    halo_pairs = [
        (b * groups + z, (b + (1 if z % 2 else -1)) % blocks * groups + z)
        for b in range(blocks)
        for z in range(groups)
    ]

    head = width * 5 // 8

    their_head = lax.ppermute(
        lax.dynamic_slice_in_dim(samples, (1 - odd) * width, head, 0), "tm", swap
    )
    flags = jnp.stack([dead_flags, section_ids])
    halo_flags = lax.ppermute(
        lax.dynamic_slice_in_dim(flags, odd * width, width, 1), both, halo_pairs
    )
    smem = pl.BlockSpec(memory_space=pltpu.SMEM)
    anywhere = pl.BlockSpec(memory_space=pl.ANY)
    sums, own_half, tail = pl.pallas_call(
        section_sums,
        out_shape=[
            jax.ShapeDtypeStruct((NSEC, wins, ns + LANE), F32),
            jax.ShapeDtypeStruct((width, wins, ns), BF16),
            jax.ShapeDtypeStruct((width - head, wins, ns), BF16),
        ],
        in_specs=[smem] * 3 + [anywhere],
        out_specs=[pl.BlockSpec(memory_space=pltpu.VMEM), anywhere, anywhere],
        scratch_shapes=[
            pltpu.VMEM(samples.shape, BF16),
            pltpu.SemaphoreType.DMA((STEPS,)),
            pltpu.SemaphoreType.DMA((2,)),
        ],
        compiler_params=pltpu.CompilerParams(vmem_limit_bytes=VMEM),
        cost_estimate=pl.CostEstimate(flops=1, bytes_accessed=1, transcendentals=0),
    )(odd[None], dead_flags, section_ids, samples)
    total, their_head = add_over(sums, "fibre", their_head)
    total, halo_flags, own_half, conv = lax.optimization_barrier(
        (total, halo_flags, own_half, conv)
    )
    their_total = lax.ppermute(total, "tm", swap)
    halo = lax.ppermute(own_half, both, halo_pairs)
    ready = (total, their_total, their_head, own_half, tail, flags, hann, conv, seg, lag)
    ready = lax.optimization_barrier(ready)
    total, their_total, their_head, own_half, tail, flags, hann, conv, seg, lag = ready
    their_tail = lax.ppermute(tail, "tm", swap)
    their_second = lax.ppermute(own_half, "tm", swap)
    halo_head = lax.ppermute(their_head, both, halo_pairs)

    side = odd[None]
    parts = (hann, conv, seg)
    a0, b0 = segments(((0, 0, 0),), 0, side, flags, (total,), (samples,), *parts)
    b0, forward = lax.optimization_barrier((b0, their_tail))
    halo_tail = lax.ppermute(forward, both, halo_pairs)
    ah, bh = segments(
        ((0, 0, 0), (1, width, width), (1, width + head, width + head)),
        1,
        side,
        halo_flags,
        (total, their_total),
        (halo, halo_head, halo_tail),
        *parts,
    )
    scale = 2.0 / ns / LAGS / math.sqrt(nf * wins * groups)
    found = stacks(
        ((0, 0, width), (0, head, width + head), (0, width, 0)),
        groups,
        scale,
        me[None],
        flags,
        their_total,
        (their_head, their_tail, their_second),
        *(hann, conv, seg, lag),
        *(a0, ah, b0, bh),
    )
    arrived = []
    for d in range(groups):
        pairs = [
            (b * groups + z, (b - z % 2) % blocks * groups + (z ^ d))
            for b in range(blocks)
            for z in range(groups)
        ]
        arrived.append(lax.ppermute(found[d], both, pairs).astype(F32))
    same = sum(arrived[2::2], arrived[0])
    other = sum(arrived[3::2], arrived[1])
    return jnp.concatenate(
        [jnp.where(odd == 0, same, other), jnp.where(odd == 0, other, same)], axis=0
    )


def solution(mesh):
    in_specs = (P("fibre", "tm", None), P(), P("fibre"), P("fibre"))
    out_specs = P("fibre", "tm", None)
    return jax.shard_map(shards, mesh=mesh, in_specs=in_specs, out_specs=out_specs, check_vma=False)
```

```python
import functools
import math

import jax
import jax.numpy as jnp
import ml_dtypes
import numpy as np
from jax import lax
from jax.experimental import pallas as pl
from jax.experimental.pallas import tpu as pltpu
from jax.sharding import PartitionSpec as P

OFFS = 128
LAGS = 128
NSEC = 2
LANE = 128
PART = 16
TILE = 256
STEPS = 4
TOGETHER = 4
VMEM = 63 * 1024 * 1024
NT = (((1,), (1,)), ((), ()))
F32 = jnp.float32
BF16 = jnp.bfloat16


def tables(ns, nf):
    tick = np.arange(ns)
    freq = np.arange(nf)
    window = 0.5 - 0.5 * np.cos(tick * (2.0 * math.pi / ns))
    waves = np.cos((freq[:, None] * tick[None, :] % ns) * (2.0 * math.pi / ns))
    waves[0] *= math.sqrt(0.5)
    size = 2 * LAGS
    bins = np.arange(size // 2)
    turn = math.pi / size * ((2 * bins[:, None] + 1) * np.arange(size)[None, :] % (2 * size))
    segment = np.stack([np.cos(turn), -np.sin(turn)], axis=1).reshape(size, size)
    lag = np.stack([np.cos(turn), -np.sin(turn)], axis=1).reshape(size, size)[:, :LAGS].T
    cast = lambda a: a.astype(np.float32).astype(ml_dtypes.bfloat16)
    return window.astype(np.float32), waves.astype(np.float32), cast(segment), cast(lag)


def section_sums(odd_ref, dead_ref, sec_ref, x_hbm, out_ref, half_hbm, tail_hbm, x, in_sem, sem):
    chans, wins, ns = x.shape
    width, length = half_hbm.shape[0], tail_hbm.shape[0]
    odd = odd_ref[0]
    part = chans // STEPS
    arriving = [
        pltpu.make_async_copy(
            x_hbm.at[pl.ds(n * part, part)], x.at[pl.ds(n * part, part)], in_sem.at[n]
        )
        for n in range(STEPS)
    ]
    for copy in arriving:
        copy.start()
    leaving = [
        pltpu.make_async_copy(x.at[pl.ds(odd * width, width)], half_hbm, sem.at[0]),
        pltpu.make_async_copy(
            x.at[pl.ds((2 - odd) * width - length, length)], tail_hbm, sem.at[1]
        ),
    ]

    def body(c, carry):
        value = x[c].astype(F32)
        live = 1 - dead_ref[c]
        sums, counts = carry
        weights = [jnp.where(sec_ref[c] == s, live, 0).astype(F32) for s in range(NSEC)]
        return (
            tuple(sums[s] + weights[s] * value for s in range(NSEC)),
            tuple(counts[s] + weights[s] for s in range(NSEC)),
        )

    zero = jnp.zeros((wins, ns), F32)
    carry = ((zero,) * NSEC, (jnp.float32(0),) * NSEC)
    for n, copy in enumerate(arriving):
        copy.wait()
        if n == STEPS - 1:
            for out in leaving:
                out.start()
        carry = lax.fori_loop(n * part, (n + 1) * part, body, carry, unroll=8)
    sums, counts = carry
    for s in range(NSEC):
        out_ref[s, :, :ns] = sums[s]
        out_ref[s, :, ns:] = jnp.zeros((wins, LANE), F32) + counts[s]
    for out in leaving:
        out.wait()


def circulant_kernel(filter_ref, out_ref):
    ns = filter_ref.shape[1]
    for t in range(0, ns, 16):
        block = jnp.broadcast_to(filter_ref[...], (16, ns))
        out_ref[t : t + 16, :] = pltpu.roll(block, t, 1, stride=1, stride_axis=0).astype(BF16)


def segment_factors(places, odd, flag_ref, tot, x, hann, conv, seg, work, copied, first=None):
    common, clean, mass, square, rows, series_all, stage = work
    _, wins, ns = x[0].shape
    chans = sum(piece.shape[0] for piece in x)
    pitch = wins + 1
    size = seg.shape[0]
    half = size // 2
    blocks = ns // half
    jw = blocks * wins
    jpitch = jw + 1
    for copy in copied["first"]:
        copy.wait()
    for g in range(len(tot)):
        for s in range(NSEC):
            common[g * NSEC + s] = tot[g][s, :, :ns] / jnp.maximum(tot[g][s, :, ns : ns + 1], 1.0)
    sign = 1.0 - 2.0 * (lax.broadcasted_iota(jnp.int32, (chans, LANE), 1) % 2).astype(F32)

    for number, (group, base, flags) in enumerate(places):
        piece = x[number]
        length = piece.shape[0]
        base = base[0] + odd * (base[1] - base[0])
        flags = flags[0] + odd * (flags[1] - flags[0])

        def clean_channel(c, _):
            at = base + c
            flag = flags + c
            live = (1 - flag_ref[0, flag]).astype(F32)
            value = (piece[c].astype(F32) - common[group * NSEC + flag_ref[1, flag]]) * (
                hann[...] * live
            )
            tiles = [value[:, t * LANE : (t + 1) * LANE] for t in range(ns // LANE)]
            row = pl.ds(at * pitch, wins)
            mass[row, :] = sum(tiles[1:], tiles[0])
            square[row, :] = sum([tile * tile for tile in tiles[1:]], tiles[0] * tiles[0])
            for t, tile in enumerate(tiles):
                clean[t, row, :] = tile
            return 0

        parts = copied["x"][number]
        part = length // len(parts)
        for n, copy in enumerate(parts):
            copy.wait()
            lax.fori_loop(n * part, (n + 1) * part, clean_channel, 0, unroll=8)
    for copy in copied["tables"]:
        copy.wait()

    for step in range(wins // TOGETHER):
        series = series_all.at[step]
        for i in range(TOGETHER):
            window = pl.ds(step * TOGETHER + i, chans, stride=pitch)
            total = mass[window, :]
            lowest = jnp.sum(total, axis=1, keepdims=True)
            highest = jnp.sum(total * sign, axis=1, keepdims=True)
            power = 0.5 * jnp.sum(square[window, :], axis=1, keepdims=True)
            power = power + (lowest * lowest - highest * highest) * (0.5 / ns)
            level = lax.rsqrt(power + 1e-06)
            for t in range(ns // LANE):
                rows[i * chans : (i + 1) * chans, t * LANE : (t + 1) * LANE] = (
                    clean[t, window, :] * level
                ).astype(BF16)
        for t in range(0, ns, TILE):
            series[half // 2 + t : half // 2 + t + TILE, :] = lax.dot_general(
                conv[t : t + TILE, :], rows[...], NT, preferred_element_type=F32
            ).astype(BF16)
        series[: half // 2, :] = series[ns : ns + half // 2, :]
        series[ns + half // 2 :, :] = series[half // 2 : half, :]

        def place(which, j, value):
            for i in range(TOGETHER):
                at = j * wins + step * TOGETHER + i
                stage[which, pl.ds(at, size, stride=jpitch), :] = value[
                    :, i * chans : (i + 1) * chans
                ]

        for j in range(blocks):
            start = j * half + half // 2
            b = jnp.dot(
                seg[:, :half], series[start : start + half, :], preferred_element_type=F32
            )
            place(1, j, b)

        if first is not None:
            source = first(step, series)
            for j in range(blocks):
                a = jnp.dot(
                    seg[...], source[j * half : j * half + size, :], preferred_element_type=F32
                )
                place(0, j, a)

    def factor(which, k, turn=False):
        real, imag = [
            stage[which, pl.ds((2 * k + part) * jpitch, jw), :] for part in range(2)
        ]
        if turn:
            real, imag = imag, -real
        return jnp.concatenate([real.astype(BF16), imag.astype(BF16)], axis=0)

    def first_factor(k, put):
        width = chans // 2
        for part in range(2):
            value = factor(0, k, part == 1).T
            rows_at = slice(part * width, (part + 1) * width)
            put(1, rows_at, value[:width])
            put(0, rows_at, value[width:])

    return first_factor, lambda k: factor(1, k)


def work_shapes(groups, chans, wins, ns):
    half = LAGS
    rows = 2 * half * (ns // half * wins + 1)
    return [
        pltpu.VMEM((groups * NSEC, wins, ns), F32),
        pltpu.VMEM((ns // LANE, chans * (wins + 1), LANE), F32),
        pltpu.VMEM((chans * (wins + 1), LANE), F32),
        pltpu.VMEM((chans * (wins + 1), LANE), F32),
        pltpu.VMEM((TOGETHER * chans, ns), BF16),
        pltpu.VMEM((wins // TOGETHER, ns + half, TOGETHER * chans), BF16),
        pltpu.VMEM((2, rows, chans), F32),
    ]


class Choice:
    def __init__(self, odd, sources, target, sem):
        self.options = [
            (odd == side, pltpu.make_async_copy(source, target, sem))
            for side, source in enumerate(sources)
        ]

    def start(self):
        for here, copy in self.options:
            pl.when(here)(copy.start)

    def wait(self):
        for here, copy in self.options:
            pl.when(here)(copy.wait)


def input_copies(odd, first, x, tables_in, sem):
    copied = {"first": [], "x": [], "tables": []}
    used = 0

    def copy(source, target):
        nonlocal used
        if isinstance(source, tuple):
            made = Choice(odd, source, target, sem.at[used])
        else:
            made = pltpu.make_async_copy(source, target, sem.at[used])
        made.start()
        used += 1
        return made

    copied["first"] = [copy(*pair) for pair in first]
    for source, target in x:
        parts = max(target.shape[0] // PART, 1)
        part = target.shape[0] // parts
        rows = [pl.ds(n * part, part) for n in range(parts)]
        copied["x"].append(
            [
                copy(
                    tuple(option.at[here] for option in source)
                    if isinstance(source, tuple)
                    else source.at[here],
                    target.at[here],
                )
                for here in rows
            ]
        )
    copied["tables"] = [copy(*pair) for pair in tables_in]
    return copied


def own_kernel(places, odd_ref, flag_ref, *rest):
    tot_hbm, x_hbm, hann_hbm, conv_hbm, seg_hbm, b_hbm, p_hbm = rest[:7]
    tot, x, hann, conv, seg = rest[7:12]
    work, (b_out, in_sem, out_sem, p_sem) = rest[12:-4], rest[-4:]
    odd = odd_ref[0]
    copied = input_copies(
        odd,
        [(tot_hbm, tot), (hann_hbm, hann)],
        [(x_hbm, x)],
        [(conv_hbm, conv), (seg_hbm, seg)],
        in_sem,
    )
    _, second = segment_factors(
        places, odd, flag_ref, [tot], [x], hann, conv, seg, work, copied
    )

    def put_second(k, stage):
        stage[k] = second(k)

    kept = pltpu.make_async_copy(work[-2], p_hbm, p_sem)
    kept.start()
    send_factor(put_second, b_out, b_hbm, out_sem)
    kept.wait()


def send_factor(factor, stage, target, sem):
    step = stage.shape[0] // STEPS
    copies = []
    for n in range(STEPS):
        part = pl.ds(n * step, step)

        def one_bin(k, _):
            factor(k, stage)
            return 0

        lax.fori_loop(n * step, (n + 1) * step, one_bin, 0, unroll=8)
        copies.append(pltpu.make_async_copy(stage.at[part], target.at[part], sem.at[n]))
        copies[-1].start()
    for copy in copies:
        copy.wait()


def second_kernel(places, odd_ref, flag_ref, *rest):
    tot_hbm, (even_hbm, odd_hbm), rest = rest[:2], (rest[2:4], rest[4:6]), rest[6:]
    halo_hbm, hann_hbm, conv_hbm, seg_hbm, p_hbm, a_hbm, b_hbm = rest[:7]
    tot, x, rest = rest[7:9], rest[9:12], rest[12:]
    hann, conv, seg, own, mixed, a_out, b_out = rest[:7]
    work, (in_sem, p_sem, out_sem) = rest[7:-3], rest[-3:]
    odd = odd_ref[0]
    copied = input_copies(
        odd,
        list(zip(tot_hbm, tot)) + [(hann_hbm, hann)],
        list(zip(zip(even_hbm, odd_hbm), x)) + [(halo_hbm, x[2])],
        [(conv_hbm, conv), (seg_hbm, seg)],
        in_sem,
    )
    kept = pltpu.make_async_copy(p_hbm, own, p_sem)
    kept.start()
    copied["tables"].append(kept)
    chans = b_out.shape[2]
    lane = lax.broadcasted_iota(jnp.int32, (1, chans), 1)

    def first(step, series):
        @pl.when(odd == 1)
        def _():
            mixed[...] = series[...]

        @pl.when(odd == 0)
        def _():
            for i in range(TOGETHER):
                columns = slice(i * chans, (i + 1) * chans)
                value = own[step, :, columns]
                turned = jnp.concatenate([value[:, chans // 2 :], value[:, : chans // 2]], axis=1)
                mixed[:, columns] = jnp.where(lane < chans // 2, series[:, columns], turned)

        return mixed

    first_factor, second_factor = segment_factors(
        places, odd, flag_ref, tot, x, hann, conv, seg, work, copied, first
    )

    def both_factors(k, stage):
        def put(group, rows, value):
            a_out[k, group, rows] = value

        first_factor(k, put)
        stage[k] = second_factor(k)

    step = b_out.shape[0] // STEPS
    copies = []
    for n in range(STEPS):
        part = pl.ds(n * step, step)

        def one_bin(k, _):
            both_factors(k, b_out)
            return 0

        lax.fori_loop(n * step, (n + 1) * step, one_bin, 0, unroll=8)
        for m, (source, target) in enumerate(((a_out, a_hbm), (b_out, b_hbm))):
            copies.append(
                pltpu.make_async_copy(source.at[part], target.at[part], out_sem.at[2 * n + m])
            )
            copies[-1].start()
    for copy in copies:
        copy.wait()


def segments(places, side, flags, totals, pieces, series, hann, conv, seg):
    chans = LANE
    _, wins, ns = pieces[0].shape
    size = seg.shape[0]
    half = size // 2
    depth = ns // half * wins * 2
    smem = pl.BlockSpec(memory_space=pltpu.SMEM)
    anywhere = pl.BlockSpec(memory_space=pl.ANY)
    b_shape = jax.ShapeDtypeStruct((half, depth, chans), BF16)
    p_shape = jax.ShapeDtypeStruct((wins // TOGETHER, ns + half, TOGETHER * chans), BF16)
    a_shape = jax.ShapeDtypeStruct((half, 2, chans, depth), BF16)
    scratch = lambda *values: [pltpu.VMEM(value.shape, value.dtype) for value in values]
    operands = list(totals) + list(pieces) + [hann, conv, seg]
    count = len(operands) + chans // PART
    if series is None:
        kernel, out = own_kernel, [b_shape, p_shape]
        held = scratch(*operands)
        last = scratch(b_shape) + [
            pltpu.SemaphoreType.DMA((count,)),
            pltpu.SemaphoreType.DMA((STEPS,)),
            pltpu.SemaphoreType.DMA,
        ]
    else:
        kernel, out = second_kernel, [a_shape, b_shape]
        held = scratch(*totals, pieces[0], pieces[1], pieces[4], hann, conv, seg, series)
        held += [pltpu.VMEM(p_shape.shape[1:], BF16)] + scratch(a_shape, b_shape)
        last = [
            pltpu.SemaphoreType.DMA((count,)),
            pltpu.SemaphoreType.DMA,
            pltpu.SemaphoreType.DMA((2 * STEPS,)),
        ]
        operands.append(series)
    return pl.pallas_call(
        functools.partial(kernel, places),
        out_shape=out,
        in_specs=[smem] * 2 + [anywhere] * len(operands),
        out_specs=[anywhere] * 2,
        scratch_shapes=held + work_shapes(len(totals), chans, wins, ns) + last,
        compiler_params=pltpu.CompilerParams(vmem_limit_bytes=VMEM),
        cost_estimate=pl.CostEstimate(
            flops=2 * wins * chans * ns * (ns + 3 * size),
            bytes_accessed=16 * 1024 * 1024,
            transcendentals=0,
        ),
    )(side, flags, *operands)


def stack_kernel(places, scale, shares, me_ref, flag_ref, *rest):
    even_hbm, odd_hbm, late_hbm, rest = rest[:2], rest[2:4], rest[4], rest[5:]
    tot_hbm, hann_hbm, conv_hbm, seg_hbm, lag_hbm = rest[:5]
    a_hbm, b0_hbm, b2_hbm, rest = *rest[5:8], rest[8:]
    outs, rest = rest[:shares], rest[shares:]
    x, rest = rest[:3], rest[3:]
    tot, hann, conv, seg, lag, a, b0, b2 = rest[:8]
    work, (b3, one, in_sem, late_sem) = rest[8:-4], rest[-4:]
    me = me_ref[0]
    odd = lax.rem(me, 2)
    copied = input_copies(
        odd,
        [(tot_hbm, tot), (hann_hbm, hann)],
        list(zip(zip(even_hbm, odd_hbm), x)) + [(late_hbm, x[2])],
        [(conv_hbm, conv), (seg_hbm, seg), (lag_hbm, lag)],
        in_sem,
    )
    late = [
        pltpu.make_async_copy(source, target, late_sem.at[n])
        for n, (source, target) in enumerate(((b0_hbm, b0), (b2_hbm, b2), (a_hbm, a)))
    ]
    for copy in late:
        copy.start()
    bins, depth, chans = b0.shape
    width = chans // 2
    nfr = lag.shape[1]
    pitch = nfr + 1
    cross = work[-1]

    _, second_factor = segment_factors(
        places, odd, flag_ref, [tot], x, hann, conv, seg, work, copied
    )

    def second(k, _):
        b3[k] = second_factor(k)
        return 0

    lax.fori_loop(0, bins, second, 0, unroll=8)
    for copy in late:
        copy.wait()

    lane = lax.broadcasted_iota(jnp.int32, (1, chans), 1)
    low, high = [jnp.where((lane < width) == (g == 0), 1.0, 0.0).astype(BF16) for g in range(2)]

    def bins_with(near, far):
        def one_bin(k, _):
            inner = near[k] * low + b3[k] * high if near is not b3 else b3[k]
            right = jnp.concatenate(
                [
                    jnp.concatenate([b0[k], b2[k] * high], axis=1),
                    jnp.concatenate([inner, far[k] * low], axis=1),
                ],
                axis=0,
            )
            left = jnp.concatenate([a[k, 0], a[k, 1]], axis=1)
            value = jnp.dot(left, right, preferred_element_type=F32)
            for p in range(2):
                for t in range(2):
                    cross[t, pl.ds(2 * k + p, width, stride=pitch), :] = value[
                        p * width : (p + 1) * width, t * chans : (t + 1) * chans
                    ]
            return 0

        lax.fori_loop(0, bins, one_bin, 0, unroll=8)

    pl.when(odd == 0)(lambda: bins_with(b2, b3))
    pl.when(odd == 1)(lambda: bins_with(b3, b2))

    row = lax.broadcasted_iota(jnp.int32, one.shape[1:], 0)
    column = lax.broadcasted_iota(jnp.int32, one.shape[1:], 1)
    turned = jnp.where(row < width, row + chans, row - width)
    place = row + (turned - row) * odd
    for t in range(2):
        here = column + t * chans
        found = (place == here) | ((here >= chans + width) & (place == here - width))
        one[t] = jnp.where(found, 1.0, 0.0)
    share = OFFS // shares

    def one_channel(c, _):
        value = jnp.concatenate(
            [cross[t, pl.ds(c * pitch, nfr), :] for t in range(2)], axis=1
        ).astype(BF16)
        starts = [c + 1 + share * (me ^ d) for d in range(shares)]
        pick = jnp.concatenate(
            [
                jnp.concatenate([one[t, pl.ds(start, share), :] for start in starts], axis=0)
                for t in range(2)
            ],
            axis=1,
        ).astype(BF16)
        lagged = jnp.dot(lag[...], value, preferred_element_type=F32) * scale
        band = lax.dot_general(pick, lagged.astype(BF16), NT, preferred_element_type=F32)
        for d, out in enumerate(outs):
            out[c] = band[d * share : (d + 1) * share, :].astype(BF16)
        return 0

    lax.fori_loop(0, width, one_channel, 0, unroll=4)


def stacks(places, shares, scale, me, flags, total, pieces, hann, conv, seg, lag, a, b0, b2):
    bins, depth, chans = b0.shape
    width = chans // 2
    _, wins, ns = pieces[0].shape
    nlag, nfr = lag.shape
    smem = pl.BlockSpec(memory_space=pltpu.SMEM)
    vmem = pl.BlockSpec(memory_space=pltpu.VMEM)
    anywhere = pl.BlockSpec(memory_space=pl.ANY)
    tables_in = [total, hann, conv, seg, lag, a, b0, b2]
    operands = [*pieces, *tables_in]
    held = [pieces[0], pieces[1], pieces[4], *tables_in]
    return pl.pallas_call(
        functools.partial(stack_kernel, places, scale, shares),
        out_shape=[jax.ShapeDtypeStruct((width, OFFS // shares, nlag), BF16)] * shares,
        in_specs=[smem] * 2 + [anywhere] * len(operands),
        out_specs=[vmem] * shares,
        scratch_shapes=[pltpu.VMEM(value.shape, value.dtype) for value in held]
        + work_shapes(1, chans, wins, ns)
        + [
            pltpu.VMEM(b0.shape, BF16),
            pltpu.VMEM((2, chans + width, chans), F32),
            pltpu.SemaphoreType.DMA((8 + chans // PART,)),
            pltpu.SemaphoreType.DMA((3,)),
        ],
        compiler_params=pltpu.CompilerParams(vmem_limit_bytes=VMEM),
        cost_estimate=pl.CostEstimate(
            flops=2 * width * bins * 4 * (2 * depth * chans + 2 * OFFS * chans),
            bytes_accessed=20 * 1024 * 1024,
            transcendentals=0,
        ),
    )(me, flags, *operands)


def add_over(value, axis, beside):
    count = lax.axis_size(axis)
    if count & (count - 1):
        return lax.psum(value, axis), beside
    bit = 1
    while bit < count:
        steps = [bit] if bit == 1 or 2 * bit == count else [bit, 2 * bit, 3 * bit]
        arrived = [lax.ppermute(value, axis, [(i, i ^ s) for i in range(count)]) for s in steps]
        bit *= 1 + len(steps)
        if bit == count:
            arrived, beside = lax.optimization_barrier((arrived, beside))
        value = sum(arrived, value)
    return value, beside


def shards(samples, band_gain, dead_flags, section_ids):
    chans, wins, ns = samples.shape
    nf = ns // 2
    width = chans // 2
    blocks = lax.axis_size("fibre")
    groups = lax.axis_size("tm")
    me = lax.axis_index("tm")
    odd = me % 2
    window, waves, seg, lag = tables(ns, nf)
    waves, seg, lag = jnp.asarray(waves), jnp.asarray(seg), jnp.asarray(lag)
    hann = jnp.asarray(np.broadcast_to(window[None, :], (wins, ns)))
    response = jnp.sum(band_gain[:, None] * waves, axis=0, keepdims=True)
    conv = pl.pallas_call(
        circulant_kernel,
        out_shape=jax.ShapeDtypeStruct((ns, ns), BF16),
        compiler_params=pltpu.CompilerParams(vmem_limit_bytes=VMEM),
        cost_estimate=pl.CostEstimate(flops=1, bytes_accessed=1, transcendentals=0),
    )(response)
    swap = [(z, z ^ 1) for z in range(groups)]
    both = ("fibre", "tm")
    halo_pairs = [
        (b * groups + z, (b + (1 if z % 2 else -1)) % blocks * groups + z)
        for b in range(blocks)
        for z in range(groups)
    ]

    head = width * 5 // 8

    their_head = lax.ppermute(
        lax.dynamic_slice_in_dim(samples, (1 - odd) * width, head, 0), "tm", swap
    )
    flags = jnp.stack([dead_flags, section_ids])
    halo_flags = lax.ppermute(
        lax.dynamic_slice_in_dim(flags, odd * width, width, 1), both, halo_pairs
    )
    smem = pl.BlockSpec(memory_space=pltpu.SMEM)
    anywhere = pl.BlockSpec(memory_space=pl.ANY)
    sums, own_half, tail = pl.pallas_call(
        section_sums,
        out_shape=[
            jax.ShapeDtypeStruct((NSEC, wins, ns + LANE), F32),
            jax.ShapeDtypeStruct((width, wins, ns), BF16),
            jax.ShapeDtypeStruct((width - head, wins, ns), BF16),
        ],
        in_specs=[smem] * 3 + [anywhere],
        out_specs=[pl.BlockSpec(memory_space=pltpu.VMEM), anywhere, anywhere],
        scratch_shapes=[
            pltpu.VMEM(samples.shape, BF16),
            pltpu.SemaphoreType.DMA((STEPS,)),
            pltpu.SemaphoreType.DMA((2,)),
        ],
        compiler_params=pltpu.CompilerParams(vmem_limit_bytes=VMEM),
        cost_estimate=pl.CostEstimate(flops=1, bytes_accessed=1, transcendentals=0),
    )(odd[None], dead_flags, section_ids, samples)
    total, their_head = add_over(sums, "fibre", their_head)
    halo_source, conv = lax.optimization_barrier((own_half, conv))
    halo = lax.ppermute(halo_source, both, halo_pairs)
    total, halo_flags, conv = lax.optimization_barrier((total, halo_flags, conv))
    their_total = lax.ppermute(total, "tm", swap)
    ready = (total, their_total, their_head, own_half, tail, flags, hann, conv, seg, lag)
    ready = lax.optimization_barrier(ready)
    total, their_total, their_head, own_half, tail, flags, hann, conv, seg, lag = ready
    their_tail = lax.ppermute(tail, "tm", swap)
    their_second = lax.ppermute(own_half, "tm", swap)
    halo_head = lax.ppermute(their_head, both, halo_pairs)

    side = odd[None]
    parts = (hann, conv, seg)
    every = jnp.concatenate([flags, halo_flags], axis=1)
    b0, series = segments(((0, (0, 0), (0, 0)),), side, flags, (total,), (samples,), None, *parts)
    b0, forward = lax.optimization_barrier((b0, their_tail))
    halo_tail = lax.ppermute(forward, both, halo_pairs)
    a, b2 = segments(
        (
            (1, (0, 0), (0, chans)),
            (1, (head, head), (head, chans + head)),
            (0, (width, width), (chans, chans)),
        ),
        side,
        every,
        (total, their_total),
        (their_head, their_tail, halo_head, halo_tail, halo),
        series,
        *parts,
    )
    scale = 2.0 / ns / LAGS / math.sqrt(nf * wins * groups)
    found = stacks(
        (
            (0, (0, width), (chans, width)),
            (0, (head, width + head), (chans + head, width + head)),
            (0, (width, 0), (width, 0)),
        ),
        groups,
        scale,
        me[None],
        every,
        their_total,
        (halo_head, halo_tail, their_head, their_tail, their_second),
        *(hann, conv, seg, lag),
        *(a, b0, b2),
    )
    arrived = []
    for d in range(groups):
        pairs = [
            (b * groups + z, (b - z % 2) % blocks * groups + (z ^ d))
            for b in range(blocks)
            for z in range(groups)
        ]
        arrived.append(lax.ppermute(found[d], both, pairs).astype(F32))
    same = sum(arrived[2::2], arrived[0])
    other = sum(arrived[3::2], arrived[1])
    return jnp.concatenate(
        [jnp.where(odd == 0, same, other), jnp.where(odd == 0, other, same)], axis=0
    )


def solution(mesh):
    in_specs = (P("fibre", "tm", None), P(), P("fibre"), P("fibre"))
    out_specs = P("fibre", "tm", None)
    return jax.shard_map(shards, mesh=mesh, in_specs=in_specs, out_specs=out_specs, check_vma=False)
```

```python
import functools
import math

import jax
import jax.numpy as jnp
import ml_dtypes
import numpy as np
from jax import lax
from jax.experimental import pallas as pl
from jax.experimental.pallas import tpu as pltpu
from jax.sharding import PartitionSpec as P

OFFS = 128
LAGS = 128
NSEC = 2
LANE = 128
PART = 16
TILE = 256
STEPS = 4
TOGETHER = 4
VMEM = 63 * 1024 * 1024
NT = (((1,), (1,)), ((), ()))
F32 = jnp.float32
BF16 = jnp.bfloat16


def tables(ns, nf):
    tick = np.arange(ns)
    freq = np.arange(nf)
    window = 0.5 - 0.5 * np.cos(tick * (2.0 * math.pi / ns))
    waves = np.cos((freq[:, None] * tick[None, :] % ns) * (2.0 * math.pi / ns))
    waves[0] *= math.sqrt(0.5)
    size = 2 * LAGS
    bins = np.arange(size // 2)
    turn = math.pi / size * ((2 * bins[:, None] + 1) * np.arange(size)[None, :] % (2 * size))
    segment = np.stack([np.cos(turn), -np.sin(turn)], axis=1).reshape(size, size)
    lag = np.stack([np.cos(turn), -np.sin(turn)], axis=1).reshape(size, size)[:, :LAGS].T
    cast = lambda a: a.astype(np.float32).astype(ml_dtypes.bfloat16)
    return window.astype(np.float32), waves.astype(np.float32), cast(segment), cast(lag)


def section_sums(odd_ref, dead_ref, sec_ref, x_hbm, out_ref, half_hbm, tail_hbm, x, in_sem, sem):
    chans, wins, ns = x.shape
    width, length = half_hbm.shape[0], tail_hbm.shape[0]
    odd = odd_ref[0]
    part = chans // STEPS
    arriving = [
        pltpu.make_async_copy(
            x_hbm.at[pl.ds(n * part, part)], x.at[pl.ds(n * part, part)], in_sem.at[n]
        )
        for n in range(STEPS)
    ]
    for copy in arriving:
        copy.start()
    leaving = [
        pltpu.make_async_copy(x.at[pl.ds(odd * width, width)], half_hbm, sem.at[0]),
        pltpu.make_async_copy(
            x.at[pl.ds((2 - odd) * width - length, length)], tail_hbm, sem.at[1]
        ),
    ]

    def body(c, carry):
        value = x[c].astype(F32)
        live = 1 - dead_ref[c]
        sums, counts = carry
        weights = [jnp.where(sec_ref[c] == s, live, 0).astype(F32) for s in range(NSEC)]
        return (
            tuple(sums[s] + weights[s] * value for s in range(NSEC)),
            tuple(counts[s] + weights[s] for s in range(NSEC)),
        )

    zero = jnp.zeros((wins, ns), F32)
    carry = ((zero,) * NSEC, (jnp.float32(0),) * NSEC)
    for n, copy in enumerate(arriving):
        copy.wait()
        if n == STEPS - 1:
            for out in leaving:
                out.start()
        carry = lax.fori_loop(n * part, (n + 1) * part, body, carry, unroll=8)
    sums, counts = carry
    for s in range(NSEC):
        out_ref[s, :, :ns] = sums[s]
        out_ref[s, :, ns:] = jnp.zeros((wins, LANE), F32) + counts[s]
    for out in leaving:
        out.wait()


def circulant_kernel(filter_ref, out_ref):
    ns = filter_ref.shape[1]
    for t in range(0, ns, 16):
        block = jnp.broadcast_to(filter_ref[...], (16, ns))
        out_ref[t : t + 16, :] = pltpu.roll(block, t, 1, stride=1, stride_axis=0).astype(BF16)


def segment_factors(places, odd, flag_ref, tot, x, hann, conv, seg, work, copied, first=None):
    common, clean, mass, square, rows, series_all, stage = work
    _, wins, ns = x[0].shape
    chans = sum(piece.shape[0] for piece in x)
    pitch = wins + 1
    size = seg.shape[0]
    half = size // 2
    blocks = ns // half
    jw = blocks * wins
    jpitch = jw + 1
    for copy in copied["first"]:
        copy.wait()
    for g in range(len(tot)):
        for s in range(NSEC):
            common[g * NSEC + s] = tot[g][s, :, :ns] / jnp.maximum(tot[g][s, :, ns : ns + 1], 1.0)
    sign = 1.0 - 2.0 * (lax.broadcasted_iota(jnp.int32, (chans, LANE), 1) % 2).astype(F32)

    for number, (group, base, flags) in enumerate(places):
        piece = x[number]
        length = piece.shape[0]
        base = base[0] + odd * (base[1] - base[0])
        flags = flags[0] + odd * (flags[1] - flags[0])

        def clean_channel(c):
            at = base + c
            flag = flags + c
            live = (1 - flag_ref[0, flag]).astype(F32)
            value = (piece[c].astype(F32) - common[group * NSEC + flag_ref[1, flag]]) * (
                hann[...] * live
            )
            tiles = [value[:, t * LANE : (t + 1) * LANE] for t in range(ns // LANE)]
            row = pl.ds(at * pitch, wins)
            mass[row, :] = sum(tiles[1:], tiles[0])
            square[row, :] = sum([tile * tile for tile in tiles[1:]], tiles[0] * tiles[0])
            for t, tile in enumerate(tiles):
                clean[t, row, :] = tile

        parts = copied["x"][number]
        part = length // len(parts)
        for n, copy in enumerate(parts):
            copy.wait()
            repeat(n * part, (n + 1) * part, clean_channel, 4)
    for copy in copied["tables"]:
        copy.wait()

    for step in range(wins // TOGETHER):
        series = series_all.at[step]
        for i in range(TOGETHER):
            window = pl.ds(step * TOGETHER + i, chans, stride=pitch)
            total = mass[window, :]
            lowest = jnp.sum(total, axis=1, keepdims=True)
            highest = jnp.sum(total * sign, axis=1, keepdims=True)
            power = 0.5 * jnp.sum(square[window, :], axis=1, keepdims=True)
            power = power + (lowest * lowest - highest * highest) * (0.5 / ns)
            level = lax.rsqrt(power + 1e-06)
            for t in range(ns // LANE):
                rows[i * chans : (i + 1) * chans, t * LANE : (t + 1) * LANE] = (
                    clean[t, window, :] * level
                ).astype(BF16)
        for t in range(0, ns, TILE):
            series[half // 2 + t : half // 2 + t + TILE, :] = lax.dot_general(
                conv[t : t + TILE, :], rows[...], NT, preferred_element_type=F32
            ).astype(BF16)
        series[: half // 2, :] = series[ns : ns + half // 2, :]
        series[ns + half // 2 :, :] = series[half // 2 : half, :]

        def place(which, j, value):
            for i in range(TOGETHER):
                at = j * wins + step * TOGETHER + i
                stage[which, pl.ds(at, size, stride=jpitch), :] = value[
                    :, i * chans : (i + 1) * chans
                ]

        for j in range(blocks):
            start = j * half + half // 2
            b = jnp.dot(
                seg[:, :half], series[start : start + half, :], preferred_element_type=F32
            )
            place(1, j, b)

        if first is not None:
            source = first(step, series)
            for j in range(blocks):
                a = jnp.dot(
                    seg[...], source[j * half : j * half + size, :], preferred_element_type=F32
                )
                place(0, j, a)

    def factor(which, k, turn=False):
        real, imag = [
            stage[which, pl.ds((2 * k + part) * jpitch, jw), :] for part in range(2)
        ]
        if turn:
            real, imag = imag, -real
        return jnp.concatenate([real.astype(BF16), imag.astype(BF16)], axis=0)

    def first_factor(k, put):
        width = chans // 2
        for part in range(2):
            value = factor(0, k, part == 1).T
            rows_at = slice(part * width, (part + 1) * width)
            put(1, rows_at, value[:width])
            put(0, rows_at, value[width:])

    return first_factor, lambda k: factor(1, k)


def work_shapes(groups, chans, wins, ns):
    half = LAGS
    rows = 2 * half * (ns // half * wins + 1)
    return [
        pltpu.VMEM((groups * NSEC, wins, ns), F32),
        pltpu.VMEM((ns // LANE, chans * (wins + 1), LANE), F32),
        pltpu.VMEM((chans * (wins + 1), LANE), F32),
        pltpu.VMEM((chans * (wins + 1), LANE), F32),
        pltpu.VMEM((TOGETHER * chans, ns), BF16),
        pltpu.VMEM((wins // TOGETHER, ns + half, TOGETHER * chans), BF16),
        pltpu.VMEM((2, rows, chans), F32),
    ]


def repeat(start, stop, body, together):
    def step(n, _):
        for i in range(together):
            body(start + n * together + i)
        return 0

    lax.fori_loop(0, (stop - start) // together, step, 0)


class Choice:
    def __init__(self, odd, sources, target, sem):
        self.options = [
            (odd == side, pltpu.make_async_copy(source, target, sem))
            for side, source in enumerate(sources)
        ]

    def start(self):
        for here, copy in self.options:
            pl.when(here)(copy.start)

    def wait(self):
        for here, copy in self.options:
            pl.when(here)(copy.wait)


def input_copies(odd, first, x, tables_in, sem):
    copied = {"first": [], "x": [], "tables": []}
    used = 0

    def copy(source, target):
        nonlocal used
        if isinstance(source, tuple):
            made = Choice(odd, source, target, sem.at[used])
        else:
            made = pltpu.make_async_copy(source, target, sem.at[used])
        made.start()
        used += 1
        return made

    copied["first"] = [copy(*pair) for pair in first]
    for source, target in x:
        parts = max(target.shape[0] // PART, 1)
        part = target.shape[0] // parts
        rows = [pl.ds(n * part, part) for n in range(parts)]
        copied["x"].append(
            [
                copy(
                    tuple(option.at[here] for option in source)
                    if isinstance(source, tuple)
                    else source.at[here],
                    target.at[here],
                )
                for here in rows
            ]
        )
    copied["tables"] = [copy(*pair) for pair in tables_in]
    return copied


def own_kernel(places, odd_ref, flag_ref, *rest):
    tot_hbm, x_hbm, hann_hbm, conv_hbm, seg_hbm, b_hbm, p_hbm = rest[:7]
    tot, x, hann, conv, seg = rest[7:12]
    work, (b_out, in_sem, out_sem, p_sem) = rest[12:-4], rest[-4:]
    odd = odd_ref[0]
    copied = input_copies(
        odd,
        [(tot_hbm, tot), (hann_hbm, hann)],
        [(x_hbm, x)],
        [(conv_hbm, conv), (seg_hbm, seg)],
        in_sem,
    )
    _, second = segment_factors(
        places, odd, flag_ref, [tot], [x], hann, conv, seg, work, copied
    )

    def put_second(k, stage):
        stage[k] = second(k)

    kept = pltpu.make_async_copy(work[-2], p_hbm, p_sem)
    kept.start()
    send_factor(put_second, b_out, b_hbm, out_sem)
    kept.wait()


def send_factor(factor, stage, target, sem):
    step = stage.shape[0] // STEPS
    copies = []
    for n in range(STEPS):
        part = pl.ds(n * step, step)

        repeat(n * step, (n + 1) * step, lambda k: factor(k, stage), 4)
        copies.append(pltpu.make_async_copy(stage.at[part], target.at[part], sem.at[n]))
        copies[-1].start()
    for copy in copies:
        copy.wait()


def second_kernel(places, odd_ref, flag_ref, *rest):
    tot_hbm, (even_hbm, odd_hbm), rest = rest[:2], (rest[2:4], rest[4:6]), rest[6:]
    halo_hbm, hann_hbm, conv_hbm, seg_hbm, p_hbm, a_hbm, b_hbm = rest[:7]
    tot, x, rest = rest[7:9], rest[9:12], rest[12:]
    hann, conv, seg, own, mixed, a_out, b_out = rest[:7]
    work, (in_sem, p_sem, out_sem) = rest[7:-3], rest[-3:]
    odd = odd_ref[0]
    copied = input_copies(
        odd,
        list(zip(tot_hbm, tot)) + [(hann_hbm, hann)],
        list(zip(zip(even_hbm, odd_hbm), x)) + [(halo_hbm, x[2])],
        [(conv_hbm, conv), (seg_hbm, seg)],
        in_sem,
    )
    kept = pltpu.make_async_copy(p_hbm, own, p_sem)
    kept.start()
    copied["tables"].append(kept)
    chans = b_out.shape[2]
    lane = lax.broadcasted_iota(jnp.int32, (1, chans), 1)

    def first(step, series):
        @pl.when(odd == 1)
        def _():
            mixed[...] = series[...]

        @pl.when(odd == 0)
        def _():
            for i in range(TOGETHER):
                columns = slice(i * chans, (i + 1) * chans)
                value = own[step, :, columns]
                turned = jnp.concatenate([value[:, chans // 2 :], value[:, : chans // 2]], axis=1)
                mixed[:, columns] = jnp.where(lane < chans // 2, series[:, columns], turned)

        return mixed

    first_factor, second_factor = segment_factors(
        places, odd, flag_ref, tot, x, hann, conv, seg, work, copied, first
    )

    def both_factors(k, stage):
        def put(group, rows, value):
            a_out[k, group, rows] = value

        first_factor(k, put)
        stage[k] = second_factor(k)

    step = b_out.shape[0] // STEPS
    copies = []
    for n in range(STEPS):
        part = pl.ds(n * step, step)

        repeat(n * step, (n + 1) * step, lambda k: both_factors(k, b_out), 4)
        for m, (source, target) in enumerate(((a_out, a_hbm), (b_out, b_hbm))):
            copies.append(
                pltpu.make_async_copy(source.at[part], target.at[part], out_sem.at[2 * n + m])
            )
            copies[-1].start()
    for copy in copies:
        copy.wait()


def segments(places, side, flags, totals, pieces, series, hann, conv, seg):
    chans = LANE
    _, wins, ns = pieces[0].shape
    size = seg.shape[0]
    half = size // 2
    depth = ns // half * wins * 2
    smem = pl.BlockSpec(memory_space=pltpu.SMEM)
    anywhere = pl.BlockSpec(memory_space=pl.ANY)
    b_shape = jax.ShapeDtypeStruct((half, depth, chans), BF16)
    p_shape = jax.ShapeDtypeStruct((wins // TOGETHER, ns + half, TOGETHER * chans), BF16)
    a_shape = jax.ShapeDtypeStruct((half, 2, chans, depth), BF16)
    scratch = lambda *values: [pltpu.VMEM(value.shape, value.dtype) for value in values]
    operands = list(totals) + list(pieces) + [hann, conv, seg]
    count = len(operands) + chans // PART
    if series is None:
        kernel, out = own_kernel, [b_shape, p_shape]
        held = scratch(*operands)
        last = scratch(b_shape) + [
            pltpu.SemaphoreType.DMA((count,)),
            pltpu.SemaphoreType.DMA((STEPS,)),
            pltpu.SemaphoreType.DMA,
        ]
    else:
        kernel, out = second_kernel, [a_shape, b_shape]
        held = scratch(*totals, pieces[0], pieces[1], pieces[4], hann, conv, seg, series)
        held += [pltpu.VMEM(p_shape.shape[1:], BF16)] + scratch(a_shape, b_shape)
        last = [
            pltpu.SemaphoreType.DMA((count,)),
            pltpu.SemaphoreType.DMA,
            pltpu.SemaphoreType.DMA((2 * STEPS,)),
        ]
        operands.append(series)
    return pl.pallas_call(
        functools.partial(kernel, places),
        out_shape=out,
        in_specs=[smem] * 2 + [anywhere] * len(operands),
        out_specs=[anywhere] * 2,
        scratch_shapes=held + work_shapes(len(totals), chans, wins, ns) + last,
        compiler_params=pltpu.CompilerParams(vmem_limit_bytes=VMEM),
        cost_estimate=pl.CostEstimate(
            flops=2 * wins * chans * ns * (ns + 3 * size),
            bytes_accessed=16 * 1024 * 1024,
            transcendentals=0,
        ),
    )(side, flags, *operands)


def stack_kernel(places, scale, shares, me_ref, flag_ref, *rest):
    even_hbm, odd_hbm, late_hbm, rest = rest[:2], rest[2:4], rest[4], rest[5:]
    tot_hbm, hann_hbm, conv_hbm, seg_hbm, lag_hbm = rest[:5]
    a_hbm, b0_hbm, b2_hbm, rest = *rest[5:8], rest[8:]
    outs, rest = rest[:shares], rest[shares:]
    x, rest = rest[:3], rest[3:]
    tot, hann, conv, seg, lag, a, b0, b2 = rest[:8]
    work, (b3, one, in_sem, late_sem) = rest[8:-4], rest[-4:]
    me = me_ref[0]
    odd = lax.rem(me, 2)
    copied = input_copies(
        odd,
        [(tot_hbm, tot), (hann_hbm, hann)],
        list(zip(zip(even_hbm, odd_hbm), x)) + [(late_hbm, x[2])],
        [(conv_hbm, conv), (seg_hbm, seg), (lag_hbm, lag)],
        in_sem,
    )
    late = [
        pltpu.make_async_copy(source, target, late_sem.at[n])
        for n, (source, target) in enumerate(((b0_hbm, b0), (b2_hbm, b2), (a_hbm, a)))
    ]
    for copy in late:
        copy.start()
    bins, depth, chans = b0.shape
    width = chans // 2
    nfr = lag.shape[1]
    pitch = nfr + 1
    cross = work[-1]

    _, second_factor = segment_factors(
        places, odd, flag_ref, [tot], x, hann, conv, seg, work, copied
    )

    def second(k):
        b3[k] = second_factor(k)

    repeat(0, bins, second, 4)
    for copy in late:
        copy.wait()

    lane = lax.broadcasted_iota(jnp.int32, (1, chans), 1)
    low, high = [jnp.where((lane < width) == (g == 0), 1.0, 0.0).astype(BF16) for g in range(2)]

    def bins_with(near, far):
        def one_bin(k):
            inner = near[k] * low + b3[k] * high if near is not b3 else b3[k]
            right = jnp.concatenate(
                [
                    jnp.concatenate([b0[k], b2[k] * high], axis=1),
                    jnp.concatenate([inner, far[k] * low], axis=1),
                ],
                axis=0,
            )
            left = jnp.concatenate([a[k, 0], a[k, 1]], axis=1)
            value = jnp.dot(left, right, preferred_element_type=F32)
            for p in range(2):
                for t in range(2):
                    cross[t, pl.ds(2 * k + p, width, stride=pitch), :] = value[
                        p * width : (p + 1) * width, t * chans : (t + 1) * chans
                    ]

        repeat(0, bins, one_bin, 4)

    pl.when(odd == 0)(lambda: bins_with(b2, b3))
    pl.when(odd == 1)(lambda: bins_with(b3, b2))

    row = lax.broadcasted_iota(jnp.int32, one.shape[1:], 0)
    column = lax.broadcasted_iota(jnp.int32, one.shape[1:], 1)
    turned = jnp.where(row < width, row + chans, row - width)
    place = row + (turned - row) * odd
    for t in range(2):
        here = column + t * chans
        found = (place == here) | ((here >= chans + width) & (place == here - width))
        one[t] = jnp.where(found, 1.0, 0.0)
    share = OFFS // shares

    def one_channel(c):
        value = jnp.concatenate(
            [cross[t, pl.ds(c * pitch, nfr), :] for t in range(2)], axis=1
        ).astype(BF16)
        starts = [c + 1 + share * (me ^ d) for d in range(shares)]
        pick = jnp.concatenate(
            [
                jnp.concatenate([one[t, pl.ds(start, share), :] for start in starts], axis=0)
                for t in range(2)
            ],
            axis=1,
        ).astype(BF16)
        lagged = jnp.dot(lag[...], value, preferred_element_type=F32) * scale
        band = lax.dot_general(pick, lagged.astype(BF16), NT, preferred_element_type=F32)
        for d, out in enumerate(outs):
            out[c] = band[d * share : (d + 1) * share, :].astype(BF16)

    repeat(0, width, one_channel, 4)


def stacks(places, shares, scale, me, flags, total, pieces, hann, conv, seg, lag, a, b0, b2):
    bins, depth, chans = b0.shape
    width = chans // 2
    _, wins, ns = pieces[0].shape
    nlag, nfr = lag.shape
    smem = pl.BlockSpec(memory_space=pltpu.SMEM)
    vmem = pl.BlockSpec(memory_space=pltpu.VMEM)
    anywhere = pl.BlockSpec(memory_space=pl.ANY)
    tables_in = [total, hann, conv, seg, lag, a, b0, b2]
    operands = [*pieces, *tables_in]
    held = [pieces[0], pieces[1], pieces[4], *tables_in]
    return pl.pallas_call(
        functools.partial(stack_kernel, places, scale, shares),
        out_shape=[jax.ShapeDtypeStruct((width, OFFS // shares, nlag), BF16)] * shares,
        in_specs=[smem] * 2 + [anywhere] * len(operands),
        out_specs=[vmem] * shares,
        scratch_shapes=[pltpu.VMEM(value.shape, value.dtype) for value in held]
        + work_shapes(1, chans, wins, ns)
        + [
            pltpu.VMEM(b0.shape, BF16),
            pltpu.VMEM((2, chans + width, chans), F32),
            pltpu.SemaphoreType.DMA((8 + chans // PART,)),
            pltpu.SemaphoreType.DMA((3,)),
        ],
        compiler_params=pltpu.CompilerParams(vmem_limit_bytes=VMEM),
        cost_estimate=pl.CostEstimate(
            flops=2 * width * bins * 4 * (2 * depth * chans + 2 * OFFS * chans),
            bytes_accessed=20 * 1024 * 1024,
            transcendentals=0,
        ),
    )(me, flags, *operands)


def add_over(value, axis, beside):
    count = lax.axis_size(axis)
    if count & (count - 1):
        return lax.psum(value, axis), beside
    bit = 1
    while bit < count:
        steps = [bit] if bit == 1 or 2 * bit == count else [bit, 2 * bit, 3 * bit]
        arrived = [lax.ppermute(value, axis, [(i, i ^ s) for i in range(count)]) for s in steps]
        bit *= 1 + len(steps)
        if bit == count:
            arrived, beside = lax.optimization_barrier((arrived, beside))
        value = sum(arrived, value)
    return value, beside


def shards(samples, band_gain, dead_flags, section_ids):
    chans, wins, ns = samples.shape
    nf = ns // 2
    width = chans // 2
    blocks = lax.axis_size("fibre")
    groups = lax.axis_size("tm")
    me = lax.axis_index("tm")
    odd = me % 2
    window, waves, seg, lag = tables(ns, nf)
    waves, seg, lag = jnp.asarray(waves), jnp.asarray(seg), jnp.asarray(lag)
    hann = jnp.asarray(window[None, :])
    response = jnp.sum(band_gain[:, None] * waves, axis=0, keepdims=True)
    conv = pl.pallas_call(
        circulant_kernel,
        out_shape=jax.ShapeDtypeStruct((ns, ns), BF16),
        compiler_params=pltpu.CompilerParams(vmem_limit_bytes=VMEM),
        cost_estimate=pl.CostEstimate(flops=1, bytes_accessed=1, transcendentals=0),
    )(response)
    swap = [(z, z ^ 1) for z in range(groups)]
    both = ("fibre", "tm")
    halo_pairs = [
        (b * groups + z, (b + (1 if z % 2 else -1)) % blocks * groups + z)
        for b in range(blocks)
        for z in range(groups)
    ]

    head = width * 5 // 8

    their_head = lax.ppermute(
        lax.dynamic_slice_in_dim(samples, (1 - odd) * width, head, 0), "tm", swap
    )
    flags = jnp.stack([dead_flags, section_ids])
    halo_flags = lax.ppermute(
        lax.dynamic_slice_in_dim(flags, odd * width, width, 1), both, halo_pairs
    )
    smem = pl.BlockSpec(memory_space=pltpu.SMEM)
    anywhere = pl.BlockSpec(memory_space=pl.ANY)
    sums, own_half, tail = pl.pallas_call(
        section_sums,
        out_shape=[
            jax.ShapeDtypeStruct((NSEC, wins, ns + LANE), F32),
            jax.ShapeDtypeStruct((width, wins, ns), BF16),
            jax.ShapeDtypeStruct((width - head, wins, ns), BF16),
        ],
        in_specs=[smem] * 3 + [anywhere],
        out_specs=[pl.BlockSpec(memory_space=pltpu.VMEM), anywhere, anywhere],
        scratch_shapes=[
            pltpu.VMEM(samples.shape, BF16),
            pltpu.SemaphoreType.DMA((STEPS,)),
            pltpu.SemaphoreType.DMA((2,)),
        ],
        compiler_params=pltpu.CompilerParams(vmem_limit_bytes=VMEM),
        cost_estimate=pl.CostEstimate(flops=1, bytes_accessed=1, transcendentals=0),
    )(odd[None], dead_flags, section_ids, samples)
    total, their_head = add_over(sums, "fibre", their_head)
    halo_source, conv = lax.optimization_barrier((own_half, conv))
    halo = lax.ppermute(halo_source, both, halo_pairs)
    total, halo_flags, conv, own_half, tail = lax.optimization_barrier(
        (total, halo_flags, conv, own_half, tail)
    )
    their_total = lax.ppermute(total, "tm", swap)
    their_tail = lax.ppermute(tail, "tm", swap)
    their_second = lax.ppermute(own_half, "tm", swap)
    ready = (total, their_total, their_head, flags, hann, conv, seg, lag)
    ready = lax.optimization_barrier(ready)
    total, their_total, their_head, flags, hann, conv, seg, lag = ready
    halo_head = lax.ppermute(their_head, both, halo_pairs)

    side = odd[None]
    parts = (hann, conv, seg)
    every = jnp.concatenate([flags, halo_flags], axis=1)
    b0, series = segments(((0, (0, 0), (0, 0)),), side, flags, (total,), (samples,), None, *parts)
    b0, forward = lax.optimization_barrier((b0, their_tail))
    halo_tail = lax.ppermute(forward, both, halo_pairs)
    a, b2 = segments(
        (
            (1, (0, 0), (0, chans)),
            (1, (head, head), (head, chans + head)),
            (0, (width, width), (chans, chans)),
        ),
        side,
        every,
        (total, their_total),
        (their_head, their_tail, halo_head, halo_tail, halo),
        series,
        *parts,
    )
    scale = 2.0 / ns / LAGS / math.sqrt(nf * wins * groups)
    found = stacks(
        (
            (0, (0, width), (chans, width)),
            (0, (head, width + head), (chans + head, width + head)),
            (0, (width, 0), (width, 0)),
        ),
        groups,
        scale,
        me[None],
        every,
        their_total,
        (halo_head, halo_tail, their_head, their_tail, their_second),
        *(hann, conv, seg, lag),
        *(a, b0, b2),
    )
    arrived = {}
    found = list(found)
    for d in reversed(range(groups)):
        if d == 1 and groups > 2:
            found[0], found[1], arrived[2] = lax.optimization_barrier(
                (found[0], found[1], arrived[2])
            )
        pairs = [
            (b * groups + z, (b - z % 2) % blocks * groups + (z ^ d))
            for b in range(blocks)
            for z in range(groups)
        ]
        arrived[d] = lax.ppermute(found[d], both, pairs)
    arrived = [arrived[d].astype(F32) for d in range(groups)]
    same = sum(arrived[2::2], arrived[0])
    other = sum(arrived[3::2], arrived[1])
    return jnp.concatenate(
        [jnp.where(odd == 0, same, other), jnp.where(odd == 0, other, same)], axis=0
    )


def solution(mesh):
    in_specs = (P("fibre", "tm", None), P(), P("fibre"), P("fibre"))
    out_specs = P("fibre", "tm", None)
    return jax.shard_map(shards, mesh=mesh, in_specs=in_specs, out_specs=out_specs, check_vma=False)
```

```python
import functools
import math

import jax
import jax.numpy as jnp
import ml_dtypes
import numpy as np
from jax import lax
from jax.experimental import pallas as pl
from jax.experimental.pallas import tpu as pltpu
from jax.sharding import PartitionSpec as P

OFFS = 128
LAGS = 128
NSEC = 2
LANE = 128
PART = 16
TILE = 256
STEPS = 4
TOGETHER = 4
VMEM = 63 * 1024 * 1024
NT = (((1,), (1,)), ((), ()))
F32 = jnp.float32
BF16 = jnp.bfloat16


def tables(ns, nf):
    tick = np.arange(ns)
    freq = np.arange(nf)
    window = 0.5 - 0.5 * np.cos(tick * (2.0 * math.pi / ns))
    waves = np.cos((freq[:, None] * tick[None, :] % ns) * (2.0 * math.pi / ns))
    waves[0] *= math.sqrt(0.5)
    size = 2 * LAGS
    bins = np.arange(size // 2)
    turn = math.pi / size * ((2 * bins[:, None] + 1) * np.arange(size)[None, :] % (2 * size))
    segment = np.stack([np.cos(turn), -np.sin(turn)], axis=1).reshape(size, size)
    lag = np.stack([np.cos(turn), -np.sin(turn)], axis=1).reshape(size, size)[:, :LAGS].T
    cast = lambda a: a.astype(np.float32).astype(ml_dtypes.bfloat16)
    return window.astype(np.float32), waves.astype(np.float32), cast(segment), cast(lag)


def section_sums(odd_ref, dead_ref, sec_ref, x_hbm, out_ref, half_hbm, tail_hbm, x, in_sem, sem):
    chans, wins, ns = x.shape
    width, length = half_hbm.shape[0], tail_hbm.shape[0]
    odd = odd_ref[0]
    part = chans // STEPS
    arriving = [
        pltpu.make_async_copy(
            x_hbm.at[pl.ds(n * part, part)], x.at[pl.ds(n * part, part)], in_sem.at[n]
        )
        for n in range(STEPS)
    ]
    for copy in arriving:
        copy.start()
    leaving = [
        pltpu.make_async_copy(x.at[pl.ds(odd * width, width)], half_hbm, sem.at[0]),
        pltpu.make_async_copy(
            x.at[pl.ds((2 - odd) * width - length, length)], tail_hbm, sem.at[1]
        ),
    ]

    def body(c, carry):
        value = x[c].astype(F32)
        live = 1 - dead_ref[c]
        sums, counts = carry
        weights = [jnp.where(sec_ref[c] == s, live, 0).astype(F32) for s in range(NSEC)]
        return (
            tuple(sums[s] + weights[s] * value for s in range(NSEC)),
            tuple(counts[s] + weights[s] for s in range(NSEC)),
        )

    zero = jnp.zeros((wins, ns), F32)
    carry = ((zero,) * NSEC, (jnp.float32(0),) * NSEC)
    for n, copy in enumerate(arriving):
        copy.wait()
        if n == STEPS - 1:
            for out in leaving:
                out.start()
        carry = lax.fori_loop(n * part, (n + 1) * part, body, carry, unroll=8)
    sums, counts = carry
    for s in range(NSEC):
        out_ref[s, :, :ns] = sums[s]
        out_ref[s, :, ns:] = jnp.zeros((wins, LANE), F32) + counts[s]
    for out in leaving:
        out.wait()


def circulant_kernel(filter_ref, out_ref):
    ns = filter_ref.shape[1]
    for t in range(0, ns, 16):
        block = jnp.broadcast_to(filter_ref[...], (16, ns))
        out_ref[t : t + 16, :] = pltpu.roll(block, t, 1, stride=1, stride_axis=0).astype(BF16)


def segment_factors(places, odd, flag_ref, tot, x, hann, conv, seg, work, copied, first=None):
    common, clean, mass, square, rows, series_all, stage = work
    _, wins, ns = x[0].shape
    chans = sum(piece.shape[0] for piece in x)
    pitch = wins + 1
    size = seg.shape[0]
    half = size // 2
    blocks = ns // half
    jw = blocks * wins
    jpitch = jw + 1
    for copy in copied["first"]:
        copy.wait()
    for g in range(len(tot)):
        for s in range(NSEC):
            common[g * NSEC + s] = tot[g][s, :, :ns] / jnp.maximum(tot[g][s, :, ns : ns + 1], 1.0)
    sign = 1.0 - 2.0 * (lax.broadcasted_iota(jnp.int32, (chans, LANE), 1) % 2).astype(F32)

    for number, (group, base, flags) in enumerate(places):
        piece = x[number]
        length = piece.shape[0]
        base = base[0] + odd * (base[1] - base[0])
        flags = flags[0] + odd * (flags[1] - flags[0])

        def clean_channel(c):
            at = base + c
            flag = flags + c
            live = (1 - flag_ref[0, flag]).astype(F32)
            value = (piece[c].astype(F32) - common[group * NSEC + flag_ref[1, flag]]) * (
                hann[...] * live
            )
            tiles = [value[:, t * LANE : (t + 1) * LANE] for t in range(ns // LANE)]
            row = pl.ds(at * pitch, wins)
            mass[row, :] = sum(tiles[1:], tiles[0])
            square[row, :] = sum([tile * tile for tile in tiles[1:]], tiles[0] * tiles[0])
            for t, tile in enumerate(tiles):
                clean[t, row, :] = tile

        parts = copied["x"][number]
        part = length // len(parts)
        for n, copy in enumerate(parts):
            copy.wait()
            repeat(n * part, (n + 1) * part, clean_channel, 8)
    for copy in copied["tables"]:
        copy.wait()

    for step in range(wins // TOGETHER):
        series = series_all.at[step]
        for i in range(TOGETHER):
            window = pl.ds(step * TOGETHER + i, chans, stride=pitch)
            total = mass[window, :]
            lowest = jnp.sum(total, axis=1, keepdims=True)
            highest = jnp.sum(total * sign, axis=1, keepdims=True)
            power = 0.5 * jnp.sum(square[window, :], axis=1, keepdims=True)
            power = power + (lowest * lowest - highest * highest) * (0.5 / ns)
            level = lax.rsqrt(power + 1e-06)
            for t in range(ns // LANE):
                rows[i * chans : (i + 1) * chans, t * LANE : (t + 1) * LANE] = (
                    clean[t, window, :] * level
                ).astype(BF16)
        for t in range(0, ns, TILE):
            series[half // 2 + t : half // 2 + t + TILE, :] = lax.dot_general(
                conv[t : t + TILE, :], rows[...], NT, preferred_element_type=F32
            ).astype(BF16)
        series[: half // 2, :] = series[ns : ns + half // 2, :]
        series[ns + half // 2 :, :] = series[half // 2 : half, :]

        def place(which, j, value):
            for i in range(TOGETHER):
                at = j * wins + step * TOGETHER + i
                stage[which, pl.ds(at, size, stride=jpitch), :] = value[
                    :, i * chans : (i + 1) * chans
                ]

        for j in range(blocks):
            start = j * half + half // 2
            b = jnp.dot(
                seg[:, :half], series[start : start + half, :], preferred_element_type=F32
            )
            place(1, j, b)

        if first is not None:
            source = first(step, series)
            for j in range(blocks):
                a = jnp.dot(
                    seg[...], source[j * half : j * half + size, :], preferred_element_type=F32
                )
                place(0, j, a)

    def factor(which, k, turn=False):
        real, imag = [
            stage[which, pl.ds((2 * k + part) * jpitch, jw), :] for part in range(2)
        ]
        if turn:
            real, imag = imag, -real
        return jnp.concatenate([real.astype(BF16), imag.astype(BF16)], axis=0)

    def first_factor(k, put):
        width = chans // 2
        for part in range(2):
            value = factor(0, k, part == 1).T
            rows_at = slice(part * width, (part + 1) * width)
            put(1, rows_at, value[:width])
            put(0, rows_at, value[width:])

    return first_factor, lambda k: factor(1, k)


def work_shapes(groups, chans, wins, ns):
    half = LAGS
    rows = 2 * half * (ns // half * wins + 1)
    return [
        pltpu.VMEM((groups * NSEC, wins, ns), F32),
        pltpu.VMEM((ns // LANE, chans * (wins + 1), LANE), F32),
        pltpu.VMEM((chans * (wins + 1), LANE), F32),
        pltpu.VMEM((chans * (wins + 1), LANE), F32),
        pltpu.VMEM((TOGETHER * chans, ns), BF16),
        pltpu.VMEM((wins // TOGETHER, ns + half, TOGETHER * chans), BF16),
        pltpu.VMEM((2, rows, chans), F32),
    ]


def repeat(start, stop, body, together):
    def step(n, _):
        body(n)
        return 0

    lax.fori_loop(start, stop, step, 0, unroll=math.gcd(together, stop - start))


class Choice:
    def __init__(self, odd, sources, target, sem):
        self.options = [
            (odd == side, pltpu.make_async_copy(source, target, sem))
            for side, source in enumerate(sources)
        ]

    def start(self):
        for here, copy in self.options:
            pl.when(here)(copy.start)

    def wait(self):
        for here, copy in self.options:
            pl.when(here)(copy.wait)


def input_copies(odd, first, x, tables_in, sem):
    copied = {"first": [], "x": [], "tables": []}
    used = 0

    def copy(source, target):
        nonlocal used
        if isinstance(source, tuple):
            made = Choice(odd, source, target, sem.at[used])
        else:
            made = pltpu.make_async_copy(source, target, sem.at[used])
        made.start()
        used += 1
        return made

    copied["first"] = [copy(*pair) for pair in first]
    for source, target in x:
        parts = max(target.shape[0] // PART, 1)
        part = target.shape[0] // parts
        rows = [pl.ds(n * part, part) for n in range(parts)]
        copied["x"].append(
            [
                copy(
                    tuple(option.at[here] for option in source)
                    if isinstance(source, tuple)
                    else source.at[here],
                    target.at[here],
                )
                for here in rows
            ]
        )
    copied["tables"] = [copy(*pair) for pair in tables_in]
    return copied


def own_kernel(places, odd_ref, flag_ref, *rest):
    tot_hbm, x_hbm, hann_hbm, conv_hbm, seg_hbm, b_hbm, p_hbm = rest[:7]
    tot, x, hann, conv, seg = rest[7:12]
    work, (b_out, in_sem, out_sem, p_sem) = rest[12:-4], rest[-4:]
    odd = odd_ref[0]
    copied = input_copies(
        odd,
        [(tot_hbm, tot), (hann_hbm, hann)],
        [(x_hbm, x)],
        [(conv_hbm, conv), (seg_hbm, seg)],
        in_sem,
    )
    _, second = segment_factors(
        places, odd, flag_ref, [tot], [x], hann, conv, seg, work, copied
    )

    def put_second(k, stage):
        stage[k] = second(k)

    kept = pltpu.make_async_copy(work[-2], p_hbm, p_sem)
    kept.start()
    send_factor(put_second, b_out, b_hbm, out_sem)
    kept.wait()


def send_factor(factor, stage, target, sem):
    step = stage.shape[0] // STEPS
    copies = []
    for n in range(STEPS):
        part = pl.ds(n * step, step)

        repeat(n * step, (n + 1) * step, lambda k: factor(k, stage), 16)
        copies.append(pltpu.make_async_copy(stage.at[part], target.at[part], sem.at[n]))
        copies[-1].start()
    for copy in copies:
        copy.wait()


def second_kernel(places, odd_ref, flag_ref, *rest):
    tot_hbm, (even_hbm, odd_hbm), rest = rest[:2], (rest[2:4], rest[4:6]), rest[6:]
    halo_hbm, hann_hbm, conv_hbm, seg_hbm, p_hbm, a_hbm, b_hbm = rest[:7]
    tot, x, rest = rest[7:9], rest[9:12], rest[12:]
    hann, conv, seg, own, mixed, a_out, b_out = rest[:7]
    work, (in_sem, p_sem, out_sem) = rest[7:-3], rest[-3:]
    odd = odd_ref[0]
    copied = input_copies(
        odd,
        list(zip(tot_hbm, tot)) + [(hann_hbm, hann)],
        list(zip(zip(even_hbm, odd_hbm), x)) + [(halo_hbm, x[2])],
        [(conv_hbm, conv), (seg_hbm, seg)],
        in_sem,
    )
    kept = pltpu.make_async_copy(p_hbm, own, p_sem)
    kept.start()
    copied["tables"].append(kept)
    chans = b_out.shape[2]
    lane = lax.broadcasted_iota(jnp.int32, (1, chans), 1)

    def first(step, series):
        @pl.when(odd == 1)
        def _():
            mixed[...] = series[...]

        @pl.when(odd == 0)
        def _():
            for i in range(TOGETHER):
                columns = slice(i * chans, (i + 1) * chans)
                value = own[step, :, columns]
                turned = jnp.concatenate([value[:, chans // 2 :], value[:, : chans // 2]], axis=1)
                mixed[:, columns] = jnp.where(lane < chans // 2, series[:, columns], turned)

        return mixed

    first_factor, second_factor = segment_factors(
        places, odd, flag_ref, tot, x, hann, conv, seg, work, copied, first
    )

    def both_factors(k, stage):
        def put(group, rows, value):
            a_out[k, group, rows] = value

        first_factor(k, put)
        stage[k] = second_factor(k)

    step = b_out.shape[0] // STEPS
    copies = []
    for n in range(STEPS):
        part = pl.ds(n * step, step)

        repeat(n * step, (n + 1) * step, lambda k: both_factors(k, b_out), 16)
        for m, (source, target) in enumerate(((a_out, a_hbm), (b_out, b_hbm))):
            copies.append(
                pltpu.make_async_copy(source.at[part], target.at[part], out_sem.at[2 * n + m])
            )
            copies[-1].start()
    for copy in copies:
        copy.wait()


def segments(places, side, flags, totals, pieces, series, hann, conv, seg):
    chans = LANE
    _, wins, ns = pieces[0].shape
    size = seg.shape[0]
    half = size // 2
    depth = ns // half * wins * 2
    smem = pl.BlockSpec(memory_space=pltpu.SMEM)
    anywhere = pl.BlockSpec(memory_space=pl.ANY)
    b_shape = jax.ShapeDtypeStruct((half, depth, chans), BF16)
    p_shape = jax.ShapeDtypeStruct((wins // TOGETHER, ns + half, TOGETHER * chans), BF16)
    a_shape = jax.ShapeDtypeStruct((half, 2, chans, depth), BF16)
    scratch = lambda *values: [pltpu.VMEM(value.shape, value.dtype) for value in values]
    operands = list(totals) + list(pieces) + [hann, conv, seg]
    count = len(operands) + chans // PART
    if series is None:
        kernel, out = own_kernel, [b_shape, p_shape]
        held = scratch(*operands)
        last = scratch(b_shape) + [
            pltpu.SemaphoreType.DMA((count,)),
            pltpu.SemaphoreType.DMA((STEPS,)),
            pltpu.SemaphoreType.DMA,
        ]
    else:
        kernel, out = second_kernel, [a_shape, b_shape]
        held = scratch(*totals, pieces[0], pieces[1], pieces[4], hann, conv, seg, series)
        held += [pltpu.VMEM(p_shape.shape[1:], BF16)] + scratch(a_shape, b_shape)
        last = [
            pltpu.SemaphoreType.DMA((count,)),
            pltpu.SemaphoreType.DMA,
            pltpu.SemaphoreType.DMA((2 * STEPS,)),
        ]
        operands.append(series)
    return pl.pallas_call(
        functools.partial(kernel, places),
        out_shape=out,
        in_specs=[smem] * 2 + [anywhere] * len(operands),
        out_specs=[anywhere] * 2,
        scratch_shapes=held + work_shapes(len(totals), chans, wins, ns) + last,
        compiler_params=pltpu.CompilerParams(vmem_limit_bytes=VMEM),
        cost_estimate=pl.CostEstimate(
            flops=2 * wins * chans * ns * (ns + 3 * size),
            bytes_accessed=16 * 1024 * 1024,
            transcendentals=0,
        ),
    )(side, flags, *operands)


def stack_kernel(places, scale, shares, me_ref, flag_ref, *rest):
    even_hbm, odd_hbm, late_hbm, rest = rest[:2], rest[2:4], rest[4], rest[5:]
    tot_hbm, hann_hbm, conv_hbm, seg_hbm, lag_hbm = rest[:5]
    a_hbm, b0_hbm, b2_hbm, rest = *rest[5:8], rest[8:]
    outs, rest = rest[:shares], rest[shares:]
    x, rest = rest[:3], rest[3:]
    tot, hann, conv, seg, lag, a, b0, b2 = rest[:8]
    work, (b3, one, in_sem, late_sem) = rest[8:-4], rest[-4:]
    me = me_ref[0]
    odd = lax.rem(me, 2)
    copied = input_copies(
        odd,
        [(tot_hbm, tot), (hann_hbm, hann)],
        list(zip(zip(even_hbm, odd_hbm), x)) + [(late_hbm, x[2])],
        [(conv_hbm, conv), (seg_hbm, seg), (lag_hbm, lag)],
        in_sem,
    )
    late = [
        pltpu.make_async_copy(source, target, late_sem.at[n])
        for n, (source, target) in enumerate(((b0_hbm, b0), (b2_hbm, b2), (a_hbm, a)))
    ]
    for copy in late:
        copy.start()
    bins, depth, chans = b0.shape
    width = chans // 2
    nfr = lag.shape[1]
    pitch = nfr + 1
    cross = work[-1]

    _, second_factor = segment_factors(
        places, odd, flag_ref, [tot], x, hann, conv, seg, work, copied
    )

    def second(k):
        b3[k] = second_factor(k)

    repeat(0, bins, second, 16)
    for copy in late:
        copy.wait()

    lane = lax.broadcasted_iota(jnp.int32, (1, chans), 1)
    low, high = [jnp.where((lane < width) == (g == 0), 1.0, 0.0).astype(BF16) for g in range(2)]

    def bins_with(near, far):
        def one_bin(k):
            inner = near[k] * low + b3[k] * high if near is not b3 else b3[k]
            right = jnp.concatenate(
                [
                    jnp.concatenate([b0[k], b2[k] * high], axis=1),
                    jnp.concatenate([inner, far[k] * low], axis=1),
                ],
                axis=0,
            )
            left = jnp.concatenate([a[k, 0], a[k, 1]], axis=1)
            value = jnp.dot(left, right, preferred_element_type=F32)
            for p in range(2):
                for t in range(2):
                    cross[t, pl.ds(2 * k + p, width, stride=pitch), :] = value[
                        p * width : (p + 1) * width, t * chans : (t + 1) * chans
                    ]

        repeat(0, bins, one_bin, 16)

    pl.when(odd == 0)(lambda: bins_with(b2, b3))
    pl.when(odd == 1)(lambda: bins_with(b3, b2))

    row = lax.broadcasted_iota(jnp.int32, one.shape[1:], 0)
    column = lax.broadcasted_iota(jnp.int32, one.shape[1:], 1)
    turned = jnp.where(row < width, row + chans, row - width)
    place = row + (turned - row) * odd
    for t in range(2):
        here = column + t * chans
        found = (place == here) | ((here >= chans + width) & (place == here - width))
        one[t] = jnp.where(found, 1.0, 0.0)
    share = OFFS // shares

    def one_channel(c):
        value = jnp.concatenate(
            [cross[t, pl.ds(c * pitch, nfr), :] for t in range(2)], axis=1
        ).astype(BF16)
        starts = [c + 1 + share * (me ^ d) for d in range(shares)]
        pick = jnp.concatenate(
            [
                jnp.concatenate([one[t, pl.ds(start, share), :] for start in starts], axis=0)
                for t in range(2)
            ],
            axis=1,
        ).astype(BF16)
        lagged = jnp.dot(lag[...], value, preferred_element_type=F32) * scale
        band = lax.dot_general(pick, lagged.astype(BF16), NT, preferred_element_type=F32)
        for d, out in enumerate(outs):
            out[c] = band[d * share : (d + 1) * share, :].astype(BF16)

    repeat(0, width, one_channel, 8)


def stacks(places, shares, scale, me, flags, total, pieces, hann, conv, seg, lag, a, b0, b2):
    bins, depth, chans = b0.shape
    width = chans // 2
    _, wins, ns = pieces[0].shape
    nlag, nfr = lag.shape
    smem = pl.BlockSpec(memory_space=pltpu.SMEM)
    vmem = pl.BlockSpec(memory_space=pltpu.VMEM)
    anywhere = pl.BlockSpec(memory_space=pl.ANY)
    tables_in = [total, hann, conv, seg, lag, a, b0, b2]
    operands = [*pieces, *tables_in]
    held = [pieces[0], pieces[1], pieces[4], *tables_in]
    return pl.pallas_call(
        functools.partial(stack_kernel, places, scale, shares),
        out_shape=[jax.ShapeDtypeStruct((width, OFFS // shares, nlag), BF16)] * shares,
        in_specs=[smem] * 2 + [anywhere] * len(operands),
        out_specs=[vmem] * shares,
        scratch_shapes=[pltpu.VMEM(value.shape, value.dtype) for value in held]
        + work_shapes(1, chans, wins, ns)
        + [
            pltpu.VMEM(b0.shape, BF16),
            pltpu.VMEM((2, chans + width, chans), F32),
            pltpu.SemaphoreType.DMA((8 + chans // PART,)),
            pltpu.SemaphoreType.DMA((3,)),
        ],
        compiler_params=pltpu.CompilerParams(vmem_limit_bytes=VMEM),
        cost_estimate=pl.CostEstimate(
            flops=2 * width * bins * 4 * (2 * depth * chans + 2 * OFFS * chans),
            bytes_accessed=20 * 1024 * 1024,
            transcendentals=0,
        ),
    )(me, flags, *operands)


def add_over(value, axis, beside):
    count = lax.axis_size(axis)
    if count & (count - 1):
        return lax.psum(value, axis), beside
    bit = 1
    while bit < count:
        steps = [bit] if bit == 1 or 2 * bit == count else [bit, 2 * bit, 3 * bit]
        arrived = [lax.ppermute(value, axis, [(i, i ^ s) for i in range(count)]) for s in steps]
        bit *= 1 + len(steps)
        if bit == count:
            arrived, beside = lax.optimization_barrier((arrived, beside))
        value = sum(arrived, value)
    return value, beside


def shards(samples, band_gain, dead_flags, section_ids):
    chans, wins, ns = samples.shape
    nf = ns // 2
    width = chans // 2
    blocks = lax.axis_size("fibre")
    groups = lax.axis_size("tm")
    me = lax.axis_index("tm")
    odd = me % 2
    window, waves, seg, lag = tables(ns, nf)
    waves, seg, lag = jnp.asarray(waves), jnp.asarray(seg), jnp.asarray(lag)
    hann = jnp.asarray(window[None, :])
    response = jnp.sum(band_gain[:, None] * waves, axis=0, keepdims=True)
    conv = pl.pallas_call(
        circulant_kernel,
        out_shape=jax.ShapeDtypeStruct((ns, ns), BF16),
        compiler_params=pltpu.CompilerParams(vmem_limit_bytes=VMEM),
        cost_estimate=pl.CostEstimate(flops=1, bytes_accessed=1, transcendentals=0),
    )(response)
    swap = [(z, z ^ 1) for z in range(groups)]
    both = ("fibre", "tm")
    halo_pairs = [
        (b * groups + z, (b + (1 if z % 2 else -1)) % blocks * groups + z)
        for b in range(blocks)
        for z in range(groups)
    ]

    head = width * 5 // 8

    their_head = lax.ppermute(
        lax.dynamic_slice_in_dim(samples, (1 - odd) * width, head, 0), "tm", swap
    )
    flags = jnp.stack([dead_flags, section_ids])
    halo_flags = lax.ppermute(
        lax.dynamic_slice_in_dim(flags, odd * width, width, 1), both, halo_pairs
    )
    smem = pl.BlockSpec(memory_space=pltpu.SMEM)
    anywhere = pl.BlockSpec(memory_space=pl.ANY)
    sums, own_half, tail = pl.pallas_call(
        section_sums,
        out_shape=[
            jax.ShapeDtypeStruct((NSEC, wins, ns + LANE), F32),
            jax.ShapeDtypeStruct((width, wins, ns), BF16),
            jax.ShapeDtypeStruct((width - head, wins, ns), BF16),
        ],
        in_specs=[smem] * 3 + [anywhere],
        out_specs=[pl.BlockSpec(memory_space=pltpu.VMEM), anywhere, anywhere],
        scratch_shapes=[
            pltpu.VMEM(samples.shape, BF16),
            pltpu.SemaphoreType.DMA((STEPS,)),
            pltpu.SemaphoreType.DMA((2,)),
        ],
        compiler_params=pltpu.CompilerParams(vmem_limit_bytes=VMEM),
        cost_estimate=pl.CostEstimate(flops=1, bytes_accessed=1, transcendentals=0),
    )(odd[None], dead_flags, section_ids, samples)
    total, their_head = add_over(sums, "fibre", their_head)
    halo_source, conv = lax.optimization_barrier((own_half, conv))
    halo = lax.ppermute(halo_source, both, halo_pairs)
    total, halo_flags, conv, own_half, tail = lax.optimization_barrier(
        (total, halo_flags, conv, own_half, tail)
    )
    their_total = lax.ppermute(total, "tm", swap)
    their_tail = lax.ppermute(tail, "tm", swap)
    their_second = lax.ppermute(own_half, "tm", swap)
    ready = (total, their_total, their_head, flags, hann, conv, seg, lag)
    ready = lax.optimization_barrier(ready)
    total, their_total, their_head, flags, hann, conv, seg, lag = ready
    halo_head = lax.ppermute(their_head, both, halo_pairs)

    side = odd[None]
    parts = (hann, conv, seg)
    every = jnp.concatenate([flags, halo_flags], axis=1)
    b0, series = segments(((0, (0, 0), (0, 0)),), side, flags, (total,), (samples,), None, *parts)
    b0, forward = lax.optimization_barrier((b0, their_tail))
    halo_tail = lax.ppermute(forward, both, halo_pairs)
    a, b2 = segments(
        (
            (1, (0, 0), (0, chans)),
            (1, (head, head), (head, chans + head)),
            (0, (width, width), (chans, chans)),
        ),
        side,
        every,
        (total, their_total),
        (their_head, their_tail, halo_head, halo_tail, halo),
        series,
        *parts,
    )
    scale = 2.0 / ns / LAGS / math.sqrt(nf * wins * groups)
    found = stacks(
        (
            (0, (0, width), (chans, width)),
            (0, (head, width + head), (chans + head, width + head)),
            (0, (width, 0), (width, 0)),
        ),
        groups,
        scale,
        me[None],
        every,
        their_total,
        (halo_head, halo_tail, their_head, their_tail, their_second),
        *(hann, conv, seg, lag),
        *(a, b0, b2),
    )
    arrived = {}
    for d in reversed(range(groups)):
        pairs = [
            (b * groups + z, (b - z % 2) % blocks * groups + (z ^ d))
            for b in range(blocks)
            for z in range(groups)
        ]
        arrived[d] = lax.ppermute(found[d], both, pairs)
    arrived = [arrived[d].astype(F32) for d in range(groups)]
    same = sum(arrived[2::2], arrived[0])
    other = sum(arrived[3::2], arrived[1])
    return jnp.concatenate(
        [jnp.where(odd == 0, same, other), jnp.where(odd == 0, other, same)], axis=0
    )


def solution(mesh):
    in_specs = (P("fibre", "tm", None), P(), P("fibre"), P("fibre"))
    out_specs = P("fibre", "tm", None)
    return jax.shard_map(shards, mesh=mesh, in_specs=in_specs, out_specs=out_specs, check_vma=False)
```

```python
import functools
import math

import jax
import jax.numpy as jnp
import ml_dtypes
import numpy as np
from jax import lax
from jax.experimental import pallas as pl
from jax.experimental.pallas import tpu as pltpu
from jax.sharding import PartitionSpec as P

OFFS = 128
LAGS = 128
NSEC = 2
LANE = 128
PART = 16
TILE = 256
STEPS = 4
TOGETHER = 4
VMEM = 63 * 1024 * 1024
NT = (((1,), (1,)), ((), ()))
F32 = jnp.float32
BF16 = jnp.bfloat16


def tables(ns, nf):
    tick = np.arange(ns)
    freq = np.arange(nf)
    window = 0.5 - 0.5 * np.cos(tick * (2.0 * math.pi / ns))
    waves = np.cos((freq[:, None] * tick[None, :] % ns) * (2.0 * math.pi / ns))
    waves[0] *= math.sqrt(0.5)
    size = 2 * LAGS
    bins = np.arange(size // 2)
    turn = math.pi / size * ((2 * bins[:, None] + 1) * np.arange(size)[None, :] % (2 * size))
    segment = np.stack([np.cos(turn), -np.sin(turn)], axis=1).reshape(size, size)
    lag = np.stack([np.cos(turn), -np.sin(turn)], axis=1).reshape(size, size)[:, :LAGS].T
    cast = lambda a: a.astype(np.float32).astype(ml_dtypes.bfloat16)
    return window.astype(np.float32), waves.astype(np.float32), cast(segment), cast(lag)


def section_sums(odd_ref, dead_ref, sec_ref, x_hbm, out_ref, half_hbm, tail_hbm, x, in_sem, sem):
    chans, wins, ns = x.shape
    width, length = half_hbm.shape[0], tail_hbm.shape[0]
    odd = odd_ref[0]
    part = chans // STEPS
    arriving = [
        pltpu.make_async_copy(
            x_hbm.at[pl.ds(n * part, part)], x.at[pl.ds(n * part, part)], in_sem.at[n]
        )
        for n in range(STEPS)
    ]
    for copy in arriving:
        copy.start()
    leaving = [
        pltpu.make_async_copy(x.at[pl.ds(odd * width, width)], half_hbm, sem.at[0]),
        pltpu.make_async_copy(
            x.at[pl.ds((2 - odd) * width - length, length)], tail_hbm, sem.at[1]
        ),
    ]

    def body(c, carry):
        value = x[c].astype(F32)
        live = 1 - dead_ref[c]
        sums, counts = carry
        weights = [jnp.where(sec_ref[c] == s, live, 0).astype(F32) for s in range(NSEC)]
        return (
            tuple(sums[s] + weights[s] * value for s in range(NSEC)),
            tuple(counts[s] + weights[s] for s in range(NSEC)),
        )

    zero = jnp.zeros((wins, ns), F32)
    carry = ((zero,) * NSEC, (jnp.float32(0),) * NSEC)
    for n, copy in enumerate(arriving):
        copy.wait()
        if n == STEPS - 1:
            for out in leaving:
                out.start()
        carry = lax.fori_loop(n * part, (n + 1) * part, body, carry, unroll=8)
    sums, counts = carry
    for s in range(NSEC):
        out_ref[s, :, :ns] = sums[s]
        out_ref[s, :, ns:] = jnp.zeros((wins, LANE), F32) + counts[s]
    for out in leaving:
        out.wait()


def circulant_kernel(filter_ref, out_ref):
    ns = filter_ref.shape[1]
    for t in range(0, TILE, 16):
        block = jnp.broadcast_to(filter_ref[...], (16, ns))
        out_ref[t : t + 16, :] = pltpu.roll(block, t, 1, stride=1, stride_axis=0).astype(BF16)


def segment_factors(places, odd, flag_ref, tot, x, hann, conv, seg, work, copied, first=None):
    common, clean, mass, square, rows, series_all, stage = work
    _, wins, ns = x[0].shape
    chans = sum(piece.shape[0] for piece in x)
    pitch = wins + 1
    size = seg.shape[0]
    half = size // 2
    blocks = ns // half
    jw = blocks * wins
    jpitch = jw + 1
    for copy in copied["first"]:
        copy.wait()
    for g in range(len(tot)):
        for s in range(NSEC):
            common[g * NSEC + s] = tot[g][s, :, :ns] / jnp.maximum(tot[g][s, :, ns : ns + 1], 1.0)
    sign = 1.0 - 2.0 * (lax.broadcasted_iota(jnp.int32, (chans, LANE), 1) % 2).astype(F32)

    for number, (group, base, flags) in enumerate(places):
        piece = x[number]
        length = piece.shape[0]
        base = base[0] + odd * (base[1] - base[0])
        flags = flags[0] + odd * (flags[1] - flags[0])

        def clean_channel(c):
            at = base + c
            flag = flags + c
            live = (1 - flag_ref[0, flag]).astype(F32)
            value = (piece[c].astype(F32) - common[group * NSEC + flag_ref[1, flag]]) * (
                hann[...] * live
            )
            tiles = [value[:, t * LANE : (t + 1) * LANE] for t in range(ns // LANE)]
            row = pl.ds(at * pitch, wins)
            mass[row, :] = sum(tiles[1:], tiles[0])
            square[row, :] = sum([tile * tile for tile in tiles[1:]], tiles[0] * tiles[0])
            for t, tile in enumerate(tiles):
                clean[t, row, :] = tile

        parts = copied["x"][number]
        part = length // len(parts)
        for n, copy in enumerate(parts):
            copy.wait()
            repeat(n * part, (n + 1) * part, clean_channel, 8)
    for copy in copied["tables"]:
        copy.wait()

    for step in range(wins // TOGETHER):
        series = series_all.at[step]
        for i in range(TOGETHER):
            window = pl.ds(step * TOGETHER + i, chans, stride=pitch)
            total = mass[window, :]
            lowest = jnp.sum(total, axis=1, keepdims=True)
            highest = jnp.sum(total * sign, axis=1, keepdims=True)
            power = 0.5 * jnp.sum(square[window, :], axis=1, keepdims=True)
            power = power + (lowest * lowest - highest * highest) * (0.5 / ns)
            level = lax.rsqrt(power + 1e-06)
            for t in range(ns // LANE):
                rows[i * chans : (i + 1) * chans, t * LANE : (t + 1) * LANE] = (
                    clean[t, window, :] * level
                ).astype(BF16)
        for t in range(0, ns, TILE):
            turned = jnp.concatenate([conv[:, ns - t :], conv[:, : ns - t]], axis=1) if t else conv[...]
            series[half // 2 + t : half // 2 + t + TILE, :] = lax.dot_general(
                turned, rows[...], NT, preferred_element_type=F32
            ).astype(BF16)
        series[: half // 2, :] = series[ns : ns + half // 2, :]
        series[ns + half // 2 :, :] = series[half // 2 : half, :]

        def place(which, j, value):
            for i in range(TOGETHER):
                at = j * wins + step * TOGETHER + i
                stage[which, pl.ds(at, size, stride=jpitch), :] = value[
                    :, i * chans : (i + 1) * chans
                ]

        for j in range(blocks):
            start = j * half + half // 2
            b = jnp.dot(
                seg[:, :half], series[start : start + half, :], preferred_element_type=F32
            )
            place(1, j, b)

        if first is not None:
            source = first(step, series)
            for j in range(blocks):
                a = jnp.dot(
                    seg[...], source[j * half : j * half + size, :], preferred_element_type=F32
                )
                place(0, j, a)

    def parts(which, k):
        return [
            stage[which, pl.ds((2 * k + part) * jpitch, jw), :].astype(BF16) for part in range(2)
        ]

    lower = lax.broadcasted_iota(jnp.int32, (1, chans), 1) < chans // 2

    def first_factor(k):
        real, imag = parts(0, k)
        return jnp.concatenate(
            [jnp.where(lower, imag, real), jnp.where(lower, real, imag)], axis=0
        ).T

    return first_factor, lambda k: jnp.concatenate(parts(1, k), axis=0)


def work_shapes(groups, chans, wins, ns):
    half = LAGS
    rows = 2 * half * (ns // half * wins + 1)
    return [
        pltpu.VMEM((groups * NSEC, wins, ns), F32),
        pltpu.VMEM((ns // LANE, chans * (wins + 1), LANE), F32),
        pltpu.VMEM((chans * (wins + 1), LANE), F32),
        pltpu.VMEM((chans * (wins + 1), LANE), F32),
        pltpu.VMEM((TOGETHER * chans, ns), BF16),
        pltpu.VMEM((wins // TOGETHER, ns + half, TOGETHER * chans), BF16),
        pltpu.VMEM((2, rows, chans), F32),
    ]


def repeat(start, stop, body, together):
    def step(n, _):
        body(n)
        return 0

    lax.fori_loop(start, stop, step, 0, unroll=math.gcd(together, stop - start))


class Choice:
    def __init__(self, odd, sources, target, sem):
        self.options = [
            (odd == side, pltpu.make_async_copy(source, target, sem))
            for side, source in enumerate(sources)
        ]

    def start(self):
        for here, copy in self.options:
            pl.when(here)(copy.start)

    def wait(self):
        for here, copy in self.options:
            pl.when(here)(copy.wait)


def input_copies(odd, first, x, tables_in, sem):
    copied = {"first": [], "x": [], "tables": []}
    used = 0

    def copy(source, target):
        nonlocal used
        if isinstance(source, tuple):
            made = Choice(odd, source, target, sem.at[used])
        else:
            made = pltpu.make_async_copy(source, target, sem.at[used])
        made.start()
        used += 1
        return made

    copied["first"] = [copy(*pair) for pair in first]
    for source, target in x:
        parts = max(target.shape[0] // PART, 1)
        part = target.shape[0] // parts
        rows = [pl.ds(n * part, part) for n in range(parts)]
        copied["x"].append(
            [
                copy(
                    tuple(option.at[here] for option in source)
                    if isinstance(source, tuple)
                    else source.at[here],
                    target.at[here],
                )
                for here in rows
            ]
        )
    copied["tables"] = [copy(*pair) for pair in tables_in]
    return copied


def own_kernel(places, odd_ref, flag_ref, *rest):
    tot_hbm, x_hbm, hann_hbm, conv_hbm, seg_hbm, b_hbm, p_hbm = rest[:7]
    tot, x, hann, conv, seg = rest[7:12]
    work, (b_out, in_sem, out_sem, p_sem) = rest[12:-4], rest[-4:]
    odd = odd_ref[0]
    copied = input_copies(
        odd,
        [(tot_hbm, tot), (hann_hbm, hann)],
        [(x_hbm, x)],
        [(conv_hbm, conv), (seg_hbm, seg)],
        in_sem,
    )
    _, second = segment_factors(
        places, odd, flag_ref, [tot], [x], hann, conv, seg, work, copied
    )

    def put_second(k, stage):
        stage[k] = second(k)

    kept = pltpu.make_async_copy(work[-2], p_hbm, p_sem)
    kept.start()
    send_factor(put_second, b_out, b_hbm, out_sem)
    kept.wait()


def send_factor(factor, stage, target, sem):
    step = stage.shape[0] // STEPS
    copies = []
    for n in range(STEPS):
        part = pl.ds(n * step, step)

        repeat(n * step, (n + 1) * step, lambda k: factor(k, stage), 32)
        copies.append(pltpu.make_async_copy(stage.at[part], target.at[part], sem.at[n]))
        copies[-1].start()
    for copy in copies:
        copy.wait()


def second_kernel(places, odd_ref, flag_ref, *rest):
    tot_hbm, (even_hbm, odd_hbm), rest = rest[:2], (rest[2:4], rest[4:6]), rest[6:]
    halo_hbm, hann_hbm, conv_hbm, seg_hbm, p_hbm, a_hbm, b_hbm = rest[:7]
    tot, x, rest = rest[7:9], rest[9:12], rest[12:]
    hann, conv, seg, own, mixed, a_out, b_out = rest[:7]
    work, (in_sem, p_sem, out_sem) = rest[7:-3], rest[-3:]
    odd = odd_ref[0]
    copied = input_copies(
        odd,
        list(zip(tot_hbm, tot)) + [(hann_hbm, hann)],
        list(zip(zip(even_hbm, odd_hbm), x)) + [(halo_hbm, x[2])],
        [(conv_hbm, conv), (seg_hbm, seg)],
        in_sem,
    )
    kept = pltpu.make_async_copy(p_hbm, own, p_sem)
    kept.start()
    copied["tables"].append(kept)
    chans = b_out.shape[2]
    lane = lax.broadcasted_iota(jnp.int32, (1, chans), 1)

    def first(step, series):
        @pl.when(odd == 1)
        def _():
            mixed[...] = series[...]

        @pl.when(odd == 0)
        def _():
            for i in range(TOGETHER):
                columns = slice(i * chans, (i + 1) * chans)
                value = own[step, :, columns]
                turned = jnp.concatenate([value[:, chans // 2 :], value[:, : chans // 2]], axis=1)
                mixed[:, columns] = jnp.where(lane < chans // 2, series[:, columns], turned)

        return mixed

    first_factor, second_factor = segment_factors(
        places, odd, flag_ref, tot, x, hann, conv, seg, work, copied, first
    )

    def both_factors(k, stage):
        value = first_factor(k)
        width = value.shape[0] // 2
        a_out[k, 1] = value[:width]
        a_out[k, 0] = value[width:]
        stage[k] = second_factor(k)

    step = b_out.shape[0] // STEPS
    copies = []
    for n in range(STEPS):
        part = pl.ds(n * step, step)

        repeat(n * step, (n + 1) * step, lambda k: both_factors(k, b_out), 16)
        for m, (source, target) in enumerate(((a_out, a_hbm), (b_out, b_hbm))):
            copies.append(
                pltpu.make_async_copy(source.at[part], target.at[part], out_sem.at[2 * n + m])
            )
            copies[-1].start()
    for copy in copies:
        copy.wait()


def segments(places, side, flags, totals, pieces, series, hann, conv, seg):
    chans = LANE
    _, wins, ns = pieces[0].shape
    size = seg.shape[0]
    half = size // 2
    depth = ns // half * wins * 2
    smem = pl.BlockSpec(memory_space=pltpu.SMEM)
    anywhere = pl.BlockSpec(memory_space=pl.ANY)
    b_shape = jax.ShapeDtypeStruct((half, depth, chans), BF16)
    p_shape = jax.ShapeDtypeStruct((wins // TOGETHER, ns + half, TOGETHER * chans), BF16)
    a_shape = jax.ShapeDtypeStruct((half, 2, chans // 2, depth), BF16)
    scratch = lambda *values: [pltpu.VMEM(value.shape, value.dtype) for value in values]
    operands = list(totals) + list(pieces) + [hann, conv, seg]
    count = len(operands) + chans // PART
    if series is None:
        kernel, out = own_kernel, [b_shape, p_shape]
        held = scratch(*operands)
        last = scratch(b_shape) + [
            pltpu.SemaphoreType.DMA((count,)),
            pltpu.SemaphoreType.DMA((STEPS,)),
            pltpu.SemaphoreType.DMA,
        ]
    else:
        kernel, out = second_kernel, [a_shape, b_shape]
        held = scratch(*totals, pieces[0], pieces[1], pieces[4], hann, conv, seg, series)
        held += [pltpu.VMEM(p_shape.shape[1:], BF16)] + scratch(a_shape, b_shape)
        last = [
            pltpu.SemaphoreType.DMA((count,)),
            pltpu.SemaphoreType.DMA,
            pltpu.SemaphoreType.DMA((2 * STEPS,)),
        ]
        operands.append(series)
    return pl.pallas_call(
        functools.partial(kernel, places),
        out_shape=out,
        in_specs=[smem] * 2 + [anywhere] * len(operands),
        out_specs=[anywhere] * 2,
        scratch_shapes=held + work_shapes(len(totals), chans, wins, ns) + last,
        compiler_params=pltpu.CompilerParams(vmem_limit_bytes=VMEM),
        cost_estimate=pl.CostEstimate(
            flops=2 * wins * chans * ns * (ns + 3 * size),
            bytes_accessed=16 * 1024 * 1024,
            transcendentals=0,
        ),
    )(side, flags, *operands)


def stack_kernel(places, scale, shares, me_ref, flag_ref, *rest):
    even_hbm, odd_hbm, late_hbm, rest = rest[:2], rest[2:4], rest[4], rest[5:]
    tot_hbm, hann_hbm, conv_hbm, seg_hbm, lag_hbm = rest[:5]
    a_hbm, b0_hbm, b2_hbm, rest = *rest[5:8], rest[8:]
    outs, rest = rest[:shares], rest[shares:]
    x, rest = rest[:3], rest[3:]
    tot, hann, conv, seg, lag, a, b0, b2 = rest[:8]
    work, (b3, one, in_sem, late_sem) = rest[8:-4], rest[-4:]
    me = me_ref[0]
    odd = lax.rem(me, 2)
    copied = input_copies(
        odd,
        [(tot_hbm, tot), (hann_hbm, hann)],
        list(zip(zip(even_hbm, odd_hbm), x)) + [(late_hbm, x[2])],
        [(conv_hbm, conv), (seg_hbm, seg), (lag_hbm, lag)],
        in_sem,
    )
    late = [
        pltpu.make_async_copy(source, target, late_sem.at[n])
        for n, (source, target) in enumerate(((b0_hbm, b0), (b2_hbm, b2), (a_hbm, a)))
    ]
    for copy in late:
        copy.start()
    bins, depth, chans = b0.shape
    width = chans // 2
    nfr = lag.shape[1]
    pitch = nfr + 1
    cross = work[-1]

    _, second_factor = segment_factors(
        places, odd, flag_ref, [tot], x, hann, conv, seg, work, copied
    )

    def second(k):
        b3[k] = second_factor(k)

    repeat(0, bins, second, 32)
    for copy in late:
        copy.wait()

    lane = lax.broadcasted_iota(jnp.int32, (1, chans), 1)
    low, high = [jnp.where((lane < width) == (g == 0), 1.0, 0.0).astype(BF16) for g in range(2)]

    lower = lane < width

    def bins_with(near, far):
        def one_bin(k):
            inner = near[k] * low + b3[k] * high if near is not b3 else b3[k]
            own = jnp.concatenate([b0[k], b2[k] * high], axis=1)
            theirs = jnp.concatenate([inner, far[k] * low], axis=1)
            part = depth // 2
            right = jnp.concatenate([own[:part], theirs[:part], theirs[part:], own[part:]], axis=0)
            real = jnp.where(lower, a[k, 0], a[k, 1])
            imag = jnp.where(lower, a[k, 1], a[k, 0])
            turn = lambda v: jnp.concatenate([v[:, part:], v[:, :part]], axis=1)
            left = jnp.concatenate(
                [
                    jnp.concatenate([real, imag], axis=1),
                    jnp.concatenate([turn(imag), -turn(real)], axis=1),
                ],
                axis=0,
            )
            value = jnp.dot(left, right, preferred_element_type=F32)
            for p in range(2):
                for t in range(2):
                    cross[t, pl.ds(2 * k + p, width, stride=pitch), :] = value[
                        p * width : (p + 1) * width, t * chans : (t + 1) * chans
                    ]

        repeat(0, bins, one_bin, 32)

    pl.when(odd == 0)(lambda: bins_with(b2, b3))
    pl.when(odd == 1)(lambda: bins_with(b3, b2))

    row = lax.broadcasted_iota(jnp.int32, one.shape[1:], 0)
    column = lax.broadcasted_iota(jnp.int32, one.shape[1:], 1)
    turned = jnp.where(row < width, row + chans, row - width)
    place = row + (turned - row) * odd
    for t in range(2):
        here = column + t * chans
        found = (place == here) | ((here >= chans + width) & (place == here - width))
        one[t] = jnp.where(found, 1.0, 0.0)
    share = OFFS // shares

    def one_channel(c):
        value = jnp.concatenate(
            [cross[t, pl.ds(c * pitch, nfr), :] for t in range(2)], axis=1
        ).astype(BF16)
        starts = [c + 1 + share * (me ^ d) for d in range(shares)]
        pick = jnp.concatenate(
            [
                jnp.concatenate([one[t, pl.ds(start, share), :] for start in starts], axis=0)
                for t in range(2)
            ],
            axis=1,
        ).astype(BF16)
        lagged = jnp.dot(lag[...], value, preferred_element_type=F32) * scale
        band = lax.dot_general(pick, lagged.astype(BF16), NT, preferred_element_type=F32)
        for d, out in enumerate(outs):
            out[c] = band[d * share : (d + 1) * share, :].astype(BF16)

    repeat(0, width, one_channel, 16)


def stacks(places, shares, scale, me, flags, total, pieces, hann, conv, seg, lag, a, b0, b2):
    bins, depth, chans = b0.shape
    width = chans // 2
    _, wins, ns = pieces[0].shape
    nlag, nfr = lag.shape
    smem = pl.BlockSpec(memory_space=pltpu.SMEM)
    vmem = pl.BlockSpec(memory_space=pltpu.VMEM)
    anywhere = pl.BlockSpec(memory_space=pl.ANY)
    tables_in = [total, hann, conv, seg, lag, a, b0, b2]
    operands = [*pieces, *tables_in]
    held = [pieces[0], pieces[1], pieces[4], *tables_in]
    return pl.pallas_call(
        functools.partial(stack_kernel, places, scale, shares),
        out_shape=[jax.ShapeDtypeStruct((width, OFFS // shares, nlag), BF16)] * shares,
        in_specs=[smem] * 2 + [anywhere] * len(operands),
        out_specs=[vmem] * shares,
        scratch_shapes=[pltpu.VMEM(value.shape, value.dtype) for value in held]
        + work_shapes(1, chans, wins, ns)
        + [
            pltpu.VMEM(b0.shape, BF16),
            pltpu.VMEM((2, chans + width, chans), F32),
            pltpu.SemaphoreType.DMA((8 + chans // PART,)),
            pltpu.SemaphoreType.DMA((3,)),
        ],
        compiler_params=pltpu.CompilerParams(vmem_limit_bytes=VMEM),
        cost_estimate=pl.CostEstimate(
            flops=2 * width * bins * 4 * (2 * depth * chans + 2 * OFFS * chans),
            bytes_accessed=20 * 1024 * 1024,
            transcendentals=0,
        ),
    )(me, flags, *operands)


def add_over(value, axis, beside):
    count = lax.axis_size(axis)
    if count & (count - 1):
        return lax.psum(value, axis), beside
    bit = 1
    while bit < count:
        steps = [bit] if bit == 1 or 2 * bit == count else [bit, 2 * bit, 3 * bit]
        arrived = [lax.ppermute(value, axis, [(i, i ^ s) for i in range(count)]) for s in steps]
        bit *= 1 + len(steps)
        if bit == count:
            arrived, beside = lax.optimization_barrier((arrived, beside))
        value = sum(arrived, value)
    return value, beside


def shards(samples, band_gain, dead_flags, section_ids):
    chans, wins, ns = samples.shape
    nf = ns // 2
    width = chans // 2
    blocks = lax.axis_size("fibre")
    groups = lax.axis_size("tm")
    me = lax.axis_index("tm")
    odd = me % 2
    window, waves, seg, lag = tables(ns, nf)
    waves, seg, lag = jnp.asarray(waves), jnp.asarray(seg), jnp.asarray(lag)
    hann = jnp.asarray(window[None, :])
    response = jnp.sum(band_gain[:, None] * waves, axis=0, keepdims=True)
    conv = pl.pallas_call(
        circulant_kernel,
        out_shape=jax.ShapeDtypeStruct((TILE, ns), BF16),
        compiler_params=pltpu.CompilerParams(vmem_limit_bytes=VMEM),
        cost_estimate=pl.CostEstimate(flops=1, bytes_accessed=1, transcendentals=0),
    )(response)
    swap = [(z, z ^ 1) for z in range(groups)]
    both = ("fibre", "tm")
    halo_pairs = [
        (b * groups + z, (b + (1 if z % 2 else -1)) % blocks * groups + z)
        for b in range(blocks)
        for z in range(groups)
    ]

    head = width * 5 // 8

    their_head = lax.ppermute(
        lax.dynamic_slice_in_dim(samples, (1 - odd) * width, head, 0), "tm", swap
    )
    flags = jnp.stack([dead_flags, section_ids])
    halo_flags = lax.ppermute(
        lax.dynamic_slice_in_dim(flags, odd * width, width, 1), both, halo_pairs
    )
    smem = pl.BlockSpec(memory_space=pltpu.SMEM)
    anywhere = pl.BlockSpec(memory_space=pl.ANY)
    sums, own_half, tail = pl.pallas_call(
        section_sums,
        out_shape=[
            jax.ShapeDtypeStruct((NSEC, wins, ns + LANE), F32),
            jax.ShapeDtypeStruct((width, wins, ns), BF16),
            jax.ShapeDtypeStruct((width - head, wins, ns), BF16),
        ],
        in_specs=[smem] * 3 + [anywhere],
        out_specs=[pl.BlockSpec(memory_space=pltpu.VMEM), anywhere, anywhere],
        scratch_shapes=[
            pltpu.VMEM(samples.shape, BF16),
            pltpu.SemaphoreType.DMA((STEPS,)),
            pltpu.SemaphoreType.DMA((2,)),
        ],
        compiler_params=pltpu.CompilerParams(vmem_limit_bytes=VMEM),
        cost_estimate=pl.CostEstimate(flops=1, bytes_accessed=1, transcendentals=0),
    )(odd[None], dead_flags, section_ids, samples)
    total, their_head = add_over(sums, "fibre", their_head)
    halo_source, conv = lax.optimization_barrier((own_half, conv))
    halo = lax.ppermute(halo_source, both, halo_pairs)
    total, halo_flags, conv, own_half, tail = lax.optimization_barrier(
        (total, halo_flags, conv, own_half, tail)
    )
    their_total = lax.ppermute(total, "tm", swap)
    their_tail = lax.ppermute(tail, "tm", swap)
    their_second = lax.ppermute(own_half, "tm", swap)
    ready = (total, their_total, their_head, flags, hann, conv, seg, lag)
    ready = lax.optimization_barrier(ready)
    total, their_total, their_head, flags, hann, conv, seg, lag = ready
    halo_head = lax.ppermute(their_head, both, halo_pairs)

    side = odd[None]
    parts = (hann, conv, seg)
    every = jnp.concatenate([flags, halo_flags], axis=1)
    b0, series = segments(((0, (0, 0), (0, 0)),), side, flags, (total,), (samples,), None, *parts)
    b0, forward = lax.optimization_barrier((b0, their_tail))
    halo_tail = lax.ppermute(forward, both, halo_pairs)
    a, b2 = segments(
        (
            (1, (0, 0), (0, chans)),
            (1, (head, head), (head, chans + head)),
            (0, (width, width), (chans, chans)),
        ),
        side,
        every,
        (total, their_total),
        (their_head, their_tail, halo_head, halo_tail, halo),
        series,
        *parts,
    )
    scale = 2.0 / ns / LAGS / math.sqrt(nf * wins * groups)
    found = stacks(
        (
            (0, (0, width), (chans, width)),
            (0, (head, width + head), (chans + head, width + head)),
            (0, (width, 0), (width, 0)),
        ),
        groups,
        scale,
        me[None],
        every,
        their_total,
        (halo_head, halo_tail, their_head, their_tail, their_second),
        *(hann, conv, seg, lag),
        *(a, b0, b2),
    )
    arrived = {}
    for d in reversed(range(groups)):
        pairs = [
            (b * groups + z, (b - z % 2) % blocks * groups + (z ^ d))
            for b in range(blocks)
            for z in range(groups)
        ]
        arrived[d] = lax.ppermute(found[d], both, pairs)
    arrived = [arrived[d].astype(F32) for d in range(groups)]
    same = sum(arrived[2::2], arrived[0])
    other = sum(arrived[3::2], arrived[1])
    return jnp.concatenate(
        [jnp.where(odd == 0, same, other), jnp.where(odd == 0, other, same)], axis=0
    )


def solution(mesh):
    in_specs = (P("fibre", "tm", None), P(), P("fibre"), P("fibre"))
    out_specs = P("fibre", "tm", None)
    return jax.shard_map(shards, mesh=mesh, in_specs=in_specs, out_specs=out_specs, check_vma=False)
```

```python
import functools
import math

import jax
import jax.numpy as jnp
import ml_dtypes
import numpy as np
from jax import lax
from jax.experimental import pallas as pl
from jax.experimental.pallas import tpu as pltpu
from jax.sharding import PartitionSpec as P

OFFS = 128
LAGS = 128
NSEC = 2
LANE = 128
PART = 32
TILE = 256
STEPS = 4
TOGETHER = 4
VMEM = 63 * 1024 * 1024
NT = (((1,), (1,)), ((), ()))
F32 = jnp.float32
BF16 = jnp.bfloat16


def tables(ns, nf):
    tick = np.arange(ns)
    freq = np.arange(nf)
    window = 0.5 - 0.5 * np.cos(tick * (2.0 * math.pi / ns))
    waves = np.cos((freq[:, None] * tick[None, :] % ns) * (2.0 * math.pi / ns))
    waves[0] *= math.sqrt(0.5)
    size = 2 * LAGS
    bins = np.arange(size // 2)
    turn = math.pi / size * ((2 * bins[:, None] + 1) * np.arange(size)[None, :] % (2 * size))
    segment = np.stack([np.cos(turn), -np.sin(turn)], axis=1).reshape(size, size)
    lag = np.stack([np.cos(turn), -np.sin(turn)], axis=1).reshape(size, size)[:, :LAGS].T
    cast = lambda a: a.astype(np.float32).astype(ml_dtypes.bfloat16)
    return window.astype(np.float32), waves.astype(np.float32), cast(segment), cast(lag)


def section_sums(odd_ref, dead_ref, sec_ref, x_hbm, out_ref, half_hbm, tail_hbm, x, in_sem, sem):
    chans, wins, ns = x.shape
    width, length = half_hbm.shape[0], tail_hbm.shape[0]
    odd = odd_ref[0]
    part = chans // STEPS
    arriving = [
        pltpu.make_async_copy(
            x_hbm.at[pl.ds(n * part, part)], x.at[pl.ds(n * part, part)], in_sem.at[n]
        )
        for n in range(STEPS)
    ]
    for copy in arriving:
        copy.start()
    leaving = [
        pltpu.make_async_copy(x.at[pl.ds(odd * width, width)], half_hbm, sem.at[0]),
        pltpu.make_async_copy(
            x.at[pl.ds((2 - odd) * width - length, length)], tail_hbm, sem.at[1]
        ),
    ]

    def body(c, carry):
        value = x[c].astype(F32)
        live = 1 - dead_ref[c]
        sums, counts = carry
        weights = [jnp.where(sec_ref[c] == s, live, 0).astype(F32) for s in range(NSEC)]
        return (
            tuple(sums[s] + weights[s] * value for s in range(NSEC)),
            tuple(counts[s] + weights[s] for s in range(NSEC)),
        )

    zero = jnp.zeros((wins, ns), F32)
    carry = ((zero,) * NSEC, (jnp.float32(0),) * NSEC)
    for n, copy in enumerate(arriving):
        copy.wait()
        if n == STEPS - 1:
            for out in leaving:
                out.start()
        carry = lax.fori_loop(n * part, (n + 1) * part, body, carry, unroll=8)
    sums, counts = carry
    for s in range(NSEC):
        out_ref[s, :, :ns] = sums[s]
        out_ref[s, :, ns:] = jnp.zeros((wins, LANE), F32) + counts[s]
    for out in leaving:
        out.wait()


def circulant_kernel(filter_ref, out_ref):
    ns = filter_ref.shape[1]
    for t in range(0, TILE, 16):
        block = jnp.broadcast_to(filter_ref[...], (16, ns))
        out_ref[t : t + 16, :] = pltpu.roll(block, t, 1, stride=1, stride_axis=0).astype(BF16)


def segment_factors(places, odd, flag_ref, tot, x, hann, conv, seg, work, copied, first=None):
    common, clean, mass, square, rows, series_all, stage = work
    _, wins, ns = x[0].shape
    chans = sum(piece.shape[0] for piece in x)
    pitch = wins + 1
    size = seg.shape[0]
    half = size // 2
    blocks = ns // half
    jw = blocks * wins
    jpitch = jw + 1
    for copy in copied["first"]:
        copy.wait()
    for g in range(len(tot)):
        for s in range(NSEC):
            common[g * NSEC + s] = tot[g][s, :, :ns] / jnp.maximum(tot[g][s, :, ns : ns + 1], 1.0)
    sign = 1.0 - 2.0 * (lax.broadcasted_iota(jnp.int32, (chans, LANE), 1) % 2).astype(F32)

    for number, (group, base, flags) in enumerate(places):
        piece = x[number]
        length = piece.shape[0]
        base = base[0] + odd * (base[1] - base[0])
        flags = flags[0] + odd * (flags[1] - flags[0])

        def clean_channel(c):
            at = base + c
            flag = flags + c
            live = (1 - flag_ref[0, flag]).astype(F32)
            value = (piece[c].astype(F32) - common[group * NSEC + flag_ref[1, flag]]) * (
                hann[...] * live
            )
            tiles = [value[:, t * LANE : (t + 1) * LANE] for t in range(ns // LANE)]
            row = pl.ds(at * pitch, wins)
            mass[row, :] = sum(tiles[1:], tiles[0])
            square[row, :] = sum([tile * tile for tile in tiles[1:]], tiles[0] * tiles[0])
            for t, tile in enumerate(tiles):
                clean[t, row, :] = tile

        parts = copied["x"][number]
        part = length // len(parts)
        for n, copy in enumerate(parts):
            copy.wait()
            repeat(n * part, (n + 1) * part, clean_channel, 16)
    for copy in copied["tables"]:
        copy.wait()

    for step in range(wins // TOGETHER):
        series = series_all.at[step]
        for i in range(TOGETHER):
            window = pl.ds(step * TOGETHER + i, chans, stride=pitch)
            total = mass[window, :]
            lowest = jnp.sum(total, axis=1, keepdims=True)
            highest = jnp.sum(total * sign, axis=1, keepdims=True)
            power = 0.5 * jnp.sum(square[window, :], axis=1, keepdims=True)
            power = power + (lowest * lowest - highest * highest) * (0.5 / ns)
            level = lax.rsqrt(power + 1e-06)
            for t in range(ns // LANE):
                rows[i * chans : (i + 1) * chans, t * LANE : (t + 1) * LANE] = (
                    clean[t, window, :] * level
                ).astype(BF16)
        for t in range(0, ns, TILE):
            turned = jnp.concatenate([conv[:, ns - t :], conv[:, : ns - t]], axis=1) if t else conv[...]
            series[half // 2 + t : half // 2 + t + TILE, :] = lax.dot_general(
                turned, rows[...], NT, preferred_element_type=F32
            ).astype(BF16)
        series[: half // 2, :] = series[ns : ns + half // 2, :]
        series[ns + half // 2 :, :] = series[half // 2 : half, :]

        def place(which, j, value):
            for i in range(TOGETHER):
                at = j * wins + step * TOGETHER + i
                stage[which, pl.ds(at, size, stride=jpitch), :] = value[
                    :, i * chans : (i + 1) * chans
                ]

        for j in range(blocks):
            start = j * half + half // 2
            b = jnp.dot(
                seg[:, :half], series[start : start + half, :], preferred_element_type=F32
            )
            place(1, j, b)

        if first is not None:
            source = first(step, series)
            for j in range(blocks):
                a = jnp.dot(
                    seg[...], source[j * half : j * half + size, :], preferred_element_type=F32
                )
                place(0, j, a)

    def parts(which, k):
        return [
            stage[which, pl.ds((2 * k + part) * jpitch, jw), :].astype(BF16) for part in range(2)
        ]

    lower = lax.broadcasted_iota(jnp.int32, (1, chans), 1) < chans // 2

    def first_factor(k):
        real, imag = parts(0, k)
        return jnp.concatenate(
            [jnp.where(lower, imag, real), jnp.where(lower, real, imag)], axis=0
        ).T

    return first_factor, lambda k: jnp.concatenate(parts(1, k), axis=0)


def work_shapes(groups, chans, wins, ns):
    half = LAGS
    rows = 2 * half * (ns // half * wins + 1)
    return [
        pltpu.VMEM((groups * NSEC, wins, ns), F32),
        pltpu.VMEM((ns // LANE, chans * (wins + 1), LANE), F32),
        pltpu.VMEM((chans * (wins + 1), LANE), F32),
        pltpu.VMEM((chans * (wins + 1), LANE), F32),
        pltpu.VMEM((TOGETHER * chans, ns), BF16),
        pltpu.VMEM((wins // TOGETHER, ns + half, TOGETHER * chans), BF16),
        pltpu.VMEM((2, rows, chans), F32),
    ]


def repeat(start, stop, body, together):
    def step(n, _):
        body(n)
        return 0

    lax.fori_loop(start, stop, step, 0, unroll=math.gcd(together, stop - start))


class Choice:
    def __init__(self, odd, sources, target, sem):
        self.options = [
            (odd == side, pltpu.make_async_copy(source, target, sem))
            for side, source in enumerate(sources)
        ]

    def start(self):
        for here, copy in self.options:
            pl.when(here)(copy.start)

    def wait(self):
        for here, copy in self.options:
            pl.when(here)(copy.wait)


def input_copies(odd, first, x, tables_in, sem):
    copied = {"first": [], "x": [], "tables": []}
    used = 0

    def copy(source, target):
        nonlocal used
        if isinstance(source, tuple):
            made = Choice(odd, source, target, sem.at[used])
        else:
            made = pltpu.make_async_copy(source, target, sem.at[used])
        made.start()
        used += 1
        return made

    copied["first"] = [copy(*pair) for pair in first]
    for source, target in x:
        parts = max(target.shape[0] // PART, 1)
        part = target.shape[0] // parts
        rows = [pl.ds(n * part, part) for n in range(parts)]
        copied["x"].append(
            [
                copy(
                    tuple(option.at[here] for option in source)
                    if isinstance(source, tuple)
                    else source.at[here],
                    target.at[here],
                )
                for here in rows
            ]
        )
    copied["tables"] = [copy(*pair) for pair in tables_in]
    return copied


def own_kernel(places, odd_ref, flag_ref, *rest):
    tot_hbm, x_hbm, hann_hbm, conv_hbm, seg_hbm, b_hbm, p_hbm = rest[:7]
    tot, x, hann, conv, seg = rest[7:12]
    work, (b_out, in_sem, out_sem, p_sem) = rest[12:-4], rest[-4:]
    odd = odd_ref[0]
    copied = input_copies(
        odd,
        [(tot_hbm, tot), (hann_hbm, hann)],
        [(x_hbm, x)],
        [(conv_hbm, conv), (seg_hbm, seg)],
        in_sem,
    )
    _, second = segment_factors(
        places, odd, flag_ref, [tot], [x], hann, conv, seg, work, copied
    )

    def put_second(k, stage):
        stage[k] = second(k)

    kept = pltpu.make_async_copy(work[-2], p_hbm, p_sem)
    kept.start()
    send_factor(put_second, b_out, b_hbm, out_sem)
    kept.wait()


def send_factor(factor, stage, target, sem):
    step = stage.shape[0] // STEPS
    copies = []
    for n in range(STEPS):
        part = pl.ds(n * step, step)

        repeat(n * step, (n + 1) * step, lambda k: factor(k, stage), 32)
        copies.append(pltpu.make_async_copy(stage.at[part], target.at[part], sem.at[n]))
        copies[-1].start()
    for copy in copies:
        copy.wait()


def second_kernel(places, odd_ref, flag_ref, *rest):
    tot_hbm, (even_hbm, odd_hbm), rest = rest[:2], (rest[2:4], rest[4:6]), rest[6:]
    halo_hbm, hann_hbm, conv_hbm, seg_hbm, p_hbm, a_hbm, b_hbm = rest[:7]
    tot, x, rest = rest[7:9], rest[9:12], rest[12:]
    hann, conv, seg, own, mixed, a_out, b_out = rest[:7]
    work, (in_sem, p_sem, out_sem) = rest[7:-3], rest[-3:]
    odd = odd_ref[0]
    copied = input_copies(
        odd,
        list(zip(tot_hbm, tot)) + [(hann_hbm, hann)],
        list(zip(zip(even_hbm, odd_hbm), x)) + [(halo_hbm, x[2])],
        [(conv_hbm, conv), (seg_hbm, seg)],
        in_sem,
    )
    kept = pltpu.make_async_copy(p_hbm, own, p_sem)
    kept.start()
    copied["tables"].append(kept)
    chans = b_out.shape[2]
    lane = lax.broadcasted_iota(jnp.int32, (1, chans), 1)

    def first(step, series):
        @pl.when(odd == 1)
        def _():
            mixed[...] = series[...]

        @pl.when(odd == 0)
        def _():
            for i in range(TOGETHER):
                columns = slice(i * chans, (i + 1) * chans)
                value = own[step, :, columns]
                turned = jnp.concatenate([value[:, chans // 2 :], value[:, : chans // 2]], axis=1)
                mixed[:, columns] = jnp.where(lane < chans // 2, series[:, columns], turned)

        return mixed

    first_factor, second_factor = segment_factors(
        places, odd, flag_ref, tot, x, hann, conv, seg, work, copied, first
    )

    def both_factors(k, stage):
        value = first_factor(k)
        width = value.shape[0] // 2
        a_out[k, 1] = value[:width]
        a_out[k, 0] = value[width:]
        stage[k] = second_factor(k)

    step = b_out.shape[0] // STEPS
    copies = []
    for n in range(STEPS):
        part = pl.ds(n * step, step)

        repeat(n * step, (n + 1) * step, lambda k: both_factors(k, b_out), 16)
        for m, (source, target) in enumerate(((a_out, a_hbm), (b_out, b_hbm))):
            copies.append(
                pltpu.make_async_copy(source.at[part], target.at[part], out_sem.at[2 * n + m])
            )
            copies[-1].start()
    for copy in copies:
        copy.wait()


def segments(places, side, flags, totals, pieces, series, hann, conv, seg):
    chans = LANE
    _, wins, ns = pieces[0].shape
    size = seg.shape[0]
    half = size // 2
    depth = ns // half * wins * 2
    smem = pl.BlockSpec(memory_space=pltpu.SMEM)
    anywhere = pl.BlockSpec(memory_space=pl.ANY)
    b_shape = jax.ShapeDtypeStruct((half, depth, chans), BF16)
    p_shape = jax.ShapeDtypeStruct((wins // TOGETHER, ns + half, TOGETHER * chans), BF16)
    a_shape = jax.ShapeDtypeStruct((half, 2, chans // 2, depth), BF16)
    scratch = lambda *values: [pltpu.VMEM(value.shape, value.dtype) for value in values]
    operands = list(totals) + list(pieces) + [hann, conv, seg]
    count = len(operands) + chans // PART
    if series is None:
        kernel, out = own_kernel, [b_shape, p_shape]
        held = scratch(*operands)
        last = scratch(b_shape) + [
            pltpu.SemaphoreType.DMA((count,)),
            pltpu.SemaphoreType.DMA((STEPS,)),
            pltpu.SemaphoreType.DMA,
        ]
    else:
        kernel, out = second_kernel, [a_shape, b_shape]
        held = scratch(*totals, pieces[0], pieces[1], pieces[4], hann, conv, seg, series)
        held += [pltpu.VMEM(p_shape.shape[1:], BF16)] + scratch(a_shape, b_shape)
        last = [
            pltpu.SemaphoreType.DMA((count,)),
            pltpu.SemaphoreType.DMA,
            pltpu.SemaphoreType.DMA((2 * STEPS,)),
        ]
        operands.append(series)
    return pl.pallas_call(
        functools.partial(kernel, places),
        out_shape=out,
        in_specs=[smem] * 2 + [anywhere] * len(operands),
        out_specs=[anywhere] * 2,
        scratch_shapes=held + work_shapes(len(totals), chans, wins, ns) + last,
        compiler_params=pltpu.CompilerParams(vmem_limit_bytes=VMEM),
        cost_estimate=pl.CostEstimate(
            flops=2 * wins * chans * ns * (ns + 3 * size),
            bytes_accessed=16 * 1024 * 1024,
            transcendentals=0,
        ),
    )(side, flags, *operands)


def stack_kernel(places, scale, shares, me_ref, flag_ref, *rest):
    even_hbm, odd_hbm, late_hbm, rest = rest[:2], rest[2:4], rest[4], rest[5:]
    tot_hbm, hann_hbm, conv_hbm, seg_hbm, lag_hbm = rest[:5]
    a_hbm, b0_hbm, b2_hbm, rest = *rest[5:8], rest[8:]
    outs, rest = rest[:shares], rest[shares:]
    x, rest = rest[:3], rest[3:]
    tot, hann, conv, seg, lag, a, b0, b2 = rest[:8]
    work, (b3, one, in_sem, late_sem) = rest[8:-4], rest[-4:]
    me = me_ref[0]
    odd = lax.rem(me, 2)
    copied = input_copies(
        odd,
        [(tot_hbm, tot), (hann_hbm, hann)],
        list(zip(zip(even_hbm, odd_hbm), x)) + [(late_hbm, x[2])],
        [(conv_hbm, conv), (seg_hbm, seg), (lag_hbm, lag)],
        in_sem,
    )
    some = b0.shape[0] // STEPS
    late = [
        pltpu.make_async_copy(
            source.at[pl.ds(n * some, some)], target.at[pl.ds(n * some, some)], late_sem.at[n, m]
        )
        for n in range(STEPS)
        for m, (source, target) in enumerate(((b0_hbm, b0), (b2_hbm, b2), (a_hbm, a)))
    ]
    for copy in late:
        copy.start()
    bins, depth, chans = b0.shape
    width = chans // 2
    nfr = lag.shape[1]
    pitch = nfr + 1
    cross = work[-1]

    _, second_factor = segment_factors(
        places, odd, flag_ref, [tot], x, hann, conv, seg, work, copied
    )

    def second(k):
        b3[k] = second_factor(k)

    repeat(0, bins, second, 32)

    lane = lax.broadcasted_iota(jnp.int32, (1, chans), 1)
    low, high = [jnp.where((lane < width) == (g == 0), 1.0, 0.0).astype(BF16) for g in range(2)]

    lower = lane < width

    def bins_with(near, far):
        def one_bin(k):
            inner = near[k] * low + b3[k] * high if near is not b3 else b3[k]
            own = jnp.concatenate([b0[k], b2[k] * high], axis=1)
            theirs = jnp.concatenate([inner, far[k] * low], axis=1)
            part = depth // 2
            right = jnp.concatenate([own[:part], theirs[:part], theirs[part:], own[part:]], axis=0)
            real = jnp.where(lower, a[k, 0], a[k, 1])
            imag = jnp.where(lower, a[k, 1], a[k, 0])
            turn = lambda v: jnp.concatenate([v[:, part:], v[:, :part]], axis=1)
            left = jnp.concatenate(
                [
                    jnp.concatenate([real, imag], axis=1),
                    jnp.concatenate([turn(imag), -turn(real)], axis=1),
                ],
                axis=0,
            )
            value = jnp.dot(left, right, preferred_element_type=F32)
            for p in range(2):
                for t in range(2):
                    cross[t, pl.ds(2 * k + p, width, stride=pitch), :] = value[
                        p * width : (p + 1) * width, t * chans : (t + 1) * chans
                    ]

        for n in range(STEPS):
            for copy in late[3 * n : 3 * (n + 1)]:
                copy.wait()
            repeat(n * some, (n + 1) * some, one_bin, 32)

    pl.when(odd == 0)(lambda: bins_with(b2, b3))
    pl.when(odd == 1)(lambda: bins_with(b3, b2))

    row = lax.broadcasted_iota(jnp.int32, one.shape[1:], 0)
    column = lax.broadcasted_iota(jnp.int32, one.shape[1:], 1)
    turned = jnp.where(row < width, row + chans, row - width)
    place = row + (turned - row) * odd
    for t in range(2):
        here = column + t * chans
        found = (place == here) | ((here >= chans + width) & (place == here - width))
        one[t] = jnp.where(found, 1.0, 0.0)
    share = OFFS // shares

    def one_channel(c):
        value = jnp.concatenate(
            [cross[t, pl.ds(c * pitch, nfr), :] for t in range(2)], axis=1
        ).astype(BF16)
        starts = [c + 1 + share * (me ^ d) for d in range(shares)]
        pick = jnp.concatenate(
            [
                jnp.concatenate([one[t, pl.ds(start, share), :] for start in starts], axis=0)
                for t in range(2)
            ],
            axis=1,
        ).astype(BF16)
        lagged = jnp.dot(lag[...], value, preferred_element_type=F32) * scale
        band = lax.dot_general(pick, lagged.astype(BF16), NT, preferred_element_type=F32)
        for d, out in enumerate(outs):
            out[c] = band[d * share : (d + 1) * share, :].astype(BF16)

    repeat(0, width, one_channel, 16)


def stacks(places, shares, scale, me, flags, total, pieces, hann, conv, seg, lag, a, b0, b2):
    bins, depth, chans = b0.shape
    width = chans // 2
    _, wins, ns = pieces[0].shape
    nlag, nfr = lag.shape
    smem = pl.BlockSpec(memory_space=pltpu.SMEM)
    vmem = pl.BlockSpec(memory_space=pltpu.VMEM)
    anywhere = pl.BlockSpec(memory_space=pl.ANY)
    tables_in = [total, hann, conv, seg, lag, a, b0, b2]
    operands = [*pieces, *tables_in]
    held = [pieces[0], pieces[1], pieces[4], *tables_in]
    return pl.pallas_call(
        functools.partial(stack_kernel, places, scale, shares),
        out_shape=[jax.ShapeDtypeStruct((width, OFFS // shares, nlag), BF16)] * shares,
        in_specs=[smem] * 2 + [anywhere] * len(operands),
        out_specs=[vmem] * shares,
        scratch_shapes=[pltpu.VMEM(value.shape, value.dtype) for value in held]
        + work_shapes(1, chans, wins, ns)
        + [
            pltpu.VMEM(b0.shape, BF16),
            pltpu.VMEM((2, chans + width, chans), F32),
            pltpu.SemaphoreType.DMA((8 + chans // PART,)),
            pltpu.SemaphoreType.DMA((STEPS, 3)),
        ],
        compiler_params=pltpu.CompilerParams(vmem_limit_bytes=VMEM),
        cost_estimate=pl.CostEstimate(
            flops=2 * width * bins * 4 * (2 * depth * chans + 2 * OFFS * chans),
            bytes_accessed=20 * 1024 * 1024,
            transcendentals=0,
        ),
    )(me, flags, *operands)


def add_over(value, axis, beside):
    count = lax.axis_size(axis)
    if count & (count - 1):
        return lax.psum(value, axis), beside
    bit = 1
    while bit < count:
        steps = [bit] if bit == 1 or 2 * bit == count else [bit, 2 * bit, 3 * bit]
        arrived = [lax.ppermute(value, axis, [(i, i ^ s) for i in range(count)]) for s in steps]
        bit *= 1 + len(steps)
        if bit == count:
            arrived, beside = lax.optimization_barrier((arrived, beside))
        value = sum(arrived, value)
    return value, beside


def shards(samples, band_gain, dead_flags, section_ids):
    chans, wins, ns = samples.shape
    nf = ns // 2
    width = chans // 2
    blocks = lax.axis_size("fibre")
    groups = lax.axis_size("tm")
    me = lax.axis_index("tm")
    odd = me % 2
    window, waves, seg, lag = tables(ns, nf)
    waves, seg, lag = jnp.asarray(waves), jnp.asarray(seg), jnp.asarray(lag)
    hann = jnp.asarray(window[None, :])
    response = jnp.sum(band_gain[:, None] * waves, axis=0, keepdims=True)
    swap = [(z, z ^ 1) for z in range(groups)]
    both = ("fibre", "tm")
    halo_pairs = [
        (b * groups + z, (b + (1 if z % 2 else -1)) % blocks * groups + z)
        for b in range(blocks)
        for z in range(groups)
    ]

    head = width * 5 // 8

    their_head = lax.ppermute(
        lax.dynamic_slice_in_dim(samples, (1 - odd) * width, head, 0), "tm", swap
    )
    flags = jnp.stack([dead_flags, section_ids])
    halo_flags = lax.ppermute(
        lax.dynamic_slice_in_dim(flags, odd * width, width, 1), both, halo_pairs
    )
    smem = pl.BlockSpec(memory_space=pltpu.SMEM)
    anywhere = pl.BlockSpec(memory_space=pl.ANY)
    sums, own_half, tail = pl.pallas_call(
        section_sums,
        out_shape=[
            jax.ShapeDtypeStruct((NSEC, wins, ns + LANE), F32),
            jax.ShapeDtypeStruct((width, wins, ns), BF16),
            jax.ShapeDtypeStruct((width - head, wins, ns), BF16),
        ],
        in_specs=[smem] * 3 + [anywhere],
        out_specs=[pl.BlockSpec(memory_space=pltpu.VMEM), anywhere, anywhere],
        scratch_shapes=[
            pltpu.VMEM(samples.shape, BF16),
            pltpu.SemaphoreType.DMA((STEPS,)),
            pltpu.SemaphoreType.DMA((2,)),
        ],
        compiler_params=pltpu.CompilerParams(vmem_limit_bytes=VMEM),
        cost_estimate=pl.CostEstimate(flops=1, bytes_accessed=1, transcendentals=0),
    )(odd[None], dead_flags, section_ids, samples)
    total, their_head = add_over(sums, "fibre", their_head)
    halo_source, halo_flags = lax.optimization_barrier((own_half, halo_flags))
    halo = lax.ppermute(halo_source, both, halo_pairs)
    total, response, own_half, tail = lax.optimization_barrier(
        (total, response, own_half, tail)
    )
    conv = pl.pallas_call(
        circulant_kernel,
        out_shape=jax.ShapeDtypeStruct((TILE, ns), BF16),
        compiler_params=pltpu.CompilerParams(vmem_limit_bytes=VMEM),
        cost_estimate=pl.CostEstimate(flops=1, bytes_accessed=1, transcendentals=0),
    )(response)
    their_total = lax.ppermute(total, "tm", swap)
    their_tail = lax.ppermute(tail, "tm", swap)
    their_second = lax.ppermute(own_half, "tm", swap)
    ready = (total, their_total, their_head, flags, hann, conv, seg, lag)
    ready = lax.optimization_barrier(ready)
    total, their_total, their_head, flags, hann, conv, seg, lag = ready
    halo_head = lax.ppermute(their_head, both, halo_pairs)

    side = odd[None]
    parts = (hann, conv, seg)
    every = jnp.concatenate([flags, halo_flags], axis=1)
    b0, series = segments(((0, (0, 0), (0, 0)),), side, flags, (total,), (samples,), None, *parts)
    b0, forward = lax.optimization_barrier((b0, their_tail))
    halo_tail = lax.ppermute(forward, both, halo_pairs)
    a, b2 = segments(
        (
            (1, (0, 0), (0, chans)),
            (1, (head, head), (head, chans + head)),
            (0, (width, width), (chans, chans)),
        ),
        side,
        every,
        (total, their_total),
        (their_head, their_tail, halo_head, halo_tail, halo),
        series,
        *parts,
    )
    scale = 2.0 / ns / LAGS / math.sqrt(nf * wins * groups)
    found = stacks(
        (
            (0, (0, width), (chans, width)),
            (0, (head, width + head), (chans + head, width + head)),
            (0, (width, 0), (width, 0)),
        ),
        groups,
        scale,
        me[None],
        every,
        their_total,
        (halo_head, halo_tail, their_head, their_tail, their_second),
        *(hann, conv, seg, lag),
        *(a, b0, b2),
    )
    arrived = {}
    for d in reversed(range(groups)):
        pairs = [
            (b * groups + z, (b - z % 2) % blocks * groups + (z ^ d))
            for b in range(blocks)
            for z in range(groups)
        ]
        arrived[d] = lax.ppermute(found[d], both, pairs)
    arrived = [arrived[d].astype(F32) for d in range(groups)]
    same = sum(arrived[2::2], arrived[0])
    other = sum(arrived[3::2], arrived[1])
    return jnp.concatenate(
        [jnp.where(odd == 0, same, other), jnp.where(odd == 0, other, same)], axis=0
    )


def solution(mesh):
    in_specs = (P("fibre", "tm", None), P(), P("fibre"), P("fibre"))
    out_specs = P("fibre", "tm", None)
    return jax.shard_map(shards, mesh=mesh, in_specs=in_specs, out_specs=out_specs, check_vma=False)
```

```python
import functools
import math

import jax
import jax.numpy as jnp
import ml_dtypes
import numpy as np
from jax import lax
from jax.experimental import pallas as pl
from jax.experimental.pallas import tpu as pltpu
from jax.sharding import PartitionSpec as P

OFFS = 128
LAGS = 128
NSEC = 2
LANE = 128
PART = 32
TILE = 256
STEPS = 4
TOGETHER = 4
VMEM = 63 * 1024 * 1024
NT = (((1,), (1,)), ((), ()))
F32 = jnp.float32
BF16 = jnp.bfloat16


def tables(ns, nf):
    tick = np.arange(ns)
    freq = np.arange(nf)
    window = 0.5 - 0.5 * np.cos(tick * (2.0 * math.pi / ns))
    waves = np.cos((freq[:, None] * tick[None, :] % ns) * (2.0 * math.pi / ns))
    waves[0] *= math.sqrt(0.5)
    size = 2 * LAGS
    bins = np.arange(size // 2)
    turn = math.pi / size * ((2 * bins[:, None] + 1) * np.arange(size)[None, :] % (2 * size))
    segment = np.stack([np.cos(turn), -np.sin(turn)], axis=1).reshape(size, size)
    lag = np.stack([np.cos(turn), -np.sin(turn)], axis=1).reshape(size, size)[:, :LAGS].T
    cast = lambda a: a.astype(np.float32).astype(ml_dtypes.bfloat16)
    return window.astype(np.float32), waves.astype(np.float32), cast(segment), cast(lag)


def section_sums(odd_ref, dead_ref, sec_ref, x_hbm, out_ref, half_hbm, tail_hbm, x, in_sem, sem):
    chans, wins, ns = x.shape
    width, length = half_hbm.shape[0], tail_hbm.shape[0]
    odd = odd_ref[0]
    part = chans // STEPS
    arriving = [
        pltpu.make_async_copy(
            x_hbm.at[pl.ds(n * part, part)], x.at[pl.ds(n * part, part)], in_sem.at[n]
        )
        for n in range(STEPS)
    ]
    for copy in arriving:
        copy.start()
    leaving = [
        pltpu.make_async_copy(x.at[pl.ds(odd * width, width)], half_hbm, sem.at[0]),
        pltpu.make_async_copy(
            x.at[pl.ds((2 - odd) * width - length, length)], tail_hbm, sem.at[1]
        ),
    ]

    def body(c, carry):
        value = x[c].astype(F32)
        live = 1 - dead_ref[c]
        sums, counts = carry
        weights = [jnp.where(sec_ref[c] == s, live, 0).astype(F32) for s in range(NSEC)]
        return (
            tuple(sums[s] + weights[s] * value for s in range(NSEC)),
            tuple(counts[s] + weights[s] for s in range(NSEC)),
        )

    zero = jnp.zeros((wins, ns), F32)
    carry = ((zero,) * NSEC, (jnp.float32(0),) * NSEC)
    for n, copy in enumerate(arriving):
        copy.wait()
        if n == STEPS - 1:
            for out in leaving:
                out.start()
        carry = lax.fori_loop(n * part, (n + 1) * part, body, carry, unroll=8)
    sums, counts = carry
    for s in range(NSEC):
        out_ref[s, :, :ns] = sums[s]
        out_ref[s, :, ns:] = jnp.zeros((wins, LANE), F32) + counts[s]
    for out in leaving:
        out.wait()


def circulant_kernel(filter_ref, out_ref):
    ns = filter_ref.shape[1]
    for t in range(0, TILE, 16):
        block = jnp.broadcast_to(filter_ref[...], (16, ns))
        out_ref[t : t + 16, :] = pltpu.roll(block, t, 1, stride=1, stride_axis=0).astype(BF16)


def segment_factors(places, odd, flag_ref, tot, x, hann, conv, seg, work, copied, first=None):
    common, clean, mass, square, rows, series_all, stage = work
    _, wins, ns = x[0].shape
    chans = sum(piece.shape[0] for piece in x)
    pitch = wins + 1
    size = seg.shape[0]
    half = size // 2
    blocks = ns // half
    jw = blocks * wins
    jpitch = jw + 1
    for copy in copied["first"]:
        copy.wait()
    for g in range(len(tot)):
        for s in range(NSEC):
            common[g * NSEC + s] = tot[g][s, :, :ns] / jnp.maximum(tot[g][s, :, ns : ns + 1], 1.0)
    sign = 1.0 - 2.0 * (lax.broadcasted_iota(jnp.int32, (chans, LANE), 1) % 2).astype(F32)

    for number, (group, base, flags) in enumerate(places):
        piece = x[number]
        length = piece.shape[0]
        base = base[0] + odd * (base[1] - base[0])
        flags = flags[0] + odd * (flags[1] - flags[0])

        def clean_channel(c):
            at = base + c
            flag = flags + c
            live = (1 - flag_ref[0, flag]).astype(F32)
            value = (piece[c].astype(F32) - common[group * NSEC + flag_ref[1, flag]]) * (
                hann[...] * live
            )
            tiles = [value[:, t * LANE : (t + 1) * LANE] for t in range(ns // LANE)]
            row = pl.ds(at * pitch, wins)
            mass[row, :] = sum(tiles[1:], tiles[0])
            square[row, :] = sum([tile * tile for tile in tiles[1:]], tiles[0] * tiles[0])
            for t, tile in enumerate(tiles):
                clean[t, row, :] = tile

        parts = copied["x"][number]
        part = length // len(parts)
        for n, copy in enumerate(parts):
            copy.wait()
            repeat(n * part, (n + 1) * part, clean_channel, 16)
    for copy in copied["tables"]:
        copy.wait()

    for step in range(wins // TOGETHER):
        series = series_all.at[step]
        for i in range(TOGETHER):
            window = pl.ds(step * TOGETHER + i, chans, stride=pitch)
            total = mass[window, :]
            lowest = jnp.sum(total, axis=1, keepdims=True)
            highest = jnp.sum(total * sign, axis=1, keepdims=True)
            power = 0.5 * jnp.sum(square[window, :], axis=1, keepdims=True)
            power = power + (lowest * lowest - highest * highest) * (0.5 / ns)
            level = lax.rsqrt(power + 1e-06)
            for t in range(ns // LANE):
                rows[i * chans : (i + 1) * chans, t * LANE : (t + 1) * LANE] = (
                    clean[t, window, :] * level
                ).astype(BF16)
        for t in range(0, ns, TILE):
            turned = jnp.concatenate([conv[:, ns - t :], conv[:, : ns - t]], axis=1) if t else conv[...]
            series[half // 2 + t : half // 2 + t + TILE, :] = lax.dot_general(
                turned, rows[...], NT, preferred_element_type=F32
            ).astype(BF16)
        series[: half // 2, :] = series[ns : ns + half // 2, :]
        series[ns + half // 2 :, :] = series[half // 2 : half, :]

        def place(which, j, value):
            for i in range(TOGETHER):
                at = j * wins + step * TOGETHER + i
                stage[which, pl.ds(at, size, stride=jpitch), :] = value[
                    :, i * chans : (i + 1) * chans
                ]

        for j in range(blocks):
            start = j * half + half // 2
            b = jnp.dot(
                seg[:, :half], series[start : start + half, :], preferred_element_type=F32
            )
            place(1, j, b)

        if first is not None:
            source = first(step, series)
            for j in range(blocks):
                a = jnp.dot(
                    seg[...], source[j * half : j * half + size, :], preferred_element_type=F32
                )
                place(0, j, a)

    def parts(which, k):
        return [
            stage[which, pl.ds((2 * k + part) * jpitch, jw), :].astype(BF16) for part in range(2)
        ]

    lower = lax.broadcasted_iota(jnp.int32, (1, chans), 1) < chans // 2

    def first_factor(k):
        real, imag = parts(0, k)
        return jnp.concatenate(
            [jnp.where(lower, imag, real), jnp.where(lower, real, imag)], axis=0
        ).T

    return first_factor, lambda k: jnp.concatenate(parts(1, k), axis=0)


def work_shapes(groups, chans, wins, ns):
    half = LAGS
    rows = 2 * half * (ns // half * wins + 1)
    return [
        pltpu.VMEM((groups * NSEC, wins, ns), F32),
        pltpu.VMEM((ns // LANE, chans * (wins + 1), LANE), F32),
        pltpu.VMEM((chans * (wins + 1), LANE), F32),
        pltpu.VMEM((chans * (wins + 1), LANE), F32),
        pltpu.VMEM((TOGETHER * chans, ns), BF16),
        pltpu.VMEM((wins // TOGETHER, ns + half, TOGETHER * chans), BF16),
        pltpu.VMEM((2, rows, chans), F32),
    ]


def repeat(start, stop, body, together):
    def step(n, _):
        body(n)
        return 0

    lax.fori_loop(start, stop, step, 0, unroll=math.gcd(together, stop - start))


class Choice:
    def __init__(self, odd, sources, target, sem):
        self.options = [
            (odd == side, pltpu.make_async_copy(source, target, sem))
            for side, source in enumerate(sources)
        ]

    def start(self):
        for here, copy in self.options:
            pl.when(here)(copy.start)

    def wait(self):
        for here, copy in self.options:
            pl.when(here)(copy.wait)


def input_copies(odd, first, x, tables_in, sem):
    copied = {"first": [], "x": [], "tables": []}
    used = 0

    def copy(source, target):
        nonlocal used
        if isinstance(source, tuple):
            made = Choice(odd, source, target, sem.at[used])
        else:
            made = pltpu.make_async_copy(source, target, sem.at[used])
        made.start()
        used += 1
        return made

    copied["first"] = [copy(*pair) for pair in first]
    for source, target in x:
        parts = max(target.shape[0] // PART, 1)
        part = target.shape[0] // parts
        rows = [pl.ds(n * part, part) for n in range(parts)]
        copied["x"].append(
            [
                copy(
                    tuple(option.at[here] for option in source)
                    if isinstance(source, tuple)
                    else source.at[here],
                    target.at[here],
                )
                for here in rows
            ]
        )
    copied["tables"] = [copy(*pair) for pair in tables_in]
    return copied


def own_kernel(places, odd_ref, flag_ref, *rest):
    tot_hbm, x_hbm, hann_hbm, conv_hbm, seg_hbm, b_hbm, p_hbm = rest[:7]
    tot, x, hann, conv, seg = rest[7:12]
    work, (b_out, in_sem, out_sem, p_sem) = rest[12:-4], rest[-4:]
    odd = odd_ref[0]
    copied = input_copies(
        odd,
        [(tot_hbm, tot), (hann_hbm, hann)],
        [(x_hbm, x)],
        [(conv_hbm, conv), (seg_hbm, seg)],
        in_sem,
    )
    _, second = segment_factors(
        places, odd, flag_ref, [tot], [x], hann, conv, seg, work, copied
    )

    def put_second(k, stage):
        stage[k] = second(k)

    kept = pltpu.make_async_copy(work[-2], p_hbm, p_sem)
    kept.start()
    send_factor(put_second, b_out, b_hbm, out_sem)
    kept.wait()


def send_factor(factor, stage, target, sem):
    step = stage.shape[0] // STEPS
    copies = []
    for n in range(STEPS):
        part = pl.ds(n * step, step)

        repeat(n * step, (n + 1) * step, lambda k: factor(k, stage), 32)
        copies.append(pltpu.make_async_copy(stage.at[part], target.at[part], sem.at[n]))
        copies[-1].start()
    for copy in copies:
        copy.wait()


def second_kernel(places, odd_ref, flag_ref, *rest):
    tot_hbm, (even_hbm, odd_hbm), rest = rest[:2], (rest[2:4], rest[4:6]), rest[6:]
    halo_hbm, hann_hbm, conv_hbm, seg_hbm, p_hbm, a_hbm, b_hbm = rest[:7]
    tot, x, rest = rest[7:9], rest[9:12], rest[12:]
    hann, conv, seg, own, mixed, a_out, b_out = rest[:7]
    work, (in_sem, p_sem, out_sem) = rest[7:-3], rest[-3:]
    odd = odd_ref[0]
    copied = input_copies(
        odd,
        list(zip(tot_hbm, tot)) + [(hann_hbm, hann)],
        list(zip(zip(even_hbm, odd_hbm), x)) + [(halo_hbm, x[2])],
        [(conv_hbm, conv), (seg_hbm, seg)],
        in_sem,
    )
    kept = pltpu.make_async_copy(p_hbm, own, p_sem)
    kept.start()
    copied["tables"].append(kept)
    chans = b_out.shape[2]
    lane = lax.broadcasted_iota(jnp.int32, (1, chans), 1)

    def first(step, series):
        @pl.when(odd == 1)
        def _():
            mixed[...] = series[...]

        @pl.when(odd == 0)
        def _():
            for i in range(TOGETHER):
                columns = slice(i * chans, (i + 1) * chans)
                value = own[step, :, columns]
                turned = jnp.concatenate([value[:, chans // 2 :], value[:, : chans // 2]], axis=1)
                mixed[:, columns] = jnp.where(lane < chans // 2, series[:, columns], turned)

        return mixed

    first_factor, second_factor = segment_factors(
        places, odd, flag_ref, tot, x, hann, conv, seg, work, copied, first
    )

    def both_factors(k, stage):
        value = first_factor(k)
        width = value.shape[0] // 2
        a_out[k, 1] = value[:width]
        a_out[k, 0] = value[width:]
        stage[k] = second_factor(k)

    step = b_out.shape[0] // STEPS
    copies = []
    for n in range(STEPS):
        part = pl.ds(n * step, step)

        repeat(n * step, (n + 1) * step, lambda k: both_factors(k, b_out), 16)
        for m, (source, target) in enumerate(((a_out, a_hbm), (b_out, b_hbm))):
            copies.append(
                pltpu.make_async_copy(source.at[part], target.at[part], out_sem.at[2 * n + m])
            )
            copies[-1].start()
    for copy in copies:
        copy.wait()


def segments(places, side, flags, totals, pieces, series, hann, conv, seg):
    chans = LANE
    _, wins, ns = pieces[0].shape
    size = seg.shape[0]
    half = size // 2
    depth = ns // half * wins * 2
    smem = pl.BlockSpec(memory_space=pltpu.SMEM)
    anywhere = pl.BlockSpec(memory_space=pl.ANY)
    b_shape = jax.ShapeDtypeStruct((half, depth, chans), BF16)
    p_shape = jax.ShapeDtypeStruct((wins // TOGETHER, ns + half, TOGETHER * chans), BF16)
    a_shape = jax.ShapeDtypeStruct((half, 2, chans // 2, depth), BF16)
    scratch = lambda *values: [pltpu.VMEM(value.shape, value.dtype) for value in values]
    operands = list(totals) + list(pieces) + [hann, conv, seg]
    count = len(operands) + chans // PART
    if series is None:
        kernel, out = own_kernel, [b_shape, p_shape]
        held = scratch(*operands)
        last = scratch(b_shape) + [
            pltpu.SemaphoreType.DMA((count,)),
            pltpu.SemaphoreType.DMA((STEPS,)),
            pltpu.SemaphoreType.DMA,
        ]
    else:
        kernel, out = second_kernel, [a_shape, b_shape]
        held = scratch(*totals, pieces[0], pieces[1], pieces[4], hann, conv, seg, series)
        held += [pltpu.VMEM(p_shape.shape[1:], BF16)] + scratch(a_shape, b_shape)
        last = [
            pltpu.SemaphoreType.DMA((count,)),
            pltpu.SemaphoreType.DMA,
            pltpu.SemaphoreType.DMA((2 * STEPS,)),
        ]
        operands.append(series)
    return pl.pallas_call(
        functools.partial(kernel, places),
        out_shape=out,
        in_specs=[smem] * 2 + [anywhere] * len(operands),
        out_specs=[anywhere] * 2,
        scratch_shapes=held + work_shapes(len(totals), chans, wins, ns) + last,
        compiler_params=pltpu.CompilerParams(vmem_limit_bytes=VMEM),
        cost_estimate=pl.CostEstimate(
            flops=2 * wins * chans * ns * (ns + 3 * size),
            bytes_accessed=16 * 1024 * 1024,
            transcendentals=0,
        ),
    )(side, flags, *operands)


def correlate(first, count, scale, shares, me, a, b0, b2, b3, lag, cross, one, outs, bins_loop):
    depth, chans = b0.shape[1:]
    width = chans // 2
    nfr = lag.shape[1]
    pitch = nfr + 1
    odd = lax.rem(me, 2)
    lane = lax.broadcasted_iota(jnp.int32, (1, chans), 1)
    low, high = [jnp.where((lane < width) == (g == 0), 1.0, 0.0).astype(BF16) for g in range(2)]
    lower = lane < width

    def bins_with(near, far):
        def one_bin(k):
            inner = near[k] * low + b3[k] * high if near is not b3 else b3[k]
            own = jnp.concatenate([b0[k], b2[k] * high], axis=1)
            theirs = jnp.concatenate([inner, far[k] * low], axis=1)
            part = depth // 2
            right = jnp.concatenate([own[:part], theirs[:part], theirs[part:], own[part:]], axis=0)
            real = jnp.where(lower, a[k, 0], a[k, 1])
            imag = jnp.where(lower, a[k, 1], a[k, 0])
            turn = lambda v: jnp.concatenate([v[:, part:], v[:, :part]], axis=1)
            left = jnp.concatenate(
                [
                    jnp.concatenate([real, imag], axis=1),
                    jnp.concatenate([turn(imag), -turn(real)], axis=1),
                ],
                axis=0,
            )
            value = jnp.dot(left, right, preferred_element_type=F32)
            for p in range(2):
                for t in range(2):
                    cross[t, pl.ds(2 * k + p, count, stride=pitch), :] = value[
                        p * count : (p + 1) * count, t * chans : (t + 1) * chans
                    ]

        bins_loop(one_bin)

    pl.when(odd == 0)(lambda: bins_with(b2, b3))
    pl.when(odd == 1)(lambda: bins_with(b3, b2))

    row = lax.broadcasted_iota(jnp.int32, one.shape[1:], 0)
    column = lax.broadcasted_iota(jnp.int32, one.shape[1:], 1)
    turned = jnp.where(row < width, row + chans, row - width)
    place = row + (turned - row) * odd
    for t in range(2):
        here = column + t * chans
        found = (place == here) | ((here >= chans + width) & (place == here - width))
        one[t] = jnp.where(found, 1.0, 0.0)
    share = OFFS // shares

    def one_channel(c):
        value = jnp.concatenate(
            [cross[t, pl.ds(c * pitch, nfr), :] for t in range(2)], axis=1
        ).astype(BF16)
        starts = [first + c + 1 + share * (me ^ d) for d in range(shares)]
        pick = jnp.concatenate(
            [
                jnp.concatenate([one[t, pl.ds(start, share), :] for start in starts], axis=0)
                for t in range(2)
            ],
            axis=1,
        ).astype(BF16)
        lagged = jnp.dot(lag[...], value, preferred_element_type=F32) * scale
        band = lax.dot_general(pick, lagged.astype(BF16), NT, preferred_element_type=F32)
        for d, out in enumerate(outs):
            out[c] = band[d * share : (d + 1) * share, :].astype(BF16)

    repeat(0, count, one_channel, 16)


def last_kernel(places, scale, shares, me_ref, flag_ref, *rest):
    even_hbm, odd_hbm, late_hbm, rest = rest[:2], rest[2:4], rest[4], rest[5:]
    tot_hbm, hann_hbm, conv_hbm, seg_hbm, lag_hbm = rest[:5]
    a_hbm, b0_hbm, b2_hbm, rest = *rest[5:8], rest[8:]
    outs, b3_hbm, rest = rest[:shares], rest[shares], rest[shares + 1 :]
    x, rest = rest[:3], rest[3:]
    tot, hann, conv, seg, lag, b0, b2 = rest[:7]
    work, (a, b3, one, in_sem, late_sem, out_sem) = rest[7:-6], rest[-6:]
    me = me_ref[0]
    odd = lax.rem(me, 2)
    copied = input_copies(
        odd,
        [(tot_hbm, tot), (hann_hbm, hann)],
        list(zip(zip(even_hbm, odd_hbm), x)) + [(late_hbm, x[2])],
        [(conv_hbm, conv), (seg_hbm, seg), (lag_hbm, lag)],
        in_sem,
    )
    count = a.shape[2]
    late = [
        pltpu.make_async_copy(source, target, late_sem.at[n])
        for n, (source, target) in enumerate(
            ((b0_hbm, b0), (b2_hbm, b2), (a_hbm.at[:, :, pl.ds(0, count)], a))
        )
    ]
    for copy in late:
        copy.start()
    _, second_factor = segment_factors(
        places, odd, flag_ref, [tot], x, hann, conv, seg, work, copied
    )
    bins = b3.shape[0]

    def second(k):
        b3[k] = second_factor(k)

    repeat(0, bins, second, 32)
    kept = pltpu.make_async_copy(b3, b3_hbm, out_sem)
    kept.start()
    for copy in late:
        copy.wait()
    correlate(
        *(0, count, scale, shares, me, a, b0, b2, b3, lag, work[-1], one, outs),
        lambda one_bin: repeat(0, bins, one_bin, 32),
    )
    kept.wait()


def rest_kernel(first, scale, shares, me_ref, *rest):
    lag_hbm, a_hbm, b0_hbm, b2_hbm, b3_hbm = rest[:5]
    outs, rest = rest[5 : 5 + shares], rest[5 + shares :]
    lag, a, b0, b2, b3, cross, one, lag_sem, sem = rest
    bins, count = b0.shape[0], a.shape[2]
    some = bins // STEPS

    def factors(n):
        part = pl.ds(n * some, some)
        return [
            pltpu.make_async_copy(source, target, sem.at[n, m])
            for m, (source, target) in enumerate(
                (
                    (b0_hbm.at[part], b0.at[part]),
                    (b2_hbm.at[part], b2.at[part]),
                    (b3_hbm.at[part], b3.at[part]),
                    (a_hbm.at[part, :, pl.ds(first, count)], a.at[part]),
                )
            )
        ]

    for n in range(STEPS):
        for copy in factors(n):
            copy.start()
    table = pltpu.make_async_copy(lag_hbm, lag, lag_sem)
    table.start()
    table.wait()

    def bins_loop(one_bin):
        def part(n, _):
            for copy in factors(n):
                copy.wait()
            repeat(0, some, lambda k: one_bin(n * some + k), some)
            return 0

        lax.fori_loop(0, STEPS, part, 0)

    correlate(first, count, scale, shares, me_ref[0], a, b0, b2, b3, lag, cross, one, outs, bins_loop)


def stacks(places, shares, scale, me, flags, total, pieces, hann, conv, seg, lag, a, b0, b2):
    bins, depth, chans = b0.shape
    width = chans // 2
    count = width // 2
    _, wins, ns = pieces[0].shape
    nlag, nfr = lag.shape
    smem = pl.BlockSpec(memory_space=pltpu.SMEM)
    vmem = pl.BlockSpec(memory_space=pltpu.VMEM)
    anywhere = pl.BlockSpec(memory_space=pl.ANY)
    out = [jax.ShapeDtypeStruct((count, OFFS // shares, nlag), BF16)] * shares
    operands = [*pieces, total, hann, conv, seg, lag, a, b0, b2]
    held = [pieces[0], pieces[1], pieces[4], total, hann, conv, seg, lag, b0, b2]
    some_a = pltpu.VMEM((bins, 2, count, depth), BF16)
    one = pltpu.VMEM((2, chans + width, chans), F32)
    params = pltpu.CompilerParams(vmem_limit_bytes=VMEM)
    cost = pl.CostEstimate(
        flops=2 * count * bins * 4 * (2 * depth * chans + 2 * OFFS * chans),
        bytes_accessed=20 * 1024 * 1024,
        transcendentals=0,
    )
    *head, b3 = pl.pallas_call(
        functools.partial(last_kernel, places, scale, shares),
        out_shape=out + [jax.ShapeDtypeStruct(b0.shape, BF16)],
        in_specs=[smem] * 2 + [anywhere] * len(operands),
        out_specs=[vmem] * shares + [anywhere],
        scratch_shapes=[pltpu.VMEM(value.shape, value.dtype) for value in held]
        + work_shapes(1, chans, wins, ns)
        + [
            some_a,
            pltpu.VMEM(b0.shape, BF16),
            one,
            pltpu.SemaphoreType.DMA((8 + chans // PART,)),
            pltpu.SemaphoreType.DMA((3,)),
            pltpu.SemaphoreType.DMA,
        ],
        compiler_params=params,
        cost_estimate=cost,
    )(me, flags, *operands)
    tail = pl.pallas_call(
        functools.partial(rest_kernel, count, scale, shares),
        out_shape=out,
        in_specs=[smem] + [anywhere] * 5,
        out_specs=[vmem] * shares,
        scratch_shapes=[
            pltpu.VMEM(lag.shape, BF16),
            some_a,
            *[pltpu.VMEM(b0.shape, BF16)] * 3,
            pltpu.VMEM((2, count * (nfr + 1), chans), F32),
            one,
            pltpu.SemaphoreType.DMA,
            pltpu.SemaphoreType.DMA((STEPS, 4)),
        ],
        compiler_params=params,
        cost_estimate=cost,
    )(me, lag, a, b0, b2, b3)
    return head, tail


def add_over(value, axis, beside):
    count = lax.axis_size(axis)
    if count & (count - 1):
        return lax.psum(value, axis), beside
    bit = 1
    while bit < count:
        steps = [bit] if bit == 1 or 2 * bit == count else [bit, 2 * bit, 3 * bit]
        arrived = [lax.ppermute(value, axis, [(i, i ^ s) for i in range(count)]) for s in steps]
        bit *= 1 + len(steps)
        if bit == count:
            arrived, beside = lax.optimization_barrier((arrived, beside))
        value = sum(arrived, value)
    return value, beside


def shards(samples, band_gain, dead_flags, section_ids):
    chans, wins, ns = samples.shape
    nf = ns // 2
    width = chans // 2
    blocks = lax.axis_size("fibre")
    groups = lax.axis_size("tm")
    me = lax.axis_index("tm")
    odd = me % 2
    window, waves, seg, lag = tables(ns, nf)
    waves, seg, lag = jnp.asarray(waves), jnp.asarray(seg), jnp.asarray(lag)
    hann = jnp.asarray(window[None, :])
    response = jnp.sum(band_gain[:, None] * waves, axis=0, keepdims=True)
    swap = [(z, z ^ 1) for z in range(groups)]
    both = ("fibre", "tm")
    halo_pairs = [
        (b * groups + z, (b + (1 if z % 2 else -1)) % blocks * groups + z)
        for b in range(blocks)
        for z in range(groups)
    ]

    head = width * 5 // 8

    their_head = lax.ppermute(
        lax.dynamic_slice_in_dim(samples, (1 - odd) * width, head, 0), "tm", swap
    )
    flags = jnp.stack([dead_flags, section_ids])
    halo_flags = lax.ppermute(
        lax.dynamic_slice_in_dim(flags, odd * width, width, 1), both, halo_pairs
    )
    smem = pl.BlockSpec(memory_space=pltpu.SMEM)
    anywhere = pl.BlockSpec(memory_space=pl.ANY)
    sums, own_half, tail = pl.pallas_call(
        section_sums,
        out_shape=[
            jax.ShapeDtypeStruct((NSEC, wins, ns + LANE), F32),
            jax.ShapeDtypeStruct((width, wins, ns), BF16),
            jax.ShapeDtypeStruct((width - head, wins, ns), BF16),
        ],
        in_specs=[smem] * 3 + [anywhere],
        out_specs=[pl.BlockSpec(memory_space=pltpu.VMEM), anywhere, anywhere],
        scratch_shapes=[
            pltpu.VMEM(samples.shape, BF16),
            pltpu.SemaphoreType.DMA((STEPS,)),
            pltpu.SemaphoreType.DMA((2,)),
        ],
        compiler_params=pltpu.CompilerParams(vmem_limit_bytes=VMEM),
        cost_estimate=pl.CostEstimate(flops=1, bytes_accessed=1, transcendentals=0),
    )(odd[None], dead_flags, section_ids, samples)
    total, their_head = add_over(sums, "fibre", their_head)
    halo_source, halo_flags = lax.optimization_barrier((own_half, halo_flags))
    halo = lax.ppermute(halo_source, both, halo_pairs)
    total, response, own_half, tail = lax.optimization_barrier(
        (total, response, own_half, tail)
    )
    conv = pl.pallas_call(
        circulant_kernel,
        out_shape=jax.ShapeDtypeStruct((TILE, ns), BF16),
        compiler_params=pltpu.CompilerParams(vmem_limit_bytes=VMEM),
        cost_estimate=pl.CostEstimate(flops=1, bytes_accessed=1, transcendentals=0),
    )(response)
    their_total = lax.ppermute(total, "tm", swap)
    their_tail = lax.ppermute(tail, "tm", swap)
    their_second = lax.ppermute(own_half, "tm", swap)
    ready = (total, their_total, their_head, flags, hann, conv, seg, lag)
    ready = lax.optimization_barrier(ready)
    total, their_total, their_head, flags, hann, conv, seg, lag = ready
    halo_head = lax.ppermute(their_head, both, halo_pairs)

    side = odd[None]
    parts = (hann, conv, seg)
    every = jnp.concatenate([flags, halo_flags], axis=1)
    b0, series = segments(((0, (0, 0), (0, 0)),), side, flags, (total,), (samples,), None, *parts)
    b0, forward = lax.optimization_barrier((b0, their_tail))
    halo_tail = lax.ppermute(forward, both, halo_pairs)
    a, b2 = segments(
        (
            (1, (0, 0), (0, chans)),
            (1, (head, head), (head, chans + head)),
            (0, (width, width), (chans, chans)),
        ),
        side,
        every,
        (total, their_total),
        (their_head, their_tail, halo_head, halo_tail, halo),
        series,
        *parts,
    )
    scale = 2.0 / ns / LAGS / math.sqrt(nf * wins * groups)
    found = stacks(
        (
            (0, (0, width), (chans, width)),
            (0, (head, width + head), (chans + head, width + head)),
            (0, (width, 0), (width, 0)),
        ),
        groups,
        scale,
        me[None],
        every,
        their_total,
        (halo_head, halo_tail, their_head, their_tail, their_second),
        *(hann, conv, seg, lag),
        *(a, b0, b2),
    )
    lower, upper = [], []
    for part in found:
        arrived = {}
        for d in reversed(range(groups)):
            pairs = [
                (b * groups + z, (b - z % 2) % blocks * groups + (z ^ d))
                for b in range(blocks)
                for z in range(groups)
            ]
            arrived[d] = lax.ppermute(part[d], both, pairs)
        arrived = [arrived[d].astype(F32) for d in range(groups)]
        same = sum(arrived[2::2], arrived[0])
        other = sum(arrived[3::2], arrived[1])
        lower.append(jnp.where(odd == 0, same, other))
        upper.append(jnp.where(odd == 0, other, same))
    return jnp.concatenate(lower + upper, axis=0)


def solution(mesh):
    in_specs = (P("fibre", "tm", None), P(), P("fibre"), P("fibre"))
    out_specs = P("fibre", "tm", None)
    return jax.shard_map(shards, mesh=mesh, in_specs=in_specs, out_specs=out_specs, check_vma=False)
```

```python
import functools
import math

import jax
import jax.numpy as jnp
import ml_dtypes
import numpy as np
from jax import lax
from jax.experimental import pallas as pl
from jax.experimental.pallas import tpu as pltpu
from jax.sharding import PartitionSpec as P

OFFS = 128
LAGS = 128
NSEC = 2
LANE = 128
PART = 32
TILE = 256
STEPS = 4
SENDS = 8
TOGETHER = 4
VMEM = 63 * 1024 * 1024
NT = (((1,), (1,)), ((), ()))
F32 = jnp.float32
BF16 = jnp.bfloat16


def tables(ns, nf):
    tick = np.arange(ns)
    freq = np.arange(nf)
    window = 0.5 - 0.5 * np.cos(tick * (2.0 * math.pi / ns))
    waves = np.cos((freq[:, None] * tick[None, :] % ns) * (2.0 * math.pi / ns))
    waves[0] *= math.sqrt(0.5)
    size = 2 * LAGS
    bins = np.arange(size // 2)
    turn = math.pi / size * ((2 * bins[:, None] + 1) * np.arange(size)[None, :] % (2 * size))
    segment = np.stack([np.cos(turn), -np.sin(turn)], axis=1).reshape(size, size)
    lag = np.stack([np.cos(turn), -np.sin(turn)], axis=1).reshape(size, size)[:, :LAGS].T
    cast = lambda a: a.astype(np.float32).astype(ml_dtypes.bfloat16)
    return window.astype(np.float32), waves.astype(np.float32), cast(segment), cast(lag)


def section_sums(odd_ref, dead_ref, sec_ref, x_hbm, out_ref, half_hbm, tail_hbm, x, in_sem, sem):
    chans, wins, ns = x.shape
    width, length = half_hbm.shape[0], tail_hbm.shape[0]
    odd = odd_ref[0]
    part = chans // STEPS
    arriving = [
        pltpu.make_async_copy(
            x_hbm.at[pl.ds(n * part, part)], x.at[pl.ds(n * part, part)], in_sem.at[n]
        )
        for n in range(STEPS)
    ]
    for copy in arriving:
        copy.start()
    leaving = [
        pltpu.make_async_copy(x.at[pl.ds(odd * width, width)], half_hbm, sem.at[0]),
        pltpu.make_async_copy(
            x.at[pl.ds((2 - odd) * width - length, length)], tail_hbm, sem.at[1]
        ),
    ]

    def body(c, carry):
        value = x[c].astype(F32)
        live = 1 - dead_ref[c]
        sums, counts = carry
        weights = [jnp.where(sec_ref[c] == s, live, 0).astype(F32) for s in range(NSEC)]
        return (
            tuple(sums[s] + weights[s] * value for s in range(NSEC)),
            tuple(counts[s] + weights[s] for s in range(NSEC)),
        )

    zero = jnp.zeros((wins, ns), F32)
    carry = ((zero,) * NSEC, (jnp.float32(0),) * NSEC)
    for n, copy in enumerate(arriving):
        copy.wait()
        if n == STEPS - 1:
            for out in leaving:
                out.start()
        carry = lax.fori_loop(n * part, (n + 1) * part, body, carry, unroll=8)
    sums, counts = carry
    for s in range(NSEC):
        out_ref[s, :, :ns] = sums[s]
        out_ref[s, :, ns:] = jnp.zeros((wins, LANE), F32) + counts[s]
    for out in leaving:
        out.wait()


def circulant_kernel(filter_ref, out_ref):
    ns = filter_ref.shape[1]
    for t in range(0, TILE, 16):
        block = jnp.broadcast_to(filter_ref[...], (16, ns))
        out_ref[t : t + 16, :] = pltpu.roll(block, t, 1, stride=1, stride_axis=0).astype(BF16)


def segment_factors(places, odd, flag_ref, tot, x, hann, conv, seg, work, copied, first=None, save=None):
    common, clean, mass, square, rows, series_all, stage = work
    _, wins, ns = x[0].shape
    chans = sum(piece.shape[0] for piece in x)
    pitch = wins + 1
    size = seg.shape[0]
    half = size // 2
    blocks = ns // half
    jw = blocks * wins
    jpitch = jw + 1
    for copy in copied["first"]:
        copy.wait()
    for g in range(len(tot)):
        for s in range(NSEC):
            common[g * NSEC + s] = tot[g][s, :, :ns] / jnp.maximum(tot[g][s, :, ns : ns + 1], 1.0)
    sign = 1.0 - 2.0 * (lax.broadcasted_iota(jnp.int32, (chans, LANE), 1) % 2).astype(F32)

    for number, (group, base, flags) in enumerate(places):
        piece = x[number]
        length = piece.shape[0]
        base = base[0] + odd * (base[1] - base[0])
        flags = flags[0] + odd * (flags[1] - flags[0])

        def clean_channel(c):
            at = base + c
            flag = flags + c
            live = (1 - flag_ref[0, flag]).astype(F32)
            value = (piece[c].astype(F32) - common[group * NSEC + flag_ref[1, flag]]) * (
                hann[...] * live
            )
            tiles = [value[:, t * LANE : (t + 1) * LANE] for t in range(ns // LANE)]
            row = pl.ds(at * pitch, wins)
            mass[row, :] = sum(tiles[1:], tiles[0])
            square[row, :] = sum([tile * tile for tile in tiles[1:]], tiles[0] * tiles[0])
            for t, tile in enumerate(tiles):
                clean[t, row, :] = tile

        parts = copied["x"][number]
        part = length // len(parts)
        for n, copy in enumerate(parts):
            copy.wait()
            repeat(n * part, (n + 1) * part, clean_channel, 16)
    for copy in copied["tables"]:
        copy.wait()

    for step in range(wins // TOGETHER):
        series = series_all.at[step]
        for i in range(TOGETHER):
            window = pl.ds(step * TOGETHER + i, chans, stride=pitch)
            total = mass[window, :]
            lowest = jnp.sum(total, axis=1, keepdims=True)
            highest = jnp.sum(total * sign, axis=1, keepdims=True)
            power = 0.5 * jnp.sum(square[window, :], axis=1, keepdims=True)
            power = power + (lowest * lowest - highest * highest) * (0.5 / ns)
            level = lax.rsqrt(power + 1e-06)
            for t in range(ns // LANE):
                rows[i * chans : (i + 1) * chans, t * LANE : (t + 1) * LANE] = (
                    clean[t, window, :] * level
                ).astype(BF16)
        for t in range(0, ns, TILE):
            turned = jnp.concatenate([conv[:, ns - t :], conv[:, : ns - t]], axis=1) if t else conv[...]
            series[half // 2 + t : half // 2 + t + TILE, :] = lax.dot_general(
                turned, rows[...], NT, preferred_element_type=F32
            ).astype(BF16)
        series[: half // 2, :] = series[ns : ns + half // 2, :]
        series[ns + half // 2 :, :] = series[half // 2 : half, :]
        if save is not None:
            save(step)

        def place(which, j, value):
            for i in range(TOGETHER):
                at = j * wins + step * TOGETHER + i
                stage[which, pl.ds(at, size, stride=jpitch), :] = value[
                    :, i * chans : (i + 1) * chans
                ]

        for j in range(blocks):
            start = j * half + half // 2
            b = jnp.dot(
                seg[:, :half], series[start : start + half, :], preferred_element_type=F32
            )
            place(1, j, b)

        if first is not None:
            source = first(step, series)
            for j in range(blocks):
                a = jnp.dot(
                    seg[...], source[j * half : j * half + size, :], preferred_element_type=F32
                )
                place(0, j, a)

    def parts(which, k):
        return [
            stage[which, pl.ds((2 * k + part) * jpitch, jw), :].astype(BF16) for part in range(2)
        ]

    lower = lax.broadcasted_iota(jnp.int32, (1, chans), 1) < chans // 2

    def first_factor(k):
        real, imag = parts(0, k)
        return jnp.concatenate(
            [jnp.where(lower, imag, real), jnp.where(lower, real, imag)], axis=0
        ).T

    return first_factor, lambda k: jnp.concatenate(parts(1, k), axis=0)


def work_shapes(groups, chans, wins, ns):
    half = LAGS
    rows = 2 * half * (ns // half * wins + 1)
    return [
        pltpu.VMEM((groups * NSEC, wins, ns), F32),
        pltpu.VMEM((ns // LANE, chans * (wins + 1), LANE), F32),
        pltpu.VMEM((chans * (wins + 1), LANE), F32),
        pltpu.VMEM((chans * (wins + 1), LANE), F32),
        pltpu.VMEM((TOGETHER * chans, ns), BF16),
        pltpu.VMEM((wins // TOGETHER, ns + half, TOGETHER * chans), BF16),
        pltpu.VMEM((2, rows, chans), F32),
    ]


def repeat(start, stop, body, together):
    def step(n, _):
        body(n)
        return 0

    lax.fori_loop(start, stop, step, 0, unroll=math.gcd(together, stop - start))


class Choice:
    def __init__(self, odd, sources, target, sem):
        self.options = [
            (odd == side, pltpu.make_async_copy(source, target, sem))
            for side, source in enumerate(sources)
        ]

    def start(self):
        for here, copy in self.options:
            pl.when(here)(copy.start)

    def wait(self):
        for here, copy in self.options:
            pl.when(here)(copy.wait)


def input_copies(odd, first, x, tables_in, sem):
    copied = {"first": [], "x": [], "tables": []}
    used = 0

    def copy(source, target):
        nonlocal used
        if isinstance(source, tuple):
            made = Choice(odd, source, target, sem.at[used])
        else:
            made = pltpu.make_async_copy(source, target, sem.at[used])
        made.start()
        used += 1
        return made

    copied["first"] = [copy(*pair) for pair in first]
    for source, target in x:
        parts = max(target.shape[0] // PART, 1)
        part = target.shape[0] // parts
        rows = [pl.ds(n * part, part) for n in range(parts)]
        copied["x"].append(
            [
                copy(
                    tuple(option.at[here] for option in source)
                    if isinstance(source, tuple)
                    else source.at[here],
                    target.at[here],
                )
                for here in rows
            ]
        )
    copied["tables"] = [copy(*pair) for pair in tables_in]
    return copied


def own_kernel(places, odd_ref, flag_ref, *rest):
    tot_hbm, x_hbm, hann_hbm, conv_hbm, seg_hbm, b_hbm, p_hbm = rest[:7]
    tot, x, hann, conv, seg = rest[7:12]
    work, (b_out, in_sem, out_sem, p_sem) = rest[12:-4], rest[-4:]
    odd = odd_ref[0]
    copied = input_copies(
        odd,
        [(tot_hbm, tot), (hann_hbm, hann)],
        [(x_hbm, x)],
        [(conv_hbm, conv), (seg_hbm, seg)],
        in_sem,
    )
    kept = [
        pltpu.make_async_copy(work[-2].at[step], p_hbm.at[step], p_sem.at[step])
        for step in range(p_hbm.shape[0])
    ]
    _, second = segment_factors(
        *(places, odd, flag_ref, [tot], [x], hann, conv, seg, work, copied),
        save=lambda step: kept[step].start(),
    )

    def put_second(k, stage):
        stage[k] = second(k)

    send_factor(put_second, b_out, b_hbm, out_sem)
    for copy in kept:
        copy.wait()


def send_factor(factor, stage, target, sem):
    step = stage.shape[0] // SENDS
    copies = []
    for n in range(SENDS):
        part = pl.ds(n * step, step)

        repeat(n * step, (n + 1) * step, lambda k: factor(k, stage), 32)
        copies.append(pltpu.make_async_copy(stage.at[part], target.at[part], sem.at[n]))
        copies[-1].start()
    for copy in copies:
        copy.wait()


def second_kernel(places, odd_ref, flag_ref, *rest):
    tot_hbm, (even_hbm, odd_hbm), rest = rest[:2], (rest[2:4], rest[4:6]), rest[6:]
    halo_hbm, hann_hbm, conv_hbm, seg_hbm, p_hbm, a_hbm, b_hbm = rest[:7]
    tot, x, rest = rest[7:9], rest[9:12], rest[12:]
    hann, conv, seg, own, mixed, a_out, b_out = rest[:7]
    work, (in_sem, p_sem, out_sem) = rest[7:-3], rest[-3:]
    odd = odd_ref[0]
    copied = input_copies(
        odd,
        list(zip(tot_hbm, tot)) + [(hann_hbm, hann)],
        list(zip(zip(even_hbm, odd_hbm), x)) + [(halo_hbm, x[2])],
        [(conv_hbm, conv), (seg_hbm, seg)],
        in_sem,
    )
    kept = pltpu.make_async_copy(p_hbm, own, p_sem)
    kept.start()
    copied["tables"].append(kept)
    chans = b_out.shape[2]
    lane = lax.broadcasted_iota(jnp.int32, (1, chans), 1)

    def first(step, series):
        @pl.when(odd == 1)
        def _():
            mixed[...] = series[...]

        @pl.when(odd == 0)
        def _():
            for i in range(TOGETHER):
                columns = slice(i * chans, (i + 1) * chans)
                value = own[step, :, columns]
                turned = jnp.concatenate([value[:, chans // 2 :], value[:, : chans // 2]], axis=1)
                mixed[:, columns] = jnp.where(lane < chans // 2, series[:, columns], turned)

        return mixed

    first_factor, second_factor = segment_factors(
        places, odd, flag_ref, tot, x, hann, conv, seg, work, copied, first
    )

    def both_factors(k, stage):
        value = first_factor(k)
        width = value.shape[0] // 2
        a_out[k, 1] = value[:width]
        a_out[k, 0] = value[width:]
        stage[k] = second_factor(k)

    step = b_out.shape[0] // SENDS
    copies = []
    for n in range(SENDS):
        part = pl.ds(n * step, step)

        repeat(n * step, (n + 1) * step, lambda k: both_factors(k, b_out), 16)
        for m, (source, target) in enumerate(((a_out, a_hbm), (b_out, b_hbm))):
            copies.append(
                pltpu.make_async_copy(source.at[part], target.at[part], out_sem.at[2 * n + m])
            )
            copies[-1].start()
    for copy in copies:
        copy.wait()


def segments(places, side, flags, totals, pieces, series, hann, conv, seg):
    chans = LANE
    _, wins, ns = pieces[0].shape
    size = seg.shape[0]
    half = size // 2
    depth = ns // half * wins * 2
    smem = pl.BlockSpec(memory_space=pltpu.SMEM)
    anywhere = pl.BlockSpec(memory_space=pl.ANY)
    b_shape = jax.ShapeDtypeStruct((half, depth, chans), BF16)
    p_shape = jax.ShapeDtypeStruct((wins // TOGETHER, ns + half, TOGETHER * chans), BF16)
    a_shape = jax.ShapeDtypeStruct((half, 2, chans // 2, depth), BF16)
    scratch = lambda *values: [pltpu.VMEM(value.shape, value.dtype) for value in values]
    operands = list(totals) + list(pieces) + [hann, conv, seg]
    count = len(operands) + chans // PART
    if series is None:
        kernel, out = own_kernel, [b_shape, p_shape]
        held = scratch(*operands)
        last = scratch(b_shape) + [
            pltpu.SemaphoreType.DMA((count,)),
            pltpu.SemaphoreType.DMA((SENDS,)),
            pltpu.SemaphoreType.DMA((wins // TOGETHER,)),
        ]
    else:
        kernel, out = second_kernel, [a_shape, b_shape]
        held = scratch(*totals, pieces[0], pieces[1], pieces[4], hann, conv, seg, series)
        held += [pltpu.VMEM(p_shape.shape[1:], BF16)] + scratch(a_shape, b_shape)
        last = [
            pltpu.SemaphoreType.DMA((count,)),
            pltpu.SemaphoreType.DMA,
            pltpu.SemaphoreType.DMA((2 * SENDS,)),
        ]
        operands.append(series)
    return pl.pallas_call(
        functools.partial(kernel, places),
        out_shape=out,
        in_specs=[smem] * 2 + [anywhere] * len(operands),
        out_specs=[anywhere] * 2,
        scratch_shapes=held + work_shapes(len(totals), chans, wins, ns) + last,
        compiler_params=pltpu.CompilerParams(vmem_limit_bytes=VMEM),
        cost_estimate=pl.CostEstimate(
            flops=2 * wins * chans * ns * (ns + 3 * size),
            bytes_accessed=16 * 1024 * 1024,
            transcendentals=0,
        ),
    )(side, flags, *operands)


def correlate(first, count, scale, shares, me, a, b0, b2, b3, lag, cross, one, outs, bins_loop):
    depth, chans = b0.shape[1:]
    width = chans // 2
    nfr = lag.shape[1]
    pitch = nfr + 1
    odd = lax.rem(me, 2)
    lane = lax.broadcasted_iota(jnp.int32, (1, chans), 1)
    low, high = [jnp.where((lane < width) == (g == 0), 1.0, 0.0).astype(BF16) for g in range(2)]
    lower = lane < width

    def bins_with(near, far):
        def one_bin(k):
            inner = near[k] * low + b3[k] * high if near is not b3 else b3[k]
            own = jnp.concatenate([b0[k], b2[k] * high], axis=1)
            theirs = jnp.concatenate([inner, far[k] * low], axis=1)
            part = depth // 2
            right = jnp.concatenate([own[:part], theirs[:part], theirs[part:], own[part:]], axis=0)
            real = jnp.where(lower, a[k, 0], a[k, 1])
            imag = jnp.where(lower, a[k, 1], a[k, 0])
            turn = lambda v: jnp.concatenate([v[:, part:], v[:, :part]], axis=1)
            left = jnp.concatenate(
                [
                    jnp.concatenate([real, imag], axis=1),
                    jnp.concatenate([turn(imag), -turn(real)], axis=1),
                ],
                axis=0,
            )
            value = jnp.dot(left, right, preferred_element_type=F32)
            for p in range(2):
                for t in range(2):
                    cross[t, pl.ds(2 * k + p, count, stride=pitch), :] = value[
                        p * count : (p + 1) * count, t * chans : (t + 1) * chans
                    ]

        bins_loop(one_bin)

    pl.when(odd == 0)(lambda: bins_with(b2, b3))
    pl.when(odd == 1)(lambda: bins_with(b3, b2))

    row = lax.broadcasted_iota(jnp.int32, one.shape[1:], 0)
    column = lax.broadcasted_iota(jnp.int32, one.shape[1:], 1)
    turned = jnp.where(row < width, row + chans, row - width)
    place = row + (turned - row) * odd
    for t in range(2):
        here = column + t * chans
        found = (place == here) | ((here >= chans + width) & (place == here - width))
        one[t] = jnp.where(found, 1.0, 0.0)
    share = OFFS // shares

    def one_channel(c):
        value = jnp.concatenate(
            [cross[t, pl.ds(c * pitch, nfr), :] for t in range(2)], axis=1
        ).astype(BF16)
        starts = [first + c + 1 + share * (me ^ d) for d in range(shares)]
        pick = jnp.concatenate(
            [
                jnp.concatenate([one[t, pl.ds(start, share), :] for start in starts], axis=0)
                for t in range(2)
            ],
            axis=1,
        ).astype(BF16)
        lagged = jnp.dot(lag[...], value, preferred_element_type=F32) * scale
        band = lax.dot_general(pick, lagged.astype(BF16), NT, preferred_element_type=F32)
        for d, out in enumerate(outs):
            out[c] = band[d * share : (d + 1) * share, :].astype(BF16)

    repeat(0, count, one_channel, 16)


def last_kernel(places, scale, shares, me_ref, flag_ref, *rest):
    even_hbm, odd_hbm, late_hbm, rest = rest[:2], rest[2:4], rest[4], rest[5:]
    tot_hbm, hann_hbm, conv_hbm, seg_hbm, lag_hbm = rest[:5]
    a_hbm, b0_hbm, b2_hbm, rest = *rest[5:8], rest[8:]
    outs, b3_hbm, rest = rest[:shares], rest[shares], rest[shares + 1 :]
    x, rest = rest[:3], rest[3:]
    tot, hann, conv, seg, lag, b0, b2 = rest[:7]
    work, (a, b3, one, in_sem, late_sem, out_sem) = rest[7:-6], rest[-6:]
    me = me_ref[0]
    odd = lax.rem(me, 2)
    copied = input_copies(
        odd,
        [(tot_hbm, tot), (hann_hbm, hann)],
        list(zip(zip(even_hbm, odd_hbm), x)) + [(late_hbm, x[2])],
        [(conv_hbm, conv), (seg_hbm, seg), (lag_hbm, lag)],
        in_sem,
    )
    count = a.shape[2]
    late = [
        pltpu.make_async_copy(source, target, late_sem.at[n])
        for n, (source, target) in enumerate(
            ((b0_hbm, b0), (b2_hbm, b2), (a_hbm.at[:, :, pl.ds(0, count)], a))
        )
    ]
    for copy in late:
        copy.start()
    _, second_factor = segment_factors(
        places, odd, flag_ref, [tot], x, hann, conv, seg, work, copied
    )
    bins = b3.shape[0]

    def second(k):
        b3[k] = second_factor(k)

    repeat(0, bins, second, 32)
    kept = pltpu.make_async_copy(b3, b3_hbm, out_sem)
    kept.start()
    for copy in late:
        copy.wait()
    correlate(
        *(0, count, scale, shares, me, a, b0, b2, b3, lag, work[-1], one, outs),
        lambda one_bin: repeat(0, bins, one_bin, 32),
    )
    kept.wait()


def rest_kernel(first, scale, shares, me_ref, *rest):
    lag_hbm, a_hbm, b0_hbm, b2_hbm, b3_hbm = rest[:5]
    outs, rest = rest[5 : 5 + shares], rest[5 + shares :]
    lag, a, b0, b2, b3, cross, one, lag_sem, sem = rest
    bins, count = b0.shape[0], a.shape[2]
    some = bins // STEPS

    def factors(n):
        part = pl.ds(n * some, some)
        return [
            pltpu.make_async_copy(source, target, sem.at[n, m])
            for m, (source, target) in enumerate(
                (
                    (b0_hbm.at[part], b0.at[part]),
                    (b2_hbm.at[part], b2.at[part]),
                    (b3_hbm.at[part], b3.at[part]),
                    (a_hbm.at[part, :, pl.ds(first, count)], a.at[part]),
                )
            )
        ]

    for n in range(STEPS):
        for copy in factors(n):
            copy.start()
    table = pltpu.make_async_copy(lag_hbm, lag, lag_sem)
    table.start()
    table.wait()

    def bins_loop(one_bin):
        def part(n, _):
            for copy in factors(n):
                copy.wait()
            repeat(0, some, lambda k: one_bin(n * some + k), some)
            return 0

        lax.fori_loop(0, STEPS, part, 0)

    correlate(first, count, scale, shares, me_ref[0], a, b0, b2, b3, lag, cross, one, outs, bins_loop)


def stacks(places, shares, scale, me, flags, total, pieces, hann, conv, seg, lag, a, b0, b2):
    bins, depth, chans = b0.shape
    width = chans // 2
    count = width // 2
    _, wins, ns = pieces[0].shape
    nlag, nfr = lag.shape
    smem = pl.BlockSpec(memory_space=pltpu.SMEM)
    vmem = pl.BlockSpec(memory_space=pltpu.VMEM)
    anywhere = pl.BlockSpec(memory_space=pl.ANY)
    out = [jax.ShapeDtypeStruct((count, OFFS // shares, nlag), BF16)] * shares
    operands = [*pieces, total, hann, conv, seg, lag, a, b0, b2]
    held = [pieces[0], pieces[1], pieces[4], total, hann, conv, seg, lag, b0, b2]
    some_a = pltpu.VMEM((bins, 2, count, depth), BF16)
    one = pltpu.VMEM((2, chans + width, chans), F32)
    params = pltpu.CompilerParams(vmem_limit_bytes=VMEM)
    cost = pl.CostEstimate(
        flops=2 * count * bins * 4 * (2 * depth * chans + 2 * OFFS * chans),
        bytes_accessed=20 * 1024 * 1024,
        transcendentals=0,
    )
    *head, b3 = pl.pallas_call(
        functools.partial(last_kernel, places, scale, shares),
        out_shape=out + [jax.ShapeDtypeStruct(b0.shape, BF16)],
        in_specs=[smem] * 2 + [anywhere] * len(operands),
        out_specs=[vmem] * shares + [anywhere],
        scratch_shapes=[pltpu.VMEM(value.shape, value.dtype) for value in held]
        + work_shapes(1, chans, wins, ns)
        + [
            some_a,
            pltpu.VMEM(b0.shape, BF16),
            one,
            pltpu.SemaphoreType.DMA((8 + chans // PART,)),
            pltpu.SemaphoreType.DMA((3,)),
            pltpu.SemaphoreType.DMA,
        ],
        compiler_params=params,
        cost_estimate=cost,
    )(me, flags, *operands)
    tail = pl.pallas_call(
        functools.partial(rest_kernel, count, scale, shares),
        out_shape=out,
        in_specs=[smem] + [anywhere] * 5,
        out_specs=[vmem] * shares,
        scratch_shapes=[
            pltpu.VMEM(lag.shape, BF16),
            some_a,
            *[pltpu.VMEM(b0.shape, BF16)] * 3,
            pltpu.VMEM((2, count * (nfr + 1), chans), F32),
            one,
            pltpu.SemaphoreType.DMA,
            pltpu.SemaphoreType.DMA((STEPS, 4)),
        ],
        compiler_params=params,
        cost_estimate=cost,
    )(me, lag, a, b0, b2, b3)
    return head, tail


def add_over(value, axis, beside):
    count = lax.axis_size(axis)
    if count & (count - 1):
        return lax.psum(value, axis), beside
    bit = 1
    while bit < count:
        steps = [bit] if bit == 1 or 2 * bit == count else [bit, 2 * bit, 3 * bit]
        arrived = [lax.ppermute(value, axis, [(i, i ^ s) for i in range(count)]) for s in steps]
        bit *= 1 + len(steps)
        if bit == count:
            arrived, beside = lax.optimization_barrier((arrived, beside))
        value = sum(arrived, value)
    return value, beside


def shards(samples, band_gain, dead_flags, section_ids):
    chans, wins, ns = samples.shape
    nf = ns // 2
    width = chans // 2
    blocks = lax.axis_size("fibre")
    groups = lax.axis_size("tm")
    me = lax.axis_index("tm")
    odd = me % 2
    window, waves, seg, lag = tables(ns, nf)
    waves, seg, lag = jnp.asarray(waves), jnp.asarray(seg), jnp.asarray(lag)
    hann = jnp.asarray(window[None, :])
    response = jnp.sum(band_gain[:, None] * waves, axis=0, keepdims=True)
    swap = [(z, z ^ 1) for z in range(groups)]
    both = ("fibre", "tm")
    halo_pairs = [
        (b * groups + z, (b + (1 if z % 2 else -1)) % blocks * groups + z)
        for b in range(blocks)
        for z in range(groups)
    ]

    head = width * 5 // 8

    their_head = lax.ppermute(
        lax.dynamic_slice_in_dim(samples, (1 - odd) * width, head, 0), "tm", swap
    )
    flags = jnp.stack([dead_flags, section_ids])
    halo_flags = lax.ppermute(
        lax.dynamic_slice_in_dim(flags, odd * width, width, 1), both, halo_pairs
    )
    smem = pl.BlockSpec(memory_space=pltpu.SMEM)
    anywhere = pl.BlockSpec(memory_space=pl.ANY)
    sums, own_half, tail = pl.pallas_call(
        section_sums,
        out_shape=[
            jax.ShapeDtypeStruct((NSEC, wins, ns + LANE), F32),
            jax.ShapeDtypeStruct((width, wins, ns), BF16),
            jax.ShapeDtypeStruct((width - head, wins, ns), BF16),
        ],
        in_specs=[smem] * 3 + [anywhere],
        out_specs=[pl.BlockSpec(memory_space=pltpu.VMEM), anywhere, anywhere],
        scratch_shapes=[
            pltpu.VMEM(samples.shape, BF16),
            pltpu.SemaphoreType.DMA((STEPS,)),
            pltpu.SemaphoreType.DMA((2,)),
        ],
        compiler_params=pltpu.CompilerParams(vmem_limit_bytes=VMEM),
        cost_estimate=pl.CostEstimate(flops=1, bytes_accessed=1, transcendentals=0),
    )(odd[None], dead_flags, section_ids, samples)
    total, their_head = add_over(sums, "fibre", their_head)
    halo_source, halo_flags = lax.optimization_barrier((own_half, halo_flags))
    halo = lax.ppermute(halo_source, both, halo_pairs)
    total, response, own_half, tail = lax.optimization_barrier(
        (total, response, own_half, tail)
    )
    conv = pl.pallas_call(
        circulant_kernel,
        out_shape=jax.ShapeDtypeStruct((TILE, ns), BF16),
        compiler_params=pltpu.CompilerParams(vmem_limit_bytes=VMEM),
        cost_estimate=pl.CostEstimate(flops=1, bytes_accessed=1, transcendentals=0),
    )(response)
    their_total = lax.ppermute(total, "tm", swap)
    their_tail = lax.ppermute(tail, "tm", swap)
    their_second = lax.ppermute(own_half, "tm", swap)
    ready = (total, their_total, their_head, flags, hann, conv, seg, lag)
    ready = lax.optimization_barrier(ready)
    total, their_total, their_head, flags, hann, conv, seg, lag = ready
    halo_head = lax.ppermute(their_head, both, halo_pairs)

    side = odd[None]
    parts = (hann, conv, seg)
    every = jnp.concatenate([flags, halo_flags], axis=1)
    b0, series = segments(((0, (0, 0), (0, 0)),), side, flags, (total,), (samples,), None, *parts)
    b0, forward = lax.optimization_barrier((b0, their_tail))
    halo_tail = lax.ppermute(forward, both, halo_pairs)
    a, b2 = segments(
        (
            (1, (0, 0), (0, chans)),
            (1, (head, head), (head, chans + head)),
            (0, (width, width), (chans, chans)),
        ),
        side,
        every,
        (total, their_total),
        (their_head, their_tail, halo_head, halo_tail, halo),
        series,
        *parts,
    )
    scale = 2.0 / ns / LAGS / math.sqrt(nf * wins * groups)
    found = stacks(
        (
            (0, (0, width), (chans, width)),
            (0, (head, width + head), (chans + head, width + head)),
            (0, (width, 0), (width, 0)),
        ),
        groups,
        scale,
        me[None],
        every,
        their_total,
        (halo_head, halo_tail, their_head, their_tail, their_second),
        *(hann, conv, seg, lag),
        *(a, b0, b2),
    )
    lower, upper = [], []
    for part in found:
        arrived = {}
        for d in reversed(range(groups)):
            pairs = [
                (b * groups + z, (b - z % 2) % blocks * groups + (z ^ d))
                for b in range(blocks)
                for z in range(groups)
            ]
            arrived[d] = lax.ppermute(part[d], both, pairs)
        arrived = [arrived[d].astype(F32) for d in range(groups)]
        same = sum(arrived[2::2], arrived[0])
        other = sum(arrived[3::2], arrived[1])
        lower.append(jnp.where(odd == 0, same, other))
        upper.append(jnp.where(odd == 0, other, same))
    return jnp.concatenate(lower + upper, axis=0)


def solution(mesh):
    in_specs = (P("fibre", "tm", None), P(), P("fibre"), P("fibre"))
    out_specs = P("fibre", "tm", None)
    return jax.shard_map(shards, mesh=mesh, in_specs=in_specs, out_specs=out_specs, check_vma=False)
```

```python
import functools
import math

import jax
import jax.numpy as jnp
import ml_dtypes
import numpy as np
from jax import lax
from jax.experimental import pallas as pl
from jax.experimental.pallas import tpu as pltpu
from jax.sharding import PartitionSpec as P

OFFS = 128
LAGS = 128
NSEC = 2
LANE = 128
PART = 32
TILE = 256
STEPS = 4
TOGETHER = 4
VMEM = 63 * 1024 * 1024
NT = (((1,), (1,)), ((), ()))
F32 = jnp.float32
BF16 = jnp.bfloat16


def tables(ns, nf):
    tick = np.arange(ns)
    freq = np.arange(nf)
    window = 0.5 - 0.5 * np.cos(tick * (2.0 * math.pi / ns))
    waves = np.cos((freq[:, None] * tick[None, :] % ns) * (2.0 * math.pi / ns))
    waves[0] *= math.sqrt(0.5)
    size = 2 * LAGS
    bins = np.arange(size // 2)
    turn = math.pi / size * ((2 * bins[:, None] + 1) * np.arange(size)[None, :] % (2 * size))
    segment = np.stack([np.cos(turn), -np.sin(turn)], axis=1).reshape(size, size)
    lag = np.stack([np.cos(turn), -np.sin(turn)], axis=1).reshape(size, size)[:, :LAGS].T
    cast = lambda a: a.astype(np.float32).astype(ml_dtypes.bfloat16)
    return window.astype(np.float32), waves.astype(np.float32), cast(segment), cast(lag)


def section_sums(odd_ref, dead_ref, sec_ref, x_hbm, out_ref, half_hbm, tail_hbm, x, in_sem, sem):
    chans, wins, ns = x.shape
    width, length = half_hbm.shape[0], tail_hbm.shape[0]
    odd = odd_ref[0]
    part = chans // STEPS
    arriving = [
        pltpu.make_async_copy(
            x_hbm.at[pl.ds(n * part, part)], x.at[pl.ds(n * part, part)], in_sem.at[n]
        )
        for n in range(STEPS)
    ]
    for copy in arriving:
        copy.start()
    leaving = [
        pltpu.make_async_copy(x.at[pl.ds(odd * width, width)], half_hbm, sem.at[0]),
        pltpu.make_async_copy(
            x.at[pl.ds((2 - odd) * width - length, length)], tail_hbm, sem.at[1]
        ),
    ]

    def body(c, carry):
        value = x[c].astype(F32)
        live = 1 - dead_ref[c]
        sums, counts = carry
        weights = [jnp.where(sec_ref[c] == s, live, 0).astype(F32) for s in range(NSEC)]
        return (
            tuple(sums[s] + weights[s] * value for s in range(NSEC)),
            tuple(counts[s] + weights[s] for s in range(NSEC)),
        )

    zero = jnp.zeros((wins, ns), F32)
    carry = ((zero,) * NSEC, (jnp.float32(0),) * NSEC)
    for n, copy in enumerate(arriving):
        copy.wait()
        if n == STEPS - 1:
            for out in leaving:
                out.start()
        carry = lax.fori_loop(n * part, (n + 1) * part, body, carry, unroll=8)
    sums, counts = carry
    for s in range(NSEC):
        out_ref[s, :, :ns] = sums[s]
        out_ref[s, :, ns:] = jnp.zeros((wins, LANE), F32) + counts[s]
    for out in leaving:
        out.wait()


def circulant_kernel(filter_ref, out_ref):
    ns = filter_ref.shape[1]
    for t in range(0, TILE, 16):
        block = jnp.broadcast_to(filter_ref[...], (16, ns))
        out_ref[t : t + 16, :] = pltpu.roll(block, t, 1, stride=1, stride_axis=0).astype(BF16)


def segment_factors(places, odd, flag_ref, tot, x, hann, conv, seg, work, copied, first=None):
    common, clean, mass, square, rows, series_all, stage = work
    _, wins, ns = x[0].shape
    chans = sum(piece.shape[0] for piece in x)
    pitch = wins + 1
    size = seg.shape[0]
    half = size // 2
    blocks = ns // half
    jw = blocks * wins
    jpitch = jw + 1
    for copy in copied["first"]:
        copy.wait()
    for g in range(len(tot)):
        for s in range(NSEC):
            common[g * NSEC + s] = tot[g][s, :, :ns] / jnp.maximum(tot[g][s, :, ns : ns + 1], 1.0)
    sign = 1.0 - 2.0 * (lax.broadcasted_iota(jnp.int32, (chans, LANE), 1) % 2).astype(F32)

    for number, (group, base, flags) in enumerate(places):
        piece = x[number]
        length = piece.shape[0]
        base = base[0] + odd * (base[1] - base[0])
        flags = flags[0] + odd * (flags[1] - flags[0])

        def clean_channel(c):
            at = base + c
            flag = flags + c
            live = (1 - flag_ref[0, flag]).astype(F32)
            value = (piece[c].astype(F32) - common[group * NSEC + flag_ref[1, flag]]) * (
                hann[...] * live
            )
            tiles = [value[:, t * LANE : (t + 1) * LANE] for t in range(ns // LANE)]
            row = pl.ds(at * pitch, wins)
            mass[row, :] = sum(tiles[1:], tiles[0])
            square[row, :] = sum([tile * tile for tile in tiles[1:]], tiles[0] * tiles[0])
            for t, tile in enumerate(tiles):
                clean[t, row, :] = tile

        parts = copied["x"][number]
        part = length // len(parts)
        for n, copy in enumerate(parts):
            copy.wait()
            repeat(n * part, (n + 1) * part, clean_channel, 16)
    for copy in copied["tables"]:
        copy.wait()

    for step in range(wins // TOGETHER):
        series = series_all.at[step]
        for i in range(TOGETHER):
            window = pl.ds(step * TOGETHER + i, chans, stride=pitch)
            total = mass[window, :]
            lowest = jnp.sum(total, axis=1, keepdims=True)
            highest = jnp.sum(total * sign, axis=1, keepdims=True)
            power = 0.5 * jnp.sum(square[window, :], axis=1, keepdims=True)
            power = power + (lowest * lowest - highest * highest) * (0.5 / ns)
            level = lax.rsqrt(power + 1e-06)
            for t in range(ns // LANE):
                rows[i * chans : (i + 1) * chans, t * LANE : (t + 1) * LANE] = (
                    clean[t, window, :] * level
                ).astype(BF16)
        for t in range(0, ns, TILE):
            turned = jnp.concatenate([conv[:, ns - t :], conv[:, : ns - t]], axis=1) if t else conv[...]
            series[half // 2 + t : half // 2 + t + TILE, :] = lax.dot_general(
                turned, rows[...], NT, preferred_element_type=F32
            ).astype(BF16)
        series[: half // 2, :] = series[ns : ns + half // 2, :]
        series[ns + half // 2 :, :] = series[half // 2 : half, :]

        def place(which, j, value):
            for i in range(TOGETHER):
                at = j * wins + step * TOGETHER + i
                stage[which, pl.ds(at, size, stride=jpitch), :] = value[
                    :, i * chans : (i + 1) * chans
                ]

        for j in range(blocks):
            start = j * half + half // 2
            b = jnp.dot(
                seg[:, :half], series[start : start + half, :], preferred_element_type=F32
            )
            place(1, j, b)

        if first is not None:
            source = first(step, series)
            for j in range(blocks):
                a = jnp.dot(
                    seg[...], source[j * half : j * half + size, :], preferred_element_type=F32
                )
                place(0, j, a)

    def parts(which, k):
        return [
            stage[which, pl.ds((2 * k + part) * jpitch, jw), :].astype(BF16) for part in range(2)
        ]

    lower = lax.broadcasted_iota(jnp.int32, (1, chans), 1) < chans // 2

    def first_factor(k):
        real, imag = parts(0, k)
        return jnp.concatenate(
            [jnp.where(lower, imag, real), jnp.where(lower, real, imag)], axis=0
        ).T

    return first_factor, lambda k: jnp.concatenate(parts(1, k), axis=0)


def work_shapes(groups, chans, wins, ns):
    half = LAGS
    rows = 2 * half * (ns // half * wins + 1)
    return [
        pltpu.VMEM((groups * NSEC, wins, ns), F32),
        pltpu.VMEM((ns // LANE, chans * (wins + 1), LANE), F32),
        pltpu.VMEM((chans * (wins + 1), LANE), F32),
        pltpu.VMEM((chans * (wins + 1), LANE), F32),
        pltpu.VMEM((TOGETHER * chans, ns), BF16),
        pltpu.VMEM((wins // TOGETHER, ns + half, TOGETHER * chans), BF16),
        pltpu.VMEM((2, rows, chans), F32),
    ]


def repeat(start, stop, body, together):
    def step(n, _):
        body(n)
        return 0

    lax.fori_loop(start, stop, step, 0, unroll=math.gcd(together, stop - start))


class Choice:
    def __init__(self, odd, sources, target, sem):
        self.options = [
            (odd == side, pltpu.make_async_copy(source, target, sem))
            for side, source in enumerate(sources)
        ]

    def start(self):
        for here, copy in self.options:
            pl.when(here)(copy.start)

    def wait(self):
        for here, copy in self.options:
            pl.when(here)(copy.wait)


def input_copies(odd, first, x, tables_in, sem):
    copied = {"first": [], "x": [], "tables": []}
    used = 0

    def copy(source, target):
        nonlocal used
        if isinstance(source, tuple):
            made = Choice(odd, source, target, sem.at[used])
        else:
            made = pltpu.make_async_copy(source, target, sem.at[used])
        made.start()
        used += 1
        return made

    copied["first"] = [copy(*pair) for pair in first]
    for source, target in x:
        parts = max(target.shape[0] // PART, 1)
        part = target.shape[0] // parts
        rows = [pl.ds(n * part, part) for n in range(parts)]
        copied["x"].append(
            [
                copy(
                    tuple(option.at[here] for option in source)
                    if isinstance(source, tuple)
                    else source.at[here],
                    target.at[here],
                )
                for here in rows
            ]
        )
    copied["tables"] = [copy(*pair) for pair in tables_in]
    return copied


def own_kernel(places, odd_ref, flag_ref, *rest):
    tot_hbm, x_hbm, hann_hbm, conv_hbm, seg_hbm, b_hbm, p_hbm = rest[:7]
    tot, x, hann, conv, seg = rest[7:12]
    work, (b_out, in_sem, out_sem, p_sem) = rest[12:-4], rest[-4:]
    odd = odd_ref[0]
    copied = input_copies(
        odd,
        [(tot_hbm, tot), (hann_hbm, hann)],
        [(x_hbm, x)],
        [(conv_hbm, conv), (seg_hbm, seg)],
        in_sem,
    )
    _, second = segment_factors(
        places, odd, flag_ref, [tot], [x], hann, conv, seg, work, copied
    )

    def put_second(k, stage):
        stage[k] = second(k)

    kept = pltpu.make_async_copy(work[-2], p_hbm, p_sem)
    kept.start()
    send_factor(put_second, b_out, b_hbm, out_sem)
    kept.wait()


def send_factor(factor, stage, target, sem):
    step = stage.shape[0] // STEPS
    copies = []
    for n in range(STEPS):
        part = pl.ds(n * step, step)

        repeat(n * step, (n + 1) * step, lambda k: factor(k, stage), 32)
        copies.append(pltpu.make_async_copy(stage.at[part], target.at[part], sem.at[n]))
        copies[-1].start()
    for copy in copies:
        copy.wait()


def second_kernel(places, odd_ref, flag_ref, *rest):
    tot_hbm, (even_hbm, odd_hbm), rest = rest[:2], (rest[2:4], rest[4:6]), rest[6:]
    halo_hbm, hann_hbm, conv_hbm, seg_hbm, p_hbm, a_hbm, b_hbm = rest[:7]
    tot, x, rest = rest[7:9], rest[9:12], rest[12:]
    hann, conv, seg, own, mixed, a_out, b_out = rest[:7]
    work, (in_sem, p_sem, out_sem) = rest[7:-3], rest[-3:]
    odd = odd_ref[0]
    copied = input_copies(
        odd,
        list(zip(tot_hbm, tot)) + [(hann_hbm, hann)],
        list(zip(zip(even_hbm, odd_hbm), x)) + [(halo_hbm, x[2])],
        [(conv_hbm, conv), (seg_hbm, seg)],
        in_sem,
    )
    kept = pltpu.make_async_copy(p_hbm, own, p_sem)
    kept.start()
    copied["tables"].append(kept)
    chans = b_out.shape[2]
    lane = lax.broadcasted_iota(jnp.int32, (1, chans), 1)

    def first(step, series):
        @pl.when(odd == 1)
        def _():
            mixed[...] = series[...]

        @pl.when(odd == 0)
        def _():
            for i in range(TOGETHER):
                columns = slice(i * chans, (i + 1) * chans)
                value = own[step, :, columns]
                turned = jnp.concatenate([value[:, chans // 2 :], value[:, : chans // 2]], axis=1)
                mixed[:, columns] = jnp.where(lane < chans // 2, series[:, columns], turned)

        return mixed

    first_factor, second_factor = segment_factors(
        places, odd, flag_ref, tot, x, hann, conv, seg, work, copied, first
    )

    def both_factors(k, stage):
        value = first_factor(k)
        width = value.shape[0] // 2
        a_out[k, 1] = value[:width]
        a_out[k, 0] = value[width:]
        stage[k] = second_factor(k)

    step = b_out.shape[0] // STEPS
    copies = []
    for n in range(STEPS):
        part = pl.ds(n * step, step)

        repeat(n * step, (n + 1) * step, lambda k: both_factors(k, b_out), 16)
        for m, (source, target) in enumerate(((a_out, a_hbm), (b_out, b_hbm))):
            copies.append(
                pltpu.make_async_copy(source.at[part], target.at[part], out_sem.at[2 * n + m])
            )
            copies[-1].start()
    for copy in copies:
        copy.wait()


def segments(places, side, flags, totals, pieces, series, hann, conv, seg):
    chans = LANE
    _, wins, ns = pieces[0].shape
    size = seg.shape[0]
    half = size // 2
    depth = ns // half * wins * 2
    smem = pl.BlockSpec(memory_space=pltpu.SMEM)
    anywhere = pl.BlockSpec(memory_space=pl.ANY)
    b_shape = jax.ShapeDtypeStruct((half, depth, chans), BF16)
    p_shape = jax.ShapeDtypeStruct((wins // TOGETHER, ns + half, TOGETHER * chans), BF16)
    a_shape = jax.ShapeDtypeStruct((half, 2, chans // 2, depth), BF16)
    scratch = lambda *values: [pltpu.VMEM(value.shape, value.dtype) for value in values]
    operands = list(totals) + list(pieces) + [hann, conv, seg]
    count = len(operands) + chans // PART
    if series is None:
        kernel, out = own_kernel, [b_shape, p_shape]
        held = scratch(*operands)
        last = scratch(b_shape) + [
            pltpu.SemaphoreType.DMA((count,)),
            pltpu.SemaphoreType.DMA((STEPS,)),
            pltpu.SemaphoreType.DMA,
        ]
    else:
        kernel, out = second_kernel, [a_shape, b_shape]
        held = scratch(*totals, pieces[0], pieces[1], pieces[4], hann, conv, seg, series)
        held += [pltpu.VMEM(p_shape.shape[1:], BF16)] + scratch(a_shape, b_shape)
        last = [
            pltpu.SemaphoreType.DMA((count,)),
            pltpu.SemaphoreType.DMA,
            pltpu.SemaphoreType.DMA((2 * STEPS,)),
        ]
        operands.append(series)
    return pl.pallas_call(
        functools.partial(kernel, places),
        out_shape=out,
        in_specs=[smem] * 2 + [anywhere] * len(operands),
        out_specs=[anywhere] * 2,
        scratch_shapes=held + work_shapes(len(totals), chans, wins, ns) + last,
        compiler_params=pltpu.CompilerParams(vmem_limit_bytes=VMEM),
        cost_estimate=pl.CostEstimate(
            flops=2 * wins * chans * ns * (ns + 3 * size),
            bytes_accessed=16 * 1024 * 1024,
            transcendentals=0,
        ),
    )(side, flags, *operands)


def correlate(first, count, scale, shares, me, a, b0, b2, b3, lag, cross, one, outs, bins_loop):
    depth, chans = b0.shape[1:]
    width = chans // 2
    nfr = lag.shape[1]
    pitch = nfr + 1
    odd = lax.rem(me, 2)
    lane = lax.broadcasted_iota(jnp.int32, (1, chans), 1)
    low, high = [jnp.where((lane < width) == (g == 0), 1.0, 0.0).astype(BF16) for g in range(2)]
    lower = lane < width

    def bins_with(near, far):
        def one_bin(k):
            inner = near[k] * low + b3[k] * high if near is not b3 else b3[k]
            own = jnp.concatenate([b0[k], b2[k] * high], axis=1)
            theirs = jnp.concatenate([inner, far[k] * low], axis=1)
            part = depth // 2
            right = jnp.concatenate([own[:part], theirs[:part], theirs[part:], own[part:]], axis=0)
            real = jnp.where(lower, a[k, 0], a[k, 1])
            imag = jnp.where(lower, a[k, 1], a[k, 0])
            turn = lambda v: jnp.concatenate([v[:, part:], v[:, :part]], axis=1)
            left = jnp.concatenate(
                [
                    jnp.concatenate([real, imag], axis=1),
                    jnp.concatenate([turn(imag), -turn(real)], axis=1),
                ],
                axis=0,
            )
            value = jnp.dot(left, right, preferred_element_type=F32)
            for p in range(2):
                for t in range(2):
                    cross[t, pl.ds(2 * k + p, count, stride=pitch), :] = value[
                        p * count : (p + 1) * count, t * chans : (t + 1) * chans
                    ]

        bins_loop(one_bin)

    pl.when(odd == 0)(lambda: bins_with(b2, b3))
    pl.when(odd == 1)(lambda: bins_with(b3, b2))

    row = lax.broadcasted_iota(jnp.int32, one.shape[1:], 0)
    column = lax.broadcasted_iota(jnp.int32, one.shape[1:], 1)
    turned = jnp.where(row < width, row + chans, row - width)
    place = row + (turned - row) * odd
    for t in range(2):
        here = column + t * chans
        found = (place == here) | ((here >= chans + width) & (place == here - width))
        one[t] = jnp.where(found, 1.0, 0.0)
    share = OFFS // shares

    def one_channel(c):
        value = jnp.concatenate(
            [cross[t, pl.ds(c * pitch, nfr), :] for t in range(2)], axis=1
        ).astype(BF16)
        starts = [first + c + 1 + share * (me ^ d) for d in range(shares)]
        pick = jnp.concatenate(
            [
                jnp.concatenate([one[t, pl.ds(start, share), :] for start in starts], axis=0)
                for t in range(2)
            ],
            axis=1,
        ).astype(BF16)
        lagged = jnp.dot(lag[...], value, preferred_element_type=F32) * scale
        band = lax.dot_general(pick, lagged.astype(BF16), NT, preferred_element_type=F32)
        for d, out in enumerate(outs):
            out[c] = band[d * share : (d + 1) * share, :].astype(BF16)

    repeat(0, count, one_channel, 16)


def last_kernel(places, scale, shares, me_ref, flag_ref, *rest):
    even_hbm, odd_hbm, late_hbm, rest = rest[:2], rest[2:4], rest[4], rest[5:]
    tot_hbm, hann_hbm, conv_hbm, seg_hbm, lag_hbm = rest[:5]
    a_hbm, b0_hbm, b2_hbm, rest = *rest[5:8], rest[8:]
    outs, b3_hbm, rest = rest[:shares], rest[shares], rest[shares + 1 :]
    x, rest = rest[:3], rest[3:]
    tot, hann, conv, seg, lag, b0, b2 = rest[:7]
    work, (a, b3, one, in_sem, late_sem, out_sem) = rest[7:-6], rest[-6:]
    me = me_ref[0]
    odd = lax.rem(me, 2)
    copied = input_copies(
        odd,
        [(tot_hbm, tot), (hann_hbm, hann)],
        list(zip(zip(even_hbm, odd_hbm), x)) + [(late_hbm, x[2])],
        [(conv_hbm, conv), (seg_hbm, seg), (lag_hbm, lag)],
        in_sem,
    )
    count = a.shape[2]
    late = [
        pltpu.make_async_copy(source, target, late_sem.at[n])
        for n, (source, target) in enumerate(
            ((b0_hbm, b0), (b2_hbm, b2), (a_hbm.at[:, :, pl.ds(0, count)], a))
        )
    ]
    for copy in late:
        copy.start()
    _, second_factor = segment_factors(
        places, odd, flag_ref, [tot], x, hann, conv, seg, work, copied
    )
    bins = b3.shape[0]

    def second(k):
        b3[k] = second_factor(k)

    repeat(0, bins, second, 32)
    kept = pltpu.make_async_copy(b3, b3_hbm, out_sem)
    kept.start()
    for copy in late:
        copy.wait()
    correlate(
        *(0, count, scale, shares, me, a, b0, b2, b3, lag, work[-1], one, outs),
        lambda one_bin: repeat(0, bins, one_bin, 32),
    )
    kept.wait()


def rest_kernel(first, scale, shares, me_ref, *rest):
    lag_hbm, a_hbm, b0_hbm, b2_hbm, b3_hbm = rest[:5]
    outs, rest = rest[5 : 5 + shares], rest[5 + shares :]
    lag, a, b0, b2, b3, cross, one, lag_sem, sem = rest
    bins, count = b0.shape[0], a.shape[2]
    some = bins // STEPS

    def factors(n):
        part = pl.ds(n * some, some)
        return [
            pltpu.make_async_copy(source, target, sem.at[n, m])
            for m, (source, target) in enumerate(
                (
                    (b0_hbm.at[part], b0.at[part]),
                    (b2_hbm.at[part], b2.at[part]),
                    (b3_hbm.at[part], b3.at[part]),
                    (a_hbm.at[part, :, pl.ds(first, count)], a.at[part]),
                )
            )
        ]

    for n in range(STEPS):
        for copy in factors(n):
            copy.start()
    table = pltpu.make_async_copy(lag_hbm, lag, lag_sem)
    table.start()
    table.wait()

    def bins_loop(one_bin):
        def part(n, _):
            for copy in factors(n):
                copy.wait()
            repeat(0, some, lambda k: one_bin(n * some + k), some)
            return 0

        lax.fori_loop(0, STEPS, part, 0)

    correlate(first, count, scale, shares, me_ref[0], a, b0, b2, b3, lag, cross, one, outs, bins_loop)


def stacks(places, shares, scale, me, flags, total, pieces, hann, conv, seg, lag, a, b0, b2):
    bins, depth, chans = b0.shape
    width = chans // 2
    count = width // 2
    _, wins, ns = pieces[0].shape
    nlag, nfr = lag.shape
    smem = pl.BlockSpec(memory_space=pltpu.SMEM)
    vmem = pl.BlockSpec(memory_space=pltpu.VMEM)
    anywhere = pl.BlockSpec(memory_space=pl.ANY)
    out = [jax.ShapeDtypeStruct((count, OFFS // shares, nlag), BF16)] * shares
    operands = [*pieces, total, hann, conv, seg, lag, a, b0, b2]
    held = [pieces[0], pieces[1], pieces[4], total, hann, conv, seg, lag, b0, b2]
    some_a = pltpu.VMEM((bins, 2, count, depth), BF16)
    one = pltpu.VMEM((2, chans + width, chans), F32)
    params = pltpu.CompilerParams(vmem_limit_bytes=VMEM)
    cost = pl.CostEstimate(
        flops=2 * count * bins * 4 * (2 * depth * chans + 2 * OFFS * chans),
        bytes_accessed=20 * 1024 * 1024,
        transcendentals=0,
    )
    *head, b3 = pl.pallas_call(
        functools.partial(last_kernel, places, scale, shares),
        out_shape=out + [jax.ShapeDtypeStruct(b0.shape, BF16)],
        in_specs=[smem] * 2 + [anywhere] * len(operands),
        out_specs=[vmem] * shares + [anywhere],
        scratch_shapes=[pltpu.VMEM(value.shape, value.dtype) for value in held]
        + work_shapes(1, chans, wins, ns)
        + [
            some_a,
            pltpu.VMEM(b0.shape, BF16),
            one,
            pltpu.SemaphoreType.DMA((8 + chans // PART,)),
            pltpu.SemaphoreType.DMA((3,)),
            pltpu.SemaphoreType.DMA,
        ],
        compiler_params=params,
        cost_estimate=cost,
    )(me, flags, *operands)
    tail = pl.pallas_call(
        functools.partial(rest_kernel, count, scale, shares),
        out_shape=out,
        in_specs=[smem] + [anywhere] * 5,
        out_specs=[vmem] * shares,
        scratch_shapes=[
            pltpu.VMEM(lag.shape, BF16),
            some_a,
            *[pltpu.VMEM(b0.shape, BF16)] * 3,
            pltpu.VMEM((2, count * (nfr + 1), chans), F32),
            one,
            pltpu.SemaphoreType.DMA,
            pltpu.SemaphoreType.DMA((STEPS, 4)),
        ],
        compiler_params=params,
        cost_estimate=cost,
    )(me, lag, a, b0, b2, b3)
    return head, tail


def add_over(value, axis, beside):
    count = lax.axis_size(axis)
    if count & (count - 1):
        return lax.psum(value, axis), beside
    bit = 1
    while bit < count:
        steps = [bit] if bit == 1 or 2 * bit == count else [bit, 2 * bit, 3 * bit]
        arrived = [lax.ppermute(value, axis, [(i, i ^ s) for i in range(count)]) for s in steps]
        bit *= 1 + len(steps)
        if bit == count:
            arrived, beside = lax.optimization_barrier((arrived, beside))
        value = sum(arrived, value)
    return value, beside


def shards(samples, band_gain, dead_flags, section_ids):
    chans, wins, ns = samples.shape
    nf = ns // 2
    width = chans // 2
    blocks = lax.axis_size("fibre")
    groups = lax.axis_size("tm")
    me = lax.axis_index("tm")
    odd = me % 2
    window, waves, seg, lag = tables(ns, nf)
    waves, seg, lag = jnp.asarray(waves), jnp.asarray(seg), jnp.asarray(lag)
    hann = jnp.asarray(window[None, :])
    response = jnp.sum(band_gain[:, None] * waves, axis=0, keepdims=True)
    swap = [(z, z ^ 1) for z in range(groups)]
    both = ("fibre", "tm")
    halo_pairs = [
        (b * groups + z, (b + (1 if z % 2 else -1)) % blocks * groups + z)
        for b in range(blocks)
        for z in range(groups)
    ]

    head = width * 5 // 8

    their_head = lax.ppermute(
        lax.dynamic_slice_in_dim(samples, (1 - odd) * width, head, 0), "tm", swap
    )
    flags = jnp.stack([dead_flags, section_ids])
    halo_flags = lax.ppermute(
        lax.dynamic_slice_in_dim(flags, odd * width, width, 1), both, halo_pairs
    )
    smem = pl.BlockSpec(memory_space=pltpu.SMEM)
    anywhere = pl.BlockSpec(memory_space=pl.ANY)
    sums, own_half, tail = pl.pallas_call(
        section_sums,
        out_shape=[
            jax.ShapeDtypeStruct((NSEC, wins, ns + LANE), F32),
            jax.ShapeDtypeStruct((width, wins, ns), BF16),
            jax.ShapeDtypeStruct((width - head, wins, ns), BF16),
        ],
        in_specs=[smem] * 3 + [anywhere],
        out_specs=[pl.BlockSpec(memory_space=pltpu.VMEM), anywhere, anywhere],
        scratch_shapes=[
            pltpu.VMEM(samples.shape, BF16),
            pltpu.SemaphoreType.DMA((STEPS,)),
            pltpu.SemaphoreType.DMA((2,)),
        ],
        compiler_params=pltpu.CompilerParams(vmem_limit_bytes=VMEM),
        cost_estimate=pl.CostEstimate(flops=1, bytes_accessed=1, transcendentals=0),
    )(odd[None], dead_flags, section_ids, samples)
    total, their_head = add_over(sums, "fibre", their_head)
    halo_source, halo_flags = lax.optimization_barrier((own_half, halo_flags))
    halo = lax.ppermute(halo_source, both, halo_pairs)
    total, response, own_half, tail = lax.optimization_barrier(
        (total, response, own_half, tail)
    )
    conv = pl.pallas_call(
        circulant_kernel,
        out_shape=jax.ShapeDtypeStruct((TILE, ns), BF16),
        compiler_params=pltpu.CompilerParams(vmem_limit_bytes=VMEM),
        cost_estimate=pl.CostEstimate(flops=1, bytes_accessed=1, transcendentals=0),
    )(response)
    their_total = lax.ppermute(total, "tm", swap)
    their_tail = lax.ppermute(tail, "tm", swap)
    their_second = lax.ppermute(own_half, "tm", swap)
    ready = (total, their_total, their_head, flags, hann, conv, seg, lag)
    ready = lax.optimization_barrier(ready)
    total, their_total, their_head, flags, hann, conv, seg, lag = ready
    halo_head = lax.ppermute(their_head, both, halo_pairs)

    side = odd[None]
    parts = (hann, conv, seg)
    every = jnp.concatenate([flags, halo_flags], axis=1)
    b0, series = segments(((0, (0, 0), (0, 0)),), side, flags, (total,), (samples,), None, *parts)
    b0, forward = lax.optimization_barrier((b0, their_tail))
    halo_tail = lax.ppermute(forward, both, halo_pairs)
    a, b2 = segments(
        (
            (1, (0, 0), (0, chans)),
            (1, (head, head), (head, chans + head)),
            (0, (width, width), (chans, chans)),
        ),
        side,
        every,
        (total, their_total),
        (their_head, their_tail, halo_head, halo_tail, halo),
        series,
        *parts,
    )
    scale = 2.0 / ns / LAGS / math.sqrt(nf * wins * groups)
    found = stacks(
        (
            (0, (0, width), (chans, width)),
            (0, (head, width + head), (chans + head, width + head)),
            (0, (width, 0), (width, 0)),
        ),
        groups,
        scale,
        me[None],
        every,
        their_total,
        (halo_head, halo_tail, their_head, their_tail, their_second),
        *(hann, conv, seg, lag),
        *(a, b0, b2),
    )
    lower, upper = [], []
    order = list(range(2, groups)) + [0, 1]
    for part in found:
        arrived = {}
        for d in order:
            pairs = [
                (b * groups + z, (b - z % 2) % blocks * groups + (z ^ d))
                for b in range(blocks)
                for z in range(groups)
            ]
            arrived[d] = lax.ppermute(part[d], both, pairs)
        for out, sides in ((lower, (0, 1)), (upper, (1, 0))):
            terms = [
                jnp.where(odd == 0, arrived[d + sides[0]], arrived[d + sides[1]]).astype(F32)
                for d in order[::2]
            ]
            out.append(sum(terms[1:], terms[0]))
    return jnp.concatenate(lower + upper, axis=0)


def solution(mesh):
    in_specs = (P("fibre", "tm", None), P(), P("fibre"), P("fibre"))
    out_specs = P("fibre", "tm", None)
    return jax.shard_map(shards, mesh=mesh, in_specs=in_specs, out_specs=out_specs, check_vma=False)
```

```python
import functools
import math

import jax
import jax.numpy as jnp
import ml_dtypes
import numpy as np
from jax import lax
from jax.experimental import pallas as pl
from jax.experimental.pallas import tpu as pltpu
from jax.sharding import PartitionSpec as P

OFFS = 128
LAGS = 128
NSEC = 2
LANE = 128
PART = 32
TILE = 256
STEPS = 4
TOGETHER = 4
VMEM = 63 * 1024 * 1024
NT = (((1,), (1,)), ((), ()))
F32 = jnp.float32
BF16 = jnp.bfloat16


def tables(ns, nf):
    tick = np.arange(ns)
    freq = np.arange(nf)
    window = 0.5 - 0.5 * np.cos(tick * (2.0 * math.pi / ns))
    waves = np.cos((freq[:, None] * tick[None, :] % ns) * (2.0 * math.pi / ns))
    waves[0] *= math.sqrt(0.5)
    size = 2 * LAGS
    bins = np.arange(size // 2)
    turn = math.pi / size * ((2 * bins[:, None] + 1) * np.arange(size)[None, :] % (2 * size))
    segment = np.stack([np.cos(turn), -np.sin(turn)], axis=1).reshape(size, size)
    lag = np.stack([np.cos(turn), -np.sin(turn)], axis=1).reshape(size, size)[:, :LAGS].T
    cast = lambda a: a.astype(np.float32).astype(ml_dtypes.bfloat16)
    return window.astype(np.float32), cast(waves), cast(segment), cast(lag)


def section_sums(odd_ref, dead_ref, sec_ref, x_hbm, out_ref, half_hbm, tail_hbm, x, in_sem, sem):
    chans, wins, ns = x.shape
    width, length = half_hbm.shape[0], tail_hbm.shape[0]
    odd = odd_ref[0]
    part = chans // STEPS
    arriving = [
        pltpu.make_async_copy(
            x_hbm.at[pl.ds(n * part, part)], x.at[pl.ds(n * part, part)], in_sem.at[n]
        )
        for n in range(STEPS)
    ]
    for copy in arriving:
        copy.start()
    leaving = [
        pltpu.make_async_copy(x.at[pl.ds(odd * width, width)], half_hbm, sem.at[0]),
        pltpu.make_async_copy(
            x.at[pl.ds((2 - odd) * width - length, length)], tail_hbm, sem.at[1]
        ),
    ]

    def body(c, carry):
        value = x[c].astype(F32)
        live = 1 - dead_ref[c]
        sums, counts = carry
        weights = [jnp.where(sec_ref[c] == s, live, 0).astype(F32) for s in range(NSEC)]
        return (
            tuple(sums[s] + weights[s] * value for s in range(NSEC)),
            tuple(counts[s] + weights[s] for s in range(NSEC)),
        )

    zero = jnp.zeros((wins, ns), F32)
    carry = ((zero,) * NSEC, (jnp.float32(0),) * NSEC)
    for n, copy in enumerate(arriving):
        copy.wait()
        if n == STEPS - 1:
            for out in leaving:
                out.start()
        carry = lax.fori_loop(n * part, (n + 1) * part, body, carry, unroll=8)
    sums, counts = carry
    for s in range(NSEC):
        out_ref[s, :, :ns] = sums[s]
        out_ref[s, :, ns:] = jnp.zeros((wins, LANE), F32) + counts[s]
    for out in leaving:
        out.wait()


def circulant_kernel(filter_ref, out_ref):
    ns = filter_ref.shape[1]
    for t in range(0, TILE, 16):
        block = jnp.broadcast_to(filter_ref[...], (16, ns))
        out_ref[t : t + 16, :] = pltpu.roll(block, t, 1, stride=1, stride_axis=0).astype(BF16)


def segment_factors(places, odd, flag_ref, tot, x, hann, conv, seg, work, copied, first=None):
    common, clean, mass, square, rows, series_all, stage = work
    _, wins, ns = x[0].shape
    chans = sum(piece.shape[0] for piece in x)
    pitch = wins + 1
    size = seg.shape[0]
    half = size // 2
    blocks = ns // half
    jw = blocks * wins
    jpitch = jw + 1
    for copy in copied["first"]:
        copy.wait()
    for g in range(len(tot)):
        for s in range(NSEC):
            common[g * NSEC + s] = tot[g][s, :, :ns] / jnp.maximum(tot[g][s, :, ns : ns + 1], 1.0)
    sign = 1.0 - 2.0 * (lax.broadcasted_iota(jnp.int32, (chans, LANE), 1) % 2).astype(F32)

    for number, (group, base, flags) in enumerate(places):
        piece = x[number]
        length = piece.shape[0]
        base = base[0] + odd * (base[1] - base[0])
        flags = flags[0] + odd * (flags[1] - flags[0])

        def clean_channel(c):
            at = base + c
            flag = flags + c
            live = (1 - flag_ref[0, flag]).astype(F32)
            value = (piece[c].astype(F32) - common[group * NSEC + flag_ref[1, flag]]) * (
                hann[...] * live
            )
            tiles = [value[:, t * LANE : (t + 1) * LANE] for t in range(ns // LANE)]
            row = pl.ds(at * pitch, wins)
            mass[row, :] = sum(tiles[1:], tiles[0])
            square[row, :] = sum([tile * tile for tile in tiles[1:]], tiles[0] * tiles[0])
            for t, tile in enumerate(tiles):
                clean[t, row, :] = tile

        parts = copied["x"][number]
        part = length // len(parts)
        for n, copy in enumerate(parts):
            copy.wait()
            repeat(n * part, (n + 1) * part, clean_channel, 16)
    for copy in copied["tables"]:
        copy.wait()

    for step in range(wins // TOGETHER):
        series = series_all.at[step]
        for i in range(TOGETHER):
            window = pl.ds(step * TOGETHER + i, chans, stride=pitch)
            total = mass[window, :]
            lowest = jnp.sum(total, axis=1, keepdims=True)
            highest = jnp.sum(total * sign, axis=1, keepdims=True)
            power = 0.5 * jnp.sum(square[window, :], axis=1, keepdims=True)
            power = power + (lowest * lowest - highest * highest) * (0.5 / ns)
            level = lax.rsqrt(power + 1e-06)
            for t in range(ns // LANE):
                rows[i * chans : (i + 1) * chans, t * LANE : (t + 1) * LANE] = (
                    clean[t, window, :] * level
                ).astype(BF16)
        for t in range(0, ns, TILE):
            turned = jnp.concatenate([conv[:, ns - t :], conv[:, : ns - t]], axis=1) if t else conv[...]
            series[half // 2 + t : half // 2 + t + TILE, :] = lax.dot_general(
                turned, rows[...], NT, preferred_element_type=F32
            ).astype(BF16)
        series[: half // 2, :] = series[ns : ns + half // 2, :]
        series[ns + half // 2 :, :] = series[half // 2 : half, :]

        def place(which, j, value):
            for i in range(TOGETHER):
                at = j * wins + step * TOGETHER + i
                stage[which, pl.ds(at, size, stride=jpitch), :] = value[
                    :, i * chans : (i + 1) * chans
                ]

        for j in range(blocks):
            start = j * half + half // 2
            b = jnp.dot(
                seg[:, :half], series[start : start + half, :], preferred_element_type=F32
            )
            place(1, j, b)

        if first is not None:
            source = first(step, series)
            for j in range(blocks):
                a = jnp.dot(
                    seg[...], source[j * half : j * half + size, :], preferred_element_type=F32
                )
                place(0, j, a)

    def parts(which, k):
        return [
            stage[which, pl.ds((2 * k + part) * jpitch, jw), :].astype(BF16) for part in range(2)
        ]

    lower = lax.broadcasted_iota(jnp.int32, (1, chans), 1) < chans // 2

    def first_factor(k):
        real, imag = parts(0, k)
        return jnp.concatenate(
            [jnp.where(lower, imag, real), jnp.where(lower, real, imag)], axis=0
        ).T

    return first_factor, lambda k: jnp.concatenate(parts(1, k), axis=0)


def work_shapes(groups, chans, wins, ns):
    half = LAGS
    rows = 2 * half * (ns // half * wins + 1)
    return [
        pltpu.VMEM((groups * NSEC, wins, ns), F32),
        pltpu.VMEM((ns // LANE, chans * (wins + 1), LANE), F32),
        pltpu.VMEM((chans * (wins + 1), LANE), F32),
        pltpu.VMEM((chans * (wins + 1), LANE), F32),
        pltpu.VMEM((TOGETHER * chans, ns), BF16),
        pltpu.VMEM((wins // TOGETHER, ns + half, TOGETHER * chans), BF16),
        pltpu.VMEM((2, rows, chans), F32),
    ]


def repeat(start, stop, body, together):
    def step(n, _):
        body(n)
        return 0

    lax.fori_loop(start, stop, step, 0, unroll=math.gcd(together, stop - start))


class Choice:
    def __init__(self, odd, sources, target, sem):
        self.options = [
            (odd == side, pltpu.make_async_copy(source, target, sem))
            for side, source in enumerate(sources)
        ]

    def start(self):
        for here, copy in self.options:
            pl.when(here)(copy.start)

    def wait(self):
        for here, copy in self.options:
            pl.when(here)(copy.wait)


def input_copies(odd, first, x, tables_in, sem):
    copied = {"first": [], "x": [], "tables": []}
    used = 0

    def copy(source, target):
        nonlocal used
        if isinstance(source, tuple):
            made = Choice(odd, source, target, sem.at[used])
        else:
            made = pltpu.make_async_copy(source, target, sem.at[used])
        made.start()
        used += 1
        return made

    copied["first"] = [copy(*pair) for pair in first]
    for source, target in x:
        parts = max(target.shape[0] // PART, 1)
        part = target.shape[0] // parts
        rows = [pl.ds(n * part, part) for n in range(parts)]
        copied["x"].append(
            [
                copy(
                    tuple(option.at[here] for option in source)
                    if isinstance(source, tuple)
                    else source.at[here],
                    target.at[here],
                )
                for here in rows
            ]
        )
    copied["tables"] = [copy(*pair) for pair in tables_in]
    return copied


def own_kernel(places, odd_ref, flag_ref, *rest):
    tot_hbm, x_hbm, hann_hbm, conv_hbm, seg_hbm, b_hbm, p_hbm = rest[:7]
    tot, x, hann, conv, seg = rest[7:12]
    work, (b_out, in_sem, out_sem, p_sem) = rest[12:-4], rest[-4:]
    odd = odd_ref[0]
    copied = input_copies(
        odd,
        [(tot_hbm, tot), (hann_hbm, hann)],
        [(x_hbm, x)],
        [(conv_hbm, conv), (seg_hbm, seg)],
        in_sem,
    )
    _, second = segment_factors(
        places, odd, flag_ref, [tot], [x], hann, conv, seg, work, copied
    )

    def put_second(k, stage):
        stage[k] = second(k)

    kept = pltpu.make_async_copy(work[-2], p_hbm, p_sem)
    kept.start()
    send_factor(put_second, b_out, b_hbm, out_sem)
    kept.wait()


def send_factor(factor, stage, target, sem):
    step = stage.shape[0] // STEPS
    copies = []
    for n in range(STEPS):
        part = pl.ds(n * step, step)

        repeat(n * step, (n + 1) * step, lambda k: factor(k, stage), 32)
        copies.append(pltpu.make_async_copy(stage.at[part], target.at[part], sem.at[n]))
        copies[-1].start()
    for copy in copies:
        copy.wait()


def second_kernel(places, odd_ref, flag_ref, *rest):
    tot_hbm, (even_hbm, odd_hbm), rest = rest[:2], (rest[2:4], rest[4:6]), rest[6:]
    halo_hbm, hann_hbm, conv_hbm, seg_hbm, p_hbm, a_hbm, b_hbm = rest[:7]
    tot, x, rest = rest[7:9], rest[9:12], rest[12:]
    hann, conv, seg, own, mixed, a_out, b_out = rest[:7]
    work, (in_sem, p_sem, out_sem) = rest[7:-3], rest[-3:]
    odd = odd_ref[0]
    copied = input_copies(
        odd,
        list(zip(tot_hbm, tot)) + [(hann_hbm, hann)],
        list(zip(zip(even_hbm, odd_hbm), x)) + [(halo_hbm, x[2])],
        [(conv_hbm, conv), (seg_hbm, seg)],
        in_sem,
    )
    kept = pltpu.make_async_copy(p_hbm, own, p_sem)
    kept.start()
    copied["tables"].append(kept)
    chans = b_out.shape[2]
    lane = lax.broadcasted_iota(jnp.int32, (1, chans), 1)

    def first(step, series):
        @pl.when(odd == 1)
        def _():
            mixed[...] = series[...]

        @pl.when(odd == 0)
        def _():
            for i in range(TOGETHER):
                columns = slice(i * chans, (i + 1) * chans)
                value = own[step, :, columns]
                turned = jnp.concatenate([value[:, chans // 2 :], value[:, : chans // 2]], axis=1)
                mixed[:, columns] = jnp.where(lane < chans // 2, series[:, columns], turned)

        return mixed

    first_factor, second_factor = segment_factors(
        places, odd, flag_ref, tot, x, hann, conv, seg, work, copied, first
    )

    def both_factors(k, stage):
        value = first_factor(k)
        width = value.shape[0] // 2
        a_out[k, 1] = value[:width]
        a_out[k, 0] = value[width:]
        stage[k] = second_factor(k)

    step = b_out.shape[0] // STEPS
    copies = []
    for n in range(STEPS):
        part = pl.ds(n * step, step)

        repeat(n * step, (n + 1) * step, lambda k: both_factors(k, b_out), 16)
        for m, (source, target) in enumerate(((a_out, a_hbm), (b_out, b_hbm))):
            copies.append(
                pltpu.make_async_copy(source.at[part], target.at[part], out_sem.at[2 * n + m])
            )
            copies[-1].start()
    for copy in copies:
        copy.wait()


def segments(places, side, flags, totals, pieces, series, hann, conv, seg):
    chans = LANE
    _, wins, ns = pieces[0].shape
    size = seg.shape[0]
    half = size // 2
    depth = ns // half * wins * 2
    smem = pl.BlockSpec(memory_space=pltpu.SMEM)
    anywhere = pl.BlockSpec(memory_space=pl.ANY)
    b_shape = jax.ShapeDtypeStruct((half, depth, chans), BF16)
    p_shape = jax.ShapeDtypeStruct((wins // TOGETHER, ns + half, TOGETHER * chans), BF16)
    a_shape = jax.ShapeDtypeStruct((half, 2, chans // 2, depth), BF16)
    scratch = lambda *values: [pltpu.VMEM(value.shape, value.dtype) for value in values]
    operands = list(totals) + list(pieces) + [hann, conv, seg]
    count = len(operands) + chans // PART
    if series is None:
        kernel, out = own_kernel, [b_shape, p_shape]
        held = scratch(*operands)
        last = scratch(b_shape) + [
            pltpu.SemaphoreType.DMA((count,)),
            pltpu.SemaphoreType.DMA((STEPS,)),
            pltpu.SemaphoreType.DMA,
        ]
    else:
        kernel, out = second_kernel, [a_shape, b_shape]
        held = scratch(*totals, pieces[0], pieces[1], pieces[4], hann, conv, seg, series)
        held += [pltpu.VMEM(p_shape.shape[1:], BF16)] + scratch(a_shape, b_shape)
        last = [
            pltpu.SemaphoreType.DMA((count,)),
            pltpu.SemaphoreType.DMA,
            pltpu.SemaphoreType.DMA((2 * STEPS,)),
        ]
        operands.append(series)
    return pl.pallas_call(
        functools.partial(kernel, places),
        out_shape=out,
        in_specs=[smem] * 2 + [anywhere] * len(operands),
        out_specs=[anywhere] * 2,
        scratch_shapes=held + work_shapes(len(totals), chans, wins, ns) + last,
        compiler_params=pltpu.CompilerParams(vmem_limit_bytes=VMEM),
        cost_estimate=pl.CostEstimate(
            flops=2 * wins * chans * ns * (ns + 3 * size),
            bytes_accessed=16 * 1024 * 1024,
            transcendentals=0,
        ),
    )(side, flags, *operands)


def correlate(first, count, scale, shares, me, a, b0, b2, b3, lag, cross, one, outs, bins_loop):
    depth, chans = b0.shape[1:]
    width = chans // 2
    nfr = lag.shape[1]
    pitch = nfr + 1
    odd = lax.rem(me, 2)
    lane = lax.broadcasted_iota(jnp.int32, (1, chans), 1)
    low, high = [jnp.where((lane < width) == (g == 0), 1.0, 0.0).astype(BF16) for g in range(2)]
    lower = lane < width

    def bins_with(near, far):
        def one_bin(k):
            inner = near[k] * low + b3[k] * high if near is not b3 else b3[k]
            own = jnp.concatenate([b0[k], b2[k] * high], axis=1)
            theirs = jnp.concatenate([inner, far[k] * low], axis=1)
            part = depth // 2
            right = jnp.concatenate([own[:part], theirs[:part], theirs[part:], own[part:]], axis=0)
            real = jnp.where(lower, a[k, 0], a[k, 1])
            imag = jnp.where(lower, a[k, 1], a[k, 0])
            turn = lambda v: jnp.concatenate([v[:, part:], v[:, :part]], axis=1)
            left = jnp.concatenate(
                [
                    jnp.concatenate([real, imag], axis=1),
                    jnp.concatenate([turn(imag), -turn(real)], axis=1),
                ],
                axis=0,
            )
            value = jnp.dot(left, right, preferred_element_type=F32)
            for p in range(2):
                for t in range(2):
                    cross[t, pl.ds(2 * k + p, count, stride=pitch), :] = value[
                        p * count : (p + 1) * count, t * chans : (t + 1) * chans
                    ]

        bins_loop(one_bin)

    pl.when(odd == 0)(lambda: bins_with(b2, b3))
    pl.when(odd == 1)(lambda: bins_with(b3, b2))

    row = lax.broadcasted_iota(jnp.int32, one.shape[1:], 0)
    column = lax.broadcasted_iota(jnp.int32, one.shape[1:], 1)
    turned = jnp.where(row < width, row + chans, row - width)
    place = row + (turned - row) * odd
    for t in range(2):
        here = column + t * chans
        found = (place == here) | ((here >= chans + width) & (place == here - width))
        one[t] = jnp.where(found, 1.0, 0.0)
    share = OFFS // shares

    def one_channel(c):
        value = jnp.concatenate(
            [cross[t, pl.ds(c * pitch, nfr), :] for t in range(2)], axis=1
        ).astype(BF16)
        starts = [first + c + 1 + share * (me ^ d) for d in range(shares)]
        pick = jnp.concatenate(
            [
                jnp.concatenate([one[t, pl.ds(start, share), :] for start in starts], axis=0)
                for t in range(2)
            ],
            axis=1,
        ).astype(BF16)
        lagged = jnp.dot(lag[...], value, preferred_element_type=F32) * scale
        band = lax.dot_general(pick, lagged.astype(BF16), NT, preferred_element_type=F32)
        for d, out in enumerate(outs):
            out[c] = band[d * share : (d + 1) * share, :].astype(BF16)

    repeat(0, count, one_channel, 16)


def last_kernel(places, scale, shares, me_ref, flag_ref, *rest):
    even_hbm, odd_hbm, late_hbm, rest = rest[:2], rest[2:4], rest[4], rest[5:]
    tot_hbm, hann_hbm, conv_hbm, seg_hbm, lag_hbm = rest[:5]
    a_hbm, b0_hbm, b2_hbm, rest = *rest[5:8], rest[8:]
    outs, b3_hbm, rest = rest[:shares], rest[shares], rest[shares + 1 :]
    x, rest = rest[:3], rest[3:]
    tot, hann, conv, seg, lag, b0, b2 = rest[:7]
    work, (a, b3, one, in_sem, late_sem, out_sem) = rest[7:-6], rest[-6:]
    me = me_ref[0]
    odd = lax.rem(me, 2)
    copied = input_copies(
        odd,
        [(tot_hbm, tot), (hann_hbm, hann)],
        list(zip(zip(even_hbm, odd_hbm), x)) + [(late_hbm, x[2])],
        [(conv_hbm, conv), (seg_hbm, seg), (lag_hbm, lag)],
        in_sem,
    )
    count = a.shape[2]
    late = [
        pltpu.make_async_copy(source, target, late_sem.at[n])
        for n, (source, target) in enumerate(
            ((b0_hbm, b0), (b2_hbm, b2), (a_hbm.at[:, :, pl.ds(0, count)], a))
        )
    ]
    for copy in late:
        copy.start()
    _, second_factor = segment_factors(
        places, odd, flag_ref, [tot], x, hann, conv, seg, work, copied
    )
    bins = b3.shape[0]

    def second(k):
        b3[k] = second_factor(k)

    repeat(0, bins, second, 32)
    kept = pltpu.make_async_copy(b3, b3_hbm, out_sem)
    kept.start()
    for copy in late:
        copy.wait()
    correlate(
        *(0, count, scale, shares, me, a, b0, b2, b3, lag, work[-1], one, outs),
        lambda one_bin: repeat(0, bins, one_bin, 32),
    )
    kept.wait()


def rest_kernel(first, scale, shares, me_ref, *rest):
    lag_hbm, a_hbm, b0_hbm, b2_hbm, b3_hbm = rest[:5]
    outs, rest = rest[5 : 5 + shares], rest[5 + shares :]
    lag, a, b0, b2, b3, cross, one, lag_sem, sem = rest
    bins, count = b0.shape[0], a.shape[2]
    some = bins // STEPS

    def factors(n):
        part = pl.ds(n * some, some)
        return [
            pltpu.make_async_copy(source, target, sem.at[n, m])
            for m, (source, target) in enumerate(
                (
                    (b0_hbm.at[part], b0.at[part]),
                    (b2_hbm.at[part], b2.at[part]),
                    (b3_hbm.at[part], b3.at[part]),
                    (a_hbm.at[part, :, pl.ds(first, count)], a.at[part]),
                )
            )
        ]

    for n in range(STEPS):
        for copy in factors(n):
            copy.start()
    table = pltpu.make_async_copy(lag_hbm, lag, lag_sem)
    table.start()
    table.wait()

    def bins_loop(one_bin):
        def part(n, _):
            for copy in factors(n):
                copy.wait()
            repeat(0, some, lambda k: one_bin(n * some + k), some)
            return 0

        lax.fori_loop(0, STEPS, part, 0)

    correlate(first, count, scale, shares, me_ref[0], a, b0, b2, b3, lag, cross, one, outs, bins_loop)


def stacks(places, shares, scale, me, flags, total, pieces, hann, conv, seg, lag, a, b0, b2):
    bins, depth, chans = b0.shape
    width = chans // 2
    count = width // 2
    _, wins, ns = pieces[0].shape
    nlag, nfr = lag.shape
    smem = pl.BlockSpec(memory_space=pltpu.SMEM)
    vmem = pl.BlockSpec(memory_space=pltpu.VMEM)
    anywhere = pl.BlockSpec(memory_space=pl.ANY)
    out = [jax.ShapeDtypeStruct((count, OFFS // shares, nlag), BF16)] * shares
    operands = [*pieces, total, hann, conv, seg, lag, a, b0, b2]
    held = [pieces[0], pieces[1], pieces[4], total, hann, conv, seg, lag, b0, b2]
    some_a = pltpu.VMEM((bins, 2, count, depth), BF16)
    one = pltpu.VMEM((2, chans + width, chans), F32)
    params = pltpu.CompilerParams(vmem_limit_bytes=VMEM)
    cost = pl.CostEstimate(
        flops=2 * count * bins * 4 * (2 * depth * chans + 2 * OFFS * chans),
        bytes_accessed=20 * 1024 * 1024,
        transcendentals=0,
    )
    *head, b3 = pl.pallas_call(
        functools.partial(last_kernel, places, scale, shares),
        out_shape=out + [jax.ShapeDtypeStruct(b0.shape, BF16)],
        in_specs=[smem] * 2 + [anywhere] * len(operands),
        out_specs=[vmem] * shares + [anywhere],
        scratch_shapes=[pltpu.VMEM(value.shape, value.dtype) for value in held]
        + work_shapes(1, chans, wins, ns)
        + [
            some_a,
            pltpu.VMEM(b0.shape, BF16),
            one,
            pltpu.SemaphoreType.DMA((8 + chans // PART,)),
            pltpu.SemaphoreType.DMA((3,)),
            pltpu.SemaphoreType.DMA,
        ],
        compiler_params=params,
        cost_estimate=cost,
    )(me, flags, *operands)
    tail = pl.pallas_call(
        functools.partial(rest_kernel, count, scale, shares),
        out_shape=out,
        in_specs=[smem] + [anywhere] * 5,
        out_specs=[vmem] * shares,
        scratch_shapes=[
            pltpu.VMEM(lag.shape, BF16),
            some_a,
            *[pltpu.VMEM(b0.shape, BF16)] * 3,
            pltpu.VMEM((2, count * (nfr + 1), chans), F32),
            one,
            pltpu.SemaphoreType.DMA,
            pltpu.SemaphoreType.DMA((STEPS, 4)),
        ],
        compiler_params=params,
        cost_estimate=cost,
    )(me, lag, a, b0, b2, b3)
    return head, tail


def add_over(value, axis, beside):
    count = lax.axis_size(axis)
    if count & (count - 1):
        return lax.psum(value, axis), beside
    bit = 1
    while bit < count:
        steps = [bit] if bit == 1 or 2 * bit == count else [bit, 2 * bit, 3 * bit]
        arrived = [lax.ppermute(value, axis, [(i, i ^ s) for i in range(count)]) for s in steps]
        bit *= 1 + len(steps)
        if bit == count:
            arrived, beside = lax.optimization_barrier((arrived, beside))
        value = sum(arrived, value)
    return value, beside


def shards(samples, band_gain, dead_flags, section_ids):
    chans, wins, ns = samples.shape
    nf = ns // 2
    width = chans // 2
    blocks = lax.axis_size("fibre")
    groups = lax.axis_size("tm")
    me = lax.axis_index("tm")
    odd = me % 2
    window, waves, seg, lag = tables(ns, nf)
    waves, seg, lag = jnp.asarray(waves), jnp.asarray(seg), jnp.asarray(lag)
    hann = jnp.asarray(window[None, :])
    response = jnp.sum(band_gain[:, None] * waves.astype(F32), axis=0, keepdims=True)
    swap = [(z, z ^ 1) for z in range(groups)]
    both = ("fibre", "tm")
    halo_pairs = [
        (b * groups + z, (b + (1 if z % 2 else -1)) % blocks * groups + z)
        for b in range(blocks)
        for z in range(groups)
    ]

    head = width * 5 // 8

    their_head = lax.ppermute(
        lax.dynamic_slice_in_dim(samples, (1 - odd) * width, head, 0), "tm", swap
    )
    flags = jnp.stack([dead_flags, section_ids])
    halo_flags = lax.ppermute(
        lax.dynamic_slice_in_dim(flags, odd * width, width, 1), both, halo_pairs
    )
    smem = pl.BlockSpec(memory_space=pltpu.SMEM)
    anywhere = pl.BlockSpec(memory_space=pl.ANY)
    sums, own_half, tail = pl.pallas_call(
        section_sums,
        out_shape=[
            jax.ShapeDtypeStruct((NSEC, wins, ns + LANE), F32),
            jax.ShapeDtypeStruct((width, wins, ns), BF16),
            jax.ShapeDtypeStruct((width - head, wins, ns), BF16),
        ],
        in_specs=[smem] * 3 + [anywhere],
        out_specs=[pl.BlockSpec(memory_space=pltpu.VMEM), anywhere, anywhere],
        scratch_shapes=[
            pltpu.VMEM(samples.shape, BF16),
            pltpu.SemaphoreType.DMA((STEPS,)),
            pltpu.SemaphoreType.DMA((2,)),
        ],
        compiler_params=pltpu.CompilerParams(vmem_limit_bytes=VMEM),
        cost_estimate=pl.CostEstimate(flops=1, bytes_accessed=1, transcendentals=0),
    )(odd[None], dead_flags, section_ids, samples)
    total, their_head = add_over(sums, "fibre", their_head)
    halo_source, halo_flags = lax.optimization_barrier((own_half, halo_flags))
    halo = lax.ppermute(halo_source, both, halo_pairs)
    total, response, own_half, tail = lax.optimization_barrier(
        (total, response, own_half, tail)
    )
    conv = pl.pallas_call(
        circulant_kernel,
        out_shape=jax.ShapeDtypeStruct((TILE, ns), BF16),
        compiler_params=pltpu.CompilerParams(vmem_limit_bytes=VMEM),
        cost_estimate=pl.CostEstimate(flops=1, bytes_accessed=1, transcendentals=0),
    )(response)
    their_total = lax.ppermute(total, "tm", swap)
    their_tail = lax.ppermute(tail, "tm", swap)
    their_second = lax.ppermute(own_half, "tm", swap)
    ready = (total, their_total, their_head, flags, hann, conv, seg, lag)
    ready = lax.optimization_barrier(ready)
    total, their_total, their_head, flags, hann, conv, seg, lag = ready
    halo_head = lax.ppermute(their_head, both, halo_pairs)

    side = odd[None]
    parts = (hann, conv, seg)
    every = jnp.concatenate([flags, halo_flags], axis=1)
    b0, series = segments(((0, (0, 0), (0, 0)),), side, flags, (total,), (samples,), None, *parts)
    b0, forward = lax.optimization_barrier((b0, their_tail))
    halo_tail = lax.ppermute(forward, both, halo_pairs)
    a, b2 = segments(
        (
            (1, (0, 0), (0, chans)),
            (1, (head, head), (head, chans + head)),
            (0, (width, width), (chans, chans)),
        ),
        side,
        every,
        (total, their_total),
        (their_head, their_tail, halo_head, halo_tail, halo),
        series,
        *parts,
    )
    scale = 2.0 / ns / LAGS / math.sqrt(nf * wins * groups)
    found = stacks(
        (
            (0, (0, width), (chans, width)),
            (0, (head, width + head), (chans + head, width + head)),
            (0, (width, 0), (width, 0)),
        ),
        groups,
        scale,
        me[None],
        every,
        their_total,
        (halo_head, halo_tail, their_head, their_tail, their_second),
        *(hann, conv, seg, lag),
        *(a, b0, b2),
    )
    lower, upper = [], []
    order = list(range(2, groups)) + [0, 1]
    for part in found:
        arrived = {}
        for d in order:
            pairs = [
                (b * groups + z, (b - z % 2) % blocks * groups + (z ^ d))
                for b in range(blocks)
                for z in range(groups)
            ]
            arrived[d] = lax.ppermute(part[d], both, pairs)
        for out, sides in ((lower, (0, 1)), (upper, (1, 0))):
            terms = [
                jnp.where(odd == 0, arrived[d + sides[0]], arrived[d + sides[1]]).astype(F32)
                for d in order[::2]
            ]
            out.append(sum(terms[1:], terms[0]))
    return jnp.concatenate(lower + upper, axis=0)


def solution(mesh):
    in_specs = (P("fibre", "tm", None), P(), P("fibre"), P("fibre"))
    out_specs = P("fibre", "tm", None)
    return jax.shard_map(shards, mesh=mesh, in_specs=in_specs, out_specs=out_specs, check_vma=False)
```

```python
import functools
import math

import jax
import jax.numpy as jnp
import ml_dtypes
import numpy as np
from jax import lax
from jax.experimental import pallas as pl
from jax.experimental.pallas import tpu as pltpu
from jax.sharding import PartitionSpec as P

OFFS = 128
LAGS = 128
NSEC = 2
LANE = 128
PART = 32
TILE = 256
STEPS = 4
TOGETHER = 4
VMEM = 63 * 1024 * 1024
NT = (((1,), (1,)), ((), ()))
F32 = jnp.float32
BF16 = jnp.bfloat16


def tables(ns, nf):
    tick = np.arange(ns)
    freq = np.arange(nf)
    window = 0.5 - 0.5 * np.cos(tick * (2.0 * math.pi / ns))
    waves = np.cos((freq[:, None] * tick[None, :] % ns) * (2.0 * math.pi / ns))
    waves[0] *= math.sqrt(0.5)
    size = 2 * LAGS
    bins = np.arange(size // 2)
    turn = math.pi / size * ((2 * bins[:, None] + 1) * np.arange(size)[None, :] % (2 * size))
    segment = np.stack([np.cos(turn), -np.sin(turn)], axis=1).reshape(size, size)
    lag = np.stack([np.cos(turn), -np.sin(turn)], axis=1).reshape(size, size)[:, :LAGS].T
    cast = lambda a: a.astype(np.float32).astype(ml_dtypes.bfloat16)
    return window.astype(np.float32), waves.astype(np.float32), cast(segment), cast(lag)


def section_sums(odd_ref, dead_ref, sec_ref, x_hbm, out_ref, half_hbm, tail_hbm, x, in_sem, sem):
    chans, wins, ns = x.shape
    width, length = half_hbm.shape[0], tail_hbm.shape[0]
    odd = odd_ref[0]
    part = chans // STEPS
    arriving = [
        pltpu.make_async_copy(
            x_hbm.at[pl.ds(n * part, part)], x.at[pl.ds(n * part, part)], in_sem.at[n]
        )
        for n in range(STEPS)
    ]
    for copy in arriving:
        copy.start()
    leaving = [
        pltpu.make_async_copy(x.at[pl.ds(odd * width, width)], half_hbm, sem.at[0]),
        pltpu.make_async_copy(
            x.at[pl.ds((2 - odd) * width - length, length)], tail_hbm, sem.at[1]
        ),
    ]

    def body(c, carry):
        value = x[c].astype(F32)
        live = 1 - dead_ref[c]
        sums, counts = carry
        weights = [jnp.where(sec_ref[c] == s, live, 0).astype(F32) for s in range(NSEC)]
        return (
            tuple(sums[s] + weights[s] * value for s in range(NSEC)),
            tuple(counts[s] + weights[s] for s in range(NSEC)),
        )

    zero = jnp.zeros((wins, ns), F32)
    carry = ((zero,) * NSEC, (jnp.float32(0),) * NSEC)
    for n, copy in enumerate(arriving):
        copy.wait()
        if n == STEPS - 1:
            for out in leaving:
                out.start()
        carry = lax.fori_loop(n * part, (n + 1) * part, body, carry, unroll=8)
    sums, counts = carry
    for s in range(NSEC):
        out_ref[s, :, :ns] = sums[s]
        out_ref[s, :, ns:] = jnp.zeros((wins, LANE), F32) + counts[s]
    for out in leaving:
        out.wait()


def circulant_kernel(filter_ref, out_ref):
    ns = filter_ref.shape[1]
    for t in range(0, TILE, 16):
        block = jnp.broadcast_to(filter_ref[...], (16, ns))
        out_ref[t : t + 16, :] = pltpu.roll(block, t, 1, stride=1, stride_axis=0).astype(BF16)


def segment_factors(places, odd, flag_ref, tot, x, hann, conv, seg, work, copied, first=None):
    common, clean, mass, square, rows, series_all, stage = work
    _, wins, ns = x[0].shape
    chans = sum(piece.shape[0] for piece in x)
    pitch = wins + 1
    size = seg.shape[0]
    half = size // 2
    blocks = ns // half
    jw = blocks * wins
    jpitch = jw + 1
    for copy in copied["first"]:
        copy.wait()
    for g in range(len(tot)):
        for s in range(NSEC):
            common[g * NSEC + s] = tot[g][s, :, :ns] / jnp.maximum(tot[g][s, :, ns : ns + 1], 1.0)
    sign = 1.0 - 2.0 * (lax.broadcasted_iota(jnp.int32, (chans, LANE), 1) % 2).astype(F32)

    for number, (group, base, flags) in enumerate(places):
        piece = x[number]
        length = piece.shape[0]
        base = base[0] + odd * (base[1] - base[0])
        flags = flags[0] + odd * (flags[1] - flags[0])

        def clean_channel(c):
            at = base + c
            flag = flags + c
            live = (1 - flag_ref[0, flag]).astype(F32)
            value = (piece[c].astype(F32) - common[group * NSEC + flag_ref[1, flag]]) * (
                hann[...] * live
            )
            tiles = [value[:, t * LANE : (t + 1) * LANE] for t in range(ns // LANE)]
            row = pl.ds(at * pitch, wins)
            mass[row, :] = sum(tiles[1:], tiles[0])
            square[row, :] = sum([tile * tile for tile in tiles[1:]], tiles[0] * tiles[0])
            for t, tile in enumerate(tiles):
                clean[t, row, :] = tile

        parts = copied["x"][number]
        part = length // len(parts)
        for n, copy in enumerate(parts):
            copy.wait()
            repeat(n * part, (n + 1) * part, clean_channel, 16)
    for copy in copied["tables"]:
        copy.wait()

    for step in range(wins // TOGETHER):
        series = series_all.at[step]
        for i in range(TOGETHER):
            window = pl.ds(step * TOGETHER + i, chans, stride=pitch)
            total = mass[window, :]
            lowest = jnp.sum(total, axis=1, keepdims=True)
            highest = jnp.sum(total * sign, axis=1, keepdims=True)
            power = 0.5 * jnp.sum(square[window, :], axis=1, keepdims=True)
            power = power + (lowest * lowest - highest * highest) * (0.5 / ns)
            level = lax.rsqrt(power + 1e-06)
            for t in range(ns // LANE):
                rows[i * chans : (i + 1) * chans, t * LANE : (t + 1) * LANE] = (
                    clean[t, window, :] * level
                ).astype(BF16)
        for t in range(0, ns, TILE):
            turned = jnp.concatenate([conv[:, ns - t :], conv[:, : ns - t]], axis=1) if t else conv[...]
            series[half // 2 + t : half // 2 + t + TILE, :] = lax.dot_general(
                turned, rows[...], NT, preferred_element_type=F32
            ).astype(BF16)
        series[: half // 2, :] = series[ns : ns + half // 2, :]
        series[ns + half // 2 :, :] = series[half // 2 : half, :]

        def place(which, j, value):
            for i in range(TOGETHER):
                at = j * wins + step * TOGETHER + i
                stage[which, pl.ds(at, size, stride=jpitch), :] = value[
                    :, i * chans : (i + 1) * chans
                ]

        for j in range(blocks):
            start = j * half + half // 2
            b = jnp.dot(
                seg[:, :half], series[start : start + half, :], preferred_element_type=F32
            )
            place(1, j, b)

        if first is not None:
            source = first(step, series)
            for j in range(blocks):
                a = jnp.dot(
                    seg[...], source[j * half : j * half + size, :], preferred_element_type=F32
                )
                place(0, j, a)

    def parts(which, k):
        return [
            stage[which, pl.ds((2 * k + part) * jpitch, jw), :].astype(BF16) for part in range(2)
        ]

    lower = lax.broadcasted_iota(jnp.int32, (1, chans), 1) < chans // 2

    def first_factor(k):
        real, imag = parts(0, k)
        return jnp.concatenate(
            [jnp.where(lower, imag, real), jnp.where(lower, real, imag)], axis=0
        ).T

    return first_factor, lambda k: jnp.concatenate(parts(1, k), axis=0)


def work_shapes(groups, chans, wins, ns):
    half = LAGS
    rows = 2 * half * (ns // half * wins + 1)
    return [
        pltpu.VMEM((groups * NSEC, wins, ns), F32),
        pltpu.VMEM((ns // LANE, chans * (wins + 1), LANE), F32),
        pltpu.VMEM((chans * (wins + 1), LANE), F32),
        pltpu.VMEM((chans * (wins + 1), LANE), F32),
        pltpu.VMEM((TOGETHER * chans, ns), BF16),
        pltpu.VMEM((wins // TOGETHER, ns + half, TOGETHER * chans), BF16),
        pltpu.VMEM((2, rows, chans), F32),
    ]


def repeat(start, stop, body, together):
    def step(n, _):
        body(n)
        return 0

    lax.fori_loop(start, stop, step, 0, unroll=math.gcd(together, stop - start))


class Choice:
    def __init__(self, odd, sources, target, sem):
        self.options = [
            (odd == side, pltpu.make_async_copy(source, target, sem))
            for side, source in enumerate(sources)
        ]

    def start(self):
        for here, copy in self.options:
            pl.when(here)(copy.start)

    def wait(self):
        for here, copy in self.options:
            pl.when(here)(copy.wait)


def input_copies(odd, first, x, tables_in, sem):
    copied = {"first": [], "x": [], "tables": []}
    used = 0

    def copy(source, target):
        nonlocal used
        if isinstance(source, tuple):
            made = Choice(odd, source, target, sem.at[used])
        else:
            made = pltpu.make_async_copy(source, target, sem.at[used])
        made.start()
        used += 1
        return made

    copied["first"] = [copy(*pair) for pair in first]
    for source, target in x:
        parts = max(target.shape[0] // PART, 1)
        part = target.shape[0] // parts
        rows = [pl.ds(n * part, part) for n in range(parts)]
        copied["x"].append(
            [
                copy(
                    tuple(option.at[here] for option in source)
                    if isinstance(source, tuple)
                    else source.at[here],
                    target.at[here],
                )
                for here in rows
            ]
        )
    copied["tables"] = [copy(*pair) for pair in tables_in]
    return copied


def own_kernel(places, odd_ref, flag_ref, *rest):
    tot_hbm, x_hbm, hann_hbm, conv_hbm, seg_hbm, b_hbm, p_hbm = rest[:7]
    tot, x, hann, conv, seg = rest[7:12]
    work, (b_out, in_sem, out_sem, p_sem) = rest[12:-4], rest[-4:]
    odd = odd_ref[0]
    copied = input_copies(
        odd,
        [(tot_hbm, tot), (hann_hbm, hann)],
        [(x_hbm, x)],
        [(conv_hbm, conv), (seg_hbm, seg)],
        in_sem,
    )
    _, second = segment_factors(
        places, odd, flag_ref, [tot], [x], hann, conv, seg, work, copied
    )

    def put_second(k, stage):
        stage[k] = second(k)

    kept = pltpu.make_async_copy(work[-2], p_hbm, p_sem)
    kept.start()
    send_factor(put_second, b_out, b_hbm, out_sem)
    kept.wait()


def send_factor(factor, stage, target, sem):
    step = stage.shape[0] // STEPS
    copies = []
    for n in range(STEPS):
        part = pl.ds(n * step, step)

        repeat(n * step, (n + 1) * step, lambda k: factor(k, stage), 32)
        copies.append(pltpu.make_async_copy(stage.at[part], target.at[part], sem.at[n]))
        copies[-1].start()
    for copy in copies:
        copy.wait()


def second_kernel(places, odd_ref, flag_ref, *rest):
    tot_hbm, (even_hbm, odd_hbm), rest = rest[:2], (rest[2:4], rest[4:6]), rest[6:]
    halo_hbm, hann_hbm, conv_hbm, seg_hbm, p_hbm, a_hbm, b_hbm = rest[:7]
    tot, x, rest = rest[7:9], rest[9:12], rest[12:]
    hann, conv, seg, own, mixed, a_out, b_out = rest[:7]
    work, (in_sem, p_sem, out_sem) = rest[7:-3], rest[-3:]
    odd = odd_ref[0]
    copied = input_copies(
        odd,
        list(zip(tot_hbm, tot)) + [(hann_hbm, hann)],
        list(zip(zip(even_hbm, odd_hbm), x)) + [(halo_hbm, x[2])],
        [(conv_hbm, conv), (seg_hbm, seg)],
        in_sem,
    )
    kept = pltpu.make_async_copy(p_hbm, own, p_sem)
    kept.start()
    copied["tables"].append(kept)
    chans = b_out.shape[2]
    lane = lax.broadcasted_iota(jnp.int32, (1, chans), 1)

    def first(step, series):
        @pl.when(odd == 1)
        def _():
            mixed[...] = series[...]

        @pl.when(odd == 0)
        def _():
            for i in range(TOGETHER):
                columns = slice(i * chans, (i + 1) * chans)
                value = own[step, :, columns]
                turned = jnp.concatenate([value[:, chans // 2 :], value[:, : chans // 2]], axis=1)
                mixed[:, columns] = jnp.where(lane < chans // 2, series[:, columns], turned)

        return mixed

    first_factor, second_factor = segment_factors(
        places, odd, flag_ref, tot, x, hann, conv, seg, work, copied, first
    )

    def both_factors(k, stage):
        value = first_factor(k)
        width = value.shape[0] // 2
        a_out[k, 1] = value[:width]
        a_out[k, 0] = value[width:]
        stage[k] = second_factor(k)

    step = b_out.shape[0] // STEPS
    copies = []
    for n in range(STEPS):
        part = pl.ds(n * step, step)

        repeat(n * step, (n + 1) * step, lambda k: both_factors(k, b_out), 32)
        for m, (source, target) in enumerate(((a_out, a_hbm), (b_out, b_hbm))):
            copies.append(
                pltpu.make_async_copy(source.at[part], target.at[part], out_sem.at[2 * n + m])
            )
            copies[-1].start()
    for copy in copies:
        copy.wait()


def segments(places, side, flags, totals, pieces, series, hann, conv, seg):
    chans = LANE
    _, wins, ns = pieces[0].shape
    size = seg.shape[0]
    half = size // 2
    depth = ns // half * wins * 2
    smem = pl.BlockSpec(memory_space=pltpu.SMEM)
    anywhere = pl.BlockSpec(memory_space=pl.ANY)
    b_shape = jax.ShapeDtypeStruct((half, depth, chans), BF16)
    p_shape = jax.ShapeDtypeStruct((wins // TOGETHER, ns + half, TOGETHER * chans), BF16)
    a_shape = jax.ShapeDtypeStruct((half, 2, chans // 2, depth), BF16)
    scratch = lambda *values: [pltpu.VMEM(value.shape, value.dtype) for value in values]
    operands = list(totals) + list(pieces) + [hann, conv, seg]
    count = len(operands) + chans // PART
    if series is None:
        kernel, out = own_kernel, [b_shape, p_shape]
        held = scratch(*operands)
        last = scratch(b_shape) + [
            pltpu.SemaphoreType.DMA((count,)),
            pltpu.SemaphoreType.DMA((STEPS,)),
            pltpu.SemaphoreType.DMA,
        ]
    else:
        kernel, out = second_kernel, [a_shape, b_shape]
        held = scratch(*totals, pieces[0], pieces[1], pieces[4], hann, conv, seg, series)
        held += [pltpu.VMEM(p_shape.shape[1:], BF16)] + scratch(a_shape, b_shape)
        last = [
            pltpu.SemaphoreType.DMA((count,)),
            pltpu.SemaphoreType.DMA,
            pltpu.SemaphoreType.DMA((2 * STEPS,)),
        ]
        operands.append(series)
    return pl.pallas_call(
        functools.partial(kernel, places),
        out_shape=out,
        in_specs=[smem] * 2 + [anywhere] * len(operands),
        out_specs=[anywhere] * 2,
        scratch_shapes=held + work_shapes(len(totals), chans, wins, ns) + last,
        compiler_params=pltpu.CompilerParams(vmem_limit_bytes=VMEM),
        cost_estimate=pl.CostEstimate(
            flops=2 * wins * chans * ns * (ns + 3 * size),
            bytes_accessed=16 * 1024 * 1024,
            transcendentals=0,
        ),
    )(side, flags, *operands)


def correlate(first, count, scale, shares, me, a, b0, b2, b3, lag, cross, one, outs, bins_loop):
    depth, chans = b0.shape[1:]
    width = chans // 2
    nfr = lag.shape[1]
    pitch = nfr + 1
    odd = lax.rem(me, 2)
    lane = lax.broadcasted_iota(jnp.int32, (1, chans), 1)
    low, high = [jnp.where((lane < width) == (g == 0), 1.0, 0.0).astype(BF16) for g in range(2)]
    lower = lane < width

    def bins_with(near, far):
        def one_bin(k):
            inner = near[k] * low + b3[k] * high if near is not b3 else b3[k]
            own = jnp.concatenate([b0[k], b2[k] * high], axis=1)
            theirs = jnp.concatenate([inner, far[k] * low], axis=1)
            part = depth // 2
            right = jnp.concatenate([own[:part], theirs[:part], theirs[part:], own[part:]], axis=0)
            real = jnp.where(lower, a[k, 0], a[k, 1])
            imag = jnp.where(lower, a[k, 1], a[k, 0])
            turn = lambda v: jnp.concatenate([v[:, part:], v[:, :part]], axis=1)
            left = jnp.concatenate(
                [
                    jnp.concatenate([real, imag], axis=1),
                    jnp.concatenate([turn(imag), -turn(real)], axis=1),
                ],
                axis=0,
            )
            value = jnp.dot(left, right, preferred_element_type=F32)
            for p in range(2):
                for t in range(2):
                    cross[t, pl.ds(2 * k + p, count, stride=pitch), :] = value[
                        p * count : (p + 1) * count, t * chans : (t + 1) * chans
                    ]

        bins_loop(one_bin)

    pl.when(odd == 0)(lambda: bins_with(b2, b3))
    pl.when(odd == 1)(lambda: bins_with(b3, b2))

    row = lax.broadcasted_iota(jnp.int32, one.shape[1:], 0)
    column = lax.broadcasted_iota(jnp.int32, one.shape[1:], 1)
    turned = jnp.where(row < width, row + chans, row - width)
    place = row + (turned - row) * odd
    for t in range(2):
        here = column + t * chans
        found = (place == here) | ((here >= chans + width) & (place == here - width))
        one[t] = jnp.where(found, 1.0, 0.0)
    share = OFFS // shares

    def one_channel(c):
        value = jnp.concatenate(
            [cross[t, pl.ds(c * pitch, nfr), :] for t in range(2)], axis=1
        ).astype(BF16)
        starts = [first + c + 1 + share * (me ^ d) for d in range(shares)]
        pick = jnp.concatenate(
            [
                jnp.concatenate([one[t, pl.ds(start, share), :] for start in starts], axis=0)
                for t in range(2)
            ],
            axis=1,
        ).astype(BF16)
        lagged = jnp.dot(lag[...], value, preferred_element_type=F32) * scale
        band = lax.dot_general(pick, lagged.astype(BF16), NT, preferred_element_type=F32)
        for d, out in enumerate(outs):
            out[c] = band[d * share : (d + 1) * share, :].astype(BF16)

    repeat(0, count, one_channel, 16)


def last_kernel(places, scale, shares, me_ref, flag_ref, *rest):
    even_hbm, odd_hbm, late_hbm, rest = rest[:2], rest[2:4], rest[4], rest[5:]
    tot_hbm, hann_hbm, conv_hbm, seg_hbm, lag_hbm = rest[:5]
    a_hbm, b0_hbm, b2_hbm, rest = *rest[5:8], rest[8:]
    outs, b3_hbm, rest = rest[:shares], rest[shares], rest[shares + 1 :]
    x, rest = rest[:3], rest[3:]
    tot, hann, conv, seg, lag, b0, b2 = rest[:7]
    work, (a, b3, one, in_sem, late_sem, out_sem) = rest[7:-6], rest[-6:]
    me = me_ref[0]
    odd = lax.rem(me, 2)
    copied = input_copies(
        odd,
        [(tot_hbm, tot), (hann_hbm, hann)],
        list(zip(zip(even_hbm, odd_hbm), x)) + [(late_hbm, x[2])],
        [(conv_hbm, conv), (seg_hbm, seg), (lag_hbm, lag)],
        in_sem,
    )
    count = a.shape[2]
    late = [
        pltpu.make_async_copy(source, target, late_sem.at[n])
        for n, (source, target) in enumerate(
            ((b0_hbm, b0), (b2_hbm, b2), (a_hbm.at[:, :, pl.ds(0, count)], a))
        )
    ]
    for copy in late:
        copy.start()
    _, second_factor = segment_factors(
        places, odd, flag_ref, [tot], x, hann, conv, seg, work, copied
    )
    bins = b3.shape[0]

    def second(k):
        b3[k] = second_factor(k)

    repeat(0, bins, second, 32)
    kept = pltpu.make_async_copy(b3, b3_hbm, out_sem)
    kept.start()
    for copy in late:
        copy.wait()
    correlate(
        *(0, count, scale, shares, me, a, b0, b2, b3, lag, work[-1], one, outs),
        lambda one_bin: repeat(0, bins, one_bin, 32),
    )
    kept.wait()


def rest_kernel(first, scale, shares, me_ref, *rest):
    lag_hbm, a_hbm, b0_hbm, b2_hbm, b3_hbm = rest[:5]
    outs, rest = rest[5 : 5 + shares], rest[5 + shares :]
    lag, a, b0, b2, b3, cross, one, lag_sem, sem = rest
    bins, count = b0.shape[0], a.shape[2]
    some = bins // STEPS

    def factors(n):
        part = pl.ds(n * some, some)
        return [
            pltpu.make_async_copy(source, target, sem.at[n, m])
            for m, (source, target) in enumerate(
                (
                    (b0_hbm.at[part], b0.at[part]),
                    (b2_hbm.at[part], b2.at[part]),
                    (b3_hbm.at[part], b3.at[part]),
                    (a_hbm.at[part, :, pl.ds(first, count)], a.at[part]),
                )
            )
        ]

    for n in range(STEPS):
        for copy in factors(n):
            copy.start()
    table = pltpu.make_async_copy(lag_hbm, lag, lag_sem)
    table.start()
    table.wait()

    def bins_loop(one_bin):
        def part(n, _):
            for copy in factors(n):
                copy.wait()
            repeat(0, some, lambda k: one_bin(n * some + k), some)
            return 0

        lax.fori_loop(0, STEPS, part, 0)

    correlate(first, count, scale, shares, me_ref[0], a, b0, b2, b3, lag, cross, one, outs, bins_loop)


def stacks(places, shares, scale, me, flags, total, pieces, hann, conv, seg, lag, a, b0, b2):
    bins, depth, chans = b0.shape
    width = chans // 2
    count = width // 2
    _, wins, ns = pieces[0].shape
    nlag, nfr = lag.shape
    smem = pl.BlockSpec(memory_space=pltpu.SMEM)
    vmem = pl.BlockSpec(memory_space=pltpu.VMEM)
    anywhere = pl.BlockSpec(memory_space=pl.ANY)
    out = [jax.ShapeDtypeStruct((count, OFFS // shares, nlag), BF16)] * shares
    operands = [*pieces, total, hann, conv, seg, lag, a, b0, b2]
    held = [pieces[0], pieces[1], pieces[4], total, hann, conv, seg, lag, b0, b2]
    some_a = pltpu.VMEM((bins, 2, count, depth), BF16)
    one = pltpu.VMEM((2, chans + width, chans), F32)
    params = pltpu.CompilerParams(vmem_limit_bytes=VMEM)
    cost = pl.CostEstimate(
        flops=2 * count * bins * 4 * (2 * depth * chans + 2 * OFFS * chans),
        bytes_accessed=20 * 1024 * 1024,
        transcendentals=0,
    )
    *head, b3 = pl.pallas_call(
        functools.partial(last_kernel, places, scale, shares),
        out_shape=out + [jax.ShapeDtypeStruct(b0.shape, BF16)],
        in_specs=[smem] * 2 + [anywhere] * len(operands),
        out_specs=[vmem] * shares + [anywhere],
        scratch_shapes=[pltpu.VMEM(value.shape, value.dtype) for value in held]
        + work_shapes(1, chans, wins, ns)
        + [
            some_a,
            pltpu.VMEM(b0.shape, BF16),
            one,
            pltpu.SemaphoreType.DMA((8 + chans // PART,)),
            pltpu.SemaphoreType.DMA((3,)),
            pltpu.SemaphoreType.DMA,
        ],
        compiler_params=params,
        cost_estimate=cost,
    )(me, flags, *operands)
    tail = pl.pallas_call(
        functools.partial(rest_kernel, count, scale, shares),
        out_shape=out,
        in_specs=[smem] + [anywhere] * 5,
        out_specs=[vmem] * shares,
        scratch_shapes=[
            pltpu.VMEM(lag.shape, BF16),
            some_a,
            *[pltpu.VMEM(b0.shape, BF16)] * 3,
            pltpu.VMEM((2, count * (nfr + 1), chans), F32),
            one,
            pltpu.SemaphoreType.DMA,
            pltpu.SemaphoreType.DMA((STEPS, 4)),
        ],
        compiler_params=params,
        cost_estimate=cost,
    )(me, lag, a, b0, b2, b3)
    return head, tail


def add_over(value, axis, beside):
    count = lax.axis_size(axis)
    if count & (count - 1):
        return lax.psum(value, axis), beside
    bit = 1
    while bit < count:
        steps = [bit] if bit == 1 or 2 * bit == count else [bit, 2 * bit, 3 * bit]
        arrived = [lax.ppermute(value, axis, [(i, i ^ s) for i in range(count)]) for s in steps]
        bit *= 1 + len(steps)
        if bit == count:
            arrived, beside = lax.optimization_barrier((arrived, beside))
        value = sum(arrived, value)
    return value, beside


def shards(samples, band_gain, dead_flags, section_ids):
    chans, wins, ns = samples.shape
    nf = ns // 2
    width = chans // 2
    blocks = lax.axis_size("fibre")
    groups = lax.axis_size("tm")
    me = lax.axis_index("tm")
    odd = me % 2
    window, waves, seg, lag = tables(ns, nf)
    waves, seg, lag = jnp.asarray(waves), jnp.asarray(seg), jnp.asarray(lag)
    hann = jnp.asarray(window[None, :])
    response = jnp.sum(band_gain[:, None] * waves, axis=0, keepdims=True)
    swap = [(z, z ^ 1) for z in range(groups)]
    both = ("fibre", "tm")
    halo_pairs = [
        (b * groups + z, (b + (1 if z % 2 else -1)) % blocks * groups + z)
        for b in range(blocks)
        for z in range(groups)
    ]

    head = width * 5 // 8

    their_head = lax.ppermute(
        lax.dynamic_slice_in_dim(samples, (1 - odd) * width, head, 0), "tm", swap
    )
    flags = jnp.stack([dead_flags, section_ids])
    halo_flags = lax.ppermute(
        lax.dynamic_slice_in_dim(flags, odd * width, width, 1), both, halo_pairs
    )
    smem = pl.BlockSpec(memory_space=pltpu.SMEM)
    anywhere = pl.BlockSpec(memory_space=pl.ANY)
    sums, own_half, tail = pl.pallas_call(
        section_sums,
        out_shape=[
            jax.ShapeDtypeStruct((NSEC, wins, ns + LANE), F32),
            jax.ShapeDtypeStruct((width, wins, ns), BF16),
            jax.ShapeDtypeStruct((width - head, wins, ns), BF16),
        ],
        in_specs=[smem] * 3 + [anywhere],
        out_specs=[pl.BlockSpec(memory_space=pltpu.VMEM), anywhere, anywhere],
        scratch_shapes=[
            pltpu.VMEM(samples.shape, BF16),
            pltpu.SemaphoreType.DMA((STEPS,)),
            pltpu.SemaphoreType.DMA((2,)),
        ],
        compiler_params=pltpu.CompilerParams(vmem_limit_bytes=VMEM),
        cost_estimate=pl.CostEstimate(flops=1, bytes_accessed=1, transcendentals=0),
    )(odd[None], dead_flags, section_ids, samples)
    total, their_head = add_over(sums, "fibre", their_head)
    halo_source, halo_flags = lax.optimization_barrier((own_half, halo_flags))
    halo = lax.ppermute(halo_source, both, halo_pairs)
    total, response, own_half, tail = lax.optimization_barrier(
        (total, response, own_half, tail)
    )
    conv = pl.pallas_call(
        circulant_kernel,
        out_shape=jax.ShapeDtypeStruct((TILE, ns), BF16),
        compiler_params=pltpu.CompilerParams(vmem_limit_bytes=VMEM),
        cost_estimate=pl.CostEstimate(flops=1, bytes_accessed=1, transcendentals=0),
    )(response)
    their_total = lax.ppermute(total, "tm", swap)
    their_tail = lax.ppermute(tail, "tm", swap)
    their_second = lax.ppermute(own_half, "tm", swap)
    ready = (total, their_total, their_head, flags, hann, conv, seg, lag)
    ready = lax.optimization_barrier(ready)
    total, their_total, their_head, flags, hann, conv, seg, lag = ready
    halo_head = lax.ppermute(their_head, both, halo_pairs)

    side = odd[None]
    parts = (hann, conv, seg)
    every = jnp.concatenate([flags, halo_flags], axis=1)
    b0, series = segments(((0, (0, 0), (0, 0)),), side, flags, (total,), (samples,), None, *parts)
    b0, forward = lax.optimization_barrier((b0, their_tail))
    halo_tail = lax.ppermute(forward, both, halo_pairs)
    a, b2 = segments(
        (
            (1, (0, 0), (0, chans)),
            (1, (head, head), (head, chans + head)),
            (0, (width, width), (chans, chans)),
        ),
        side,
        every,
        (total, their_total),
        (their_head, their_tail, halo_head, halo_tail, halo),
        series,
        *parts,
    )
    scale = 2.0 / ns / LAGS / math.sqrt(nf * wins * groups)
    found = stacks(
        (
            (0, (0, width), (chans, width)),
            (0, (head, width + head), (chans + head, width + head)),
            (0, (width, 0), (width, 0)),
        ),
        groups,
        scale,
        me[None],
        every,
        their_total,
        (halo_head, halo_tail, their_head, their_tail, their_second),
        *(hann, conv, seg, lag),
        *(a, b0, b2),
    )
    lower, upper = [], []
    order = list(range(2, groups)) + [0, 1]
    for part in found:
        arrived = {}
        for d in order:
            pairs = [
                (b * groups + z, (b - z % 2) % blocks * groups + (z ^ d))
                for b in range(blocks)
                for z in range(groups)
            ]
            arrived[d] = lax.ppermute(part[d], both, pairs)
        for out, sides in ((lower, (0, 1)), (upper, (1, 0))):
            terms = [
                jnp.where(odd == 0, arrived[d + sides[0]], arrived[d + sides[1]]).astype(F32)
                for d in order[::2]
            ]
            out.append(sum(terms[1:], terms[0]))
    return jnp.concatenate(lower + upper, axis=0)


def solution(mesh):
    in_specs = (P("fibre", "tm", None), P(), P("fibre"), P("fibre"))
    out_specs = P("fibre", "tm", None)
    return jax.shard_map(shards, mesh=mesh, in_specs=in_specs, out_specs=out_specs, check_vma=False)
```
